32 devices in a mesh: section: 2 (over core), dp: 4 (over y, x), tensor: 4 (over z).
Axes of the slice: x: 2, y: 2, z: 4, core: 2. Of those that a mesh axis runs over, the one named last changes fastest.
Arguments:
- inputs: bfloat16 [8192, 1024], P('dp'), may hold values from -6 to 6
- out_grad: bfloat16 [8192, 1024], P('dp'), may hold values from -6 to 6
- w_query: bfloat16 [2, 1024, 1024], P('section', None, 'tensor'), may hold values from -0.1875 to 0.1875
- w_latent: bfloat16 [2, 1024, 512], P('section'), may hold values from -0.1875 to 0.1875
- w_key_up: bfloat16 [2, 256, 1024], P('section', None, 'tensor'), may hold values from -0.375 to 0.375
- w_value_up: bfloat16 [2, 256, 1024], P('section', None, 'tensor'), may hold values from -0.375 to 0.375
- w_out: bfloat16 [2, 1024, 1024], P('section', 'tensor'), may hold values from -3 to 3
- w_gate: bfloat16 [2, 1024, 2816], P('section', None, 'tensor'), may hold values from -0.1875 to 0.1875
- w_up: bfloat16 [2, 1024, 2816], P('section', None, 'tensor'), may hold values from -0.1875 to 0.1875
- w_down: bfloat16 [2, 2816, 1024], P('section', 'tensor'), may hold values from -0.109375 to 0.109375
- norm_attn: float32 [2, 1024], P('section'), may hold values from 0.1 to 1.9
- norm_mlp: float32 [2, 1024], P('section'), may hold values from 0.1 to 1.9
Outputs:
- layer_out: bfloat16 [2, 8192, 1024], P('section', 'dp')
- input_grad: bfloat16 [2, 8192, 1024], P('section', 'dp')
- grad_query: float32 [2, 1024, 1024], P('section', None, 'tensor')
- grad_latent: float32 [2, 1024, 512], P('section', 'tensor')
- grad_key_up: float32 [2, 256, 1024], P('section', None, 'tensor')
- grad_value_up: float32 [2, 256, 1024], P('section', None, 'tensor')
- grad_out: float32 [2, 1024, 1024], P('section', 'tensor')
- grad_gate: float32 [2, 1024, 2816], P('section', None, 'tensor')
- grad_up: float32 [2, 1024, 2816], P('section', None, 'tensor')
- grad_down: float32 [2, 2816, 1024], P('section', 'tensor')
- grad_norm_attn: float32 [2, 1024], P('section', 'tensor')
- grad_norm_mlp: float32 [2, 1024], P('section', 'tensor')
The draws below stay inside these ranges and needn't reach their ends.
All inputs are finite; a program needn't handle non-finite values.
Results may differ from the reference program's by a relative error of at most 0.035.
Values may be sent and summed in bfloat16 or wider, within the bound.
A program may use at most 256 MiB of HBM per device.

```python
from functools import partial
import jax
import jax.numpy as jnp
from jax import lax

D = 1024
QH = 16
HD = 64
KVH = 2
LH = 256
FF = 2816
LEN = 1024
TOKENS = 8192
LAYERS = 2


def levels(rng, dims, split, low, high):
    loudness, own = 1.0, jax.random.fold_in(rng, 6)
    for axis_at, shards_of in split:
        heights = jnp.exp(jax.random.uniform(jax.random.fold_in(own, axis_at), (shards_of,), jnp.float32, low / len(split), high / len(split)))
        loudness = loudness * jnp.repeat(heights, dims[axis_at] // shards_of).reshape([-1 if axis == axis_at else 1 for axis in range(len(dims))])
    return loudness


def noise(key, dims, scale, bound, pieces=(), held_as=jnp.bfloat16):
    drawn = scale * jax.random.normal(key, dims, jnp.float32)
    if pieces:
        drawn = drawn * levels(key, dims, pieces, -0.22, 0.18)
    return jnp.clip(drawn, -bound, bound).astype(held_as)


def setup_inputs(seed: int = 0) -> dict:
    streams_of = jax.random.split(jax.random.key(seed), 13)
    return {
        "inputs": noise(streams_of[0], (TOKENS, D), 1.0, 6.0, ((0, 4),)),
        "out_grad": noise(streams_of[1], (TOKENS, D), 1.0, 6.0, ((0, 4),)),
        "w_query": noise(streams_of[2], (LAYERS, D, QH * HD), D ** -0.5, 0.1875, ((0, 2), (2, 4))),
        "w_latent": noise(streams_of[3], (LAYERS, D, KVH * LH), D ** -0.5, 0.1875, ((0, 2),)),
        "w_key_up": noise(streams_of[4], (LAYERS, LH, QH * HD), LH ** -0.5, 0.375, ((0, 2), (2, 4))),
        "w_value_up": noise(streams_of[5], (LAYERS, LH, QH * HD), LH ** -0.5, 0.375, ((0, 2), (2, 4))),
        "w_out": noise(streams_of[6], (LAYERS, QH * HD, D), (max(1, QH * HD * 4 // LEN)) ** -0.5, 3.0, ((0, 2), (1, 4))),
        "w_gate": noise(streams_of[7], (LAYERS, D, FF), D ** -0.5, 0.1875, ((0, 2), (2, 4))),
        "w_up": noise(streams_of[8], (LAYERS, D, FF), D ** -0.5, 0.1875, ((0, 2), (2, 4))),
        "w_down": noise(streams_of[9], (LAYERS, FF, D), FF ** -0.5, 0.109375, ((0, 2), (1, 4))),
        "norm_attn": jnp.clip(1.0 + 0.18 * jax.random.normal(streams_of[10], (LAYERS, D), jnp.float32), 0.1, 1.9),
        "norm_mlp": jnp.clip(1.0 + 0.18 * jax.random.normal(streams_of[11], (LAYERS, D), jnp.float32), 0.1, 1.9),
    }


norm_epsilon = 1e-05
highest = lax.Precision.HIGHEST

@jax.custom_vjp
def low(v):
    return lax.optimization_barrier(v.astype(jnp.bfloat16)).astype(jnp.float32)

@jax.custom_vjp
def low_back(v):
    return v

def low_keep(v):
    return (low(v), None)

def low_pass(kept, grad):
    return (grad,)

def back_keep(v):
    return (v, None)

def back_low(kept, grad):
    return (low(grad),)
low.defvjp(low_keep, low_pass)
low_back.defvjp(back_keep, back_low)

def matmul(left_side, right_side):
    return jnp.dot(left_side, right_side, precision=highest, preferred_element_type=jnp.float32)

def rms_scale(features):
    return features * lax.rsqrt(lax.optimization_barrier(jnp.mean(features * features, axis=-1, keepdims=True)) + norm_epsilon)

def attend_block(query_block, keys_seen, values_seen, first_row):
    scores = jnp.einsum('qhd,khd->hqk', query_block, keys_seen, precision=highest)
    scores = low_back(scores * HD ** (-0.5))
    key_places = jnp.arange(keys_seen.shape[0])
    query_places = first_row + jnp.arange(query_block.shape[0])
    allowed = key_places[None, :] <= query_places[:, None]
    scores = jnp.where(allowed[None], scores, -jnp.inf)
    attn_probs = low(jax.nn.softmax(scores, axis=-1))
    return jnp.einsum('hqk,khd->qhd', attn_probs, values_seen, precision=highest)

def layer(layer_input, weights):
    w_query, w_latent, w_key_up, w_value_up, w_out, w_gate, w_up, w_down, norm_attn, norm_mlp = weights
    source = low_back(layer_input)
    attn_in = low(rms_scale(source) * norm_attn)
    queries = low_back(low(matmul(attn_in, w_query)))
    latents = low(matmul(attn_in, w_latent))
    group_width = QH // KVH * HD
    key_parts = []
    value_parts = []
    for group_index in range(KVH):
        latent_group = latents[:, group_index * LH:(group_index + 1) * LH]
        columns = slice(group_index * group_width, (group_index + 1) * group_width)
        key_parts.append(matmul(latent_group, w_key_up[:, columns]))
        value_parts.append(matmul(latent_group, w_value_up[:, columns]))
    key_rows = low_back(low(jnp.concatenate(key_parts, axis=1)))
    value_rows = low_back(low(jnp.concatenate(value_parts, axis=1)))
    row_count = source.shape[0]
    query_heads = queries.reshape(row_count, QH, HD)
    key_heads = key_rows.reshape(row_count, QH, HD)
    value_heads = value_rows.reshape(row_count, QH, HD)
    block_rows = min(512, LEN)
    outputs = []
    for block_start in range(0, row_count, block_rows):
        block_end = block_start + block_rows
        block_fn = jax.checkpoint(partial(attend_block, first_row=block_start))
        outputs.append(block_fn(query_heads[block_start:block_end], key_heads[:block_end], value_heads[:block_end]))
    heads_out = low_back(low(jnp.concatenate(outputs, axis=0).reshape(row_count, QH * HD)))
    residual = source + low_back(matmul(heads_out, w_out))
    mlp_in = low(rms_scale(residual) * norm_mlp)
    gate_values = low_back(matmul(mlp_in, w_gate))
    up_values = low_back(matmul(mlp_in, w_up))
    hidden = low(jax.nn.silu(gate_values) * up_values)
    return residual + low_back(matmul(hidden, w_down))

def reference(inputs, out_grad, w_query, w_latent, w_key_up, w_value_up, w_out, w_gate, w_up, w_down, norm_attn, norm_mlp):
    params = tuple((weight.astype(jnp.float32) for weight in (w_query, w_latent, w_key_up, w_value_up, w_out, w_gate, w_up, w_down, norm_attn, norm_mlp)))
    sequence_count = inputs.shape[0] // LEN
    sequences = inputs.astype(jnp.float32).reshape(sequence_count, LEN, D)
    cotangents = out_grad.astype(jnp.float32).reshape(sequence_count, LEN, D)

    def both_layers(weights, first_input, offset):
        first_layer = tuple((weight[0] for weight in weights))
        second_layer = tuple((weight[1] for weight in weights))
        first_output = low(layer(first_input, first_layer))
        second_output = low(layer(first_output + offset, second_layer))
        return (first_output, second_output)

    def one_sequence(totals, pair_item):
        sequence, cotangent = pair_item
        zero_field = jnp.zeros_like(sequence)
        outputs_pair, pullback = jax.vjp(both_layers, params, sequence, zero_field)
        weight_grads, grad_first, grad_second = pullback((zero_field, cotangent))
        totals = jax.tree.map(lambda running, update: running + update, totals, weight_grads)
        return (totals, (outputs_pair[0], outputs_pair[1], grad_first, grad_second))
    start_totals = tuple((jnp.zeros_like(weight) for weight in params))
    totals, collected = lax.scan(one_sequence, start_totals, (sequences, cotangents))
    first_output, second_output, grad_first, grad_second = collected
    layer_out = jnp.stack([first_output.reshape(-1, D), second_output.reshape(-1, D)]).astype(jnp.bfloat16)
    input_grad = jnp.stack([grad_first.reshape(-1, D), grad_second.reshape(-1, D)]).astype(jnp.bfloat16)
    return (layer_out, input_grad, totals[0], totals[1], totals[2], totals[3], totals[4], totals[5], totals[6], totals[7], totals[8], totals[9])
```

```python
import functools
import math

import jax
import jax.numpy as jnp
from jax import lax
from jax.experimental import pallas as pl
from jax.experimental.pallas import tpu as pltpu
from jax.sharding import PartitionSpec as P

QH = 16
HD = 64
KVH = 2
LH = 256
LEN = 1024
EPS = 1e-05
F32 = jnp.float32
BF16 = jnp.bfloat16
SEC, DP, TEN = "section", "dp", "tensor"
LOG2_SCALE = HD**-0.5 * math.log2(math.e)
KEY_ROWS = 256


def mm(left, right, left_dim=1, right_dim=0):
    dims = (((left_dim,), (right_dim,)), ((), ()))
    return lax.dot_general(left, right, dims, preferred_element_type=F32)


def head_masks(width):
    if width == HD:
        return [None]
    lane = lax.broadcasted_iota(jnp.int32, (1, width), 1)
    return [lane // HD == j for j in range(width // HD)]


def keep_head(block, mask):
    return block if mask is None else jnp.where(mask, block, jnp.zeros_like(block))


def attend_kernel(q_ref, k_ref, v_ref, o_ref, norm_ref):
    width = q_ref.shape[1]
    masks = head_masks(width)
    rows = KEY_ROWS
    place_k = lax.broadcasted_iota(jnp.int32, (rows, rows), 0)
    place_q = lax.broadcasted_iota(jnp.int32, (rows, rows), 1)
    for start in range(0, LEN, rows):
        query = q_ref[start : start + rows, :]
        total = None
        for j, mask in enumerate(masks):
            query_j = keep_head(query, mask)
            scores = mm(k_ref[start : start + rows, :], query_j, 1, 1) * LOG2_SCALE
            scores = jnp.where(place_k <= place_q, scores, -jnp.inf)
            largest = jnp.max(scores, axis=0, keepdims=True)
            if start:
                before = mm(k_ref[0:start, :], query_j, 1, 1) * LOG2_SCALE
                largest = jnp.maximum(largest, jnp.max(before, axis=0, keepdims=True))
            weight = jnp.exp2(scores - largest)
            norm = jnp.sum(weight, axis=0, keepdims=True)
            value = keep_head(v_ref[start : start + rows, :], mask)
            out = mm(value, weight.astype(BF16), 0, 0)
            if start:
                weight = jnp.exp2(before - largest)
                norm = norm + jnp.sum(weight, axis=0, keepdims=True)
                value = keep_head(v_ref[0:start, :], mask)
                out = out + mm(value, weight.astype(BF16), 0, 0)
            out = out / norm
            total = out if total is None else total + out
            norm_ref[0, j : j + 1, start : start + rows] = largest + jnp.log2(norm)
        o_ref[start : start + rows, :] = total.T.astype(BF16)


def attend_forward(queries, keys, values):
    rows, columns = queries.shape
    width = min(2 * HD, columns)
    heads = width // HD
    spec = pl.BlockSpec((rows, width), lambda i: (0, i))
    return pl.pallas_call(
        attend_kernel,
        grid=(columns // width,),
        in_specs=[spec] * 3,
        out_specs=[spec, pl.BlockSpec((1, heads, rows), lambda i: (i, 0, 0))],
        out_shape=[
            jax.ShapeDtypeStruct((rows, columns), BF16),
            jax.ShapeDtypeStruct((columns // width, heads, rows), F32),
        ],
        compiler_params=pltpu.CompilerParams(vmem_limit_bytes=40 * 2**20),
        cost_estimate=pl.CostEstimate(
            flops=rows * rows * columns * 8, bytes_accessed=rows * columns * 8, transcendentals=0
        ),
    )(queries, keys, values)


def attend_back_kernel(q_ref, k_ref, v_ref, o_ref, g_ref, norm_ref, dq_ref, dk_ref, dv_ref, acc):
    width = q_ref.shape[1]
    masks = head_masks(width)
    rows = KEY_ROWS
    place_k = lax.broadcasted_iota(jnp.int32, (rows, rows), 0)
    place_q = lax.broadcasted_iota(jnp.int32, (rows, rows), 1)
    product = g_ref[...].astype(F32) * o_ref[...].astype(F32)
    product = product.T
    acc[...] = jnp.zeros_like(acc)
    deltas = [
        jnp.sum(product[j * HD : (j + 1) * HD, :], axis=0, keepdims=True)
        for j in range(len(masks))
    ]
    for start in range(0, LEN, rows):
        end = start + rows
        key = k_ref[start:end, :]
        value = v_ref[start:end, :]
        grad_key = grad_value = None
        for j, mask in enumerate(masks):
            query_j = keep_head(q_ref[start:, :], mask)
            grad_j = keep_head(g_ref[start:, :], mask)
            scores = mm(key, query_j, 1, 1) * LOG2_SCALE
            probs = jnp.exp2(scores - norm_ref[0, j : j + 1, start:])
            first = jnp.where(place_k <= place_q, probs[:, :rows], 0.0)
            probs = first if end == LEN else jnp.concatenate([first, probs[:, rows:]], axis=1)
            grad_probs = mm(value, grad_j, 1, 1)
            grad_scores = (probs * (grad_probs - deltas[j][:, start:])).astype(BF16)
            value_term = mm(probs.astype(BF16), grad_j)
            key_term = mm(grad_scores, query_j)
            grad_key = key_term if grad_key is None else grad_key + key_term
            grad_value = value_term if grad_value is None else grad_value + value_term
            acc[:, start:] += mm(keep_head(key, mask), grad_scores, 0, 0)
        dk_ref[start:end, :] = (grad_key * HD**-0.5).astype(BF16)
        dv_ref[start:end, :] = grad_value.astype(BF16)
    dq_ref[...] = (acc[...].T * HD**-0.5).astype(BF16)


def attend_backward(queries, keys, values, heads_out, grad_heads, norms):
    rows, columns = queries.shape
    width = min(2 * HD, columns)
    heads = width // HD
    spec = pl.BlockSpec((rows, width), lambda i: (0, i))
    shape = jax.ShapeDtypeStruct((rows, columns), BF16)
    return pl.pallas_call(
        attend_back_kernel,
        grid=(columns // width,),
        in_specs=[spec] * 5 + [pl.BlockSpec((1, heads, rows), lambda i: (i, 0, 0))],
        out_specs=[spec] * 3,
        out_shape=[shape] * 3,
        scratch_shapes=[pltpu.VMEM((width, rows), F32)],
        compiler_params=pltpu.CompilerParams(vmem_limit_bytes=40 * 2**20),
        cost_estimate=pl.CostEstimate(
            flops=rows * rows * columns * 20, bytes_accessed=rows * columns * 16, transcendentals=0
        ),
    )(queries, keys, values, heads_out, grad_heads, norms)


def rms_scale(features):
    return features * lax.rsqrt(jnp.mean(features * features, axis=-1, keepdims=True) + EPS)


def norm_backward(source, gain, upstream):
    inverse = lax.rsqrt(jnp.mean(source * source, axis=-1, keepdims=True) + EPS)
    normed = source * inverse
    scaled = upstream * gain
    grad_source = inverse * (scaled - normed * jnp.mean(scaled * normed, axis=-1, keepdims=True))
    return grad_source, jnp.sum(upstream * normed, axis=0)


class Place:
    def __init__(self):
        self.count = lax.axis_size(TEN)
        self.team = self.count // 2
        self.z = lax.axis_index(TEN)
        self.core = lax.axis_index(SEC)
        self.dp = lax.axis_index(DP)
        self.sequence = self.z // self.team
        self.first = self.core == 0

    def swap(self, block):
        return lax.ppermute(block, SEC, [(0, 1), (1, 0)])

    def opposite(self, block, cores=(0, 1)):
        n, t = self.count, self.team
        route = [(c * n + z, c * n + (z + t) % n) for c in cores for z in range(n)]
        return lax.ppermute(block, (SEC, TEN), route)

    def across(self, block, cores=(0, 1)):
        n, t = self.count, self.team
        route = [(c * n + z, (1 - c) * n + (z + t) % n) for c in cores for z in range(n)]
        return lax.ppermute(block, (SEC, TEN), route)

    def team_sum(self, block):
        n, t = self.count, self.team
        parts = [block]
        for step in range(1, t):
            route = [(z, z // t * t + (z - step) % t) for z in range(n)]
            parts.append(lax.ppermute(block, TEN, route))
        if t == 2:
            return parts[0].astype(F32) + parts[1].astype(F32)
        stacked = jnp.roll(jnp.stack(parts), self.z % t, axis=0)
        return jnp.sum(stacked.astype(F32), axis=0)

    def own_half(self, block):
        half = block.shape[0] // 2
        return lax.dynamic_slice_in_dim(block, self.core * half, half, 0)

    def other_half(self, block):
        half = block.shape[0] // 2
        return lax.dynamic_slice_in_dim(block, (1 - self.core) * half, half, 0)

    def reduce(self, partial):
        got = self.swap(self.other_half(partial.astype(BF16)))
        mine = self.own_half(partial) + got.astype(F32)
        return self.team_sum(mine.astype(BF16))

    def join(self, own):
        other = self.swap(own)
        return jnp.concatenate(
            [jnp.where(self.first, own, other), jnp.where(self.first, other, own)], axis=0
        )


def pack_columns(matrix, width):
    return [matrix[:, i : i + width] for i in range(0, matrix.shape[1], width)]


def pack_attention(query, key_up, value_up, out):
    width = query.shape[1]
    return jnp.concatenate([query, key_up, value_up] + pack_columns(out, width), axis=0)


def unpack_attention(packed, model):
    width = packed.shape[1]
    query = packed[:model]
    key_up = packed[model : model + LH]
    value_up = packed[model + LH : model + 2 * LH]
    rest = packed[model + 2 * LH :]
    out = jnp.concatenate([rest[i : i + width] for i in range(0, rest.shape[0], width)], axis=1)
    return query, key_up, value_up, out


CHUNKS = 2


def chunk(block, index):
    rows = block.shape[0] // CHUNKS
    return block[index * rows : (index + 1) * rows]


def layer_forward(at, source, weights):
    w_query, w_key_up, w_value_up, w_out, w_gate, w_up, w_down, w_latent, gain_attn, gain_mlp = weights
    attn_in = (rms_scale(source.astype(F32)) * gain_attn).astype(BF16)
    queries = mm(attn_in, w_query).astype(BF16)
    latents = mm(attn_in, w_latent).astype(BF16)
    keys = mm(latents, w_key_up).astype(BF16)
    values = mm(latents, w_value_up).astype(BF16)
    heads_out, norms = attend_forward(queries, keys, values)
    residuals, mlp_ins, gates, ups, hiddens, outputs = [], [], [], [], [], []
    for i in range(CHUNKS):
        attended = at.reduce(mm(chunk(heads_out, i), w_out))
        residual = at.own_half(chunk(source, i)).astype(F32) + attended
        residuals.append(residual)
        mlp_ins.append(at.join((rms_scale(residual) * gain_mlp).astype(BF16)))
    for i in range(CHUNKS):
        gate = mm(mlp_ins[i], w_gate)
        up = mm(mlp_ins[i], w_up)
        hidden = (jax.nn.silu(gate) * up).astype(BF16)
        output = residuals[i] + at.reduce(mm(hidden, w_down))
        outputs.append(at.join(output.astype(BF16)))
        gates.append(gate)
        ups.append(up)
        hiddens.append(hidden)
    whole = functools.partial(jnp.concatenate, axis=0)
    kept = (
        source,
        attn_in,
        queries,
        latents,
        keys,
        values,
        heads_out,
        norms,
        residuals,
        whole(mlp_ins),
        whole(gates),
        whole(ups),
        whole(hiddens),
    )
    return whole(outputs), kept


def layer_backward(at, kept, upstream, weights):
    w_query, w_key_up, w_value_up, w_out, w_gate, w_up, w_down, w_latent, gain_attn, gain_mlp = weights
    source, attn_in, queries, latents, keys, values, heads_out, norms, residuals, mlp_in, gate, up, hidden = kept
    grad_hidden = mm(upstream, w_down, 1, 1)
    sigmoid = jax.nn.sigmoid(gate)
    d_gate = (grad_hidden * up * sigmoid * (1.0 + gate * (1.0 - sigmoid))).astype(BF16)
    d_up = (grad_hidden * gate * sigmoid).astype(BF16)
    d_residuals, gain_mlp_grad = [], 0.0
    joined = []
    for i in range(CHUNKS):
        term = mm(chunk(d_gate, i), w_gate, 1, 1) + mm(chunk(d_up, i), w_up, 1, 1)
        part, gain_part = norm_backward(residuals[i], gain_mlp, at.reduce(term))
        d_residual = at.own_half(chunk(upstream, i)).astype(F32) + part
        d_residuals.append(d_residual)
        gain_mlp_grad = gain_mlp_grad + gain_part
        joined.append(at.join(d_residual.astype(BF16)))
    g_down = mm(hidden, upstream, 0, 0).astype(BF16)
    g_gate = mm(mlp_in, d_gate, 0, 0).astype(BF16)
    g_up = mm(mlp_in, d_up, 0, 0).astype(BF16)
    res_grad = jnp.concatenate(joined, axis=0)
    d_heads = mm(res_grad, w_out, 1, 1).astype(BF16)
    d_queries, d_keys, d_values = attend_backward(queries, keys, values, heads_out, d_heads, norms)
    d_latents = (mm(d_keys, w_key_up, 1, 1) + mm(d_values, w_value_up, 1, 1)).astype(BF16)
    grads, gain_attn_grad = [], 0.0
    for i in range(CHUNKS):
        term = mm(chunk(d_queries, i), w_query, 1, 1) + mm(chunk(d_latents, i), w_latent, 1, 1)
        part, gain_part = norm_backward(
            at.own_half(chunk(source, i)).astype(F32), gain_attn, at.reduce(term)
        )
        gain_attn_grad = gain_attn_grad + gain_part
        grads.append(at.join((d_residuals[i] + part).astype(BF16)))
    g_out = mm(heads_out, res_grad, 0, 0).astype(BF16)
    g_query = mm(attn_in, d_queries, 0, 0).astype(BF16)
    g_key_up = mm(latents, d_keys, 0, 0).astype(BF16)
    g_value_up = mm(latents, d_values, 0, 0).astype(BF16)
    g_latent = mm(attn_in, d_latents, 0, 0).astype(BF16)
    attention = pack_attention(g_query, g_key_up, g_value_up, g_out)
    return jnp.concatenate(grads, axis=0), (
        (attention, g_gate, g_up, g_down),
        g_latent,
        (gain_attn_grad, gain_mlp_grad),
    )


def local(
    inputs,
    out_grad,
    w_query,
    w_latent,
    w_key_up,
    w_value_up,
    w_out,
    w_gate,
    w_up,
    w_down,
    norm_attn,
    norm_mlp,
):
    at = Place()
    model = inputs.shape[1]
    heads = w_query.shape[2] // HD
    dp_count = lax.axis_size(DP)

    def group_of(shard):
        return shard * heads // (QH // KVH)

    opposite_z = (at.z + at.team) % at.count

    def latent_of(shard):
        return lax.dynamic_slice_in_dim(w_latent[0], group_of(shard) * LH, LH, 1)

    def fetch(matrix):
        rows = matrix.shape[0] // dp_count
        piece = lax.dynamic_slice_in_dim(matrix, at.dp * rows, rows, 0)
        return lax.all_gather(at.across(piece), DP, axis=0, tiled=True)

    own_packed = pack_attention(w_query[0], w_key_up[0], w_value_up[0], w_out[0])
    far_attention = unpack_attention(fetch(own_packed), model)
    far_latent = at.swap(latent_of(opposite_z))
    far_gains = at.swap(jnp.concatenate([norm_attn, norm_mlp], axis=0))
    far = far_attention + (fetch(w_gate[0]), fetch(w_up[0]), fetch(w_down[0]))
    far = far + (far_latent, far_gains[0], far_gains[1])
    own = (w_query[0], w_key_up[0], w_value_up[0], w_out[0], w_gate[0], w_up[0], w_down[0])
    own = own + (latent_of(at.z), norm_attn[0], norm_mlp[0])
    weights = [
        tuple(jnp.where(at.first, a, b) for a, b in zip(own, far)),
        tuple(jnp.where(at.first, b, a) for a, b in zip(own, far)),
    ]

    def sequence_rows(block):
        return lax.dynamic_slice_in_dim(block, at.sequence * LEN, LEN, 0)

    source = sequence_rows(inputs)
    first_out, first_kept = layer_forward(at, source, weights[0])
    second_out, second_kept = layer_forward(at, first_out, weights[1])
    second_grad, second_totals = layer_backward(at, second_kept, sequence_rows(out_grad), weights[1])
    first_grad, first_totals = layer_backward(at, first_kept, second_grad, weights[0])

    def both_sequences(mine, other):
        top = at.sequence == 0
        return jnp.concatenate([jnp.where(top, mine, other), jnp.where(top, other, mine)], axis=0)[None]

    layer_mine = jnp.where(at.first, first_out, second_out)
    layer_out = both_sequences(layer_mine, at.opposite(layer_mine))
    grad_mine = jnp.where(at.first, first_grad, second_grad)
    grad_far = at.opposite(second_grad, (1,)) + at.opposite(first_grad, (0,))
    input_grad = both_sequences(grad_mine, grad_far)

    def scatter(matrix):
        return lax.psum_scatter(matrix, DP, scatter_dimension=0, tiled=True)

    totals = []
    for one, two in zip(first_totals[0], second_totals[0]):
        one, two = scatter(one), scatter(two)
        far_part = at.across(two, (0,)) + at.across(one, (1,))
        mine = jnp.where(at.first, one, two).astype(F32) + far_part.astype(F32)
        totals.append(lax.all_gather(mine.astype(BF16), DP, axis=0, tiled=True).astype(F32))
    g_query, g_key_up, g_value_up, g_out = unpack_attention(totals[0], model)

    def latent_rows(mine, shard):
        wide = lax.dynamic_update_slice_in_dim(
            jnp.zeros((model, KVH * LH), BF16), mine, group_of(shard) * LH, 1
        )
        return lax.psum_scatter(wide, TEN, scatter_dimension=0, tiled=True)

    one = latent_rows(first_totals[1], jnp.where(at.first, at.z, opposite_z))
    two = latent_rows(second_totals[1], jnp.where(at.first, opposite_z, at.z))
    mine = jnp.where(at.first, one, two) + at.swap(jnp.where(at.first, two, one))
    g_latent = lax.psum(mine, DP).astype(F32)
    gains = lax.psum(jnp.stack(first_totals[2] + second_totals[2]), (SEC, DP, TEN)) / at.team
    gains = jnp.where(at.first, gains[:2], gains[2:])
    width = model // at.count
    gains = lax.dynamic_slice_in_dim(gains, at.z * width, width, 1)
    return (
        layer_out,
        input_grad,
        g_query[None],
        g_latent[None],
        g_key_up[None],
        g_value_up[None],
        g_out[None],
        totals[1][None],
        totals[2][None],
        totals[3][None],
        gains[0:1],
        gains[1:2],
    )


def solution(mesh):
    columns = P(SEC, None, TEN)
    rows = P(SEC, TEN, None)
    return jax.shard_map(
        local,
        mesh=mesh,
        in_specs=(
            P(DP, None),
            P(DP, None),
            columns,
            P(SEC, None, None),
            columns,
            columns,
            rows,
            columns,
            columns,
            rows,
            P(SEC, None),
            P(SEC, None),
        ),
        out_specs=(
            P(SEC, DP, None),
            P(SEC, DP, None),
            columns,
            rows,
            columns,
            columns,
            rows,
            columns,
            columns,
            rows,
            P(SEC, TEN),
            P(SEC, TEN),
        ),
        check_vma=False,
    )
```

```python
import functools
import math

import jax
import jax.numpy as jnp
from jax import lax
from jax.experimental import pallas as pl
from jax.experimental.pallas import tpu as pltpu
from jax.sharding import PartitionSpec as P

QH = 16
HD = 64
KVH = 2
LH = 256
LEN = 1024
EPS = 1e-05
F32 = jnp.float32
BF16 = jnp.bfloat16
SEC, DP, TEN = "section", "dp", "tensor"
LOG2_SCALE = HD**-0.5 * math.log2(math.e)
KEY_ROWS = 256


def mm(left, right, left_dim=1, right_dim=0):
    dims = (((left_dim,), (right_dim,)), ((), ()))
    return lax.dot_general(left, right, dims, preferred_element_type=F32)


def head_masks(width):
    if width == HD:
        return [None]
    lane = lax.broadcasted_iota(jnp.int32, (1, width), 1)
    return [lane // HD == j for j in range(width // HD)]


def keep_head(block, mask):
    return block if mask is None else jnp.where(mask, block, jnp.zeros_like(block))


def attend_kernel(q_ref, k_ref, v_ref, o_ref, norm_ref):
    width = q_ref.shape[1]
    masks = head_masks(width)
    rows = KEY_ROWS
    place_k = lax.broadcasted_iota(jnp.int32, (rows, rows), 0)
    place_q = lax.broadcasted_iota(jnp.int32, (rows, rows), 1)
    for start in range(0, LEN, rows):
        query = q_ref[start : start + rows, :]
        total = None
        for j, mask in enumerate(masks):
            query_j = keep_head(query, mask)
            scores = mm(k_ref[start : start + rows, :], query_j, 1, 1) * LOG2_SCALE
            scores = jnp.where(place_k <= place_q, scores, -jnp.inf)
            largest = jnp.max(scores, axis=0, keepdims=True)
            if start:
                before = mm(k_ref[0:start, :], query_j, 1, 1) * LOG2_SCALE
                largest = jnp.maximum(largest, jnp.max(before, axis=0, keepdims=True))
            weight = jnp.exp2(scores - largest)
            norm = jnp.sum(weight, axis=0, keepdims=True)
            value = keep_head(v_ref[start : start + rows, :], mask)
            out = mm(value, weight.astype(BF16), 0, 0)
            if start:
                weight = jnp.exp2(before - largest)
                norm = norm + jnp.sum(weight, axis=0, keepdims=True)
                value = keep_head(v_ref[0:start, :], mask)
                out = out + mm(value, weight.astype(BF16), 0, 0)
            out = out / norm
            total = out if total is None else total + out
            norm_ref[0, j : j + 1, start : start + rows] = largest + jnp.log2(norm)
        o_ref[start : start + rows, :] = total.T.astype(BF16)


def attend_forward(queries, keys, values):
    rows, columns = queries.shape
    width = min(2 * HD, columns)
    heads = width // HD
    spec = pl.BlockSpec((rows, width), lambda i: (0, i))
    return pl.pallas_call(
        attend_kernel,
        grid=(columns // width,),
        in_specs=[spec] * 3,
        out_specs=[spec, pl.BlockSpec((1, heads, rows), lambda i: (i, 0, 0))],
        out_shape=[
            jax.ShapeDtypeStruct((rows, columns), BF16),
            jax.ShapeDtypeStruct((columns // width, heads, rows), F32),
        ],
        compiler_params=pltpu.CompilerParams(vmem_limit_bytes=40 * 2**20),
        cost_estimate=pl.CostEstimate(
            flops=rows * rows * columns * 8, bytes_accessed=rows * columns * 8, transcendentals=0
        ),
    )(queries, keys, values)


def attend_back_kernel(q_ref, k_ref, v_ref, o_ref, g_ref, norm_ref, dq_ref, dk_ref, dv_ref, acc):
    width = q_ref.shape[1]
    masks = head_masks(width)
    rows = KEY_ROWS
    place_k = lax.broadcasted_iota(jnp.int32, (rows, rows), 0)
    place_q = lax.broadcasted_iota(jnp.int32, (rows, rows), 1)
    product = g_ref[...].astype(F32) * o_ref[...].astype(F32)
    product = product.T
    acc[...] = jnp.zeros_like(acc)
    deltas = [
        jnp.sum(product[j * HD : (j + 1) * HD, :], axis=0, keepdims=True)
        for j in range(len(masks))
    ]
    for start in range(0, LEN, rows):
        end = start + rows
        key = k_ref[start:end, :]
        value = v_ref[start:end, :]
        grad_key = grad_value = None
        for j, mask in enumerate(masks):
            query_j = keep_head(q_ref[start:, :], mask)
            grad_j = keep_head(g_ref[start:, :], mask)
            scores = mm(key, query_j, 1, 1) * LOG2_SCALE
            probs = jnp.exp2(scores - norm_ref[0, j : j + 1, start:])
            first = jnp.where(place_k <= place_q, probs[:, :rows], 0.0)
            probs = first if end == LEN else jnp.concatenate([first, probs[:, rows:]], axis=1)
            grad_probs = mm(value, grad_j, 1, 1)
            grad_scores = (probs * (grad_probs - deltas[j][:, start:])).astype(BF16)
            value_term = mm(probs.astype(BF16), grad_j)
            key_term = mm(grad_scores, query_j)
            grad_key = key_term if grad_key is None else grad_key + key_term
            grad_value = value_term if grad_value is None else grad_value + value_term
            acc[:, start:] += mm(keep_head(key, mask), grad_scores, 0, 0)
        dk_ref[start:end, :] = (grad_key * HD**-0.5).astype(BF16)
        dv_ref[start:end, :] = grad_value.astype(BF16)
    dq_ref[...] = (acc[...].T * HD**-0.5).astype(BF16)


def attend_backward(queries, keys, values, heads_out, grad_heads, norms):
    rows, columns = queries.shape
    width = min(2 * HD, columns)
    heads = width // HD
    spec = pl.BlockSpec((rows, width), lambda i: (0, i))
    shape = jax.ShapeDtypeStruct((rows, columns), BF16)
    return pl.pallas_call(
        attend_back_kernel,
        grid=(columns // width,),
        in_specs=[spec] * 5 + [pl.BlockSpec((1, heads, rows), lambda i: (i, 0, 0))],
        out_specs=[spec] * 3,
        out_shape=[shape] * 3,
        scratch_shapes=[pltpu.VMEM((width, rows), F32)],
        compiler_params=pltpu.CompilerParams(vmem_limit_bytes=40 * 2**20),
        cost_estimate=pl.CostEstimate(
            flops=rows * rows * columns * 20, bytes_accessed=rows * columns * 16, transcendentals=0
        ),
    )(queries, keys, values, heads_out, grad_heads, norms)


def rms_scale(features):
    return features * lax.rsqrt(jnp.mean(features * features, axis=-1, keepdims=True) + EPS)


class Place:
    def __init__(self):
        self.count = lax.axis_size(TEN)
        self.team = self.count // 2
        self.z = lax.axis_index(TEN)
        self.core = lax.axis_index(SEC)
        self.dp = lax.axis_index(DP)
        self.sequence = self.z // self.team
        self.first = self.core == 0

    def swap(self, block):
        return lax.ppermute(block, SEC, [(0, 1), (1, 0)])

    def opposite(self, block, cores=(0, 1)):
        n, t = self.count, self.team
        route = [(c * n + z, c * n + (z + t) % n) for c in cores for z in range(n)]
        return lax.ppermute(block, (SEC, TEN), route)

    def across(self, block, cores=(0, 1)):
        n, t = self.count, self.team
        route = [(c * n + z, (1 - c) * n + (z + t) % n) for c in cores for z in range(n)]
        return lax.ppermute(block, (SEC, TEN), route)


def pack_columns(matrix, width):
    return [matrix[:, i : i + width] for i in range(0, matrix.shape[1], width)]


def pack_attention(query, key_up, value_up, out):
    width = query.shape[1]
    return jnp.concatenate([query, key_up, value_up] + pack_columns(out, width), axis=0)


def unpack_attention(packed, model):
    width = packed.shape[1]
    query = packed[:model]
    key_up = packed[model : model + LH]
    value_up = packed[model + LH : model + 2 * LH]
    rest = packed[model + 2 * LH :]
    out = jnp.concatenate([rest[i : i + width] for i in range(0, rest.shape[0], width)], axis=1)
    return query, key_up, value_up, out


MESH = pl.DeviceIdType.MESH
PIECES = 4
VMEM_LIMIT = 56 * 2**20


def reciprocal_rms(features):
    return lax.rsqrt(jnp.mean(features * features, axis=-1, keepdims=True) + EPS)


class Team:
    def __init__(self):
        count = lax.axis_size(TEN)
        self.size = count // 2
        self.core = lax.axis_index(SEC)
        z = lax.axis_index(TEN)
        self.place = lax.rem(z, self.size)
        self.base = z - self.place
        self.other = {SEC: 1 - self.core}

    def peer(self, step):
        place = lax.rem(self.place + step, self.size)
        return place, {TEN: self.base + place}

    def greet(self):
        barrier = pltpu.get_barrier_semaphore()
        pl.semaphore_signal(barrier, inc=1, device_id=self.other, device_id_type=MESH)
        for step in range(1, self.size):
            pl.semaphore_signal(barrier, inc=1, device_id=self.peer(step)[1], device_id_type=MESH)
        pl.semaphore_wait(barrier, self.size)


def exchange_scratch(team, rows, model):
    half = rows // PIECES // 2
    return [
        pltpu.VMEM((2, half, model), F32),
        pltpu.VMEM((PIECES, half, model), F32),
        pltpu.VMEM((PIECES, half, model), BF16),
        pltpu.VMEM((PIECES, half, model), BF16),
        pltpu.VMEM((team, PIECES, half, model), BF16),
        pltpu.SemaphoreType.DMA((PIECES,)),
        pltpu.SemaphoreType.DMA((PIECES,)),
        pltpu.SemaphoreType.DMA((team, PIECES)),
        pltpu.SemaphoreType.DMA((team, PIECES)),
        pltpu.SemaphoreType.DMA((PIECES,)),
        pltpu.SemaphoreType.DMA((PIECES,)),
    ]


class Exchange:
    def __init__(self, team, refs):
        self.team = team
        (self.part, self.keep, self.out, self.got, self.far) = refs[:5]
        (self.core_sent, self.core_here, self.far_sent, self.far_here) = refs[5:9]
        (self.join_sent, self.join_here) = refs[9:]

    def core_copy(self, i):
        return pltpu.make_async_remote_copy(
            src_ref=self.out.at[i],
            dst_ref=self.got.at[i],
            send_sem=self.core_sent.at[i],
            recv_sem=self.core_here.at[i],
            device_id=self.team.other,
            device_id_type=MESH,
        )

    def far_copy(self, i, step, place):
        return pltpu.make_async_remote_copy(
            src_ref=self.far.at[place, i],
            dst_ref=self.far.at[place, i],
            send_sem=self.far_sent.at[step, i],
            recv_sem=self.far_here.at[place, i],
            device_id=self.team.peer(step)[1],
            device_id_type=MESH,
        )

    def join_copy(self, i, whole):
        core = self.team.core
        return pltpu.make_async_remote_copy(
            src_ref=whole.at[i, core],
            dst_ref=whole.at[i, core],
            send_sem=self.join_sent.at[i],
            recv_sem=self.join_here.at[i],
            device_id=self.team.other,
            device_id_type=MESH,
        )

    def push(self, i, product):
        core = self.team.core
        self.part[...] = product.reshape(self.part.shape)
        self.out[i] = self.part[1 - core].astype(BF16)
        self.core_copy(i).start()
        self.keep[i] = self.part[core]

    def combine(self, i):
        self.core_copy(i).wait_recv()
        self.far[self.team.place, i] = (self.keep[i] + self.got[i].astype(F32)).astype(BF16)
        for step in range(1, self.team.size):
            self.far_copy(i, step, self.team.place).start()

    def total(self, i):
        for step in range(1, self.team.size):
            self.far_copy(i, step, self.team.peer(step)[0]).wait_recv()
        total = self.far[0, i].astype(F32)
        for place in range(1, self.team.size):
            total = total + self.far[place, i].astype(F32)
        return total

    def join(self, i, whole, half):
        whole[i, self.team.core] = half
        self.join_copy(i, whole).start()

    def finish(self, whole, joined=False):
        def drain(i, _):
            self.core_copy(i).wait_send()
            for step in range(1, self.team.size):
                self.far_copy(i, step, self.team.place).wait_send()
            self.join_copy(i, whole).wait_send()
            if not joined:
                self.join_copy(i, whole).wait_recv()
            return 0

        lax.fori_loop(0, PIECES, drain, 0)


def each_piece(body):
    lax.fori_loop(0, PIECES, lambda i, _: (body(i), 0)[1], 0)


def piece_rows(i, rows):
    size = rows // PIECES
    return pl.ds(pl.multiple_of(i * size, size), size)


def project_out_kernel(heads, w_out, source, gain, residual, mlp_in, *refs):
    team = Team()
    ex = Exchange(team, refs)
    team.greet()
    rows = heads.shape[0]

    def send(i):
        ex.push(i, mm(heads[piece_rows(i, rows), :], w_out[...]))

        @pl.when(i > 0)
        def _():
            ex.combine(i - 1)

    each_piece(send)
    ex.combine(PIECES - 1)

    def receive(i):
        block = source[i, team.core].astype(F32) + ex.total(i)
        residual[i] = block
        ex.join(i, mlp_in, (block * reciprocal_rms(block) * gain[...]).astype(BF16))

    each_piece(receive)
    ex.finish(mlp_in)


def feed_forward_kernel(mlp_in, w_gate, w_up, w_down, residual, gate, up, hidden, output, *refs):
    team = Team()
    ex = Exchange(team, refs)
    team.greet()
    rows = mlp_in.shape[0]

    def send(i):
        at = piece_rows(i, rows)
        block = mlp_in[at, :]
        gate_block = mm(block, w_gate[...])
        up_block = mm(block, w_up[...])
        hidden_block = (jax.nn.silu(gate_block) * up_block).astype(BF16)
        gate[at, :] = gate_block
        up[at, :] = up_block
        hidden[at, :] = hidden_block
        ex.push(i, mm(hidden_block, w_down[...]))

        @pl.when(i > 0)
        def _():
            ex.combine(i - 1)

    each_piece(send)
    ex.combine(PIECES - 1)
    each_piece(lambda i: ex.join(i, output, (residual[i] + ex.total(i)).astype(BF16)))
    ex.finish(output)


def rms_back(block, gain, upstream):
    inverse = reciprocal_rms(block)
    normed = block * inverse
    scaled = upstream * gain
    grad = inverse * (scaled - normed * jnp.mean(scaled * normed, axis=-1, keepdims=True))
    return grad, jnp.sum(upstream * normed, axis=0, keepdims=True)


def feed_back_kernel(
    upstream, w_gate, w_up, w_down, gate, up, hidden, mlp_in, residual, gain,
    d_residual, res_grad, gain_grad, grads, d_gate, d_up, *refs
):
    team = Team()
    ex = Exchange(team, refs)
    team.greet()
    rows = mlp_in.shape[0]
    model = mlp_in.shape[1]
    shape = (rows // PIECES, model)

    def send(i):
        at = piece_rows(i, rows)
        grad_hidden = mm(upstream[i].reshape(shape), w_down[...], 1, 1)
        gate_block = gate[at, :]
        sigmoid = jax.nn.sigmoid(gate_block)
        silu = gate_block * sigmoid
        d_gate_block = grad_hidden * up[at, :] * (sigmoid + silu * (1.0 - sigmoid))
        d_gate[at, :] = d_gate_block.astype(BF16)
        d_up[at, :] = (grad_hidden * silu).astype(BF16)
        ex.push(i, mm(d_gate[at, :], w_gate[...], 1, 1) + mm(d_up[at, :], w_up[...], 1, 1))

        @pl.when(i > 0)
        def _():
            ex.combine(i - 1)

    each_piece(send)
    ex.combine(PIECES - 1)
    grads[0:model, :] = mm(mlp_in[...], d_gate[...], 0, 0).astype(BF16)
    grads[model : 2 * model, :] = mm(mlp_in[...], d_up[...], 0, 0).astype(BF16)
    whole = upstream[...].reshape(rows, model)
    grads[2 * model :, :] = mm(whole, hidden[...], 0, 0).astype(BF16)
    gain_grad[...] = jnp.zeros_like(gain_grad)

    def receive(i):
        part, gain_part = rms_back(residual[i], gain[...], ex.total(i))
        block = upstream[i, team.core].astype(F32) + part
        d_residual[i] = block
        gain_grad[...] += gain_part
        ex.join(i, res_grad, block.astype(BF16))

    each_piece(receive)
    ex.finish(res_grad)


def attend_in_back_kernel(
    d_queries, d_latents, w_query, w_latent, source, d_residual, gain, attn_in,
    heads_out, res_grad, latents, d_keys, d_values,
    input_grad, gain_grad, grads, g_latent, *refs
):
    team = Team()
    ex = Exchange(team, refs)
    team.greet()
    rows = d_queries.shape[0]

    def send(i):
        at = piece_rows(i, rows)
        ex.push(i, mm(d_queries[at, :], w_query[...], 1, 1) + mm(d_latents[at, :], w_latent[...], 1, 1))

        @pl.when(i > 0)
        def _():
            ex.combine(i - 1)

    each_piece(send)
    ex.combine(PIECES - 1)
    model, width = w_query.shape
    grads[0:model, :] = mm(attn_in[...], d_queries[...], 0, 0).astype(BF16)
    g_latent[...] = mm(attn_in[...], d_latents[...], 0, 0).astype(BF16)
    grads[model : model + LH, :] = mm(latents[...], d_keys[...], 0, 0).astype(BF16)
    grads[model + LH : model + 2 * LH, :] = mm(latents[...], d_values[...], 0, 0).astype(BF16)
    g_out = mm(heads_out[...], res_grad[...], 0, 0).astype(BF16)
    for j, block in enumerate(pack_columns(g_out, width)):
        start = model + 2 * LH + j * width
        grads[start : start + width, :] = block
    gain_grad[...] = jnp.zeros_like(gain_grad)

    def receive(i):
        part, gain_part = rms_back(source[i, team.core].astype(F32), gain[...], ex.total(i))
        gain_grad[...] += gain_part
        ex.join(i, input_grad, (d_residual[i] + part).astype(BF16))

    each_piece(receive)
    ex.finish(input_grad)


def team_call(kernel, number, model, outs, operands, scratch=(), flops=0):
    team = lax.axis_size(TEN) // 2
    vmem = pl.BlockSpec(memory_space=pltpu.VMEM)
    return pl.pallas_call(
        kernel,
        in_specs=[vmem] * len(operands),
        out_specs=[vmem] * len(outs),
        out_shape=[jax.ShapeDtypeStruct(*out) for out in outs],
        scratch_shapes=list(scratch) + exchange_scratch(team, LEN, model),
        compiler_params=pltpu.CompilerParams(
            collective_id=number, has_side_effects=True, vmem_limit_bytes=VMEM_LIMIT
        ),
        cost_estimate=pl.CostEstimate(flops=flops, bytes_accessed=2**22, transcendentals=0),
    )(*operands)


def pieces_of(block):
    return block.reshape(PIECES, 2, block.shape[0] // PIECES // 2, block.shape[1])


def layer_forward(source, weights):
    w_query, w_key_up, w_value_up, w_out, w_gate, w_up, w_down, w_latent, gain_attn, gain_mlp = weights
    rows, model = source.shape
    hidden_width = w_gate.shape[1]
    attn_in = (rms_scale(source.astype(F32)) * gain_attn).astype(BF16)
    queries = mm(attn_in, w_query).astype(BF16)
    latents = mm(attn_in, w_latent).astype(BF16)
    keys = mm(latents, w_key_up).astype(BF16)
    values = mm(latents, w_value_up).astype(BF16)
    heads_out, norms = attend_forward(queries, keys, values)
    split = (PIECES, 2, rows // PIECES // 2, model)
    own = (PIECES, rows // PIECES // 2, model)
    residual, mlp_in = team_call(
        project_out_kernel, 0, model, [(own, F32), (split, BF16)],
        (heads_out, w_out, pieces_of(source), gain_mlp[None]),
        flops=LINK_FLOPS,
    )
    mlp_in = mlp_in.reshape(rows, model)
    wide = (rows, hidden_width)
    gate, up, hidden, output = team_call(
        feed_forward_kernel, 1, model, [(wide, F32), (wide, F32), (wide, BF16), (split, BF16)],
        (mlp_in, w_gate, w_up, w_down, residual),
        flops=LINK_FLOPS,
    )
    kept = (source, attn_in, queries, latents, keys, values, heads_out, norms)
    return output.reshape(rows, model), kept + (residual, mlp_in, gate, up, hidden)


LINK_FLOPS = 30 * 10**9


def feed_back(kept, upstream, weights):
    w_query, w_key_up, w_value_up, w_out, w_gate, w_up, w_down, w_latent, gain_attn, gain_mlp = weights
    residual, mlp_in, gate, up, hidden = kept[8:]
    rows, model = upstream.shape
    split = (PIECES, 2, rows // PIECES // 2, model)
    own = (PIECES, rows // PIECES // 2, model)
    width = w_gate.shape[1]
    return team_call(
        feed_back_kernel, 2, model,
        [(own, F32), (split, BF16), ((1, model), F32), ((3 * model, width), BF16)],
        (pieces_of(upstream), w_gate, w_up, w_down, gate, up, hidden, mlp_in, residual, gain_mlp[None]),
        scratch=[pltpu.VMEM((rows, width), BF16), pltpu.VMEM((rows, width), BF16)],
        flops=LINK_FLOPS,
    )


def attend_back(kept, d_residual, res_grad, weights):
    w_query, w_key_up, w_value_up, w_out, w_gate, w_up, w_down, w_latent, gain_attn, gain_mlp = weights
    source, attn_in, queries, latents, keys, values, heads_out, norms = kept[:8]
    rows, model = source.shape
    split = (PIECES, 2, rows // PIECES // 2, model)
    width = w_query.shape[1]
    res_grad = res_grad.reshape(rows, model)
    d_heads = mm(res_grad, w_out, 1, 1).astype(BF16)
    d_queries, d_keys, d_values = attend_backward(queries, keys, values, heads_out, d_heads, norms)
    d_latents = (mm(d_keys, w_key_up, 1, 1) + mm(d_values, w_value_up, 1, 1)).astype(BF16)
    input_grad, gain_grad, grads, g_latent = team_call(
        attend_in_back_kernel, 3, model,
        [(split, BF16), ((1, model), F32), ((2 * model + 2 * LH, width), BF16), (w_latent.shape, BF16)],
        (d_queries, d_latents, w_query, w_latent, pieces_of(source), d_residual, gain_attn[None], attn_in,
         heads_out, res_grad, latents, d_keys, d_values),
        flops=LINK_FLOPS,
    )
    return input_grad.reshape(rows, model), gain_grad, grads, g_latent


def local(
    inputs,
    out_grad,
    w_query,
    w_latent,
    w_key_up,
    w_value_up,
    w_out,
    w_gate,
    w_up,
    w_down,
    norm_attn,
    norm_mlp,
):
    at = Place()
    model = inputs.shape[1]
    heads = w_query.shape[2] // HD
    dp_count = lax.axis_size(DP)

    def group_of(shard):
        return shard * heads // (QH // KVH)

    opposite_z = (at.z + at.team) % at.count

    def latent_of(shard):
        return lax.dynamic_slice_in_dim(w_latent[0], group_of(shard) * LH, LH, 1)

    def fetch(matrix):
        rows = matrix.shape[0] // dp_count
        piece = lax.dynamic_slice_in_dim(matrix, at.dp * rows, rows, 0)
        return lax.all_gather(at.across(piece), DP, axis=0, tiled=True)

    own_packed = pack_attention(w_query[0], w_key_up[0], w_value_up[0], w_out[0])
    far_attention = unpack_attention(fetch(own_packed), model)
    far_latent = at.swap(latent_of(opposite_z))
    far_gains = at.swap(jnp.concatenate([norm_attn, norm_mlp], axis=0))
    far = far_attention + (fetch(w_gate[0]), fetch(w_up[0]), fetch(w_down[0]))
    far = far + (far_latent, far_gains[0], far_gains[1])
    own = (w_query[0], w_key_up[0], w_value_up[0], w_out[0], w_gate[0], w_up[0], w_down[0])
    own = own + (latent_of(at.z), norm_attn[0], norm_mlp[0])
    weights = [
        tuple(jnp.where(at.first, a, b) for a, b in zip(own, far)),
        tuple(jnp.where(at.first, b, a) for a, b in zip(own, far)),
    ]

    def sequence_rows(block):
        return lax.dynamic_slice_in_dim(block, at.sequence * LEN, LEN, 0)

    source = sequence_rows(inputs)
    first_out, first_kept = layer_forward(source, weights[0])
    second_out, second_kept = layer_forward(first_out, weights[1])
    layer_mine = jnp.where(at.first, first_out, second_out)
    layer_far = at.opposite(layer_mine)

    def scatter(matrix):
        return lax.psum_scatter(matrix, DP, scatter_dimension=0, tiled=True)

    d_residual, res_grad, mlp_gain_two, feed_two = feed_back(
        second_kept, sequence_rows(out_grad), weights[1]
    )
    feed_two = scatter(feed_two)
    second_grad, attn_gain_two, attend_two, latent_two = attend_back(
        second_kept, d_residual, res_grad, weights[1]
    )
    second_grad, layer_far = lax.optimization_barrier((second_grad, layer_far))
    attend_two = scatter(attend_two)
    d_residual, res_grad, mlp_gain_one, feed_one = feed_back(first_kept, second_grad, weights[0])
    d_residual, feed_two = lax.optimization_barrier((d_residual, feed_two))
    feed_one = scatter(feed_one)
    first_grad, attn_gain_one, attend_one, latent_one = attend_back(
        first_kept, d_residual, res_grad, weights[0]
    )
    attend_one = scatter(attend_one)

    def both_sequences(mine, other):
        top = at.sequence == 0
        return jnp.concatenate([jnp.where(top, mine, other), jnp.where(top, other, mine)], axis=0)[None]

    layer_out = both_sequences(layer_mine, layer_far)
    grad_mine = jnp.where(at.first, first_grad, second_grad)
    grad_far = at.opposite(second_grad, (1,)) + at.opposite(first_grad, (0,))
    input_grad = both_sequences(grad_mine, grad_far)

    def gather(one, two):
        far_part = at.across(two, (0,)) + at.across(one, (1,))
        mine = jnp.where(at.first, one, two).astype(F32) + far_part.astype(F32)
        return lax.all_gather(mine.astype(BF16), DP, axis=0, tiled=True).astype(F32)

    g_feed = gather(feed_one, feed_two)
    g_query, g_key_up, g_value_up, g_out = unpack_attention(gather(attend_one, attend_two), model)

    def latent_rows(mine, shard):
        wide = lax.dynamic_update_slice_in_dim(
            jnp.zeros((model, KVH * LH), BF16), mine, group_of(shard) * LH, 1
        )
        return lax.psum_scatter(wide, TEN, scatter_dimension=0, tiled=True)

    one = latent_rows(latent_one, jnp.where(at.first, at.z, opposite_z))
    two = latent_rows(latent_two, jnp.where(at.first, opposite_z, at.z))
    mine = jnp.where(at.first, one, two) + at.swap(jnp.where(at.first, two, one))
    g_latent = lax.psum(mine, DP).astype(F32)
    gains = lax.psum(jnp.concatenate([attn_gain_one, mlp_gain_one, attn_gain_two, mlp_gain_two], axis=0), (SEC, DP, TEN)) / at.team
    gains = jnp.where(at.first, gains[:2], gains[2:])
    width = model // at.count
    gains = lax.dynamic_slice_in_dim(gains, at.z * width, width, 1)
    return (
        layer_out,
        input_grad,
        g_query[None],
        g_latent[None],
        g_key_up[None],
        g_value_up[None],
        g_out[None],
        g_feed[None, :model],
        g_feed[None, model : 2 * model],
        g_feed[2 * model :].T[None],
        gains[0:1],
        gains[1:2],
    )


def solution(mesh):
    columns = P(SEC, None, TEN)
    rows = P(SEC, TEN, None)
    return jax.shard_map(
        local,
        mesh=mesh,
        in_specs=(
            P(DP, None),
            P(DP, None),
            columns,
            P(SEC, None, None),
            columns,
            columns,
            rows,
            columns,
            columns,
            rows,
            P(SEC, None),
            P(SEC, None),
        ),
        out_specs=(
            P(SEC, DP, None),
            P(SEC, DP, None),
            columns,
            rows,
            columns,
            columns,
            rows,
            columns,
            columns,
            rows,
            P(SEC, TEN),
            P(SEC, TEN),
        ),
        check_vma=False,
    )
```

```python
import functools
import math

import jax
import jax.numpy as jnp
from jax import lax
from jax.experimental import pallas as pl
from jax.experimental.pallas import tpu as pltpu
from jax.sharding import PartitionSpec as P

QH = 16
HD = 64
KVH = 2
LH = 256
LEN = 1024
EPS = 1e-05
F32 = jnp.float32
BF16 = jnp.bfloat16
SEC, DP, TEN = "section", "dp", "tensor"
LOG2_SCALE = HD**-0.5 * math.log2(math.e)
KEY_ROWS = 256


def mm(left, right, left_dim=1, right_dim=0):
    dims = (((left_dim,), (right_dim,)), ((), ()))
    return lax.dot_general(left, right, dims, preferred_element_type=F32)


def head_masks(width):
    if width == HD:
        return [None]
    lane = lax.broadcasted_iota(jnp.int32, (1, width), 1)
    return [lane // HD == j for j in range(width // HD)]


def keep_head(block, mask):
    return block if mask is None else jnp.where(mask, block, jnp.zeros_like(block))


def attend_kernel(q_ref, k_ref, v_ref, o_ref, norm_ref):
    width = q_ref.shape[1]
    masks = head_masks(width)
    rows = KEY_ROWS
    place_k = lax.broadcasted_iota(jnp.int32, (rows, rows), 0)
    place_q = lax.broadcasted_iota(jnp.int32, (rows, rows), 1)
    for start in range(0, LEN, rows):
        query = q_ref[start : start + rows, :]
        total = None
        for j, mask in enumerate(masks):
            query_j = keep_head(query, mask)
            scores = mm(k_ref[start : start + rows, :], query_j, 1, 1) * LOG2_SCALE
            scores = jnp.where(place_k <= place_q, scores, -jnp.inf)
            largest = jnp.max(scores, axis=0, keepdims=True)
            if start:
                before = mm(k_ref[0:start, :], query_j, 1, 1) * LOG2_SCALE
                largest = jnp.maximum(largest, jnp.max(before, axis=0, keepdims=True))
            weight = jnp.exp2(scores - largest)
            norm = jnp.sum(weight, axis=0, keepdims=True)
            value = keep_head(v_ref[start : start + rows, :], mask)
            out = mm(value, weight.astype(BF16), 0, 0)
            if start:
                weight = jnp.exp2(before - largest)
                norm = norm + jnp.sum(weight, axis=0, keepdims=True)
                value = keep_head(v_ref[0:start, :], mask)
                out = out + mm(value, weight.astype(BF16), 0, 0)
            out = out / norm
            total = out if total is None else total + out
            norm_ref[0, j : j + 1, start : start + rows] = largest + jnp.log2(norm)
        o_ref[start : start + rows, :] = total.T.astype(BF16)


def attend_forward(queries, keys, values):
    rows, columns = queries.shape
    width = min(2 * HD, columns)
    heads = width // HD
    spec = pl.BlockSpec((rows, width), lambda i: (0, i))
    return pl.pallas_call(
        attend_kernel,
        grid=(columns // width,),
        in_specs=[spec] * 3,
        out_specs=[spec, pl.BlockSpec((1, heads, rows), lambda i: (i, 0, 0))],
        out_shape=[
            jax.ShapeDtypeStruct((rows, columns), BF16),
            jax.ShapeDtypeStruct((columns // width, heads, rows), F32),
        ],
        compiler_params=pltpu.CompilerParams(vmem_limit_bytes=40 * 2**20),
        cost_estimate=pl.CostEstimate(
            flops=rows * rows * columns * 8, bytes_accessed=rows * columns * 8, transcendentals=0
        ),
    )(queries, keys, values)


def attend_back_kernel(q_ref, k_ref, v_ref, o_ref, g_ref, norm_ref, dq_ref, dk_ref, dv_ref, acc):
    width = q_ref.shape[1]
    masks = head_masks(width)
    rows = KEY_ROWS
    place_k = lax.broadcasted_iota(jnp.int32, (rows, rows), 0)
    place_q = lax.broadcasted_iota(jnp.int32, (rows, rows), 1)
    product = g_ref[...].astype(F32) * o_ref[...].astype(F32)
    product = product.T
    acc[...] = jnp.zeros_like(acc)
    deltas = [
        jnp.sum(product[j * HD : (j + 1) * HD, :], axis=0, keepdims=True)
        for j in range(len(masks))
    ]
    for start in range(0, LEN, rows):
        end = start + rows
        key = k_ref[start:end, :]
        value = v_ref[start:end, :]
        grad_key = grad_value = None
        for j, mask in enumerate(masks):
            query_j = keep_head(q_ref[start:, :], mask)
            grad_j = keep_head(g_ref[start:, :], mask)
            scores = mm(key, query_j, 1, 1) * LOG2_SCALE
            probs = jnp.exp2(scores - norm_ref[0, j : j + 1, start:])
            first = jnp.where(place_k <= place_q, probs[:, :rows], 0.0)
            probs = first if end == LEN else jnp.concatenate([first, probs[:, rows:]], axis=1)
            grad_probs = mm(value, grad_j, 1, 1)
            grad_scores = (probs * (grad_probs - deltas[j][:, start:])).astype(BF16)
            value_term = mm(probs.astype(BF16), grad_j)
            key_term = mm(grad_scores, query_j)
            grad_key = key_term if grad_key is None else grad_key + key_term
            grad_value = value_term if grad_value is None else grad_value + value_term
            acc[:, start:] += mm(keep_head(key, mask), grad_scores, 0, 0)
        dk_ref[start:end, :] = (grad_key * HD**-0.5).astype(BF16)
        dv_ref[start:end, :] = grad_value.astype(BF16)
    dq_ref[...] = (acc[...].T * HD**-0.5).astype(BF16)


def attend_backward(queries, keys, values, heads_out, grad_heads, norms):
    rows, columns = queries.shape
    width = min(2 * HD, columns)
    heads = width // HD
    spec = pl.BlockSpec((rows, width), lambda i: (0, i))
    shape = jax.ShapeDtypeStruct((rows, columns), BF16)
    return pl.pallas_call(
        attend_back_kernel,
        grid=(columns // width,),
        in_specs=[spec] * 5 + [pl.BlockSpec((1, heads, rows), lambda i: (i, 0, 0))],
        out_specs=[spec] * 3,
        out_shape=[shape] * 3,
        scratch_shapes=[pltpu.VMEM((width, rows), F32)],
        compiler_params=pltpu.CompilerParams(vmem_limit_bytes=40 * 2**20),
        cost_estimate=pl.CostEstimate(
            flops=rows * rows * columns * 20, bytes_accessed=rows * columns * 16, transcendentals=0
        ),
    )(queries, keys, values, heads_out, grad_heads, norms)


def rms_scale(features):
    return features * lax.rsqrt(jnp.mean(features * features, axis=-1, keepdims=True) + EPS)


class Place:
    def __init__(self):
        self.count = lax.axis_size(TEN)
        self.team = self.count // 2
        self.z = lax.axis_index(TEN)
        self.core = lax.axis_index(SEC)
        self.dp = lax.axis_index(DP)
        self.sequence = self.z // self.team
        self.first = self.core == 0

    def swap(self, block):
        return lax.ppermute(block, SEC, [(0, 1), (1, 0)])

    def opposite(self, block, cores=(0, 1)):
        n, t = self.count, self.team
        route = [(c * n + z, c * n + (z + t) % n) for c in cores for z in range(n)]
        return lax.ppermute(block, (SEC, TEN), route)

    def across(self, block, cores=(0, 1)):
        n, t = self.count, self.team
        route = [(c * n + z, (1 - c) * n + (z + t) % n) for c in cores for z in range(n)]
        return lax.ppermute(block, (SEC, TEN), route)


def pack_columns(matrix, width):
    return [matrix[:, i : i + width] for i in range(0, matrix.shape[1], width)]


def pack_attention(query, key_up, value_up, out):
    width = query.shape[1]
    return jnp.concatenate([query, key_up, value_up] + pack_columns(out, width), axis=0)


def unpack_attention(packed, model):
    width = packed.shape[1]
    query = packed[:model]
    key_up = packed[model : model + LH]
    value_up = packed[model + LH : model + 2 * LH]
    rest = packed[model + 2 * LH :]
    out = jnp.concatenate([rest[i : i + width] for i in range(0, rest.shape[0], width)], axis=1)
    return query, key_up, value_up, out


MESH = pl.DeviceIdType.MESH
PIECES = 4
VMEM_LIMIT = 56 * 2**20


def reciprocal_rms(features):
    return lax.rsqrt(jnp.mean(features * features, axis=-1, keepdims=True) + EPS)


class Team:
    def __init__(self):
        count = lax.axis_size(TEN)
        self.size = count // 2
        self.core = lax.axis_index(SEC)
        z = lax.axis_index(TEN)
        self.place = lax.rem(z, self.size)
        self.base = z - self.place
        self.other = {SEC: 1 - self.core}

    def peer(self, step):
        place = lax.rem(self.place + step, self.size)
        return place, {TEN: self.base + place}

    def greet(self, others=()):
        partners = [self.other] + [self.peer(step)[1] for step in range(1, self.size)]
        greet(partners + list(others))


def greet(partners):
    barrier = pltpu.get_barrier_semaphore()
    for partner in partners:
        pl.semaphore_signal(barrier, inc=1, device_id=partner, device_id_type=MESH)
    pl.semaphore_wait(barrier, len(partners))


class Plane:
    def __init__(self):
        self.count = lax.axis_size(DP)
        self.me = lax.axis_index(DP)

    def peer(self, step):
        place = lax.rem(self.me + step, self.count)
        return place, {DP: place}

    def peers(self):
        return [self.peer(step)[1] for step in range(1, self.count)]

    def scatters(self, loads, refs):
        items = []
        for load in loads:
            items.append(Scatter(self, load, *refs[:3]))
            refs = refs[3:]
        return items, refs


def scatter_scratch(load):
    count = load.shape[0]
    return [
        pltpu.VMEM(load.shape, BF16),
        pltpu.SemaphoreType.DMA((count,)),
        pltpu.SemaphoreType.DMA((count,)),
    ]


class Scatter:
    def __init__(self, plane, load, slots, sent, here):
        self.plane, self.load, self.slots, self.sent, self.here = plane, load, slots, sent, here

    def copy(self, step, piece, slot):
        return pltpu.make_async_remote_copy(
            src_ref=self.load.at[piece],
            dst_ref=self.slots.at[slot],
            send_sem=self.sent.at[step],
            recv_sem=self.here.at[slot],
            device_id=self.plane.peer(step)[1],
            device_id_type=MESH,
        )

    def start(self):
        for step in range(1, self.plane.count):
            self.copy(step, self.plane.peer(step)[0], self.plane.me).start()

    def total(self):
        total = self.load[self.plane.me].astype(F32)
        for step in range(1, self.plane.count):
            place = self.plane.peer(step)[0]
            self.copy(step, place, place).wait_recv()
            total = total + self.slots[place].astype(F32)
        return total

    def drain(self):
        for step in range(1, self.plane.count):
            self.copy(step, self.plane.peer(step)[0], self.plane.me).wait_send()


class Gather:
    def __init__(self, plane, whole, sent, here):
        self.plane, self.whole, self.sent, self.here = plane, whole, sent, here

    def copy(self, step, piece):
        return pltpu.make_async_remote_copy(
            src_ref=self.whole.at[piece],
            dst_ref=self.whole.at[piece],
            send_sem=self.sent.at[step],
            recv_sem=self.here.at[piece],
            device_id=self.plane.peer(step)[1],
            device_id_type=MESH,
        )

    def start(self):
        for step in range(1, self.plane.count):
            self.copy(step, self.plane.me).start()

    def finish(self):
        for step in range(1, self.plane.count):
            self.copy(step, self.plane.peer(step)[0]).wait_recv()
            self.copy(step, self.plane.me).wait_send()


FEED = 3


def finish_kernel(groups, *refs):
    zero, one = refs[:5], refs[5:10]
    grad = refs[10]
    outs = refs[11:16]
    grad_far = refs[16]
    refs = refs[17:]
    leave, come = refs[:5], refs[5:10]
    slots, held = refs[10], refs[11]
    cross_sent, cross_here, gather_sent, gather_here = refs[12:16]
    block_sent, block_here, grad_sent, grad_here = refs[16:20]
    plane = Plane()
    beside, _ = plane.scatters(zero[FEED:], refs[20:])
    count = lax.axis_size(TEN)
    z = lax.axis_index(TEN)
    core = lax.axis_index(SEC)
    first = core == 0
    opposite = lax.rem(z + count // 2, count)
    across = {SEC: 1 - core, TEN: opposite}
    chips = [lax.rem(z + step, count) for step in range(1, count)]
    greet(plane.peers() + [across] + [{TEN: chip} for chip in chips])
    for scatter in beside:
        scatter.start()

    def cross(k):
        return pltpu.make_async_remote_copy(
            src_ref=leave[k],
            dst_ref=come[k],
            send_sem=cross_sent.at[k],
            recv_sem=cross_here.at[k],
            device_id=across,
            device_id_type=MESH,
        )

    def depart(k, part):
        leave[k][...] = jnp.where(first, one[k][...], part)
        cross(k).start()

    def arrive(k, part):
        cross(k).wait_recv()
        return jnp.where(first, part, one[k][...]).astype(F32) + come[k][...].astype(F32)

    gathers = [Gather(plane, outs[k], gather_sent.at[k], gather_here.at[k]) for k in range(5)]

    def spread(k, total):
        outs[k][plane.me] = total.astype(BF16)
        gathers[k].start()

    for k in range(FEED):
        depart(k, zero[k][...])
    grad_copy = pltpu.make_async_remote_copy(
        src_ref=grad,
        dst_ref=grad_far,
        send_sem=grad_sent,
        recv_sem=grad_here,
        device_id={TEN: opposite},
        device_id_type=MESH,
    )

    @pl.when(first)
    def _():
        grad_copy.start()

    late = []
    for k, scatter in enumerate(beside):
        held_part = scatter.total().astype(BF16)
        late.append(held_part)
        depart(FEED + k, held_part)
    for k in range(FEED):
        spread(k, arrive(k, zero[k][...]))
    spread(FEED, arrive(FEED, late[0]))
    held[...] = arrive(FEED + 1, late[1]).astype(BF16).reshape(held.shape)

    def block(step, chip, slot):
        return pltpu.make_async_remote_copy(
            src_ref=held.at[chip],
            dst_ref=slots.at[slot],
            send_sem=block_sent.at[step],
            recv_sem=block_here.at[slot],
            device_id={TEN: chip},
            device_id_type=MESH,
        )

    for step, chip in enumerate(chips):
        block(step, chip, z).start()
    slots[z] = held[z]
    for step, chip in enumerate(chips):
        block(step, chip, chip).wait_recv()
    shares = [slots[shard].astype(F32) for shard in range(count)]
    sums = [sum(s for s, g in zip(shares, groups) if g == group) for group in range(KVH)]
    gain_rows = sums[0]
    for extra in sums[1:]:
        gain_rows = gain_rows + extra
    depth = gain_rows.shape[0] - GAIN_ROWS
    gain_rows = gain_rows * (2.0 / count)
    blocks = [
        jnp.concatenate([part[:depth], gain_rows[depth:]], axis=0) for part in sums
    ]
    spread(FEED + 1, jnp.concatenate(blocks, axis=1))
    for gather in gathers:
        gather.finish()
    for scatter in beside:
        scatter.drain()
    for k in range(5):
        cross(k).wait_send()
    for step, chip in enumerate(chips):
        block(step, chip, z).wait_send()

    @pl.when(first)
    def _():
        grad_copy.wait()


GAIN_ROWS = 16


def exchange_scratch(team, rows, model):
    half = rows // PIECES // 2
    return [
        pltpu.VMEM((2, half, model), F32),
        pltpu.VMEM((PIECES, half, model), F32),
        pltpu.VMEM((PIECES, half, model), BF16),
        pltpu.VMEM((PIECES, half, model), BF16),
        pltpu.VMEM((team, PIECES, half, model), BF16),
        pltpu.SemaphoreType.DMA((PIECES,)),
        pltpu.SemaphoreType.DMA((PIECES,)),
        pltpu.SemaphoreType.DMA((team, PIECES)),
        pltpu.SemaphoreType.DMA((team, PIECES)),
        pltpu.SemaphoreType.DMA((PIECES,)),
        pltpu.SemaphoreType.DMA((PIECES,)),
    ]


class Exchange:
    def __init__(self, team, refs):
        self.team = team
        (self.part, self.keep, self.out, self.got, self.far) = refs[:5]
        (self.core_sent, self.core_here, self.far_sent, self.far_here) = refs[5:9]
        (self.join_sent, self.join_here) = refs[9:]

    def core_copy(self, i):
        return pltpu.make_async_remote_copy(
            src_ref=self.out.at[i],
            dst_ref=self.got.at[i],
            send_sem=self.core_sent.at[i],
            recv_sem=self.core_here.at[i],
            device_id=self.team.other,
            device_id_type=MESH,
        )

    def far_copy(self, i, step, place):
        return pltpu.make_async_remote_copy(
            src_ref=self.far.at[place, i],
            dst_ref=self.far.at[place, i],
            send_sem=self.far_sent.at[step, i],
            recv_sem=self.far_here.at[place, i],
            device_id=self.team.peer(step)[1],
            device_id_type=MESH,
        )

    def join_copy(self, i, whole):
        core = self.team.core
        return pltpu.make_async_remote_copy(
            src_ref=whole.at[i, core],
            dst_ref=whole.at[i, core],
            send_sem=self.join_sent.at[i],
            recv_sem=self.join_here.at[i],
            device_id=self.team.other,
            device_id_type=MESH,
        )

    def push(self, i, product):
        core = self.team.core
        self.part[...] = product.reshape(self.part.shape)
        self.out[i] = self.part[1 - core].astype(BF16)
        self.core_copy(i).start()
        self.keep[i] = self.part[core]

    def combine(self, i):
        self.core_copy(i).wait_recv()
        self.far[self.team.place, i] = (self.keep[i] + self.got[i].astype(F32)).astype(BF16)
        for step in range(1, self.team.size):
            self.far_copy(i, step, self.team.place).start()

    def total(self, i):
        for step in range(1, self.team.size):
            self.far_copy(i, step, self.team.peer(step)[0]).wait_recv()
        total = self.far[0, i].astype(F32)
        for place in range(1, self.team.size):
            total = total + self.far[place, i].astype(F32)
        return total

    def join(self, i, whole, half):
        whole[i, self.team.core] = half
        self.join_copy(i, whole).start()

    def finish(self, whole, joined=False):
        def drain(i, _):
            self.core_copy(i).wait_send()
            for step in range(1, self.team.size):
                self.far_copy(i, step, self.team.place).wait_send()
            self.join_copy(i, whole).wait_send()
            if not joined:
                self.join_copy(i, whole).wait_recv()
            return 0

        lax.fori_loop(0, PIECES, drain, 0)


def each_piece(body):
    lax.fori_loop(0, PIECES, lambda i, _: (body(i), 0)[1], 0)


def piece_rows(i, rows):
    size = rows // PIECES
    return pl.ds(pl.multiple_of(i * size, size), size)


def project_out_kernel(heads, w_out, source, gain, residual, mlp_in, *refs):
    team = Team()
    ex = Exchange(team, refs)
    team.greet()
    rows = heads.shape[0]

    def send(i):
        ex.push(i, mm(heads[piece_rows(i, rows), :], w_out[...]))

        @pl.when(i > 0)
        def _():
            ex.combine(i - 1)

    each_piece(send)
    ex.combine(PIECES - 1)

    def receive(i):
        block = source[i, team.core].astype(F32) + ex.total(i)
        residual[i] = block
        ex.join(i, mlp_in, (block * reciprocal_rms(block) * gain[...]).astype(BF16))

    each_piece(receive)
    ex.finish(mlp_in)


def feed_forward_kernel(mlp_in, w_gate, w_up, w_down, residual, gate, up, hidden, output, *refs):
    team = Team()
    ex = Exchange(team, refs)
    team.greet()
    rows = mlp_in.shape[0]

    def send(i):
        at = piece_rows(i, rows)
        block = mlp_in[at, :]
        gate_block = mm(block, w_gate[...])
        up_block = mm(block, w_up[...])
        hidden_block = (jax.nn.silu(gate_block) * up_block).astype(BF16)
        gate[at, :] = gate_block
        up[at, :] = up_block
        hidden[at, :] = hidden_block
        ex.push(i, mm(hidden_block, w_down[...]))

        @pl.when(i > 0)
        def _():
            ex.combine(i - 1)

    each_piece(send)
    ex.combine(PIECES - 1)
    each_piece(lambda i: ex.join(i, output, (residual[i] + ex.total(i)).astype(BF16)))
    ex.finish(output)


def rms_back(block, gain, upstream):
    inverse = reciprocal_rms(block)
    normed = block * inverse
    scaled = upstream * gain
    grad = inverse * (scaled - normed * jnp.mean(scaled * normed, axis=-1, keepdims=True))
    return grad, jnp.sum(upstream * normed, axis=0, keepdims=True)


def feed_back_kernel(
    upstream, w_gate, w_up, w_down, gate, up, hidden, mlp_in, residual, gain, *rest
):
    count = (len(rest) - 19) // 5
    loads, rest = rest[:count], rest[count:]
    d_residual, res_grad, gain_grad, g_gate, g_up, g_down = rest[:6]
    sums, rest = rest[6 : 6 + count], rest[6 + count :]
    (d_gate, d_up), rest = rest[:2], rest[2:]
    team = Team()
    plane = Plane()
    beside, refs = plane.scatters(loads, rest)
    ex = Exchange(team, refs)
    team.greet(plane.peers() if loads else [])
    for scatter in beside:
        scatter.start()
    rows = mlp_in.shape[0]
    model = mlp_in.shape[1]
    shape = (rows // PIECES, model)

    def send(i):
        at = piece_rows(i, rows)
        grad_hidden = mm(upstream[i].reshape(shape), w_down[...], 1, 1)
        gate_block = gate[at, :]
        sigmoid = jax.nn.sigmoid(gate_block)
        silu = gate_block * sigmoid
        d_gate_block = grad_hidden * up[at, :] * (sigmoid + silu * (1.0 - sigmoid))
        d_gate[at, :] = d_gate_block.astype(BF16)
        d_up[at, :] = (grad_hidden * silu).astype(BF16)
        ex.push(i, mm(d_gate[at, :], w_gate[...], 1, 1) + mm(d_up[at, :], w_up[...], 1, 1))

        @pl.when(i > 0)
        def _():
            ex.combine(i - 1)

    each_piece(send)
    ex.combine(PIECES - 1)
    g_gate[...] = mm(mlp_in[...], d_gate[...], 0, 0).astype(BF16)
    g_up[...] = mm(mlp_in[...], d_up[...], 0, 0).astype(BF16)
    whole = upstream[...].reshape(rows, model)
    g_down[...] = mm(hidden[...], whole, 0, 0).astype(BF16)
    gain_grad[...] = jnp.zeros_like(gain_grad)

    def receive(i):
        part, gain_part = rms_back(residual[i], gain[...], ex.total(i))
        block = upstream[i, team.core].astype(F32) + part
        d_residual[i] = block
        gain_grad[...] += gain_part
        ex.join(i, res_grad, block.astype(BF16))

    each_piece(receive)
    for scatter, total in zip(beside, sums):
        total[...] = scatter.total().astype(BF16)
    ex.finish(res_grad)
    for scatter in beside:
        scatter.drain()


def attend_in_back_kernel(
    d_queries, d_latents, w_query, w_latent, source, d_residual, gain, attn_in,
    heads_out, res_grad, latents, d_keys, d_values, *rest
):
    count = (len(rest) - 15) // 5
    loads, rest = rest[:count], rest[count:]
    input_grad, gain_grad, grads, g_latent = rest[:4]
    sums, rest = rest[4 : 4 + count], rest[4 + count :]
    team = Team()
    plane = Plane()
    beside, refs = plane.scatters(loads, rest)
    ex = Exchange(team, refs)
    team.greet(plane.peers())
    for scatter in beside:
        scatter.start()
    rows = d_queries.shape[0]

    def send(i):
        at = piece_rows(i, rows)
        ex.push(i, mm(d_queries[at, :], w_query[...], 1, 1) + mm(d_latents[at, :], w_latent[...], 1, 1))

        @pl.when(i > 0)
        def _():
            ex.combine(i - 1)

    each_piece(send)
    ex.combine(PIECES - 1)
    model, width = w_query.shape
    grads[0:model, :] = mm(attn_in[...], d_queries[...], 0, 0).astype(BF16)
    g_latent[...] = mm(attn_in[...], d_latents[...], 0, 0).astype(BF16)
    grads[model : model + LH, :] = mm(latents[...], d_keys[...], 0, 0).astype(BF16)
    grads[model + LH : model + 2 * LH, :] = mm(latents[...], d_values[...], 0, 0).astype(BF16)
    g_out = mm(heads_out[...], res_grad[...], 0, 0).astype(BF16)
    for j, block in enumerate(pack_columns(g_out, width)):
        start = model + 2 * LH + j * width
        grads[start : start + width, :] = block
    gain_grad[...] = jnp.zeros_like(gain_grad)

    def receive(i):
        part, gain_part = rms_back(source[i, team.core].astype(F32), gain[...], ex.total(i))
        gain_grad[...] += gain_part
        ex.join(i, input_grad, (d_residual[i] + part).astype(BF16))

    each_piece(receive)
    for scatter, total in zip(beside, sums):
        total[...] = scatter.total().astype(BF16)
    ex.finish(input_grad)
    for scatter in beside:
        scatter.drain()


def team_call(kernel, number, model, outs, operands, scratch=(), flops=0, loads=()):
    operands = tuple(operands) + tuple(loads)
    outs = outs + [(load.shape[1:], BF16) for load in loads]
    beside = [item for load in loads for item in scatter_scratch(load)]
    team = lax.axis_size(TEN) // 2
    vmem = pl.BlockSpec(memory_space=pltpu.VMEM)
    return pl.pallas_call(
        kernel,
        in_specs=[vmem] * len(operands),
        out_specs=[vmem] * len(outs),
        out_shape=[jax.ShapeDtypeStruct(*out) for out in outs],
        scratch_shapes=list(scratch) + beside + exchange_scratch(team, LEN, model),
        compiler_params=pltpu.CompilerParams(
            collective_id=number, has_side_effects=True, vmem_limit_bytes=VMEM_LIMIT
        ),
        cost_estimate=pl.CostEstimate(flops=flops, bytes_accessed=2**22, transcendentals=0),
    )(*operands)


def pieces_of(block):
    return block.reshape(PIECES, 2, block.shape[0] // PIECES // 2, block.shape[1])


def layer_forward(source, weights):
    w_query, w_key_up, w_value_up, w_out, w_gate, w_up, w_down, w_latent, gain_attn, gain_mlp = weights
    rows, model = source.shape
    hidden_width = w_gate.shape[1]
    attn_in = (rms_scale(source.astype(F32)) * gain_attn).astype(BF16)
    queries = mm(attn_in, w_query).astype(BF16)
    latents = mm(attn_in, w_latent).astype(BF16)
    keys = mm(latents, w_key_up).astype(BF16)
    values = mm(latents, w_value_up).astype(BF16)
    heads_out, norms = attend_forward(queries, keys, values)
    split = (PIECES, 2, rows // PIECES // 2, model)
    own = (PIECES, rows // PIECES // 2, model)
    residual, mlp_in = team_call(
        project_out_kernel, 0, model, [(own, F32), (split, BF16)],
        (heads_out, w_out, pieces_of(source), gain_mlp[None]),
        flops=LINK_FLOPS,
    )
    mlp_in = mlp_in.reshape(rows, model)
    wide = (rows, hidden_width)
    gate, up, hidden, output = team_call(
        feed_forward_kernel, 1, model, [(wide, F32), (wide, F32), (wide, BF16), (split, BF16)],
        (mlp_in, w_gate, w_up, w_down, residual),
        flops=LINK_FLOPS,
    )
    kept = (source, attn_in, queries, latents, keys, values, heads_out, norms)
    return output.reshape(rows, model), kept + (residual, mlp_in, gate, up, hidden)


LINK_FLOPS = 30 * 10**9


def feed_back(kept, upstream, weights, number, loads=()):
    w_query, w_key_up, w_value_up, w_out, w_gate, w_up, w_down, w_latent, gain_attn, gain_mlp = weights
    residual, mlp_in, gate, up, hidden = kept[8:]
    rows, model = upstream.shape
    split = (PIECES, 2, rows // PIECES // 2, model)
    own = (PIECES, rows // PIECES // 2, model)
    width = w_gate.shape[1]
    d_residual, res_grad, gain_grad, *grads = team_call(
        feed_back_kernel, number, model,
        [(own, F32), (split, BF16), ((1, model), F32), (w_gate.shape, BF16), (w_gate.shape, BF16), (w_down.shape, BF16)],
        (pieces_of(upstream), w_gate, w_up, w_down, gate, up, hidden, mlp_in, residual, gain_mlp[None]),
        scratch=[pltpu.VMEM((rows, width), BF16), pltpu.VMEM((rows, width), BF16)],
        flops=LINK_FLOPS,
        loads=loads,
    )
    return d_residual, res_grad, gain_grad, [by_dp(g) for g in grads[:3]], grads[3:]


def by_dp(matrix):
    count = lax.axis_size(DP)
    return matrix.reshape(count, matrix.shape[0] // count, matrix.shape[1])


def latent_parts(g_latent, gain_attn, gain_mlp):
    count, pieces = lax.axis_size(TEN), lax.axis_size(DP)
    model = g_latent.shape[0]
    depth = model // count // pieces
    rows = g_latent.reshape(count, pieces, depth, LH).transpose(1, 0, 2, 3)
    gains = jnp.stack([gain_attn[0], gain_mlp[0]]).astype(BF16).reshape(2, count, model // count)
    gains = gains.transpose(1, 0, 2)
    gains = jnp.pad(gains, ((0, 0), (0, GAIN_ROWS - 2), (0, LH - model // count)))
    gains = jnp.pad(gains[None], ((0, pieces - 1), (0, 0), (0, 0), (0, 0)))
    return jnp.concatenate([rows, gains], axis=2).reshape(pieces, count * (depth + GAIN_ROWS), LH)


def attend_back(kept, d_residual, res_grad, gain_mlp_grad, weights, loads):
    w_query, w_key_up, w_value_up, w_out, w_gate, w_up, w_down, w_latent, gain_attn, gain_mlp = weights
    source, attn_in, queries, latents, keys, values, heads_out, norms = kept[:8]
    rows, model = source.shape
    split = (PIECES, 2, rows // PIECES // 2, model)
    width = w_query.shape[1]
    res_grad = res_grad.reshape(rows, model)
    d_heads = mm(res_grad, w_out, 1, 1).astype(BF16)
    d_queries, d_keys, d_values = attend_backward(queries, keys, values, heads_out, d_heads, norms)
    d_latents = (mm(d_keys, w_key_up, 1, 1) + mm(d_values, w_value_up, 1, 1)).astype(BF16)
    input_grad, gain_grad, grads, g_latent, *sums = team_call(
        attend_in_back_kernel, 3, model,
        [(split, BF16), ((1, model), F32), ((2 * model + 2 * LH, width), BF16), (w_latent.shape, BF16)],
        (d_queries, d_latents, w_query, w_latent, pieces_of(source), d_residual, gain_attn[None], attn_in,
         heads_out, res_grad, latents, d_keys, d_values),
        flops=LINK_FLOPS,
        loads=loads,
    )
    parts = [by_dp(grads), latent_parts(g_latent, gain_grad, gain_mlp_grad)]
    return input_grad.reshape(rows, model), parts, sums


def finish(groups, zero, one, grad):
    pieces, count = lax.axis_size(DP), lax.axis_size(TEN)
    vmem = pl.BlockSpec(memory_space=pltpu.VMEM)
    depth = one[4].shape[0] // count
    outs = [(pieces,) + part.shape for part in one[:4]] + [(pieces, depth, KVH * LH), grad.shape]
    dma = pltpu.SemaphoreType.DMA
    shapes = [pltpu.VMEM(part.shape, BF16) for part in one]
    blocks = pltpu.VMEM((count, depth, LH), BF16)
    return pl.pallas_call(
        functools.partial(finish_kernel, groups),
        in_specs=[vmem] * 11,
        out_specs=[vmem] * 6,
        out_shape=[jax.ShapeDtypeStruct(out, BF16) for out in outs],
        scratch_shapes=shapes + shapes + [blocks, blocks]
        + [dma((5,)), dma((5,)), dma((5, pieces)), dma((5, pieces)), dma((count,)), dma((count,)), dma, dma]
        + scatter_scratch(zero[3]) + scatter_scratch(zero[4]),
        compiler_params=pltpu.CompilerParams(
            collective_id=5, has_side_effects=True, vmem_limit_bytes=VMEM_LIMIT
        ),
    )(*zero, *one, grad)


def local(
    inputs,
    out_grad,
    w_query,
    w_latent,
    w_key_up,
    w_value_up,
    w_out,
    w_gate,
    w_up,
    w_down,
    norm_attn,
    norm_mlp,
):
    at = Place()
    model = inputs.shape[1]
    heads = w_query.shape[2] // HD
    dp_count = lax.axis_size(DP)

    def group_of(shard):
        return shard * heads // (QH // KVH)

    opposite_z = (at.z + at.team) % at.count

    def latent_of(shard):
        return lax.dynamic_slice_in_dim(w_latent[0], group_of(shard) * LH, LH, 1)

    def fetch(matrix):
        rows = matrix.shape[0] // dp_count
        piece = lax.dynamic_slice_in_dim(matrix, at.dp * rows, rows, 0)
        return lax.all_gather(at.across(piece), DP, axis=0, tiled=True)

    own_packed = pack_attention(w_query[0], w_key_up[0], w_value_up[0], w_out[0])
    far_attention = unpack_attention(fetch(own_packed), model)
    far_latent = at.swap(latent_of(opposite_z))
    far_gains = at.swap(jnp.concatenate([norm_attn, norm_mlp], axis=0))
    far = far_attention + (fetch(w_gate[0]), fetch(w_up[0]), fetch(w_down[0]))
    far = far + (far_latent, far_gains[0], far_gains[1])
    own = (w_query[0], w_key_up[0], w_value_up[0], w_out[0], w_gate[0], w_up[0], w_down[0])
    own = own + (latent_of(at.z), norm_attn[0], norm_mlp[0])
    weights = [
        tuple(jnp.where(at.first, a, b) for a, b in zip(own, far)),
        tuple(jnp.where(at.first, b, a) for a, b in zip(own, far)),
    ]

    def sequence_rows(block):
        return lax.dynamic_slice_in_dim(block, at.sequence * LEN, LEN, 0)

    source = sequence_rows(inputs)
    first_out, first_kept = layer_forward(source, weights[0])
    second_out, second_kept = layer_forward(first_out, weights[1])
    first_far = at.opposite(first_out, (0,))
    second_far = at.opposite(second_out, (1,))
    cotangent, first_far = lax.optimization_barrier((sequence_rows(out_grad), first_far))
    d_residual, res_grad, mlp_gain, feed_two, _ = feed_back(second_kept, cotangent, weights[1], 2)
    second_grad, late_two, feed_two = attend_back(
        second_kept, d_residual, res_grad, mlp_gain, weights[1], feed_two
    )
    upstream, second_far = lax.optimization_barrier((second_grad, second_far))
    grad_far = at.opposite(second_grad, (1,))
    d_residual, res_grad, mlp_gain, feed_one, late_two = feed_back(
        first_kept, upstream, weights[0], 4, late_two
    )
    first_grad, late_one, feed_one = attend_back(
        first_kept, d_residual, res_grad, mlp_gain, weights[0], feed_one
    )
    late_one[0], grad_far = lax.optimization_barrier((late_one[0], grad_far))
    groups = tuple(group_of(shard) for shard in range(at.count))
    *wide, packed, latent, first_grad_far = finish(
        groups, feed_one + late_one, feed_two + late_two, first_grad
    )

    def both_sequences(mine, other):
        top = at.sequence == 0
        return jnp.concatenate([jnp.where(top, mine, other), jnp.where(top, other, mine)], axis=0)[None]

    layer_out = both_sequences(
        jnp.where(at.first, first_out, second_out), jnp.where(at.first, first_far, second_far)
    )
    input_grad = both_sequences(
        jnp.where(at.first, first_grad, second_grad), jnp.where(at.first, first_grad_far, grad_far)
    )
    g_gate, g_up, g_down = [part.reshape(-1, part.shape[2]).astype(F32) for part in wide]
    packed = packed.reshape(-1, packed.shape[2]).astype(F32)
    g_query, g_key_up, g_value_up, g_out = unpack_attention(packed, model)
    width = model // at.count
    depth = latent.shape[1] - GAIN_ROWS
    g_latent = latent[:, :depth].reshape(width, KVH * LH).astype(F32)
    gains = latent[0, depth : depth + 2, :width].astype(F32)
    return (
        layer_out,
        input_grad,
        g_query[None],
        g_latent[None],
        g_key_up[None],
        g_value_up[None],
        g_out[None],
        g_gate[None],
        g_up[None],
        g_down[None],
        gains[0:1],
        gains[1:2],
    )


def solution(mesh):
    columns = P(SEC, None, TEN)
    rows = P(SEC, TEN, None)
    return jax.shard_map(
        local,
        mesh=mesh,
        in_specs=(
            P(DP, None),
            P(DP, None),
            columns,
            P(SEC, None, None),
            columns,
            columns,
            rows,
            columns,
            columns,
            rows,
            P(SEC, None),
            P(SEC, None),
        ),
        out_specs=(
            P(SEC, DP, None),
            P(SEC, DP, None),
            columns,
            rows,
            columns,
            columns,
            rows,
            columns,
            columns,
            rows,
            P(SEC, TEN),
            P(SEC, TEN),
        ),
        check_vma=False,
    )
```

```python
import functools
import math

import jax
import jax.numpy as jnp
from jax import lax
from jax.experimental import pallas as pl
from jax.experimental.pallas import tpu as pltpu
from jax.sharding import PartitionSpec as P

QH = 16
HD = 64
KVH = 2
LH = 256
LEN = 1024
EPS = 1e-05
F32 = jnp.float32
BF16 = jnp.bfloat16
SEC, DP, TEN = "section", "dp", "tensor"
LOG2_SCALE = HD**-0.5 * math.log2(math.e)
KEY_ROWS = 256


def mm(left, right, left_dim=1, right_dim=0):
    dims = (((left_dim,), (right_dim,)), ((), ()))
    return lax.dot_general(left, right, dims, preferred_element_type=F32)


def head_masks(width):
    if width == HD:
        return [None]
    lane = lax.broadcasted_iota(jnp.int32, (1, width), 1)
    return [lane // HD == j for j in range(width // HD)]


def keep_head(block, mask):
    return block if mask is None else jnp.where(mask, block, jnp.zeros_like(block))


def attend_kernel(q_ref, k_ref, v_ref, o_ref, norm_ref):
    width = q_ref.shape[1]
    masks = head_masks(width)
    rows = KEY_ROWS
    place_k = lax.broadcasted_iota(jnp.int32, (rows, rows), 0)
    place_q = lax.broadcasted_iota(jnp.int32, (rows, rows), 1)
    for start in range(0, LEN, rows):
        query = q_ref[start : start + rows, :]
        total = None
        for j, mask in enumerate(masks):
            query_j = keep_head(query, mask)
            scores = mm(k_ref[start : start + rows, :], query_j, 1, 1) * LOG2_SCALE
            scores = jnp.where(place_k <= place_q, scores, -jnp.inf)
            largest = jnp.max(scores, axis=0, keepdims=True)
            if start:
                before = mm(k_ref[0:start, :], query_j, 1, 1) * LOG2_SCALE
                largest = jnp.maximum(largest, jnp.max(before, axis=0, keepdims=True))
            weight = jnp.exp2(scores - largest)
            norm = jnp.sum(weight, axis=0, keepdims=True)
            value = keep_head(v_ref[start : start + rows, :], mask)
            out = mm(value, weight.astype(BF16), 0, 0)
            if start:
                weight = jnp.exp2(before - largest)
                norm = norm + jnp.sum(weight, axis=0, keepdims=True)
                value = keep_head(v_ref[0:start, :], mask)
                out = out + mm(value, weight.astype(BF16), 0, 0)
            out = out / norm
            total = out if total is None else total + out
            norm_ref[0, j : j + 1, start : start + rows] = largest + jnp.log2(norm)
        o_ref[start : start + rows, :] = total.T.astype(BF16)


def attend_forward(queries, keys, values):
    rows, columns = queries.shape
    width = min(2 * HD, columns)
    heads = width // HD
    spec = pl.BlockSpec((rows, width), lambda i: (0, i))
    return pl.pallas_call(
        attend_kernel,
        grid=(columns // width,),
        in_specs=[spec] * 3,
        out_specs=[spec, pl.BlockSpec((1, heads, rows), lambda i: (i, 0, 0))],
        out_shape=[
            jax.ShapeDtypeStruct((rows, columns), BF16),
            jax.ShapeDtypeStruct((columns // width, heads, rows), F32),
        ],
        compiler_params=pltpu.CompilerParams(vmem_limit_bytes=40 * 2**20),
        cost_estimate=pl.CostEstimate(
            flops=rows * rows * columns * 8, bytes_accessed=rows * columns * 8, transcendentals=0
        ),
    )(queries, keys, values)


def attend_back_kernel(q_ref, k_ref, v_ref, o_ref, g_ref, norm_ref, dq_ref, dk_ref, dv_ref, acc):
    width = q_ref.shape[1]
    masks = head_masks(width)
    rows = KEY_ROWS
    place_k = lax.broadcasted_iota(jnp.int32, (rows, rows), 0)
    place_q = lax.broadcasted_iota(jnp.int32, (rows, rows), 1)
    product = g_ref[...].astype(F32) * o_ref[...].astype(F32)
    product = product.T
    acc[...] = jnp.zeros_like(acc)
    deltas = [
        jnp.sum(product[j * HD : (j + 1) * HD, :], axis=0, keepdims=True)
        for j in range(len(masks))
    ]
    for start in range(0, LEN, rows):
        end = start + rows
        key = k_ref[start:end, :]
        value = v_ref[start:end, :]
        grad_key = grad_value = None
        for j, mask in enumerate(masks):
            query_j = keep_head(q_ref[start:, :], mask)
            grad_j = keep_head(g_ref[start:, :], mask)
            scores = mm(key, query_j, 1, 1) * LOG2_SCALE
            probs = jnp.exp2(scores - norm_ref[0, j : j + 1, start:])
            first = jnp.where(place_k <= place_q, probs[:, :rows], 0.0)
            probs = first if end == LEN else jnp.concatenate([first, probs[:, rows:]], axis=1)
            grad_probs = mm(value, grad_j, 1, 1)
            grad_scores = (probs * (grad_probs - deltas[j][:, start:])).astype(BF16)
            value_term = mm(probs.astype(BF16), grad_j)
            key_term = mm(grad_scores, query_j)
            grad_key = key_term if grad_key is None else grad_key + key_term
            grad_value = value_term if grad_value is None else grad_value + value_term
            acc[:, start:] += mm(keep_head(key, mask), grad_scores, 0, 0)
        dk_ref[start:end, :] = (grad_key * HD**-0.5).astype(BF16)
        dv_ref[start:end, :] = grad_value.astype(BF16)
    dq_ref[...] = (acc[...].T * HD**-0.5).astype(BF16)


def attend_backward(queries, keys, values, heads_out, grad_heads, norms):
    rows, columns = queries.shape
    width = min(2 * HD, columns)
    heads = width // HD
    spec = pl.BlockSpec((rows, width), lambda i: (0, i))
    shape = jax.ShapeDtypeStruct((rows, columns), BF16)
    return pl.pallas_call(
        attend_back_kernel,
        grid=(columns // width,),
        in_specs=[spec] * 5 + [pl.BlockSpec((1, heads, rows), lambda i: (i, 0, 0))],
        out_specs=[spec] * 3,
        out_shape=[shape] * 3,
        scratch_shapes=[pltpu.VMEM((width, rows), F32)],
        compiler_params=pltpu.CompilerParams(vmem_limit_bytes=40 * 2**20),
        cost_estimate=pl.CostEstimate(
            flops=rows * rows * columns * 20, bytes_accessed=rows * columns * 16, transcendentals=0
        ),
    )(queries, keys, values, heads_out, grad_heads, norms)


def rms_scale(features):
    return features * lax.rsqrt(jnp.mean(features * features, axis=-1, keepdims=True) + EPS)


class Place:
    def __init__(self):
        self.count = lax.axis_size(TEN)
        self.team = self.count // 2
        self.z = lax.axis_index(TEN)
        self.core = lax.axis_index(SEC)
        self.dp = lax.axis_index(DP)
        self.sequence = self.z // self.team
        self.first = self.core == 0

    def opposite(self, block, cores=(0, 1)):
        n, t = self.count, self.team
        route = [(core * n + z, core * n + (z + t) % n) for core in cores for z in range(n)]
        return lax.ppermute(block, (SEC, TEN), route)

    def across(self, block, core):
        n, t = self.count, self.team
        route = [(core * n + z, (1 - core) * n + (z + t) % n) for z in range(n)]
        return lax.ppermute(block, (SEC, TEN), route)


def pack_columns(matrix, width):
    return [matrix[:, i : i + width] for i in range(0, matrix.shape[1], width)]


def pack_attention(query, key_up, value_up, out):
    width = query.shape[1]
    return jnp.concatenate([query, key_up, value_up] + pack_columns(out, width), axis=0)


def unpack_attention(packed, model):
    width = packed.shape[1]
    query = packed[:model]
    key_up = packed[model : model + LH]
    value_up = packed[model + LH : model + 2 * LH]
    rest = packed[model + 2 * LH :]
    out = jnp.concatenate([rest[i : i + width] for i in range(0, rest.shape[0], width)], axis=1)
    return query, key_up, value_up, out


def by_dp(matrix):
    count = lax.axis_size(DP)
    return matrix.reshape(count, matrix.shape[0] // count, matrix.shape[1])


def whole_of(pieces):
    return pieces.reshape(-1, pieces.shape[2])


MESH = pl.DeviceIdType.MESH
PIECES = 4
VMEM_LIMIT = 58 * 2**20
LINK_FLOPS = 30 * 10**9
GAIN_ROWS = 16
DMA = pltpu.SemaphoreType.DMA


def reciprocal_rms(features):
    return lax.rsqrt(jnp.mean(features * features, axis=-1, keepdims=True) + EPS)


def send_to(source, target, sent, here, device):
    return pltpu.make_async_remote_copy(
        src_ref=source,
        dst_ref=target,
        send_sem=sent,
        recv_sem=here,
        device_id=device,
        device_id_type=MESH,
    )


def greet(partners):
    barrier = pltpu.get_barrier_semaphore()
    for partner in partners:
        pl.semaphore_signal(barrier, inc=1, device_id=partner, device_id_type=MESH)
    pl.semaphore_wait(barrier, len(partners))


class Team:
    def __init__(self):
        count = lax.axis_size(TEN)
        self.size = count // 2
        self.core = lax.axis_index(SEC)
        z = lax.axis_index(TEN)
        self.place = lax.rem(z, self.size)
        self.base = z - self.place
        self.other = {SEC: 1 - self.core}

    def peer(self, step):
        place = lax.rem(self.place + step, self.size)
        return place, {TEN: self.base + place}

    def partners(self):
        return [self.other] + [self.peer(step)[1] for step in range(1, self.size)]


class Plane:
    def __init__(self):
        me = lax.axis_index(DP)
        self.me = me
        self.one = me + 1 - 2 * lax.rem(me, 2)
        self.two = lax.rem(me + 2, 4)
        self.both = lax.rem(self.one + 2, 4)

    def partners(self):
        return [{DP: self.one}, {DP: self.two}]

    def order(self, turn):
        return (self.one, self.two) if turn % 2 == 0 else (self.two, self.one)


def scatter_scratch(load):
    return [
        pltpu.VMEM((3,) + load.shape[1:], BF16),
        pltpu.VMEM(load.shape[1:], BF16),
        DMA((3,)),
        DMA((3,)),
    ]


class Scatter:
    def __init__(self, plane, turn, load, slots, part, sent, here):
        self.load, self.slots, self.part = load, slots, part
        self.me, self.both = plane.me, plane.both
        self.near, self.far = plane.order(turn)
        self.copies = [
            send_to(load.at[self.near], slots.at[0], sent.at[0], here.at[0], {DP: self.near}),
            send_to(load.at[self.both], slots.at[1], sent.at[1], here.at[1], {DP: self.near}),
            send_to(part, slots.at[2], sent.at[2], here.at[2], {DP: self.far}),
        ]

    def start(self):
        self.copies[1].start()
        self.copies[0].start()

    def middle(self):
        self.copies[1].wait_recv()
        self.part[...] = (self.load[self.far].astype(F32) + self.slots[1].astype(F32)).astype(BF16)
        self.copies[2].start()

    def total(self):
        self.copies[0].wait_recv()
        total = self.load[self.me].astype(F32) + self.slots[0].astype(F32)
        self.copies[2].wait_recv()
        return total + self.slots[2].astype(F32)

    def drain(self):
        for copy in self.copies:
            copy.wait_send()


class Gather:
    def __init__(self, plane, turn, whole, sent, here, active=None):
        self.whole, self.me, self.both, self.active = whole, plane.me, plane.both, active
        self.near, self.far = plane.order(turn)

        def copy(k, piece, device):
            at = whole.at[piece]
            return send_to(at, at, sent.at[k], here.at[piece], {DP: device})

        self.first = copy(0, self.me, self.near)
        self.second = [copy(1, self.me, self.far), copy(2, self.near, self.far)]
        self.coming = [copy(0, piece, self.near) for piece in (self.near, self.far, self.both)]

    def when(self, body):
        if self.active is None:
            body()
        else:
            pl.when(self.active)(body)

    def start(self, piece):
        def body():
            self.whole[self.me] = piece[...]
            self.first.start()
            self.second[0].start()

        self.when(body)

    def middle(self):
        def body():
            self.coming[0].wait_recv()
            self.second[1].start()

        self.when(body)

    def finish(self):
        def body():
            self.coming[1].wait_recv()
            self.coming[2].wait_recv()
            for copy in [self.first] + self.second:
                copy.wait_send()

        self.when(body)


def exchange_scratch(rows, model):
    team = lax.axis_size(TEN) // 2
    half = rows // PIECES // 2
    return [
        pltpu.VMEM((2, half, model), F32),
        pltpu.VMEM((PIECES, half, model), F32),
        pltpu.VMEM((PIECES, half, model), BF16),
        pltpu.VMEM((PIECES, half, model), BF16),
        pltpu.VMEM((team, PIECES, half, model), BF16),
        DMA((PIECES,)),
        DMA((PIECES,)),
        DMA((team, PIECES)),
        DMA((team, PIECES)),
        DMA((PIECES,)),
        DMA((PIECES,)),
    ]


EXCHANGE = 11


class Exchange:
    def __init__(self, team, refs):
        self.team = team
        (self.part, self.keep, self.out, self.got, self.far) = refs[:5]
        (self.core_sent, self.core_here, self.far_sent, self.far_here) = refs[5:9]
        (self.join_sent, self.join_here) = refs[9:]

    def core_copy(self, i):
        return send_to(
            self.out.at[i], self.got.at[i], self.core_sent.at[i], self.core_here.at[i], self.team.other
        )

    def far_copy(self, i, step, place):
        at = self.far.at[place, i]
        return send_to(
            at, at, self.far_sent.at[step, i], self.far_here.at[place, i], self.team.peer(step)[1]
        )

    def join_copy(self, i, whole):
        at = whole.at[i, self.team.core]
        return send_to(at, at, self.join_sent.at[i], self.join_here.at[i], self.team.other)

    def push(self, i, product):
        core = self.team.core
        self.part[...] = product.reshape(self.part.shape)
        self.out[i] = self.part[1 - core].astype(BF16)
        self.core_copy(i).start()
        self.keep[i] = self.part[core]

    def combine(self, i):
        self.core_copy(i).wait_recv()
        self.far[self.team.place, i] = (self.keep[i] + self.got[i].astype(F32)).astype(BF16)
        for step in range(1, self.team.size):
            self.far_copy(i, step, self.team.place).start()

    def send_all(self, product):
        def send(i):
            self.push(i, product(i))

            @pl.when(i > 0)
            def _():
                self.combine(i - 1)

        each_piece(send)
        self.combine(PIECES - 1)

    def total(self, i):
        for step in range(1, self.team.size):
            self.far_copy(i, step, self.team.peer(step)[0]).wait_recv()
        total = self.far[0, i].astype(F32)
        for place in range(1, self.team.size):
            total = total + self.far[place, i].astype(F32)
        return total

    def join(self, i, whole, half):
        whole[i, self.team.core] = half
        self.join_copy(i, whole).start()

    def finish(self, whole):
        def drain(i):
            self.core_copy(i).wait_send()
            for step in range(1, self.team.size):
                self.far_copy(i, step, self.team.place).wait_send()
            self.join_copy(i, whole).wait()

        each_piece(drain)


def each_piece(body):
    lax.fori_loop(0, PIECES, lambda i, _: (body(i), 0)[1], 0)


def piece_rows(i, rows):
    size = rows // PIECES
    return pl.ds(pl.multiple_of(i * size, size), size)


class Weights:
    def __init__(self, layer, refs, held, sems):
        self.held = held
        self.copies = []
        mine = lax.axis_index(SEC) == layer
        for k in range(3):
            own, far = (pltpu.make_async_copy(refs[3 * s + k], held[k], sems.at[k]) for s in range(2))
            pl.when(mine)(own.start)
            pl.when(jnp.logical_not(mine))(far.start)
            self.copies.append(own)

    def wait(self):
        for copy in self.copies:
            copy.wait()


def weights_scratch(own):
    return [pltpu.VMEM(matrix.shape, BF16) for matrix in own] + [DMA((3,))]


def team_kernel(body, counts, core, *refs):
    inner, loads, pieces, outs, scratch = counts

    def take(count):
        nonlocal refs
        taken, refs = refs[:count], refs[count:]
        return taken

    inner, loads, pieces = take(inner), take(loads), take(pieces)
    outs, sums, wholes = take(outs), take(len(loads)), take(len(pieces))
    scratch = take(scratch)
    team = Team()
    plane = Plane()
    scatters = [Scatter(plane, k, load, *take(4)) for k, load in enumerate(loads)]
    active = lax.axis_index(SEC) == core
    gathers = [Gather(plane, k, whole, *take(2), active) for k, whole in enumerate(wholes)]
    ex = Exchange(team, refs)
    greet(team.partners() + (plane.partners() if loads or pieces else []))
    for scatter in scatters:
        scatter.start()
    for gather, piece in zip(gathers, pieces):
        gather.start(piece)

    def middle():
        for item in gathers + scatters:
            item.middle()

    body(ex, middle, *inner, *outs, *scratch)
    for scatter, total in zip(scatters, sums):
        total[...] = scatter.total().astype(BF16)
        scatter.drain()
    for gather in gathers:
        gather.finish()


def team_call(body, number, model, outs, operands, scratch=(), loads=(), pieces=(), core=0, far=0):
    vmem = pl.BlockSpec(memory_space=pltpu.VMEM)
    dp = lax.axis_size(DP)
    counts = (len(operands), len(loads), len(pieces), len(outs), len(scratch))
    outs = outs + [(load.shape[1:], BF16) for load in loads]
    outs = outs + [((dp,) + piece.shape, BF16) for piece in pieces]
    beside = [item for load in loads for item in scatter_scratch(load)]
    beside = beside + [DMA((3,)), DMA((dp,))] * len(pieces)
    specs = [vmem] * (len(operands) - far) + [pl.BlockSpec(memory_space=pl.ANY)] * far
    return pl.pallas_call(
        functools.partial(team_kernel, body, counts, core),
        in_specs=specs + [vmem] * (len(loads) + len(pieces)),
        out_specs=[vmem] * len(outs),
        out_shape=[jax.ShapeDtypeStruct(*out) for out in outs],
        scratch_shapes=list(scratch) + beside + exchange_scratch(LEN, model),
        compiler_params=pltpu.CompilerParams(
            collective_id=number, has_side_effects=True, vmem_limit_bytes=VMEM_LIMIT
        ),
        cost_estimate=pl.CostEstimate(flops=LINK_FLOPS, bytes_accessed=2**22, transcendentals=0),
    )(*operands, *loads, *pieces)


def project_out(ex, middle, heads, w_out, source, gain, residual, mlp_in):
    rows = heads.shape[0]
    ex.send_all(lambda i: mm(heads[piece_rows(i, rows), :], w_out[...]))
    middle()

    def receive(i):
        block = source[i, ex.team.core].astype(F32) + ex.total(i)
        residual[i] = block
        ex.join(i, mlp_in, (block * reciprocal_rms(block) * gain[...]).astype(BF16))

    each_piece(receive)
    ex.finish(mlp_in)


def feed_forward(layer, ex, middle, mlp_in, residual, *refs):
    weights = Weights(layer, refs[:6], refs[10:13], refs[13])
    gate, up, hidden, output, w_gate, w_up, w_down = refs[6:13]
    rows = mlp_in.shape[0]
    weights.wait()

    def product(i):
        at = piece_rows(i, rows)
        block = mlp_in[at, :]
        gate_block = mm(block, w_gate[...], 1, 1)
        up_block = mm(block, w_up[...], 1, 1)
        hidden_block = (jax.nn.silu(gate_block) * up_block).astype(BF16)
        gate[at, :] = gate_block
        up[at, :] = up_block
        hidden[at, :] = hidden_block
        return mm(hidden_block, w_down[...])

    ex.send_all(product)
    middle()
    each_piece(lambda i: ex.join(i, output, (residual[i] + ex.total(i)).astype(BF16)))
    ex.finish(output)


def rms_back(block, gain, upstream):
    inverse = reciprocal_rms(block)
    normed = block * inverse
    scaled = upstream * gain
    grad = inverse * (scaled - normed * jnp.mean(scaled * normed, axis=-1, keepdims=True))
    return grad, jnp.sum(upstream * normed, axis=0, keepdims=True)


def feed_back(layer, ex, middle, upstream, gate, up, hidden, mlp_in, residual, gain, *refs):
    weights = Weights(layer, refs[:6], refs[14:17], refs[17])
    d_residual, res_grad, gain_grad, g_gate, g_up, g_down = refs[6:12]
    d_gate, d_up, w_gate, w_up, w_down = refs[12:17]
    rows, model = mlp_in.shape
    shape = (rows // PIECES, model)
    weights.wait()

    def product(i):
        at = piece_rows(i, rows)
        grad_hidden = mm(upstream[i].reshape(shape), w_down[...], 1, 1)
        gate_block = gate[at, :]
        sigmoid = jax.nn.sigmoid(gate_block)
        silu = gate_block * sigmoid
        d_gate_block = grad_hidden * up[at, :] * (sigmoid + silu * (1.0 - sigmoid))
        d_gate[at, :] = d_gate_block.astype(BF16)
        d_up[at, :] = (grad_hidden * silu).astype(BF16)
        return mm(d_gate[at, :], w_gate[...]) + mm(d_up[at, :], w_up[...])

    ex.send_all(product)
    g_gate[...] = mm(d_gate[...], mlp_in[...], 0, 0).astype(BF16)
    g_up[...] = mm(d_up[...], mlp_in[...], 0, 0).astype(BF16)
    g_down[...] = mm(hidden[...], upstream[...].reshape(rows, model), 0, 0).astype(BF16)
    middle()
    gain_grad[...] = jnp.zeros_like(gain_grad)

    def receive(i):
        part, gain_part = rms_back(residual[i], gain[...], ex.total(i))
        block = upstream[i, ex.team.core].astype(F32) + part
        d_residual[i] = block
        gain_grad[...] += gain_part
        ex.join(i, res_grad, block.astype(BF16))

    each_piece(receive)
    ex.finish(res_grad)


def attend_in_back(
    ex, middle, d_queries, d_latents, w_query, w_latent, source, d_residual, gain, attn_in,
    heads_out, res_grad, latents, d_keys, d_values, input_grad, gain_grad, grads, g_latent
):
    rows = d_queries.shape[0]

    def product(i):
        at = piece_rows(i, rows)
        return mm(d_queries[at, :], w_query[...], 1, 1) + mm(d_latents[at, :], w_latent[...], 1, 1)

    ex.send_all(product)
    model, width = w_query.shape
    grads[0:model, :] = mm(attn_in[...], d_queries[...], 0, 0).astype(BF16)
    g_latent[...] = mm(attn_in[...], d_latents[...], 0, 0).astype(BF16)
    grads[model : model + LH, :] = mm(latents[...], d_keys[...], 0, 0).astype(BF16)
    grads[model + LH : model + 2 * LH, :] = mm(latents[...], d_values[...], 0, 0).astype(BF16)
    g_out = mm(heads_out[...], res_grad[...], 0, 0).astype(BF16)
    for j, block in enumerate(pack_columns(g_out, width)):
        start = model + 2 * LH + j * width
        grads[start : start + width, :] = block
    middle()
    gain_grad[...] = jnp.zeros_like(gain_grad)

    def receive(i):
        part, gain_part = rms_back(source[i, ex.team.core].astype(F32), gain[...], ex.total(i))
        gain_grad[...] += gain_part
        ex.join(i, input_grad, (d_residual[i] + part).astype(BF16))

    each_piece(receive)
    ex.finish(input_grad)


def fetch_kernel(packed, latent, gains, whole, far_latent, far_gains, sent, here, gather_sent, gather_here):
    plane = Plane()
    count = lax.axis_size(TEN)
    core = lax.axis_index(SEC)
    opposite = lax.rem(lax.axis_index(TEN) + count // 2, count)
    other, across = {SEC: 1 - core}, {SEC: 1 - core, TEN: opposite}
    greet(plane.partners() + [other, across])
    piece = send_to(packed.at[plane.me], whole.at[plane.me], sent.at[0], here.at[0], across)
    small = [
        send_to(latent, far_latent, sent.at[1], here.at[1], other),
        send_to(gains, far_gains, sent.at[2], here.at[2], other),
    ]
    pl.when(core == 0)(piece.start)
    for copy in small:
        copy.start()
    gather = Gather(plane, 0, whole, gather_sent, gather_here)

    @pl.when(core == 1)
    def _():
        piece.wait_recv()
        gather.first.start()
        gather.second[0].start()
        gather.middle()
        gather.finish()

    for copy in small:
        copy.wait()
    pl.when(core == 0)(piece.wait_send)


def fetch(packed, latent, gains):
    vmem = pl.BlockSpec(memory_space=pltpu.VMEM)
    shapes = [jax.ShapeDtypeStruct(x.shape, x.dtype) for x in (packed, latent, gains)]
    return pl.pallas_call(
        fetch_kernel,
        in_specs=[vmem] * 3,
        out_specs=[vmem] * 3,
        out_shape=shapes,
        scratch_shapes=[DMA((3,)), DMA((3,)), DMA((3,)), DMA((4,))],
        compiler_params=pltpu.CompilerParams(
            collective_id=8, has_side_effects=True, vmem_limit_bytes=16 * 2**20
        ),
        cost_estimate=pl.CostEstimate(flops=LINK_FLOPS // 2, bytes_accessed=2**21, transcendentals=0),
    )(packed, latent, gains)


def finish_kernel(groups, *refs):
    feed, late, done, grad = refs[:3], refs[3:5], refs[5:7], refs[7]
    outs, grad_far = refs[8:13], refs[13]
    refs = refs[14:]
    come, leave, slots, held = refs[:5], refs[5:7], refs[7], refs[8]
    cross_sent, cross_here, gather_sent, gather_here = refs[9:13]
    block_sent, block_here, grad_sent, grad_here = refs[13:17]
    plane = Plane()
    team = Team()
    scatters = [Scatter(plane, k, late[k], *refs[17 + 4 * k : 21 + 4 * k]) for k in range(2)]
    count = lax.axis_size(TEN)
    z = lax.axis_index(TEN)
    core = lax.axis_index(SEC)
    first, second = core == 0, core == 1
    opposite = lax.rem(z + count // 2, count)
    across = {SEC: 1 - core, TEN: opposite}
    chips = [lax.rem(z + step, count) for step in range(1, count)]
    greet(plane.partners() + [across] + [{TEN: chip} for chip in chips])
    for scatter in scatters:
        scatter.start()
    sources = list(feed) + list(leave)
    crosses = [
        send_to(sources[k], come[k], cross_sent.at[k], cross_here.at[k], across) for k in range(5)
    ]

    @pl.when(second)
    def _():
        for k in range(3):
            crosses[k].start()

    share = grad.at[team.place], grad_far.at[team.place]
    grad_copies = [send_to(*share, grad_sent.at[0], grad_here.at[team.place], {TEN: opposite})]
    grad_coming = []
    for step in range(1, team.size):
        place, peer = team.peer(step)
        grad_copies.append(send_to(share[1], share[1], grad_sent.at[step], grad_here.at[team.place], peer))
        theirs = grad_far.at[place]
        grad_coming.append(send_to(theirs, theirs, grad_sent.at[step], grad_here.at[place], peer))
    pl.when(first)(grad_copies[0].start)
    actives = [first] * 3 + [None] * 2
    gathers = [
        Gather(plane, k, outs[k], gather_sent.at[k], gather_here.at[k], actives[k]) for k in range(5)
    ]

    def spread(k, total):
        outs[k][plane.me] = total
        gathers[k].first.start()
        gathers[k].second[0].start()

    for scatter in scatters:
        scatter.middle()
    for k, scatter in enumerate(scatters):
        leave[k][...] = scatter.total().astype(BF16)
        pl.when(second)(crosses[3 + k].start)

    def arrive(k):
        crosses[k].wait_recv()
        return (sources[k][...].astype(F32) + come[k][...].astype(F32)).astype(BF16)

    @pl.when(first)
    def _():
        for k in range(3):
            spread(k, arrive(k))
        grad_copies[0].wait_recv()
        for copy in grad_copies[1:]:
            copy.start()
        spread(3, arrive(3))
        held[...] = arrive(4).reshape(held.shape)

    @pl.when(second)
    def _():
        spread(3, done[0][...])
        held[...] = done[1][...].reshape(held.shape)

    def block(step, chip, slot):
        return send_to(held.at[chip], slots.at[slot], block_sent.at[step], block_here.at[slot], {TEN: chip})

    for step, chip in enumerate(chips):
        block(step, chip, z).start()
    slots[z] = held[z]
    for gather in gathers[:4]:
        gather.middle()
    for step, chip in enumerate(chips):
        block(step, chip, chip).wait_recv()
    shares = [slots[shard].astype(F32) for shard in range(count)]
    sums = [sum(s for s, g in zip(shares, groups) if g == group) for group in range(KVH)]
    gain_rows = sums[0]
    for extra in sums[1:]:
        gain_rows = gain_rows + extra
    depth = gain_rows.shape[0] - GAIN_ROWS
    gain_rows = gain_rows * (2.0 / count)
    blocks = [jnp.concatenate([part[:depth], gain_rows[depth:]], axis=0) for part in sums]
    spread(4, jnp.concatenate(blocks, axis=1).astype(BF16))
    gathers[4].middle()
    for gather in gathers:
        gather.finish()
    for scatter in scatters:
        scatter.drain()
    for step, chip in enumerate(chips):
        block(step, chip, z).wait_send()

    @pl.when(second)
    def _():
        for copy in crosses:
            copy.wait_send()

    @pl.when(first)
    def _():
        for copy in grad_copies:
            copy.wait_send()
        for copy in grad_coming:
            copy.wait_recv()


def finish(groups, feed, late, done, grad):
    pieces, count = lax.axis_size(DP), lax.axis_size(TEN)
    vmem = pl.BlockSpec(memory_space=pltpu.VMEM)
    depth = done[1].shape[0] // count
    ours = list(feed) + list(done)
    outs = [(pieces,) + part.shape for part in ours[:4]] + [(pieces, depth, KVH * LH), grad.shape]
    blocks = pltpu.VMEM((count, depth, LH), BF16)
    return pl.pallas_call(
        functools.partial(finish_kernel, groups),
        in_specs=[vmem] * 8,
        out_specs=[vmem] * 6,
        out_shape=[jax.ShapeDtypeStruct(out, BF16) for out in outs],
        scratch_shapes=[pltpu.VMEM(part.shape, BF16) for part in ours + list(done)] + [blocks, blocks]
        + [DMA((5,)), DMA((5,)), DMA((5, 3)), DMA((5, pieces)), DMA((count,)), DMA((count,))]
        + [DMA((count // 2,)), DMA((count // 2,))]
        + scatter_scratch(late[0]) + scatter_scratch(late[1]),
        compiler_params=pltpu.CompilerParams(
            collective_id=9, has_side_effects=True, vmem_limit_bytes=VMEM_LIMIT
        ),
    )(*feed, *late, *done, grad)


def pieces_of(block):
    return block.reshape(PIECES, 2, block.shape[0] // PIECES // 2, block.shape[1])


def attend_layer(source, weights):
    w_query, w_key_up, w_value_up, w_out, w_latent, gain_attn, gain_mlp = weights
    attn_in = (rms_scale(source.astype(F32)) * gain_attn).astype(BF16)
    queries = mm(attn_in, w_query).astype(BF16)
    latents = mm(attn_in, w_latent).astype(BF16)
    keys = mm(latents, w_key_up).astype(BF16)
    values = mm(latents, w_value_up).astype(BF16)
    heads_out, norms = attend_forward(queries, keys, values)
    return source, attn_in, queries, latents, keys, values, heads_out, norms


def shapes_of(rows, model):
    return (PIECES, 2, rows // PIECES // 2, model), (PIECES, rows // PIECES // 2, model)


def project_layer(number, kept, weights, pieces=(), core=1):
    source, heads_out = kept[0], kept[6]
    rows, model = source.shape
    split, own = shapes_of(rows, model)
    residual, mlp_in, *wholes = team_call(
        project_out, number, model, [(own, F32), (split, BF16)],
        (heads_out, weights[3], pieces_of(source), weights[6][None]),
        pieces=pieces, core=core,
    )
    return residual, mlp_in.reshape(rows, model), [whole_of(w) for w in wholes]


def feed_layer(number, layer, residual, mlp_in, own, far, pieces=()):
    rows, model = mlp_in.shape
    wide = (rows, own[0].shape[0])
    gate, up, hidden, output, *wholes = team_call(
        functools.partial(feed_forward, layer), number, model,
        [(wide, F32), (wide, F32), (wide, BF16), (shapes_of(rows, model)[0], BF16)],
        (mlp_in, residual, *own, *far),
        scratch=weights_scratch(own), pieces=pieces, core=0, far=6,
    )
    return output.reshape(rows, model), (gate, up, hidden), [whole_of(w) for w in wholes]


def feed_layer_back(number, layer, upstream, feed_kept, residual, mlp_in, gain, own, far, loads=()):
    rows, model = upstream.shape
    split, half = shapes_of(rows, model)
    wide = pltpu.VMEM((rows, own[0].shape[0]), BF16)
    outs = [(half, F32), (split, BF16), ((1, model), F32)] + [(w.shape, BF16) for w in own]
    d_residual, res_grad, gain_grad, *grads = team_call(
        functools.partial(feed_back, layer), number, model, outs,
        (pieces_of(upstream), *feed_kept, mlp_in, residual, gain[None], *own, *far),
        scratch=[wide, wide] + weights_scratch(own), loads=loads, far=6,
    )
    res_grad = res_grad.reshape(rows, model)
    return d_residual, res_grad, gain_grad, [by_dp(g) for g in grads[:3]], grads[3:]


def latent_parts(g_latent, gain_attn, gain_mlp):
    count, pieces = lax.axis_size(TEN), lax.axis_size(DP)
    model = g_latent.shape[0]
    depth = model // count // pieces
    rows = g_latent.reshape(count, pieces, depth, LH).transpose(1, 0, 2, 3)
    gains = jnp.stack([gain_attn[0], gain_mlp[0]]).astype(BF16).reshape(2, count, model // count)
    gains = gains.transpose(1, 0, 2)
    gains = jnp.pad(gains, ((0, 0), (0, GAIN_ROWS - 2), (0, LH - model // count)))
    gains = jnp.pad(gains[None], ((0, pieces - 1), (0, 0), (0, 0), (0, 0)))
    return jnp.concatenate([rows, gains], axis=2).reshape(pieces, count * (depth + GAIN_ROWS), LH)


def attend_layer_back(number, kept, d_residual, res_grad, gain_mlp_grad, weights, loads=(), pieces=()):
    w_query, w_key_up, w_value_up, w_out, w_latent, gain_attn, gain_mlp = weights
    source, attn_in, queries, latents, keys, values, heads_out, norms = kept
    rows, model = source.shape
    d_heads = mm(res_grad, w_out, 1, 1).astype(BF16)
    d_queries, d_keys, d_values = attend_backward(queries, keys, values, heads_out, d_heads, norms)
    d_latents = (mm(d_keys, w_key_up, 1, 1) + mm(d_values, w_value_up, 1, 1)).astype(BF16)
    packed = (2 * model + 2 * LH, w_query.shape[1])
    input_grad, gain_grad, grads, g_latent, *rest = team_call(
        attend_in_back, number, model,
        [(shapes_of(rows, model)[0], BF16), ((1, model), F32), (packed, BF16), (w_latent.shape, BF16)],
        (d_queries, d_latents, w_query, w_latent, pieces_of(source), d_residual, gain_attn[None], attn_in,
         heads_out, res_grad, latents, d_keys, d_values),
        loads=loads, pieces=pieces, core=1,
    )
    parts = [by_dp(grads), latent_parts(g_latent, gain_grad, gain_mlp_grad)]
    sums, wholes = rest[: len(loads)], rest[len(loads) :]
    return input_grad.reshape(rows, model), parts, sums, [whole_of(w) for w in wholes]


def tie(*arrays):
    return lax.optimization_barrier(arrays)


def local(
    inputs,
    out_grad,
    w_query,
    w_latent,
    w_key_up,
    w_value_up,
    w_out,
    w_gate,
    w_up,
    w_down,
    norm_attn,
    norm_mlp,
):
    at = Place()
    model = inputs.shape[1]
    heads = w_query.shape[2] // HD

    def group_of(shard):
        return shard * heads // (QH // KVH)

    opposite_z = (at.z + at.team) % at.count

    def latent_of(shard):
        return lax.dynamic_slice_in_dim(w_latent[0], group_of(shard) * LH, LH, 1)

    def dp_piece(matrix):
        rows = matrix.shape[0] // lax.axis_size(DP)
        return lax.dynamic_slice_in_dim(matrix, at.dp * rows, rows, 0)

    def sequence_rows(block):
        return lax.dynamic_slice_in_dim(block, at.sequence * LEN, LEN, 0)

    own_feed = (w_gate[0].T, w_up[0].T, w_down[0])
    own_packed = pack_attention(w_query[0], w_key_up[0], w_value_up[0], w_out[0])
    own_gains = jnp.concatenate([norm_attn, norm_mlp], axis=0)
    own_latent = latent_of(at.z)
    feed_zero = [at.across(dp_piece(w), 0) for w in own_feed]
    packed_zero, far_latent, far_gains = fetch(by_dp(own_packed), latent_of(opposite_z), own_gains)

    def attention_weights(mine, far_packed):
        packed = jnp.where(mine, own_packed, far_packed)
        gains = jnp.where(mine, own_gains, far_gains)
        latent = jnp.where(mine, own_latent, far_latent)
        return unpack_attention(packed, model) + (latent, gains[0], gains[1])

    weights_zero = attention_weights(at.first, whole_of(packed_zero))
    kept_zero = attend_layer(sequence_rows(inputs), weights_zero)
    heads_out, own_packed, *feed_zero = tie(kept_zero[6], own_packed, *feed_zero)
    kept_zero = kept_zero[:6] + (heads_out,) + kept_zero[7:]
    packed_one = at.across(dp_piece(own_packed), 1)
    residual_zero, mlp_zero, far_zero = project_layer(0, kept_zero, weights_zero, feed_zero)
    residual_zero, packed_one, *late_feed = tie(residual_zero, packed_one, *own_feed)
    feed_one = [at.across(dp_piece(w), 1) for w in late_feed]
    first_out, feed_kept_zero, (packed_one,) = feed_layer(
        1, 0, residual_zero, mlp_zero, own_feed, far_zero, [packed_one]
    )

    weights_one = attention_weights(jnp.logical_not(at.first), packed_one)
    kept_one = attend_layer(first_out, weights_one)
    heads_out, *feed_one = tie(kept_one[6], *feed_one)
    kept_one = kept_one[:6] + (heads_out,) + kept_one[7:]
    residual_one, mlp_one, far_one = project_layer(2, kept_one, weights_one, feed_one, 0)
    second_out, feed_kept_one, _ = feed_layer(3, 1, residual_one, mlp_one, own_feed, far_one)

    d_residual, res_grad, mlp_gain, feed_one, _ = feed_layer_back(
        4, 1, sequence_rows(out_grad), feed_kept_one, residual_one, mlp_one, weights_one[6], own_feed, far_one
    )
    layer_mine, d_residual = tie(jnp.where(at.first, first_out, second_out), d_residual)
    layer_far = at.opposite(layer_mine)
    second_grad, late_one, feed_one, _ = attend_layer_back(
        5, kept_one, d_residual, res_grad, mlp_gain, weights_one, feed_one
    )
    feed_cross = [at.across(part, 0) for part in feed_one]
    upstream, layer_far = tie(second_grad, layer_far)
    d_residual, res_grad, mlp_gain, feed_zero, late_one = feed_layer_back(
        6, 0, upstream, feed_kept_zero, residual_zero, mlp_zero, weights_zero[6], own_feed, far_zero, late_one
    )
    d_residual, second_grad, *feed_cross = tie(d_residual, second_grad, *feed_cross)
    grad_far = at.opposite(second_grad, (1,))

    def total(mine, other):
        return (mine.astype(F32) + other.astype(F32)).astype(BF16)

    feed_one = [total(mine, other) for mine, other in zip(feed_one, feed_cross)]
    late_cross = [at.across(part, 0) for part in late_one]
    first_grad, late_zero, feed_zero, wide_one = attend_layer_back(
        7, kept_zero, d_residual, res_grad, mlp_gain, weights_zero, feed_zero, feed_one
    )
    first_grad, grad_far, *late_cross = tie(first_grad, grad_far, *late_cross)
    late_one = [total(mine, other) for mine, other in zip(late_one, late_cross)]
    groups = tuple(group_of(shard) for shard in range(at.count))
    shared = first_grad.reshape(at.team, first_grad.shape[0] // at.team, model)
    *wide_zero, packed, latent, first_grad_far = finish(groups, feed_zero, late_zero, late_one, shared)

    def both_sequences(mine, other):
        both = jnp.broadcast_to(other[None], (2,) + other.shape)
        both = lax.dynamic_update_slice_in_dim(both, mine[None], at.sequence, 0)
        return both.reshape(1, 2 * other.shape[0], model)

    layer_out = both_sequences(layer_mine, layer_far)
    input_grad = both_sequences(
        jnp.where(at.first, first_grad, second_grad),
        jnp.where(at.first, first_grad_far.reshape(first_grad.shape), grad_far),
    )
    g_gate, g_up, g_down = [
        jnp.where(at.first, whole_of(zero), one).astype(F32) for zero, one in zip(wide_zero, wide_one)
    ]
    g_query, g_key_up, g_value_up, g_out = unpack_attention(whole_of(packed).astype(F32), model)
    width = model // at.count
    depth = latent.shape[1] - GAIN_ROWS
    g_latent = latent[:, :depth].reshape(width, KVH * LH).astype(F32)
    gains = latent[0, depth : depth + 2, :width].astype(F32)
    return (
        layer_out,
        input_grad,
        g_query[None],
        g_latent[None],
        g_key_up[None],
        g_value_up[None],
        g_out[None],
        g_gate.T[None],
        g_up.T[None],
        g_down[None],
        gains[0:1],
        gains[1:2],
    )


def solution(mesh):
    columns = P(SEC, None, TEN)
    rows = P(SEC, TEN, None)
    return jax.shard_map(
        local,
        mesh=mesh,
        in_specs=(
            P(DP, None),
            P(DP, None),
            columns,
            P(SEC, None, None),
            columns,
            columns,
            rows,
            columns,
            columns,
            rows,
            P(SEC, None),
            P(SEC, None),
        ),
        out_specs=(
            P(SEC, DP, None),
            P(SEC, DP, None),
            columns,
            rows,
            columns,
            columns,
            rows,
            columns,
            columns,
            rows,
            P(SEC, TEN),
            P(SEC, TEN),
        ),
        check_vma=False,
    )
```

```python
import functools
import math
import types

import jax
import jax.numpy as jnp
from jax import lax
from jax.experimental import pallas as pl
from jax.experimental.pallas import tpu as pltpu
from jax.sharding import PartitionSpec as P

QH = 16
HD = 64
KVH = 2
LH = 256
LEN = 1024
EPS = 1e-05
F32 = jnp.float32
BF16 = jnp.bfloat16
SEC, DP, TEN = "section", "dp", "tensor"
LOG2_SCALE = HD**-0.5 * math.log2(math.e)
KEY_ROWS = 256


def mm(left, right, left_dim=1, right_dim=0):
    dims = (((left_dim,), (right_dim,)), ((), ()))
    return lax.dot_general(left, right, dims, preferred_element_type=F32)


def head_masks(width):
    if width == HD:
        return [None]
    lane = lax.broadcasted_iota(jnp.int32, (1, width), 1)
    return [lane // HD == j for j in range(width // HD)]


def keep_head(block, mask):
    return block if mask is None else jnp.where(mask, block, jnp.zeros_like(block))


def attend_rows(start, q_ref, k_ref, v_ref, o_ref, norm_ref):
    columns = q_ref.shape[1]
    width = min(2 * HD, columns)
    masks = head_masks(width)
    rows = KEY_ROWS
    place_k = lax.broadcasted_iota(jnp.int32, (rows, rows), 0)
    place_q = lax.broadcasted_iota(jnp.int32, (rows, rows), 1)
    for pair in range(columns // width):
        lanes = slice(pair * width, (pair + 1) * width)
        query = q_ref[start : start + rows, lanes]
        total = None
        for j, mask in enumerate(masks):
            query_j = keep_head(query, mask)
            scores = mm(k_ref[start : start + rows, lanes], query_j, 1, 1) * LOG2_SCALE
            scores = jnp.where(place_k <= place_q, scores, -jnp.inf)
            largest = jnp.max(scores, axis=0, keepdims=True)
            if start:
                before = mm(k_ref[0:start, lanes], query_j, 1, 1) * LOG2_SCALE
                largest = jnp.maximum(largest, jnp.max(before, axis=0, keepdims=True))
            weight = jnp.exp2(scores - largest)
            norm = jnp.sum(weight, axis=0, keepdims=True)
            value = keep_head(v_ref[start : start + rows, lanes], mask)
            out = mm(value, weight.astype(BF16), 0, 0)
            if start:
                weight = jnp.exp2(before - largest)
                norm = norm + jnp.sum(weight, axis=0, keepdims=True)
                value = keep_head(v_ref[0:start, lanes], mask)
                out = out + mm(value, weight.astype(BF16), 0, 0)
            out = out / norm
            total = out if total is None else total + out
            norm_ref[pair, j : j + 1, start : start + rows] = largest + jnp.log2(norm)
        o_ref[start : start + rows, lanes] = total.T.astype(BF16)


def attend_back_kernel(q_ref, k_ref, v_ref, o_ref, g_ref, norm_ref, dq_ref, dk_ref, dv_ref, acc):
    width = q_ref.shape[1]
    masks = head_masks(width)
    rows = KEY_ROWS
    place_k = lax.broadcasted_iota(jnp.int32, (rows, rows), 0)
    place_q = lax.broadcasted_iota(jnp.int32, (rows, rows), 1)
    product = g_ref[...].astype(F32) * o_ref[...].astype(F32)
    product = product.T
    acc[...] = jnp.zeros_like(acc)
    deltas = [
        jnp.sum(product[j * HD : (j + 1) * HD, :], axis=0, keepdims=True)
        for j in range(len(masks))
    ]
    for start in range(0, LEN, rows):
        end = start + rows
        key = k_ref[start:end, :]
        value = v_ref[start:end, :]
        grad_key = grad_value = None
        for j, mask in enumerate(masks):
            query_j = keep_head(q_ref[start:, :], mask)
            grad_j = keep_head(g_ref[start:, :], mask)
            scores = mm(key, query_j, 1, 1) * LOG2_SCALE
            probs = jnp.exp2(scores - norm_ref[0, j : j + 1, start:])
            first = jnp.where(place_k <= place_q, probs[:, :rows], 0.0)
            probs = first if end == LEN else jnp.concatenate([first, probs[:, rows:]], axis=1)
            grad_probs = mm(value, grad_j, 1, 1)
            grad_scores = (probs * (grad_probs - deltas[j][:, start:])).astype(BF16)
            value_term = mm(probs.astype(BF16), grad_j)
            key_term = mm(grad_scores, query_j)
            grad_key = key_term if grad_key is None else grad_key + key_term
            grad_value = value_term if grad_value is None else grad_value + value_term
            acc[:, start:] += mm(keep_head(key, mask), grad_scores, 0, 0)
        dk_ref[start:end, :] = (grad_key * HD**-0.5).astype(BF16)
        dv_ref[start:end, :] = grad_value.astype(BF16)
    dq_ref[...] = (acc[...].T * HD**-0.5).astype(BF16)


def attend_backward(queries, keys, values, heads_out, grad_heads, norms):
    rows, columns = queries.shape
    width = min(2 * HD, columns)
    heads = width // HD
    spec = pl.BlockSpec((rows, width), lambda i: (0, i))
    shape = jax.ShapeDtypeStruct((rows, columns), BF16)
    return pl.pallas_call(
        attend_back_kernel,
        grid=(columns // width,),
        in_specs=[spec] * 5 + [pl.BlockSpec((1, heads, rows), lambda i: (i, 0, 0))],
        out_specs=[spec] * 3,
        out_shape=[shape] * 3,
        scratch_shapes=[pltpu.VMEM((width, rows), F32)],
        compiler_params=pltpu.CompilerParams(vmem_limit_bytes=40 * 2**20),
        cost_estimate=pl.CostEstimate(
            flops=rows * rows * columns * 20, bytes_accessed=rows * columns * 16, transcendentals=0
        ),
    )(queries, keys, values, heads_out, grad_heads, norms)


def rms_scale(features):
    return features * lax.rsqrt(jnp.mean(features * features, axis=-1, keepdims=True) + EPS)


class Place:
    def __init__(self):
        self.count = lax.axis_size(TEN)
        self.team = self.count // 2
        self.z = lax.axis_index(TEN)
        self.core = lax.axis_index(SEC)
        self.dp = lax.axis_index(DP)
        self.sequence = self.z // self.team
        self.first = self.core == 0

    def opposite(self, block, cores=(0, 1)):
        n, t = self.count, self.team
        route = [(core * n + z, core * n + (z + t) % n) for core in cores for z in range(n)]
        return lax.ppermute(block, (SEC, TEN), route)

    def across(self, block, core):
        n, t = self.count, self.team
        route = [(core * n + z, (1 - core) * n + (z + t) % n) for z in range(n)]
        return lax.ppermute(block, (SEC, TEN), route)


def pack_columns(matrix, width):
    return [matrix[:, i : i + width] for i in range(0, matrix.shape[1], width)]


def pack_attention(query, key_up, value_up, out):
    width = query.shape[1]
    return jnp.concatenate([query, key_up, value_up] + pack_columns(out, width), axis=0)


def unpack_attention(packed, model):
    width = packed.shape[1]
    query = packed[:model]
    key_up = packed[model : model + LH]
    value_up = packed[model + LH : model + 2 * LH]
    rest = packed[model + 2 * LH :]
    out = jnp.concatenate([rest[i : i + width] for i in range(0, rest.shape[0], width)], axis=1)
    return query, key_up, value_up, out


def by_dp(matrix):
    count = lax.axis_size(DP)
    return matrix.reshape(count, matrix.shape[0] // count, matrix.shape[1])


def whole_of(pieces):
    return pieces.reshape(-1, pieces.shape[2])


MESH = pl.DeviceIdType.MESH
PIECES = 4
VMEM_LIMIT = 58 * 2**20
LINK_FLOPS = 4 * 10**9
GAIN_ROWS = 16
DMA = pltpu.SemaphoreType.DMA


def reciprocal_rms(features):
    return lax.rsqrt(jnp.mean(features * features, axis=-1, keepdims=True) + EPS)


def send_to(source, target, sent, here, device):
    return pltpu.make_async_remote_copy(
        src_ref=source,
        dst_ref=target,
        send_sem=sent,
        recv_sem=here,
        device_id=device,
        device_id_type=MESH,
    )


def greet(partners):
    barrier = pltpu.get_barrier_semaphore()
    for partner in partners:
        pl.semaphore_signal(barrier, inc=1, device_id=partner, device_id_type=MESH)
    pl.semaphore_wait(barrier, len(partners))


class Team:
    def __init__(self):
        count = lax.axis_size(TEN)
        self.size = count // 2
        self.core = lax.axis_index(SEC)
        z = lax.axis_index(TEN)
        self.place = lax.rem(z, self.size)
        self.base = z - self.place
        self.other = {SEC: 1 - self.core}

    def peer(self, step):
        place = lax.rem(self.place + step, self.size)
        return place, {TEN: self.base + place}

    def partners(self):
        return [self.other] + [self.peer(step)[1] for step in range(1, self.size)]


class Plane:
    def __init__(self):
        me = lax.axis_index(DP)
        self.me = me
        self.one = me + 1 - 2 * lax.rem(me, 2)
        self.two = lax.rem(me + 2, 4)
        self.both = lax.rem(self.one + 2, 4)

    def partners(self):
        return [{DP: self.one}, {DP: self.two}]

    def order(self, turn):
        return (self.one, self.two) if turn % 2 == 0 else (self.two, self.one)


def scatter_scratch(load):
    return [
        pltpu.VMEM((3,) + load.shape[1:], BF16),
        pltpu.VMEM(load.shape[1:], BF16),
        DMA((3,)),
        DMA((3,)),
    ]


class Scatter:
    def __init__(self, plane, turn, load, slots, part, sent, here):
        self.load, self.slots, self.part = load, slots, part
        self.me, self.both = plane.me, plane.both
        self.near, self.far = plane.order(turn)
        self.copies = [
            send_to(load.at[self.near], slots.at[0], sent.at[0], here.at[0], {DP: self.near}),
            send_to(load.at[self.both], slots.at[1], sent.at[1], here.at[1], {DP: self.near}),
            send_to(part, slots.at[2], sent.at[2], here.at[2], {DP: self.far}),
        ]

    def start(self):
        self.copies[1].start()
        self.copies[0].start()

    def middle(self):
        self.copies[1].wait_recv()
        self.part[...] = (self.load[self.far].astype(F32) + self.slots[1].astype(F32)).astype(BF16)
        self.copies[2].start()

    def total(self):
        self.copies[0].wait_recv()
        total = self.load[self.me].astype(F32) + self.slots[0].astype(F32)
        self.copies[2].wait_recv()
        return total + self.slots[2].astype(F32)

    def drain(self):
        for copy in self.copies:
            copy.wait_send()


class Gather:
    def __init__(self, plane, turn, whole, sent, here, active=None):
        self.whole, self.me, self.both, self.active = whole, plane.me, plane.both, active
        self.near, self.far = plane.order(turn)

        def copy(k, piece, device):
            at = whole.at[piece]
            return send_to(at, at, sent.at[k], here.at[piece], {DP: device})

        self.first = copy(0, self.me, self.near)
        self.second = [copy(1, self.me, self.far), copy(2, self.near, self.far)]
        self.coming = [copy(0, piece, self.near) for piece in (self.near, self.far, self.both)]

    def when(self, body):
        if self.active is None:
            body()
        else:
            pl.when(self.active)(body)

    def start(self, piece):
        def body():
            self.whole[self.me] = piece[...]
            self.first.start()
            self.second[0].start()

        self.when(body)

    def middle(self):
        def body():
            self.coming[0].wait_recv()
            self.second[1].start()

        self.when(body)

    def finish(self):
        def body():
            self.coming[1].wait_recv()
            self.coming[2].wait_recv()
            for copy in [self.first] + self.second:
                copy.wait_send()

        self.when(body)


def exchange_scratch(rows, model):
    team = lax.axis_size(TEN) // 2
    half = rows // PIECES // 2
    return [
        pltpu.VMEM((2, half, model), F32),
        pltpu.VMEM((PIECES, half, model), F32),
        pltpu.VMEM((PIECES, half, model), BF16),
        pltpu.VMEM((PIECES, half, model), BF16),
        pltpu.VMEM((team, PIECES, half, model), BF16),
        DMA((PIECES,)),
        DMA((PIECES,)),
        DMA((team, PIECES)),
        DMA((team, PIECES)),
        DMA((PIECES,)),
        DMA((PIECES,)),
    ]


EXCHANGE = 11


class Exchange:
    def __init__(self, team, refs):
        self.team = team
        (self.part, self.keep, self.out, self.got, self.far) = refs[:5]
        (self.core_sent, self.core_here, self.far_sent, self.far_here) = refs[5:9]
        (self.join_sent, self.join_here) = refs[9:]

    def core_copy(self, i):
        return send_to(
            self.out.at[i], self.got.at[i], self.core_sent.at[i], self.core_here.at[i], self.team.other
        )

    def far_copy(self, i, step, place):
        at = self.far.at[place, i]
        return send_to(
            at, at, self.far_sent.at[step, i], self.far_here.at[place, i], self.team.peer(step)[1]
        )

    def join_copy(self, i, whole):
        at = whole.at[i, self.team.core]
        return send_to(at, at, self.join_sent.at[i], self.join_here.at[i], self.team.other)

    def push(self, i, product):
        core = self.team.core
        self.part[...] = product.reshape(self.part.shape)
        self.out[i] = self.part[1 - core].astype(BF16)
        self.core_copy(i).start()
        self.keep[i] = self.part[core]

    def combine(self, i):
        self.core_copy(i).wait_recv()
        self.far[self.team.place, i] = (self.keep[i] + self.got[i].astype(F32)).astype(BF16)
        for step in range(1, self.team.size):
            self.far_copy(i, step, self.team.place).start()

    def send_all(self, product):
        def send(i):
            self.push(i, product(i))

            @pl.when(i > 0)
            def _():
                self.combine(i - 1)

        each_piece(send)
        self.combine(PIECES - 1)

    def total(self, i):
        for step in range(1, self.team.size):
            self.far_copy(i, step, self.team.peer(step)[0]).wait_recv()
        total = self.far[0, i].astype(F32)
        for place in range(1, self.team.size):
            total = total + self.far[place, i].astype(F32)
        return total

    def join(self, i, whole, half):
        whole[i, self.team.core] = half
        self.join_copy(i, whole).start()

    def finish(self, whole, coming=True):
        def drain(i):
            self.core_copy(i).wait_send()
            for step in range(1, self.team.size):
                self.far_copy(i, step, self.team.place).wait_send()
            self.join_copy(i, whole).wait_send()
            if coming:
                self.join_copy(i, whole).wait_recv()

        each_piece(drain)


def each_piece(body):
    lax.fori_loop(0, PIECES, lambda i, _: (body(i), 0)[1], 0)


def piece_rows(i, rows):
    size = rows // PIECES
    return pl.ds(pl.multiple_of(i * size, size), size)


class Weights:
    def __init__(self, layer, refs, held, sems):
        self.held = held
        self.copies = []
        mine = lax.axis_index(SEC) == layer
        for k in range(3):
            own, far = (pltpu.make_async_copy(refs[3 * s + k], held[k], sems.at[k]) for s in range(2))
            pl.when(mine)(own.start)
            pl.when(jnp.logical_not(mine))(far.start)
            self.copies.append(own)

    def wait(self):
        for copy in self.copies:
            copy.wait()


def weights_scratch(own):
    return [pltpu.VMEM(matrix.shape, BF16) for matrix in own] + [DMA((3,))]


class Beside:
    def __init__(self, loads=(), pieces=(), core=0, crosses=(), sender=0, add=False):
        self.loads, self.pieces, self.crosses = list(loads), list(pieces), list(crosses)
        self.core, self.sender, self.add = core, sender, add

    def operands(self):
        return self.loads + self.pieces + self.crosses

    def cross_shape(self, cross):
        return cross.shape if self.add else cross.shape[1:]

    def outs(self):
        dp = lax.axis_size(DP)
        shapes = [load.shape[1:] for load in self.loads]
        shapes = shapes + [(dp,) + piece.shape for piece in self.pieces]
        return [(shape, BF16) for shape in shapes + [self.cross_shape(c) for c in self.crosses]]

    def specs(self):
        vmem = pl.BlockSpec(memory_space=pltpu.VMEM)
        held = len(self.loads) + len(self.pieces)
        cross = vmem if self.add else pl.BlockSpec(memory_space=pl.ANY)
        return [vmem] * held + [cross] * len(self.crosses)

    def scratch(self):
        items = [item for load in self.loads for item in scatter_scratch(load)]
        items = items + [DMA((3,)), DMA((lax.axis_size(DP),))] * len(self.pieces)
        return items + [DMA, DMA] * len(self.crosses)

    def counts(self):
        return len(self.loads), len(self.pieces), len(self.crosses)


def across_device():
    count = lax.axis_size(TEN)
    opposite = lax.rem(lax.axis_index(TEN) + count // 2, count)
    return {SEC: 1 - lax.axis_index(SEC), TEN: opposite}


def team_kernel(body, counts, beside, add, cores, *refs):
    inner, outs, scratch = counts
    loads, pieces, crosses = beside
    gather_core, sender = cores

    def take(count):
        nonlocal refs
        taken, refs = refs[:count], refs[count:]
        return taken

    inner, loads, pieces, crosses = take(inner), take(loads), take(pieces), take(crosses)
    outs, sums, wholes = take(outs), take(len(loads)), take(len(pieces))
    comes, scratch = take(len(crosses)), take(scratch)
    team = Team()
    plane = Plane()
    core = lax.axis_index(SEC)
    scatters = [Scatter(plane, k, load, *take(4)) for k, load in enumerate(loads)]
    gathers = [Gather(plane, k, whole, *take(2), core == gather_core) for k, whole in enumerate(wholes)]
    across = across_device()
    sources = [cross if add else cross.at[plane.me] for cross in crosses]
    copies = [send_to(source, come, *take(2), across) for source, come in zip(sources, comes)]
    ex = Exchange(team, refs)
    partners = team.partners()
    if loads or pieces:
        partners = partners + plane.partners()
    if crosses:
        partners = partners + [across]
    greet(partners)
    for scatter in scatters:
        scatter.start()
    for gather, piece in zip(gathers, pieces):
        gather.start(piece)
    for copy in copies:
        pl.when(core == sender)(copy.start)

    def middle():
        for item in gathers + scatters:
            item.middle()

    body(ex, middle, *inner, *outs, *scratch)
    for scatter, total in zip(scatters, sums):
        total[...] = scatter.total().astype(BF16)
        scatter.drain()
    for gather in gathers:
        gather.finish()
    for copy in copies:
        pl.when(core == sender)(copy.wait_send)

    @pl.when(core != sender)
    def _():
        for copy, source, come in zip(copies, sources, comes):
            copy.wait_recv()
            if add:
                come[...] = (source[...].astype(F32) + come[...].astype(F32)).astype(BF16)


def team_call(body, number, model, outs, operands, scratch=(), beside=None, far=0):
    vmem = pl.BlockSpec(memory_space=pltpu.VMEM)
    beside = beside or Beside()
    counts = (len(operands), len(outs), len(scratch))
    outs = outs + beside.outs()
    specs = [vmem] * (len(operands) - far) + [pl.BlockSpec(memory_space=pl.ANY)] * far
    cores = (beside.core, beside.sender)
    return pl.pallas_call(
        functools.partial(team_kernel, body, counts, beside.counts(), beside.add, cores),
        in_specs=specs + beside.specs(),
        out_specs=[vmem] * len(outs),
        out_shape=[jax.ShapeDtypeStruct(*out) for out in outs],
        scratch_shapes=list(scratch) + beside.scratch() + exchange_scratch(LEN, model),
        compiler_params=pltpu.CompilerParams(
            collective_id=number, has_side_effects=True, vmem_limit_bytes=VMEM_LIMIT
        ),
        cost_estimate=pl.CostEstimate(flops=LINK_FLOPS, bytes_accessed=2**20, transcendentals=0),
    )(*operands, *beside.operands())


def rms_back(block, gain, upstream):
    inverse = reciprocal_rms(block)
    normed = block * inverse
    scaled = upstream * gain
    grad = inverse * (scaled - normed * jnp.mean(scaled * normed, axis=-1, keepdims=True))
    return grad, jnp.sum(upstream * normed, axis=0, keepdims=True)


def feed_back(layer, ex, middle, upstream, gate, up, hidden, mlp_in, residual, gain, *refs):
    weights = Weights(layer, refs[:6], refs[14:17], refs[17])
    d_residual, res_grad, gain_grad, g_gate, g_up, g_down = refs[6:12]
    d_gate, d_up, w_gate, w_up, w_down = refs[12:17]
    rows, model = mlp_in.shape
    shape = (rows // PIECES, model)
    weights.wait()

    def product(i):
        at = piece_rows(i, rows)
        grad_hidden = mm(upstream[i].reshape(shape), w_down[...], 1, 1)
        gate_block = gate[at, :]
        sigmoid = jax.nn.sigmoid(gate_block)
        silu = gate_block * sigmoid
        d_gate_block = grad_hidden * up[at, :] * (sigmoid + silu * (1.0 - sigmoid))
        d_gate[at, :] = d_gate_block.astype(BF16)
        d_up[at, :] = (grad_hidden * silu).astype(BF16)
        return mm(d_gate[at, :], w_gate[...]) + mm(d_up[at, :], w_up[...])

    ex.send_all(product)
    g_gate[...] = mm(d_gate[...], mlp_in[...], 0, 0).astype(BF16)
    g_up[...] = mm(d_up[...], mlp_in[...], 0, 0).astype(BF16)
    g_down[...] = mm(hidden[...], upstream[...].reshape(rows, model), 0, 0).astype(BF16)
    middle()
    gain_grad[...] = jnp.zeros_like(gain_grad)

    def receive(i):
        part, gain_part = rms_back(residual[i], gain[...], ex.total(i))
        block = upstream[i, ex.team.core].astype(F32) + part
        d_residual[i] = block
        gain_grad[...] += gain_part
        ex.join(i, res_grad, block.astype(BF16))

    each_piece(receive)
    ex.finish(res_grad)


def attend_in_back(
    ex, middle, d_queries, d_latents, w_query, w_latent, source, d_residual, gain, attn_in,
    heads_out, res_grad, latents, d_keys, d_values, input_grad, gain_grad, grads, g_latent
):
    rows = d_queries.shape[0]

    def product(i):
        at = piece_rows(i, rows)
        return mm(d_queries[at, :], w_query[...], 1, 1) + mm(d_latents[at, :], w_latent[...], 1, 1)

    ex.send_all(product)
    model, width = w_query.shape
    grads[0:model, :] = mm(attn_in[...], d_queries[...], 0, 0).astype(BF16)
    g_latent[...] = mm(attn_in[...], d_latents[...], 0, 0).astype(BF16)
    grads[model : model + LH, :] = mm(latents[...], d_keys[...], 0, 0).astype(BF16)
    grads[model + LH : model + 2 * LH, :] = mm(latents[...], d_values[...], 0, 0).astype(BF16)
    g_out = mm(heads_out[...], res_grad[...], 0, 0).astype(BF16)
    for j, block in enumerate(pack_columns(g_out, width)):
        start = model + 2 * LH + j * width
        grads[start : start + width, :] = block
    middle()
    gain_grad[...] = jnp.zeros_like(gain_grad)

    def receive(i):
        part, gain_part = rms_back(source[i, ex.team.core].astype(F32), gain[...], ex.total(i))
        gain_grad[...] += gain_part
        ex.join(i, input_grad, (d_residual[i] + part).astype(BF16))

    each_piece(receive)
    ex.finish(input_grad)


def named_call(kernel, number, ins, far, outs, scratch, flops=LINK_FLOPS):
    ins, far, outs, scratch = (dict(group) for group in (ins, far, outs, scratch))
    spec = {id(ins): pl.BlockSpec(memory_space=pltpu.VMEM), id(far): pl.BlockSpec(memory_space=pl.ANY)}
    operands, specs, shapes, items = [], [], [], []
    layout = []
    for group, store in ((ins, operands), (far, operands), (outs, shapes), (scratch, items)):
        for name, value in group.items():
            values = value if isinstance(value, list) else [value]
            layout.append((name, len(values) if isinstance(value, list) else None))
            store.extend(values)
            if store is operands:
                specs.extend([spec[id(group)]] * len(values))

    def body(*refs):
        named, refs = {}, list(refs)
        for name, count in layout:
            taken, refs = refs[: count if count is not None else 1], refs[count if count is not None else 1 :]
            named[name] = taken if count is not None else taken[0]
        kernel(types.SimpleNamespace(**named))

    results = pl.pallas_call(
        body,
        in_specs=specs,
        out_specs=[pl.BlockSpec(memory_space=pl.ANY if len(out) > 2 else pltpu.VMEM) for out in shapes],
        out_shape=[jax.ShapeDtypeStruct(*out[:2]) for out in shapes],
        scratch_shapes=items,
        compiler_params=pltpu.CompilerParams(
            collective_id=number, has_side_effects=True, vmem_limit_bytes=VMEM_LIMIT
        ),
        cost_estimate=pl.CostEstimate(flops=flops, bytes_accessed=2**20, transcendentals=0),
    )(*operands)
    named, results = {}, list(results)
    for name, value in outs.items():
        if isinstance(value, list):
            named[name], results = results[: len(value)], results[len(value) :]
        else:
            named[name], results = results[0], results[1:]
    return types.SimpleNamespace(**named)


def forward_kernel(layer, r):
    team = Team()
    plane = Plane()
    core = lax.axis_index(SEC)
    holder = core == layer
    taker = jnp.logical_not(holder)
    across = across_device()
    ex_a, ex_b = Exchange(team, r.ex_a), Exchange(team, r.ex_b)
    abroad = across if layer == 0 else {TEN: across[TEN]}
    greet(team.partners() + plane.partners() + [abroad])
    rows, width = r.queries.shape
    model = r.w_latent.shape[0]
    size = rows // PIECES
    feeds = range(3)

    own_copies = [pltpu.make_async_copy(r.own_feed[k], r.feed[k], r.own_sem.at[k]) for k in feeds]
    for copy in own_copies:
        pl.when(holder)(copy.start)
    gathers = [
        Gather(plane, k, r.feed[k], r.gather_sent.at[k], r.gather_here.at[k], taker) for k in feeds
    ]

    def cross(k, source, target):
        return send_to(source, target, r.cross_sent.at[k], r.cross_here.at[k], across)

    if layer == 0:
        mine = cross(0, r.own_packed.at[plane.me], r.packed.at[plane.me])
        small = [
            send_to(r.pass_latent, r.far_latent, r.small_sent.at[0], r.small_here.at[0], team.other),
            send_to(r.own_gains, r.far_gains, r.small_sent.at[1], r.small_here.at[1], team.other),
        ]
        come = [cross(1 + k, r.own_feed[k].at[plane.me], r.come[k]) for k in feeds]
        next_packed = cross(4, r.own_packed.at[plane.me], r.packed_next.at[plane.me])
        next_feed = [cross(5 + k, r.own_feed[k].at[plane.me], r.feed_next[k]) for k in feeds]
        packed_gather = Gather(plane, 0, r.packed, r.packed_sent, r.packed_here)
        next_gather = Gather(plane, 1, r.packed_next, r.next_sent, r.next_here)
        pl.when(holder)(mine.start)
        for copy in small:
            copy.start()
        for copy in small:
            copy.wait()
    else:
        before = send_to(r.before, r.before_far, r.before_sent, r.before_here, abroad)
        pl.when(core == 0)(before.start)
        for k in feeds:
            gathers[k].start(r.pieces[k])
    gains = jnp.where(holder, r.own_gains[...], r.far_gains[...])
    r.gains[...] = gains
    r.w_latent[...] = jnp.where(holder, r.own_latent[...], r.far_latent[...])

    def norm(i):
        block = r.source[i].reshape(size, model).astype(F32)
        r.attn_in[piece_rows(i, rows), :] = (block * reciprocal_rms(block) * gains[0:1]).astype(BF16)

    each_piece(norm)
    if layer == 0:

        @pl.when(taker)
        def _():
            mine.wait_recv()
            packed_gather.first.start()
            packed_gather.second[0].start()
            packed_gather.middle()
            packed_gather.finish()
            r.packed_next[...] = r.own_packed[...]

        @pl.when(holder)
        def _():
            r.packed[...] = r.own_packed[...]
            mine.wait_send()
            for copy in come:
                copy.start()

    weights = r.packed[...].reshape(2 * model + 2 * LH, width)

    def project(i):
        at = piece_rows(i, rows)
        block = r.attn_in[at, :]
        r.queries[at, :] = mm(block, weights[:model]).astype(BF16)
        latents = mm(block, r.w_latent[...]).astype(BF16)
        r.latents[at, :] = latents
        r.keys[at, :] = mm(latents, weights[model : model + LH]).astype(BF16)
        r.values[at, :] = mm(latents, weights[model + LH : model + 2 * LH]).astype(BF16)

    each_piece(project)
    w_out = [
        weights[model + 2 * LH + start : model + 2 * LH + start + width] for start in range(0, model, width)
    ]
    for i in range(PIECES):
        attend_rows(i * size, r.queries, r.keys, r.values, r.heads_out, r.norms)
        heads = r.heads_out[i * size : (i + 1) * size, :]
        ex_a.push(i, jnp.concatenate([mm(heads, block) for block in w_out], axis=1))
        if i:
            ex_a.combine(i - 1)
    ex_a.combine(PIECES - 1)
    if layer == 0:
        pl.when(taker)(next_packed.start)

        @pl.when(taker)
        def _():
            for k in feeds:
                come[k].wait_recv()
                gathers[k].whole[plane.me] = r.come[k][...]
                gathers[k].first.start()
                gathers[k].second[0].start()

    def receive(i):
        block = r.source[i, core].astype(F32) + ex_a.total(i)
        r.residual[i] = block
        ex_a.join(i, r.mlp_in, (block * reciprocal_rms(block) * gains[1:2]).astype(BF16))

    def feed(i):
        ex_a.join_copy(i, r.mlp_in).wait_recv()
        at = piece_rows(i, rows)
        block = r.mlp_in[i].reshape(size, model)
        shape = (r.hidden.shape[1], model)
        gate = mm(block, r.feed[0][...].reshape(shape), 1, 1)
        up = mm(block, r.feed[1][...].reshape(shape), 1, 1)
        hidden = (jax.nn.silu(gate) * up).astype(BF16)
        r.gate[at, :] = gate
        r.up[at, :] = up
        r.hidden[at, :] = hidden
        ex_b.push(i, mm(hidden, r.feed[2][...].reshape(shape)))

    receive(0)
    for gather in gathers:
        gather.middle()

    @pl.when(holder)
    def _():
        for copy in own_copies:
            copy.wait()

    for gather in gathers:
        gather.finish()
    receive(1)
    feed(0)
    if layer == 0:

        @pl.when(taker)
        def _():
            for copy in next_feed:
                copy.start()

        @pl.when(holder)
        def _():
            next_packed.wait_recv()
            next_gather.first.start()
            next_gather.second[0].start()

    def steady(i, _):
        receive(i)
        feed(i - 1)
        ex_b.combine(i - 2)
        return 0

    lax.fori_loop(2, PIECES, steady, 0)
    feed(PIECES - 1)
    ex_b.combine(PIECES - 2)
    ex_b.combine(PIECES - 1)
    if layer == 0:
        pl.when(holder)(next_gather.middle)
    each_piece(lambda i: ex_b.join(i, r.output, (r.residual[i] + ex_b.total(i)).astype(BF16)))
    ex_a.finish(r.mlp_in, False)
    ex_b.finish(r.output)
    if layer == 0:

        @pl.when(holder)
        def _():
            next_gather.finish()
            for copy in come:
                copy.wait_send()
            for copy in next_feed:
                copy.wait_recv()

        @pl.when(taker)
        def _():
            next_packed.wait_send()
            for copy in next_feed:
                copy.wait_send()
    else:
        pl.when(core == 0)(before.wait)


def finish_kernel(groups, *refs):
    feed, late, done, grad = refs[:3], refs[3:5], refs[5:7], refs[7]
    outs, grad_far = refs[8:13], refs[13]
    refs = refs[14:]
    come, leave, slots, held = refs[:5], refs[5:7], refs[7], refs[8]
    cross_sent, cross_here, gather_sent, gather_here = refs[9:13]
    block_sent, block_here, grad_sent, grad_here = refs[13:17]
    plane = Plane()
    team = Team()
    scatters = [Scatter(plane, k, late[k], *refs[17 + 4 * k : 21 + 4 * k]) for k in range(2)]
    count = lax.axis_size(TEN)
    z = lax.axis_index(TEN)
    core = lax.axis_index(SEC)
    first, second = core == 0, core == 1
    opposite = lax.rem(z + count // 2, count)
    across = {SEC: 1 - core, TEN: opposite}
    chips = [lax.rem(z + step, count) for step in range(1, count)]
    greet(plane.partners() + [across] + [{TEN: chip} for chip in chips])
    for scatter in scatters:
        scatter.start()
    sources = list(feed) + list(leave)
    crosses = [
        send_to(sources[k], come[k], cross_sent.at[k], cross_here.at[k], across) for k in range(5)
    ]

    @pl.when(second)
    def _():
        for k in range(3):
            crosses[k].start()

    share = grad.at[team.place], grad_far.at[team.place]
    grad_copies = [send_to(*share, grad_sent.at[0], grad_here.at[team.place], {TEN: opposite})]
    grad_coming = []
    for step in range(1, team.size):
        place, peer = team.peer(step)
        grad_copies.append(send_to(share[1], share[1], grad_sent.at[step], grad_here.at[team.place], peer))
        theirs = grad_far.at[place]
        grad_coming.append(send_to(theirs, theirs, grad_sent.at[step], grad_here.at[place], peer))
    actives = [first] * 3 + [None] * 2
    gathers = [
        Gather(plane, k, outs[k], gather_sent.at[k], gather_here.at[k], actives[k]) for k in range(5)
    ]

    def spread(k, total):
        outs[k][plane.me] = total
        gathers[k].first.start()
        gathers[k].second[0].start()

    def arrive(k):
        crosses[k].wait_recv()
        return (sources[k][...].astype(F32) + come[k][...].astype(F32)).astype(BF16)

    for scatter in scatters:
        scatter.middle()
    for k, scatter in enumerate(scatters):
        leave[k][...] = scatter.total().astype(BF16)
        pl.when(second)(crosses[3 + k].start)

    @pl.when(first)
    def _():
        spread(0, arrive(0))
        grad_copies[0].start()
        spread(1, arrive(1))
        spread(2, arrive(2))
        spread(3, arrive(3))
        held[...] = arrive(4).reshape(held.shape)

    @pl.when(second)
    def _():
        spread(3, done[0][...])
        held[...] = done[1][...].reshape(held.shape)

    def block(step, chip, slot):
        return send_to(held.at[chip], slots.at[slot], block_sent.at[step], block_here.at[slot], {TEN: chip})

    for step, chip in enumerate(chips):
        block(step, chip, z).start()
    slots[z] = held[z]
    for gather in gathers[:4]:
        gather.middle()
    for step, chip in enumerate(chips):
        block(step, chip, chip).wait_recv()

    @pl.when(first)
    def _():
        grad_copies[0].wait_recv()
        for copy in grad_copies[1:]:
            copy.start()

    shares = [slots[shard].astype(F32) for shard in range(count)]
    sums = [sum(s for s, g in zip(shares, groups) if g == group) for group in range(KVH)]
    gain_rows = sums[0]
    for extra in sums[1:]:
        gain_rows = gain_rows + extra
    depth = gain_rows.shape[0] - GAIN_ROWS
    gain_rows = gain_rows * (2.0 / count)
    blocks = [jnp.concatenate([part[:depth], gain_rows[depth:]], axis=0) for part in sums]
    spread(4, jnp.concatenate(blocks, axis=1).astype(BF16))
    gathers[4].middle()
    for gather in gathers:
        gather.finish()
    for scatter in scatters:
        scatter.drain()
    for step, chip in enumerate(chips):
        block(step, chip, z).wait_send()

    @pl.when(second)
    def _():
        for copy in crosses:
            copy.wait_send()

    @pl.when(first)
    def _():
        for copy in grad_copies:
            copy.wait_send()
        for copy in grad_coming:
            copy.wait_recv()


def finish(groups, feed, late, done, grad):
    pieces, count = lax.axis_size(DP), lax.axis_size(TEN)
    vmem = pl.BlockSpec(memory_space=pltpu.VMEM)
    depth = done[1].shape[0] // count
    ours = list(feed) + list(done)
    outs = [(pieces,) + part.shape for part in ours[:4]] + [(pieces, depth, KVH * LH), grad.shape]
    blocks = pltpu.VMEM((count, depth, LH), BF16)
    return pl.pallas_call(
        functools.partial(finish_kernel, groups),
        in_specs=[vmem] * 8,
        out_specs=[vmem] * 6,
        out_shape=[jax.ShapeDtypeStruct(out, BF16) for out in outs],
        scratch_shapes=[pltpu.VMEM(part.shape, BF16) for part in ours + list(done)] + [blocks, blocks]
        + [DMA((5,)), DMA((5,)), DMA((5, 3)), DMA((5, pieces)), DMA((count,)), DMA((count,))]
        + [DMA((count // 2,)), DMA((count // 2,))]
        + scatter_scratch(late[0]) + scatter_scratch(late[1]),
        compiler_params=pltpu.CompilerParams(
            collective_id=9, has_side_effects=True, vmem_limit_bytes=VMEM_LIMIT
        ),
    )(*feed, *late, *done, grad)


def pieces_of(block):
    return block.reshape(PIECES, 2, block.shape[0] // PIECES // 2, block.shape[1])


def shapes_of(rows, model):
    return (PIECES, 2, rows // PIECES // 2, model), (PIECES, rows // PIECES // 2, model)


def forward_layer(layer, number, source, ins, far):
    rows, model = source.shape
    split, own = shapes_of(rows, model)
    packed = ins[dict_key(ins, 0)]
    pieces, depth, width = packed.shape
    feed = far[dict_key(far, 0)]
    wide = (rows, pieces * feed[0].shape[1])
    pair = min(2 * HD, width)
    narrow = ((rows, width), BF16)
    outs = dict(
        attn_in=((rows, model), BF16),
        queries=narrow,
        latents=((rows, LH), BF16),
        keys=narrow,
        values=narrow,
        heads_out=narrow,
        norms=((width // pair, pair // HD, rows), F32),
        residual=(own, F32),
        mlp_in=(split, BF16),
        gate=(wide, F32),
        up=(wide, F32),
        hidden=(wide, BF16),
        output=(split, BF16),
        w_latent=((model, LH), BF16),
        gains=((2, model), F32),
        feed=[(w.shape, BF16) for w in feed],
    )
    scratch = dict(
        ex_a=exchange_scratch(rows, model),
        ex_b=exchange_scratch(rows, model),
        own_sem=DMA((3,)),
        gather_sent=DMA((3, 3)),
        gather_here=DMA((3, pieces)),
        cross_sent=DMA((8,)),
        cross_here=DMA((8,)),
    )
    if layer == 0:
        outs.update(
            packed=(packed.shape, BF16),
            far_latent=((model, LH), BF16),
            far_gains=((2, model), F32),
            packed_next=(packed.shape, BF16),
            feed_next=[(w.shape[1:], BF16) for w in feed],
        )
        scratch.update(
            come=[pltpu.VMEM(w.shape[1:], BF16) for w in feed],
            small_sent=DMA((2,)),
            small_here=DMA((2,)),
            packed_sent=DMA((3,)),
            packed_here=DMA((pieces,)),
            next_sent=DMA((3,)),
            next_here=DMA((pieces,)),
        )
    else:
        outs.update(before_far=((rows, model), BF16, True))
        scratch.update(before_sent=DMA, before_here=DMA)
    ins = dict(source=pieces_of(source), **ins)
    return named_call(functools.partial(forward_kernel, layer), number, ins, far, outs, scratch)


def dict_key(group, index):
    return list(group)[index]


def feed_layer_back(number, layer, upstream, feed_kept, residual, mlp_in, gain, own, far, beside=None):
    rows, model = upstream.shape
    split, half = shapes_of(rows, model)
    wide = pltpu.VMEM((rows, own[0].shape[0]), BF16)
    outs = [(half, F32), (split, BF16), ((1, model), F32)] + [(w.shape, BF16) for w in own]
    d_residual, res_grad, gain_grad, *grads = team_call(
        functools.partial(feed_back, layer), number, model, outs,
        (pieces_of(upstream), *feed_kept, mlp_in, residual, gain[None], *own, *far),
        scratch=[wide, wide] + weights_scratch(own), beside=beside, far=6,
    )
    res_grad = res_grad.reshape(rows, model)
    return d_residual, res_grad, gain_grad, [by_dp(g) for g in grads[:3]], grads[3:]


def latent_parts(g_latent, gain_attn, gain_mlp):
    count, pieces = lax.axis_size(TEN), lax.axis_size(DP)
    model = g_latent.shape[0]
    depth = model // count // pieces
    rows = g_latent.reshape(count, pieces, depth, LH).transpose(1, 0, 2, 3)
    gains = jnp.stack([gain_attn[0], gain_mlp[0]]).astype(BF16).reshape(2, count, model // count)
    gains = gains.transpose(1, 0, 2)
    gains = jnp.pad(gains, ((0, 0), (0, GAIN_ROWS - 2), (0, LH - model // count)))
    gains = jnp.pad(gains[None], ((0, pieces - 1), (0, 0), (0, 0), (0, 0)))
    return jnp.concatenate([rows, gains], axis=2).reshape(pieces, count * (depth + GAIN_ROWS), LH)


def attend_layer_back(number, kept, d_residual, res_grad, gain_mlp_grad, weights, beside):
    w_query, w_key_up, w_value_up, w_out, w_latent, gain_attn, gain_mlp = weights
    source, attn_in, queries, latents, keys, values, heads_out, norms = kept
    rows, model = source.shape
    d_heads = mm(res_grad, w_out, 1, 1).astype(BF16)
    d_queries, d_keys, d_values = attend_backward(queries, keys, values, heads_out, d_heads, norms)
    d_latents = (mm(d_keys, w_key_up, 1, 1) + mm(d_values, w_value_up, 1, 1)).astype(BF16)
    packed = (2 * model + 2 * LH, w_query.shape[1])
    input_grad, gain_grad, grads, g_latent, *rest = team_call(
        attend_in_back, number, model,
        [(shapes_of(rows, model)[0], BF16), ((1, model), F32), (packed, BF16), (w_latent.shape, BF16)],
        (d_queries, d_latents, w_query, w_latent, pieces_of(source), d_residual, gain_attn[None], attn_in,
         heads_out, res_grad, latents, d_keys, d_values),
        beside=beside,
    )
    parts = [by_dp(grads), latent_parts(g_latent, gain_grad, gain_mlp_grad)]
    return input_grad.reshape(rows, model), parts, rest


def tie(*arrays):
    return lax.optimization_barrier(arrays)


def local(
    inputs,
    out_grad,
    w_query,
    w_latent,
    w_key_up,
    w_value_up,
    w_out,
    w_gate,
    w_up,
    w_down,
    norm_attn,
    norm_mlp,
):
    at = Place()
    model = inputs.shape[1]
    heads = w_query.shape[2] // HD

    def group_of(shard):
        return shard * heads // (QH // KVH)

    opposite_z = (at.z + at.team) % at.count

    def latent_of(shard):
        return lax.dynamic_slice_in_dim(w_latent[0], group_of(shard) * LH, LH, 1)

    def sequence_rows(block):
        return lax.dynamic_slice_in_dim(block, at.sequence * LEN, LEN, 0)

    own_feed = [by_dp(w) for w in (w_gate[0].T, w_up[0].T, w_down[0])]
    own_packed = by_dp(pack_attention(w_query[0], w_key_up[0], w_value_up[0], w_out[0]))
    own_gains = jnp.concatenate([norm_attn, norm_mlp], axis=0)
    own_latent = latent_of(at.z)
    zero = forward_layer(
        0,
        0,
        sequence_rows(inputs),
        dict(own_packed=own_packed, own_gains=own_gains, own_latent=own_latent, pass_latent=latent_of(opposite_z)),
        dict(own_feed=own_feed),
    )
    first_out = zero.output.reshape(LEN, model)
    one = forward_layer(
        1,
        1,
        first_out,
        dict(
            packed=zero.packed_next,
            own_gains=own_gains,
            far_gains=zero.far_gains,
            own_latent=own_latent,
            far_latent=zero.far_latent,
            pieces=zero.feed_next,
        ),
        dict(own_feed=own_feed, before=first_out),
    )
    second_out = one.output.reshape(LEN, model)
    first_far = one.before_far

    def attention_weights(packed, result):
        return unpack_attention(whole_of(packed), model) + (result.w_latent, result.gains[0], result.gains[1])

    def kept_of(source, result):
        attention = (source, result.attn_in, result.queries, result.latents, result.keys, result.values)
        attention = attention + (result.heads_out, result.norms)
        return attention, (result.gate, result.up, result.hidden), [whole_of(w) for w in result.feed]

    weights_zero = attention_weights(zero.packed, zero)
    weights_one = attention_weights(zero.packed_next, one)
    kept_zero, feed_kept_zero, far_zero = kept_of(sequence_rows(inputs), zero)
    kept_one, feed_kept_one, far_one = kept_of(first_out, one)
    residual_zero, mlp_zero = zero.residual, zero.mlp_in.reshape(LEN, model)
    residual_one, mlp_one = one.residual, one.mlp_in.reshape(LEN, model)

    d_residual, res_grad, mlp_gain, feed_one, _ = feed_layer_back(
        4, 1, sequence_rows(out_grad), feed_kept_one, residual_one, mlp_one, weights_one[6], far_one, far_one
    )
    second_sent, d_residual = tie(second_out, d_residual)
    second_far = at.opposite(second_sent, (1,))
    second_grad, late_one, feed_one = attend_layer_back(
        5, kept_one, d_residual, res_grad, mlp_gain, weights_one, Beside(loads=feed_one)
    )
    upstream, second_far = tie(second_grad, second_far)
    beside = Beside(loads=late_one, crosses=feed_one, sender=0, add=True)
    d_residual, res_grad, mlp_gain, feed_zero, rest = feed_layer_back(
        6, 0, upstream, feed_kept_zero, residual_zero, mlp_zero, weights_zero[6], far_zero, far_zero, beside
    )
    late_one, feed_one = rest[:2], rest[2:]
    d_residual, second_sent = tie(d_residual, second_grad)
    grad_far = at.opposite(second_sent, (1,))
    beside = Beside(loads=feed_zero, pieces=feed_one, core=1, crosses=late_one, sender=0, add=True)
    first_grad, late_zero, rest = attend_layer_back(
        7, kept_zero, d_residual, res_grad, mlp_gain, weights_zero, beside
    )
    feed_zero, wide_one, late_one = rest[:3], [whole_of(w) for w in rest[3:6]], rest[6:]
    first_grad, grad_far = tie(first_grad, grad_far)
    groups = tuple(group_of(shard) for shard in range(at.count))
    shared = first_grad.reshape(at.team, first_grad.shape[0] // at.team, model)
    *wide_zero, packed, latent, first_grad_far = finish(groups, feed_zero, late_zero, late_one, shared)

    def both_sequences(mine, other):
        both = jnp.broadcast_to(other[None], (2,) + other.shape)
        both = lax.dynamic_update_slice_in_dim(both, mine[None], at.sequence, 0)
        return both.reshape(1, 2 * other.shape[0], model)

    layer_out = both_sequences(
        jnp.where(at.first, first_out, second_out), jnp.where(at.first, first_far, second_far)
    )
    input_grad = both_sequences(
        jnp.where(at.first, first_grad, second_grad),
        jnp.where(at.first, first_grad_far.reshape(first_grad.shape), grad_far),
    )
    g_gate, g_up, g_down = [
        jnp.where(at.first, whole_of(zero), one).astype(F32) for zero, one in zip(wide_zero, wide_one)
    ]
    g_query, g_key_up, g_value_up, g_out = unpack_attention(whole_of(packed).astype(F32), model)
    width = model // at.count
    depth = latent.shape[1] - GAIN_ROWS
    g_latent = latent[:, :depth].reshape(width, KVH * LH).astype(F32)
    gains = latent[0, depth : depth + 2, :width].astype(F32)
    return (
        layer_out,
        input_grad,
        g_query[None],
        g_latent[None],
        g_key_up[None],
        g_value_up[None],
        g_out[None],
        g_gate.T[None],
        g_up.T[None],
        g_down[None],
        gains[0:1],
        gains[1:2],
    )


def solution(mesh):
    columns = P(SEC, None, TEN)
    rows = P(SEC, TEN, None)
    return jax.shard_map(
        local,
        mesh=mesh,
        in_specs=(
            P(DP, None),
            P(DP, None),
            columns,
            P(SEC, None, None),
            columns,
            columns,
            rows,
            columns,
            columns,
            rows,
            P(SEC, None),
            P(SEC, None),
        ),
        out_specs=(
            P(SEC, DP, None),
            P(SEC, DP, None),
            columns,
            rows,
            columns,
            columns,
            rows,
            columns,
            columns,
            rows,
            P(SEC, TEN),
            P(SEC, TEN),
        ),
        check_vma=False,
    )
```

```python
import functools
import math
import types

import jax
import jax.numpy as jnp
from jax import lax
from jax.experimental import pallas as pl
from jax.experimental.pallas import tpu as pltpu
from jax.sharding import PartitionSpec as P

QH = 16
HD = 64
KVH = 2
LH = 256
LEN = 1024
EPS = 1e-05
F32 = jnp.float32
BF16 = jnp.bfloat16
SEC, DP, TEN = "section", "dp", "tensor"
LOG2_SCALE = HD**-0.5 * math.log2(math.e)
KEY_ROWS = 256


def mm(left, right, left_dim=1, right_dim=0):
    dims = (((left_dim,), (right_dim,)), ((), ()))
    return lax.dot_general(left, right, dims, preferred_element_type=F32)


def head_masks(width):
    if width == HD:
        return [None]
    lane = lax.broadcasted_iota(jnp.int32, (1, width), 1)
    return [lane // HD == j for j in range(width // HD)]


def keep_head(block, mask):
    return block if mask is None else jnp.where(mask, block, jnp.zeros_like(block))


def attend_rows(start, q_ref, k_ref, v_ref, o_ref, norm_ref):
    columns = q_ref.shape[1]
    width = min(2 * HD, columns)
    masks = head_masks(width)
    rows = KEY_ROWS
    place_k = lax.broadcasted_iota(jnp.int32, (rows, rows), 0)
    place_q = lax.broadcasted_iota(jnp.int32, (rows, rows), 1)
    for pair in range(columns // width):
        lanes = slice(pair * width, (pair + 1) * width)
        query = q_ref[start : start + rows, lanes]
        total = None
        for j, mask in enumerate(masks):
            query_j = keep_head(query, mask)
            scores = mm(k_ref[start : start + rows, lanes], query_j, 1, 1) * LOG2_SCALE
            scores = jnp.where(place_k <= place_q, scores, -jnp.inf)
            largest = jnp.max(scores, axis=0, keepdims=True)
            if start:
                before = mm(k_ref[0:start, lanes], query_j, 1, 1) * LOG2_SCALE
                largest = jnp.maximum(largest, jnp.max(before, axis=0, keepdims=True))
            weight = jnp.exp2(scores - largest)
            norm = jnp.sum(weight, axis=0, keepdims=True)
            value = keep_head(v_ref[start : start + rows, lanes], mask)
            out = mm(value, weight.astype(BF16), 0, 0)
            if start:
                weight = jnp.exp2(before - largest)
                norm = norm + jnp.sum(weight, axis=0, keepdims=True)
                value = keep_head(v_ref[0:start, lanes], mask)
                out = out + mm(value, weight.astype(BF16), 0, 0)
            out = out / norm
            total = out if total is None else total + out
            norm_ref[pair, j : j + 1, start : start + rows] = largest + jnp.log2(norm)
        o_ref[start : start + rows, lanes] = total.T.astype(BF16)


def attend_rows_back(start, q_ref, k_ref, v_ref, o_ref, g_ref, norm_ref, dq_ref, key_total, value_total):
    columns = q_ref.shape[1]
    width = min(2 * HD, columns)
    masks = head_masks(width)
    rows = KEY_ROWS
    end = start + rows
    place_k = lax.broadcasted_iota(jnp.int32, (rows, rows), 0)
    place_q = lax.broadcasted_iota(jnp.int32, (rows, rows), 1)
    for pair in range(columns // width):
        lanes = slice(pair * width, (pair + 1) * width)
        query, grad = q_ref[start:end, lanes], g_ref[start:end, lanes]
        key, value = k_ref[0:end, lanes], v_ref[0:end, lanes]
        product = (grad.astype(F32) * o_ref[start:end, lanes].astype(F32)).T
        grad_query = grad_key = grad_value = None
        for j, mask in enumerate(masks):
            query_j = keep_head(query, mask)
            grad_j = keep_head(grad, mask)
            delta = jnp.sum(product[j * HD : (j + 1) * HD, :], axis=0, keepdims=True)
            scores = mm(key, query_j, 1, 1) * LOG2_SCALE
            probs = jnp.exp2(scores - norm_ref[pair, j : j + 1, start:end])
            last = jnp.where(place_k <= place_q, probs[start:], 0.0)
            probs = jnp.concatenate([probs[:start], last], axis=0) if start else last
            grad_probs = mm(value, grad_j, 1, 1)
            grad_scores = (probs * (grad_probs - delta)).astype(BF16)
            value_term = mm(probs.astype(BF16), grad_j)
            key_term = mm(grad_scores, query_j)
            query_term = mm(keep_head(key, mask), grad_scores, 0, 0)
            grad_key = key_term if grad_key is None else grad_key + key_term
            grad_value = value_term if grad_value is None else grad_value + value_term
            grad_query = query_term if grad_query is None else grad_query + query_term
        dq_ref[start:end, lanes] = (grad_query.T * HD**-0.5).astype(BF16)
        if end == LEN:
            key_total[:, lanes] = grad_key
            value_total[:, lanes] = grad_value
        else:
            key_total[0:end, lanes] += grad_key
            value_total[0:end, lanes] += grad_value


def rms_scale(features):
    return features * lax.rsqrt(jnp.mean(features * features, axis=-1, keepdims=True) + EPS)


class Place:
    def __init__(self):
        self.count = lax.axis_size(TEN)
        self.team = self.count // 2
        self.z = lax.axis_index(TEN)
        self.core = lax.axis_index(SEC)
        self.dp = lax.axis_index(DP)
        self.sequence = self.z // self.team
        self.first = self.core == 0

    def opposite(self, block, cores=(0, 1)):
        n, t = self.count, self.team
        route = [(core * n + z, core * n + (z + t) % n) for core in cores for z in range(n)]
        return lax.ppermute(block, (SEC, TEN), route)

    def across(self, block, core):
        n, t = self.count, self.team
        route = [(core * n + z, (1 - core) * n + (z + t) % n) for z in range(n)]
        return lax.ppermute(block, (SEC, TEN), route)


def pack_columns(matrix, width):
    return [matrix[:, i : i + width] for i in range(0, matrix.shape[1], width)]


def pack_attention(query, key_up, value_up, out):
    width = query.shape[1]
    return jnp.concatenate([query, key_up, value_up] + pack_columns(out, width), axis=0)


def by_dp(matrix):
    count = lax.axis_size(DP)
    return matrix.reshape(count, matrix.shape[0] // count, matrix.shape[1])


def whole_of(pieces):
    return pieces.reshape(-1, pieces.shape[2])


MESH = pl.DeviceIdType.MESH
PIECES = 4
VMEM_LIMIT = 58 * 2**20
LINK_FLOPS = 4 * 10**9
GAIN_ROWS = 16
FEED = 3
DMA = pltpu.SemaphoreType.DMA


def reciprocal_rms(features):
    return lax.rsqrt(jnp.mean(features * features, axis=-1, keepdims=True) + EPS)


def send_to(source, target, sent, here, device):
    return pltpu.make_async_remote_copy(
        src_ref=source,
        dst_ref=target,
        send_sem=sent,
        recv_sem=here,
        device_id=device,
        device_id_type=MESH,
    )


def greet(partners):
    barrier = pltpu.get_barrier_semaphore()
    for partner in partners:
        pl.semaphore_signal(barrier, inc=1, device_id=partner, device_id_type=MESH)
    pl.semaphore_wait(barrier, len(partners))


class Team:
    def __init__(self):
        count = lax.axis_size(TEN)
        self.size = count // 2
        self.core = lax.axis_index(SEC)
        z = lax.axis_index(TEN)
        self.place = lax.rem(z, self.size)
        self.base = z - self.place
        self.other = {SEC: 1 - self.core}

    def peer(self, step):
        place = lax.rem(self.place + step, self.size)
        return place, {TEN: self.base + place}

    def partners(self):
        return [self.other] + [self.peer(step)[1] for step in range(1, self.size)]


class Plane:
    def __init__(self):
        me = lax.axis_index(DP)
        self.me = me
        self.one = me + 1 - 2 * lax.rem(me, 2)
        self.two = lax.rem(me + 2, 4)
        self.both = lax.rem(self.one + 2, 4)

    def partners(self):
        return [{DP: self.one}, {DP: self.two}]

    def order(self, turn):
        return (self.one, self.two) if turn % 2 == 0 else (self.two, self.one)


def scatter_scratch(load):
    piece = load.shape[1:]
    return [pltpu.VMEM((3,) + piece, BF16), pltpu.VMEM((3,) + piece, BF16), DMA((3,)), DMA((3,)), DMA((2,))]


class Scatter:
    def __init__(self, plane, turn, load, slots, held, sent, here, local):
        near, far = plane.order(turn)
        self.slots, self.held = slots, held
        self.copies = [
            send_to(load.at[near], slots.at[0], sent.at[0], here.at[0], {DP: near}),
            send_to(load.at[plane.both], slots.at[1], sent.at[1], here.at[1], {DP: near}),
            send_to(held.at[2], slots.at[2], sent.at[2], here.at[2], {DP: far}),
        ]
        self.local = [
            pltpu.make_async_copy(load.at[plane.me], held.at[0], local.at[0]),
            pltpu.make_async_copy(load.at[far], held.at[1], local.at[1]),
        ]

    def start(self):
        self.copies[1].start()
        self.copies[0].start()
        for copy in self.local:
            copy.start()

    def middle(self):
        self.local[1].wait()
        self.copies[1].wait_recv()
        self.held[2] = (self.held[1].astype(F32) + self.slots[1].astype(F32)).astype(BF16)
        self.copies[2].start()

    def total(self):
        self.local[0].wait()
        self.copies[0].wait_recv()
        total = self.held[0].astype(F32) + self.slots[0].astype(F32)
        self.copies[2].wait_recv()
        return total + self.slots[2].astype(F32)

    def drain(self):
        for copy in self.copies:
            copy.wait_send()


class Gather:
    def __init__(self, plane, turn, whole, sent, here, active=None, piece=None, local=None):
        self.active = active
        near, far = plane.order(turn)
        me = plane.me
        source = whole.at[me] if piece is None else piece

        def copy(k, source, place, device):
            return send_to(source, whole.at[place], sent.at[k], here.at[place], {DP: device})

        self.first = copy(0, source, me, near)
        self.second = [copy(1, source, me, far), copy(2, whole.at[near], near, far)]
        self.coming = [copy(0, whole.at[place], place, near) for place in (near, far, plane.both)]
        self.local = [] if piece is None else [pltpu.make_async_copy(piece, whole.at[me], local)]

    def when(self, body):
        if self.active is None:
            body()
        else:
            pl.when(self.active)(body)

    def start(self):
        def body():
            for copy in [self.first, self.second[0]] + self.local:
                copy.start()

        self.when(body)

    def middle(self):
        def body():
            self.coming[0].wait_recv()
            self.second[1].start()

        self.when(body)

    def finish(self):
        def body():
            self.coming[1].wait_recv()
            self.coming[2].wait_recv()
            for copy in [self.first] + self.second:
                copy.wait_send()
            for copy in self.local:
                copy.wait()

        self.when(body)


def across_device():
    count = lax.axis_size(TEN)
    opposite = lax.rem(lax.axis_index(TEN) + count // 2, count)
    return {SEC: 1 - lax.axis_index(SEC), TEN: opposite}


class Beside:
    def __init__(self, loads=(), crosses=(), gathered=False, shares=(), spreads=()):
        team = lax.axis_size(TEN) // 2
        self.shared = [[core for _, core in group] for group in (shares, spreads)]
        shares, spreads = ([block for block, _ in group] for group in (shares, spreads))
        self.far = dict(loads=list(loads), crosses=list(crosses), shares=shares, spreads=spreads)
        pieces = [cross.shape for cross in crosses]
        dp = lax.axis_size(DP)
        self.outs = dict(
            sums=[(load.shape[1:], BF16) for load in loads], totals=[(piece, BF16) for piece in pieces]
        )
        self.far_outs = dict(
            wholes=[((dp,) + piece, BF16) for piece in pieces] if gathered else [],
            shares_here=[(block.shape[1:], BF16) for block in shares],
            spreads_here=[((team,) + block.shape, BF16) for block in spreads],
        )
        count = max(1, len(pieces))
        self.scratch = dict(
            scatter=[item for load in loads for item in scatter_scratch(load)],
            comes=[pltpu.VMEM(piece, BF16) for piece in pieces],
            cross_sems=[DMA((count,)), DMA((count,)), DMA((count,)), DMA((count,))],
            gather_sems=[DMA((count, 3)), DMA((count, dp))],
            share_sems=[DMA, DMA] * len(shares),
            spread_sems=[DMA((team,)), DMA((team,)), DMA] * len(spreads),
        )


class BesideRun:
    def __init__(self, r, plane, sender, shared):
        self.outputs = Outputs(r, shared)
        self.totals, self.comes, self.sums = r.totals, r.comes, r.sums
        self.scatters = [
            Scatter(plane, k, load, *r.scatter[5 * k : 5 * k + 5]) for k, load in enumerate(r.loads)
        ]
        self.sends = lax.axis_index(SEC) == sender
        self.takes = jnp.logical_not(self.sends)
        across = across_device()
        sent, here, own, local = r.cross_sems
        self.copies = [
            send_to(cross, r.comes[k], sent.at[k], here.at[k], across) for k, cross in enumerate(r.crosses)
        ]
        self.own = [pltpu.make_async_copy(cross, r.totals[k], own.at[k]) for k, cross in enumerate(r.crosses)]
        self.gathers = [
            Gather(
                plane, k, whole, r.gather_sems[0].at[k], r.gather_sems[1].at[k], self.takes, r.totals[k], local.at[k]
            )
            for k, whole in enumerate(r.wholes)
        ]
        self.partners = (plane.partners() if self.scatters or self.gathers else []) + (
            [across] if self.copies else []
        )
        self.partners = self.partners + self.outputs.partners

    def start(self):
        self.outputs.start()
        for scatter in self.scatters:
            scatter.start()
        for copy, own in zip(self.copies, self.own):
            pl.when(self.sends)(copy.start)
            own.start()

    def add(self):
        for own in self.own:
            own.wait()

        @pl.when(self.takes)
        def _():
            for copy, come, total in zip(self.copies, self.comes, self.totals):
                copy.wait_recv()
                total[...] = (total[...].astype(F32) + come[...].astype(F32)).astype(BF16)

    def middle(self):
        for scatter in self.scatters:
            scatter.middle()
        if self.gathers:
            self.add()
            for gather in self.gathers:
                gather.start()

    def late(self):
        for gather in self.gathers:
            gather.middle()

    def finish(self):
        for scatter, total in zip(self.scatters, self.sums):
            total[...] = scatter.total().astype(BF16)
            scatter.drain()
        if self.copies and not self.gathers:
            self.add()
        for gather in self.gathers:
            gather.finish()
        for copy in self.copies:
            pl.when(self.sends)(copy.wait_send)
        self.outputs.finish()


class Outputs:
    def __init__(self, r, shared):
        team = Team()
        core = lax.axis_index(SEC)
        opposite = {TEN: across_device()[TEN]}
        self.partners = [opposite] if r.shares else []
        self.items = []
        for k, block in enumerate(r.shares):
            copy = send_to(block.at[team.place], r.shares_here[k], *r.share_sems[2 * k : 2 * k + 2], opposite)
            self.items.append((core == shared[0][k], [copy], [copy], []))
        for k, block in enumerate(r.spreads):
            sent, here, own = r.spread_sems[3 * k : 3 * k + 3]
            whole = r.spreads_here[k]
            local = pltpu.make_async_copy(block, whole.at[team.place], own)
            out, come = [], []
            for step in range(1, team.size):
                place, peer = team.peer(step)
                out.append(send_to(block, whole.at[team.place], sent.at[step], here.at[team.place], peer))
                come.append(send_to(block, whole.at[place], sent.at[step], here.at[place], peer))
            self.items.append((core == shared[1][k], out, come, [local]))

    def start(self):
        for active, out, _, local in self.items:

            @pl.when(active)
            def _():
                for copy in out + local:
                    copy.start()

    def finish(self):
        for active, out, come, local in self.items:

            @pl.when(active)
            def _():
                for copy in out:
                    copy.wait_send()
                for copy in come:
                    copy.wait_recv()
                for copy in local:
                    copy.wait()


def exchange_scratch(rows, model):
    team = lax.axis_size(TEN) // 2
    half = rows // PIECES // 2
    return [
        pltpu.VMEM((2, half, model), F32),
        pltpu.VMEM((PIECES, half, model), F32),
        pltpu.VMEM((PIECES, half, model), BF16),
        pltpu.VMEM((PIECES, half, model), BF16),
        pltpu.VMEM((team, PIECES, half, model), BF16),
        DMA((PIECES,)),
        DMA((PIECES,)),
        DMA((team, PIECES)),
        DMA((team, PIECES)),
        DMA((PIECES,)),
        DMA((PIECES,)),
    ]


EXCHANGE = 11


class Exchange:
    def __init__(self, team, refs):
        self.team = team
        (self.part, self.keep, self.out, self.got, self.far) = refs[:5]
        (self.core_sent, self.core_here, self.far_sent, self.far_here) = refs[5:9]
        (self.join_sent, self.join_here) = refs[9:]

    def core_copy(self, i):
        return send_to(
            self.out.at[i], self.got.at[i], self.core_sent.at[i], self.core_here.at[i], self.team.other
        )

    def far_copy(self, i, step, place):
        at = self.far.at[place, i]
        return send_to(
            at, at, self.far_sent.at[step, i], self.far_here.at[place, i], self.team.peer(step)[1]
        )

    def join_copy(self, i, whole):
        at = whole.at[i, self.team.core]
        return send_to(at, at, self.join_sent.at[i], self.join_here.at[i], self.team.other)

    def push(self, i, product):
        core = self.team.core
        self.part[...] = product.reshape(self.part.shape)
        self.out[i] = self.part[1 - core].astype(BF16)
        self.core_copy(i).start()
        self.keep[i] = self.part[core]

    def combine(self, i):
        self.core_copy(i).wait_recv()
        self.far[self.team.place, i] = (self.keep[i] + self.got[i].astype(F32)).astype(BF16)
        for step in range(1, self.team.size):
            self.far_copy(i, step, self.team.place).start()

    def send_all(self, product):
        def send(i):
            self.push(i, product(i))

            @pl.when(i > 0)
            def _():
                self.combine(i - 1)

        each_piece(send)
        self.combine(PIECES - 1)

    def total(self, i):
        for step in range(1, self.team.size):
            self.far_copy(i, step, self.team.peer(step)[0]).wait_recv()
        total = self.far[0, i].astype(F32)
        for place in range(1, self.team.size):
            total = total + self.far[place, i].astype(F32)
        return total

    def join(self, i, whole, half):
        whole[i, self.team.core] = half
        self.join_copy(i, whole).start()

    def finish(self, whole, coming=True):
        def drain(i):
            self.core_copy(i).wait_send()
            for step in range(1, self.team.size):
                self.far_copy(i, step, self.team.place).wait_send()
            self.join_copy(i, whole).wait_send()
            if coming:
                self.join_copy(i, whole).wait_recv()

        each_piece(drain)


def each_piece(body):
    lax.fori_loop(0, PIECES, lambda i, _: (body(i), 0)[1], 0)


def piece_rows(i, rows):
    size = rows // PIECES
    return pl.ds(pl.multiple_of(i * size, size), size)


def rms_back(block, gain, upstream):
    inverse = reciprocal_rms(block)
    normed = block * inverse
    scaled = upstream * gain
    grad = inverse * (scaled - normed * jnp.mean(scaled * normed, axis=-1, keepdims=True))
    return grad, jnp.sum(upstream * normed, axis=0, keepdims=True)


def feed_back(shared, r):
    team, plane = Team(), Plane()
    ex = Exchange(team, r.exchange)
    beside = BesideRun(r, plane, 0, shared)
    greet(team.partners() + beside.partners)
    beside.start()
    rows, model = r.mlp_in.shape
    size = rows // PIECES
    shape = (size, model)
    wide = (r.d_gate.shape[1], model)
    width = r.queries.shape[1]
    last = PIECES - 1
    upstream, gate, up, d_gate, d_up = r.upstream, r.gate, r.up, r.d_gate, r.d_up
    w_gate, w_up, w_down = r.feed
    r.ready(upstream, gate, up, *r.feed)

    def product(i):
        at = piece_rows(i, rows)
        grad_hidden = mm(upstream[i].reshape(shape), w_down[...].reshape(wide), 1, 1)
        gate_block = gate[at, :]
        sigmoid = jax.nn.sigmoid(gate_block)
        silu = gate_block * sigmoid
        d_gate_block = grad_hidden * up[at, :] * (sigmoid + silu * (1.0 - sigmoid))
        d_gate[at, :] = d_gate_block.astype(BF16)
        d_up[at, :] = (grad_hidden * silu).astype(BF16)
        term = mm(d_gate[at, :], w_gate[...].reshape(wide))
        return term + mm(d_up[at, :], w_up[...].reshape(wide))

    def send(step, _):
        i = last - step
        ex.push(i, product(i))

        @pl.when(step > 0)
        def _():
            ex.combine(i + 1)

        return 0

    lax.fori_loop(0, PIECES, send, 0)
    ex.combine(0)
    r.ready(r.mlp_in, r.hidden)
    g_gate, g_up, g_down = r.grads
    g_gate[...] = mm(d_gate[...], r.mlp_in[...], 0, 0).astype(BF16).reshape(g_gate.shape)
    g_up[...] = mm(d_up[...], r.mlp_in[...], 0, 0).astype(BF16).reshape(g_up.shape)
    g_down[...] = mm(r.hidden[...], upstream[...].reshape(rows, model), 0, 0).astype(BF16).reshape(g_down.shape)
    r.flush(*r.grads)
    beside.middle()
    r.ready(r.residual, r.packed, r.queries, r.keys, r.values, r.heads_out, r.norms)
    gain_grad, res_grad = r.gain_grad, r.res_grad
    gain_grad[...] = jnp.zeros_like(gain_grad)
    weights = r.packed[...].reshape(2 * model + 2 * LH, width)
    w_out = weights[model + 2 * LH :]

    def receive(i):
        part, gain_part = rms_back(r.residual[i], r.gain[...], ex.total(i))
        block = upstream[i, ex.team.core].astype(F32) + part
        r.d_residual[i] = block
        gain_grad[...] += gain_part
        ex.join(i, res_grad, block.astype(BF16))

    def attend(i):
        ex.join_copy(i, res_grad).wait_recv()
        at = slice(i * size, (i + 1) * size)
        block = res_grad[i].reshape(shape)
        total = None
        for j in range(model // width):
            columns = slice(j * width, (j + 1) * width)
            term = mm(block[:, columns], w_out[columns], 1, 1)
            total = term if total is None else total + term
        r.d_heads[at, :] = total.astype(BF16)
        attend_rows_back(
            i * size, r.queries, r.keys, r.values, r.heads_out, r.d_heads, r.norms,
            r.d_queries, r.key_total, r.value_total,
        )

    receive(last)
    for i in range(last, 0, -1):
        receive(i - 1)
        if i == 2:
            beside.late()
        attend(i)
    r.flush(r.d_residual)
    attend(0)
    ex.finish(res_grad, False)
    r.flush(res_grad, r.d_queries)
    r.d_keys[...] = (r.key_total[...] * HD**-0.5).astype(BF16)
    r.d_values[...] = r.value_total[...].astype(BF16)
    term = mm(r.d_keys[...], weights[model : model + LH], 1, 1)
    term = term + mm(r.d_values[...], weights[model + LH : model + 2 * LH], 1, 1)
    r.d_latents[...] = term.astype(BF16)
    r.flush(r.d_keys, r.d_values, r.d_latents)
    beside.finish()


def attend_in_back(shared, r):
    team, plane = Team(), Plane()
    ex = Exchange(team, r.exchange)
    beside = BesideRun(r, plane, 0, shared)
    greet(team.partners() + beside.partners)
    beside.start()
    rows, model = r.attn_in.shape
    width = r.d_queries.shape[1]
    r.ready(r.d_queries, r.d_latents, r.packed, r.w_latent)
    w_query = r.packed[...].reshape(2 * model + 2 * LH, width)[:model]

    def product(i):
        at = piece_rows(i, rows)
        return mm(r.d_queries[at, :], w_query, 1, 1) + mm(r.d_latents[at, :], r.w_latent[...], 1, 1)

    ex.send_all(product)
    r.ready(r.attn_in, r.latents, r.heads_out, r.d_keys, r.d_values, r.res_grad)
    half = model + LH
    grads = r.grads
    grads[0:model, :] = mm(r.attn_in[...], r.d_queries[...], 0, 0).astype(BF16)
    count, pieces = lax.axis_size(TEN), r.g_latent.shape[0]
    span = model // count
    depth = span // pieces
    stride = depth + GAIN_ROWS
    g_latent = mm(r.attn_in[...], r.d_latents[...], 0, 0).astype(BF16)
    for piece in range(pieces):
        for chip in range(count):
            start = chip * span + piece * depth
            r.g_latent[piece, chip * stride : chip * stride + depth, :] = g_latent[start : start + depth]
    grads[model:half, :] = mm(r.latents[...], r.d_keys[...], 0, 0).astype(BF16)
    grads[half : half + LH, :] = mm(r.latents[...], r.d_values[...], 0, 0).astype(BF16)
    g_out = mm(r.heads_out[...], r.res_grad[...].reshape(rows, model), 0, 0).astype(BF16)
    for j, block in enumerate(pack_columns(g_out, width)):
        start = half + LH + j * width
        grads[start : start + width, :] = block
    r.g_packed[0][...] = grads[:half].reshape(r.g_packed[0].shape)
    r.g_packed[1][...] = grads[half:].reshape(r.g_packed[1].shape)
    r.flush(*r.g_packed)
    beside.middle()
    r.ready(r.source, r.d_residual)
    r.gain_grad[...] = jnp.zeros_like(r.gain_grad)

    def receive(i):
        part, gain_part = rms_back(r.source[i, team.core].astype(F32), r.gain[...], ex.total(i))
        r.gain_grad[...] += gain_part
        ex.join(i, r.input_grad, (r.d_residual[i] + part).astype(BF16))

    each_piece(receive)
    place = lax.broadcasted_iota(jnp.int32, (GAIN_ROWS, LH), 0)
    nothing = jnp.zeros((GAIN_ROWS, LH), F32)
    for chip in range(count):
        columns = slice(chip * span, (chip + 1) * span)
        rows_of = slice(chip * stride + depth, (chip + 1) * stride)
        gains = [grad[:, columns] for grad in (r.gain_grad, r.mlp_gain)]
        if span < LH:
            gains = [jnp.concatenate([part, jnp.zeros((1, LH - span), F32)], axis=1) for part in gains]
        gains = jnp.where(place == 0, gains[0], jnp.where(place == 1, gains[1], nothing))
        r.g_latent[0, rows_of, :] = gains.astype(BF16)
        for piece in range(1, pieces):
            r.g_latent[piece, rows_of, :] = nothing.astype(BF16)
    r.flush(r.g_latent)
    beside.late()
    ex.finish(r.input_grad)
    r.flush(r.input_grad)
    beside.finish()


def named_call(kernel, number, ins=(), lazy=(), far=(), outs=(), late=(), far_outs=(), scratch=()):
    groups = [dict(group) for group in (ins, lazy, far, outs, late, far_outs, scratch)]

    def listed(group):
        return [(k, v if isinstance(v, list) else [v], isinstance(v, list)) for k, v in group.items()]

    groups = [listed(group) for group in groups]
    ins, lazy, far, outs, late, far_outs, scratch = groups
    vmem, anywhere = pl.BlockSpec(memory_space=pltpu.VMEM), pl.BlockSpec(memory_space=pl.ANY)

    def flat(*parts):
        return [value for part in parts for _, values, _ in part for value in values]

    stages = [pltpu.VMEM(x.shape, x.dtype) for x in flat(lazy)] + [pltpu.VMEM(*x) for x in flat(late)]
    lazy_count, late_count = len(flat(lazy)), len(flat(late))

    def body(*refs):
        refs = list(refs)

        def take(count):
            taken, refs[:] = refs[:count], refs[count:]
            return taken

        named = {}

        def name(part, taken):
            for key, values, is_list in part:
                mine, taken = taken[: len(values)], taken[len(values) :]
                named[key] = mine if is_list else mine[0]

        name(ins, take(len(flat(ins))))
        lazy_refs = take(lazy_count)
        name(far, take(len(flat(far))))
        name(outs, take(len(flat(outs))))
        late_refs = take(late_count)
        name(far_outs, take(len(flat(far_outs))))
        lazy_held, late_held = take(lazy_count), take(late_count)
        in_sem, out_sem = take(1)[0], take(1)[0]
        name(lazy, lazy_held)
        name(late, late_held)
        name(scratch, take(len(flat(scratch))))
        arrive = {
            id(held): pltpu.make_async_copy(ref, held, in_sem.at[k])
            for k, (ref, held) in enumerate(zip(lazy_refs, lazy_held))
        }
        leave = {
            id(held): pltpu.make_async_copy(held, ref, out_sem.at[k])
            for k, (ref, held) in enumerate(zip(late_refs, late_held))
        }
        for copy in arrive.values():
            copy.start()

        def ready(*buffers):
            for buffer in buffers:
                arrive[id(buffer)].wait()

        def flush(*buffers):
            for buffer in buffers:
                leave[id(buffer)].start()

        kernel(types.SimpleNamespace(ready=ready, flush=flush, **named))
        for copy in leave.values():
            copy.wait()

    results = pl.pallas_call(
        body,
        in_specs=[vmem] * len(flat(ins)) + [anywhere] * len(flat(lazy, far)),
        out_specs=[vmem] * len(flat(outs)) + [anywhere] * len(flat(late, far_outs)),
        out_shape=[jax.ShapeDtypeStruct(*x) for x in flat(outs, late, far_outs)],
        scratch_shapes=stages + [DMA((max(1, lazy_count),)), DMA((max(1, late_count),))] + flat(scratch),
        compiler_params=pltpu.CompilerParams(
            collective_id=number, has_side_effects=True, vmem_limit_bytes=VMEM_LIMIT
        ),
        cost_estimate=pl.CostEstimate(flops=LINK_FLOPS, bytes_accessed=2**20, transcendentals=0),
    )(*flat(ins, lazy, far))
    named, results = {}, list(results)
    for key, values, is_list in outs + late + far_outs:
        mine, results = results[: len(values)], results[len(values) :]
        named[key] = mine if is_list else mine[0]
    return types.SimpleNamespace(**named)


def forward_kernel(layer, r):
    team = Team()
    plane = Plane()
    core = lax.axis_index(SEC)
    holder = core == layer
    taker = jnp.logical_not(holder)
    across = across_device()
    ex_a, ex_b = Exchange(team, r.ex_a), Exchange(team, r.ex_b)
    greet(team.partners() + plane.partners() + [across])
    rows, width = r.queries.shape
    model = r.w_latent.shape[0]
    size = rows // PIECES
    feeds = range(3)

    own_copies = [pltpu.make_async_copy(r.own_feed[k], r.feed[k], r.own_sem.at[k]) for k in feeds]
    for copy in own_copies:
        pl.when(holder)(copy.start)
    gathers = [
        Gather(plane, k, r.feed[k], r.gather_sent.at[k], r.gather_here.at[k], taker) for k in feeds
    ]

    def cross(k, source, target):
        return send_to(source, target, r.cross_sent.at[k], r.cross_here.at[k], across)

    come = [cross(1 + k, r.own_feed[k].at[plane.me], r.come[k]) for k in feeds]
    if layer == 0:
        mine = cross(0, r.own_packed.at[plane.me], r.packed.at[plane.me])
        small = [
            send_to(r.pass_latent, r.far_latent, r.small_sent.at[0], r.small_here.at[0], team.other),
            send_to(r.own_gains, r.far_gains, r.small_sent.at[1], r.small_here.at[1], team.other),
        ]
        next_packed = cross(4, r.own_packed.at[plane.me], r.packed_next.at[plane.me])
        packed_gather = Gather(plane, 0, r.packed, r.packed_sent, r.packed_here)
        next_gather = Gather(plane, 1, r.packed_next, r.next_sent, r.next_here)
        own_packed = [
            pltpu.make_async_copy(r.own_packed, target, r.own_sem.at[3]) for target in (r.packed, r.packed_next)
        ]
        pl.when(holder)(mine.start)
        pl.when(holder)(own_packed[0].start)
        pl.when(taker)(own_packed[1].start)
        for copy in small:
            copy.start()
        for copy in small:
            copy.wait()
    else:

        @pl.when(holder)
        def _():
            for copy in come:
                copy.start()

    gains = jnp.where(holder, r.own_gains[...], r.far_gains[...])
    r.gains[...] = gains
    r.w_latent[...] = jnp.where(holder, r.own_latent[...], r.far_latent[...])
    r.flush(r.w_latent)
    r.ready(r.source)

    def norm(i):
        block = r.source[i].reshape(size, model).astype(F32)
        r.attn_in[piece_rows(i, rows), :] = (block * reciprocal_rms(block) * gains[0:1]).astype(BF16)

    each_piece(norm)
    r.flush(r.attn_in)
    if layer == 0:

        @pl.when(taker)
        def _():
            mine.wait_recv()
            packed_gather.start()
            packed_gather.middle()
            packed_gather.finish()

        @pl.when(holder)
        def _():
            own_packed[0].wait()
            mine.wait_send()
            for copy in come:
                copy.start()

        r.flush(r.packed)
    else:
        r.ready(r.packed)
    weights = r.packed[...].reshape(2 * model + 2 * LH, width)

    def project(i):
        at = piece_rows(i, rows)
        block = r.attn_in[at, :]
        r.queries[at, :] = mm(block, weights[:model]).astype(BF16)
        latents = mm(block, r.w_latent[...]).astype(BF16)
        r.latents[at, :] = latents
        r.keys[at, :] = mm(latents, weights[model : model + LH]).astype(BF16)
        r.values[at, :] = mm(latents, weights[model + LH : model + 2 * LH]).astype(BF16)

    each_piece(project)
    r.flush(r.queries, r.latents, r.keys, r.values)
    w_out = [
        weights[model + 2 * LH + start : model + 2 * LH + start + width] for start in range(0, model, width)
    ]
    for i in range(PIECES):
        attend_rows(i * size, r.queries, r.keys, r.values, r.heads_out, r.norms)
        heads = r.heads_out[i * size : (i + 1) * size, :]
        ex_a.push(i, jnp.concatenate([mm(heads, block) for block in w_out], axis=1))
        if i:
            ex_a.combine(i - 1)
    ex_a.combine(PIECES - 1)
    r.flush(r.heads_out, r.norms)
    if layer == 0:

        @pl.when(taker)
        def _():
            next_packed.start()

    @pl.when(taker)
    def _():
        for k in feeds:
            come[k].wait_recv()
            r.feed[k][plane.me] = r.come[k][...]

    for gather in gathers:
        gather.start()

    def receive(i):
        block = r.source[i, core].astype(F32) + ex_a.total(i)
        r.residual[i] = block
        ex_a.join(i, r.mlp_in, (block * reciprocal_rms(block) * gains[1:2]).astype(BF16))

    def feed(i):
        ex_a.join_copy(i, r.mlp_in).wait_recv()
        at = piece_rows(i, rows)
        block = r.mlp_in[i].reshape(size, model)
        shape = (r.hidden.shape[1], model)
        gate = mm(block, r.feed[0][...].reshape(shape), 1, 1)
        up = mm(block, r.feed[1][...].reshape(shape), 1, 1)
        hidden = (jax.nn.silu(gate) * up).astype(BF16)
        r.gate[at, :] = gate
        r.up[at, :] = up
        r.hidden[at, :] = hidden
        ex_b.push(i, mm(hidden, r.feed[2][...].reshape(shape)))

    receive(0)
    for gather in gathers:
        gather.middle()

    @pl.when(holder)
    def _():
        for copy in own_copies:
            copy.wait()

    for gather in gathers:
        gather.finish()
    r.flush(*r.feed)
    receive(1)
    feed(0)
    if layer == 0:

        @pl.when(holder)
        def _():
            next_packed.wait_recv()
            next_gather.start()

    def steady(i, _):
        receive(i)
        feed(i - 1)
        ex_b.combine(i - 2)
        return 0

    lax.fori_loop(2, PIECES, steady, 0)
    feed(PIECES - 1)
    ex_b.combine(PIECES - 2)
    ex_b.combine(PIECES - 1)
    ex_a.finish(r.mlp_in, False)
    r.flush(r.residual, r.mlp_in, r.gate, r.up, r.hidden)
    if layer == 0:

        @pl.when(holder)
        def _():
            next_gather.middle()
            next_gather.finish()

        @pl.when(taker)
        def _():
            own_packed[1].wait()
            next_packed.wait_send()

        r.flush(r.packed_next)
    each_piece(lambda i: ex_b.join(i, r.output, (r.residual[i] + ex_b.total(i)).astype(BF16)))
    ex_b.finish(r.output)
    r.flush(r.output)

    @pl.when(holder)
    def _():
        for copy in come:
            copy.wait_send()


def finish_kernel(groups, r):
    plane = Plane()
    team = Team()
    late = len(r.late)
    scatters = [Scatter(plane, k, r.late[k], *r.scatter[5 * k : 5 * k + 5]) for k in range(late)]
    count = lax.axis_size(TEN)
    z = lax.axis_index(TEN)
    core = lax.axis_index(SEC)
    first, second = core == 0, core == 1
    across = across_device()
    opposite = {TEN: across[TEN]}
    chips = [lax.rem(z + step, count) for step in range(1, count)]
    greet(plane.partners() + [across] + [{TEN: chip} for chip in chips])
    for scatter in scatters:
        scatter.start()
    sources = r.pieces + r.leave
    cross_sent, cross_here = r.cross_sems
    crosses = [
        send_to(source, r.come[k], cross_sent.at[k], cross_here.at[k], across) for k, source in enumerate(sources)
    ]

    @pl.when(second)
    def _():
        for copy in crosses[:FEED]:
            copy.start()

    grad_sent, grad_here = r.grad_sems
    share = r.grad.at[team.place], r.grad_far.at[team.place]
    grad_copies = [send_to(*share, grad_sent.at[0], grad_here.at[team.place], opposite)]
    grad_coming = []
    for step in range(1, team.size):
        place, peer = team.peer(step)
        grad_copies.append(send_to(share[1], share[1], grad_sent.at[step], grad_here.at[team.place], peer))
        theirs = r.grad_far.at[place]
        grad_coming.append(send_to(theirs, theirs, grad_sent.at[step], grad_here.at[place], peer))
    gather_sent, gather_here, gather_own = r.gather_sems
    gathers = [
        Gather(
            plane, k, whole, gather_sent.at[k], gather_here.at[k], first if k < FEED else None,
            r.total[k], gather_own.at[k],
        )
        for k, whole in enumerate(r.wholes)
    ]
    last = FEED + late - 1

    def arrive(k):
        crosses[k].wait_recv()
        return (sources[k][...].astype(F32) + r.come[k][...].astype(F32)).astype(BF16)

    for scatter in scatters:
        scatter.middle()

    @pl.when(first)
    def _():
        r.total[0][...] = arrive(0)

    gathers[0].start()
    for k, scatter in enumerate(scatters):
        r.leave[k][...] = scatter.total().astype(BF16)
        pl.when(second)(crosses[FEED + k].start)
    pl.when(first)(grad_copies[0].start)
    for k in range(1, FEED):

        @pl.when(first)
        def _():
            r.total[k][...] = arrive(k)

        gathers[k].start()
        gathers[k - 1].middle()
    gathers[FEED - 1].middle()

    @pl.when(first)
    def _():
        for k in range(FEED, last):
            r.total[k][...] = arrive(k)
        r.held[...] = arrive(last).reshape(r.held.shape)

    @pl.when(second)
    def _():
        for k in range(FEED, last):
            r.total[k][...] = r.done[k - FEED][...]
        r.held[...] = r.done[late - 1][...].reshape(r.held.shape)

    for k in range(FEED, last):
        gathers[k].start()
    block_sent, block_here = r.block_sems

    def block(step, chip, slot):
        return send_to(r.held.at[chip], r.slots.at[slot], block_sent.at[step], block_here.at[slot], {TEN: chip})

    for step, chip in enumerate(chips):
        block(step, chip, z).start()
    r.slots[z] = r.held[z]
    for step, chip in enumerate(chips):
        block(step, chip, chip).wait_recv()
    shares = [r.slots[shard].astype(F32) for shard in range(count)]
    sums = [sum(s for s, g in zip(shares, groups) if g == group) for group in range(KVH)]
    gain_rows = sums[0]
    for extra in sums[1:]:
        gain_rows = gain_rows + extra
    depth = gain_rows.shape[0] - GAIN_ROWS
    gain_rows = gain_rows * (2.0 / count)
    blocks = [jnp.concatenate([part[:depth], gain_rows[depth:]], axis=0) for part in sums]
    r.total[last][...] = jnp.concatenate(blocks, axis=1).astype(BF16)
    gathers[last].start()
    for k in range(FEED, last + 1):
        gathers[k].middle()

    @pl.when(first)
    def _():
        grad_copies[0].wait_recv()
        for copy in grad_copies[1:]:
            copy.start()

    for gather in gathers:
        gather.finish()
    for scatter in scatters:
        scatter.drain()
    for step, chip in enumerate(chips):
        block(step, chip, z).wait_send()

    @pl.when(second)
    def _():
        for copy in crosses:
            copy.wait_send()

    @pl.when(first)
    def _():
        for copy in grad_copies:
            copy.wait_send()
        for copy in grad_coming:
            copy.wait_recv()


def finish(number, groups, feed, late, done, grad):
    dp, count = lax.axis_size(DP), lax.axis_size(TEN)
    depth = done[-1].shape[0] // count
    shapes = [part.shape for part in list(feed) + list(done)]
    totals = shapes[:-1] + [(depth, KVH * LH)]
    items = len(shapes)
    blocks = pltpu.VMEM((count, depth, LH), BF16)
    return named_call(
        functools.partial(finish_kernel, groups),
        number,
        ins=dict(pieces=list(feed), done=list(done)),
        far=dict(late=list(late), grad=grad),
        far_outs=dict(wholes=[((dp,) + total, BF16) for total in totals], grad_far=(grad.shape, BF16)),
        scratch=dict(
            scatter=[item for load in late for item in scatter_scratch(load)],
            come=[pltpu.VMEM(shape, BF16) for shape in shapes],
            leave=[pltpu.VMEM(part.shape, BF16) for part in done],
            total=[pltpu.VMEM(total, BF16) for total in totals],
            slots=blocks,
            held=blocks,
            cross_sems=[DMA((items,)), DMA((items,))],
            gather_sems=[DMA((items, 3)), DMA((items, dp)), DMA((items,))],
            block_sems=[DMA((count,)), DMA((count,))],
            grad_sems=[DMA((count // 2,)), DMA((count // 2,))],
        ),
    )


def pieces_of(block):
    return block.reshape(PIECES, 2, block.shape[0] // PIECES // 2, block.shape[1])


def shapes_of(rows, model):
    return (PIECES, 2, rows // PIECES // 2, model), (PIECES, rows // PIECES // 2, model)


def forward_layer(layer, number, source, own_feed, own_packed=None, packed=None, **small):
    rows, model = source.shape
    split, own = shapes_of(rows, model)
    pieces, depth, width = (packed if own_packed is None else own_packed).shape
    wide = (rows, pieces * own_feed[0].shape[1])
    pair = min(2 * HD, width)
    narrow = ((rows, width), BF16)
    outs = dict(gains=((2, model), F32))
    late = dict(
        w_latent=((model, LH), BF16),
        attn_in=((rows, model), BF16),
        queries=narrow,
        latents=((rows, LH), BF16),
        keys=narrow,
        values=narrow,
        heads_out=narrow,
        norms=((width // pair, pair // HD, rows), F32),
        residual=(own, F32),
        mlp_in=(split, BF16),
        gate=(wide, F32),
        up=(wide, F32),
        hidden=(wide, BF16),
        output=(split, BF16),
        feed=[(w.shape, BF16) for w in own_feed],
    )
    scratch = dict(
        ex_a=exchange_scratch(rows, model),
        ex_b=exchange_scratch(rows, model),
        come=[pltpu.VMEM(w.shape[1:], BF16) for w in own_feed],
        own_sem=DMA((4,)),
        gather_sent=DMA((3, 3)),
        gather_here=DMA((3, pieces)),
        cross_sent=DMA((5,)),
        cross_here=DMA((5,)),
    )
    lazy, far = dict(source=pieces_of(source)), dict(own_feed=own_feed)
    if layer == 0:
        far.update(own_packed=own_packed)
        outs.update(far_latent=((model, LH), BF16), far_gains=((2, model), F32))
        late.update(packed=((pieces, depth, width), BF16), packed_next=((pieces, depth, width), BF16))
        scratch.update(
            small_sent=DMA((2,)),
            small_here=DMA((2,)),
            packed_sent=DMA((3,)),
            packed_here=DMA((pieces,)),
            next_sent=DMA((3,)),
            next_here=DMA((pieces,)),
        )
    else:
        lazy.update(packed=packed)
    return named_call(
        functools.partial(forward_kernel, layer),
        number,
        ins=small,
        lazy=lazy,
        far=far,
        outs=outs,
        late=late,
        scratch=scratch,
    )


def feed_layer_back(number, upstream, result, beside):
    rows, model = upstream.shape
    split, half = shapes_of(rows, model)
    columns = result.queries.shape[1]
    wide = pltpu.VMEM(result.hidden.shape, BF16)
    narrow = ((rows, columns), BF16)
    total = pltpu.VMEM((rows, columns), F32)
    return named_call(
        functools.partial(feed_back, beside.shared),
        number,
        ins=dict(gain=result.gains[1:2]),
        lazy=dict(
            upstream=pieces_of(upstream),
            feed=result.feed,
            gate=result.gate,
            up=result.up,
            mlp_in=result.mlp_in.reshape(rows, model),
            hidden=result.hidden,
            residual=result.residual,
            packed=result.packed,
            queries=result.queries,
            keys=result.keys,
            values=result.values,
            heads_out=result.heads_out,
            norms=result.norms,
        ),
        far=beside.far,
        outs=dict(gain_grad=((1, model), F32), **beside.outs),
        late=dict(
            d_residual=(half, F32),
            res_grad=(split, BF16),
            grads=[(w.shape, BF16) for w in result.feed],
            d_queries=narrow,
            d_keys=narrow,
            d_values=narrow,
            d_latents=((rows, LH), BF16),
        ),
        far_outs=beside.far_outs,
        scratch=dict(
            exchange=exchange_scratch(rows, model),
            d_gate=wide,
            d_up=wide,
            d_heads=pltpu.VMEM((rows, columns), BF16),
            key_total=total,
            value_total=total,
            **beside.scratch,
        ),
    )


def attend_layer_back(number, source, result, back, beside):
    rows, model = source.shape
    pieces, depth, width = result.packed.shape
    out = named_call(
        functools.partial(attend_in_back, beside.shared),
        number,
        ins=dict(gain=result.gains[0:1], mlp_gain=back.gain_grad),
        lazy=dict(
            d_queries=back.d_queries,
            d_latents=back.d_latents,
            packed=result.packed,
            w_latent=result.w_latent,
            attn_in=result.attn_in,
            latents=result.latents,
            heads_out=result.heads_out,
            d_keys=back.d_keys,
            d_values=back.d_values,
            res_grad=back.res_grad,
            source=pieces_of(source),
            d_residual=back.d_residual,
        ),
        far=beside.far,
        outs=beside.outs,
        late=dict(
            input_grad=(shapes_of(rows, model)[0], BF16),
            g_packed=[((pieces, depth // 2, width), BF16)] * 2,
            g_latent=((pieces, model // pieces + lax.axis_size(TEN) * GAIN_ROWS, LH), BF16),
        ),
        far_outs=beside.far_outs,
        scratch=dict(
            exchange=exchange_scratch(rows, model),
            grads=pltpu.VMEM((pieces * depth, width), BF16),
            gain_grad=pltpu.VMEM((1, model), F32),
            **beside.scratch,
        ),
    )
    out.parts = out.g_packed + [out.g_latent]
    out.input_grad = out.input_grad.reshape(rows, model)
    return out


def tie(*arrays):
    return lax.optimization_barrier(arrays)


def local(
    inputs,
    out_grad,
    w_query,
    w_latent,
    w_key_up,
    w_value_up,
    w_out,
    w_gate,
    w_up,
    w_down,
    norm_attn,
    norm_mlp,
):
    at = Place()
    model = inputs.shape[1]
    heads = w_query.shape[2] // HD

    def group_of(shard):
        return shard * heads // (QH // KVH)

    opposite_z = (at.z + at.team) % at.count

    def latent_of(shard):
        return lax.dynamic_slice_in_dim(w_latent[0], group_of(shard) * LH, LH, 1)

    def sequence_rows(block):
        return lax.dynamic_slice_in_dim(block, at.sequence * LEN, LEN, 0)

    own_feed = [by_dp(w) for w in (w_gate[0].T, w_up[0].T, w_down[0])]
    own_packed = by_dp(pack_attention(w_query[0], w_key_up[0], w_value_up[0], w_out[0]))
    own_gains = jnp.concatenate([norm_attn, norm_mlp], axis=0)
    own_latent = latent_of(at.z)
    source = sequence_rows(inputs)
    zero = forward_layer(
        0,
        0,
        source,
        own_feed,
        own_packed=own_packed,
        own_gains=own_gains,
        own_latent=own_latent,
        pass_latent=latent_of(opposite_z),
    )
    first_out = zero.output.reshape(LEN, model)
    one = forward_layer(
        1,
        1,
        first_out,
        own_feed,
        packed=zero.packed_next,
        own_gains=own_gains,
        far_gains=zero.far_gains,
        own_latent=own_latent,
        far_latent=zero.far_latent,
    )
    one.packed = zero.packed_next
    second_out = one.output.reshape(LEN, model)

    def shared(block):
        return block.reshape(at.team, LEN // at.team, model)

    back = feed_layer_back(2, sequence_rows(out_grad), one, Beside(shares=[(shared(first_out), 0)]))
    beside = Beside(back.grads, shares=[(shared(second_out), 1)], spreads=[(back.shares_here[0], 0)])
    above = attend_layer_back(3, first_out, one, back, beside)
    first_far = above.spreads_here[0]
    second_grad = above.input_grad
    beside = Beside(
        above.parts, above.sums, True, [(shared(second_grad), 1)], [(above.shares_here[0], 1)]
    )
    back = feed_layer_back(4, second_grad, zero, beside)
    wide_one = back.wholes
    second_far = back.spreads_here[0]
    beside = Beside(back.grads, back.sums, spreads=[(back.shares_here[0], 1)])
    below = attend_layer_back(5, source, zero, back, beside)
    grad_far = below.spreads_here[0]
    first_grad = below.input_grad
    first_far, second_far, grad_far = (far.reshape(LEN, model) for far in (first_far, second_far, grad_far))
    groups = tuple(group_of(shard) for shard in range(at.count))
    last = finish(6, groups, below.sums, below.parts, below.totals, shared(first_grad))
    *wide_zero, low_part, high_part, latent = last.wholes

    def both_sequences(mine, other):
        both = jnp.broadcast_to(other[None], (2,) + other.shape)
        both = lax.dynamic_update_slice_in_dim(both, mine[None], at.sequence, 0)
        return both.reshape(1, 2 * other.shape[0], model)

    layer_out = both_sequences(
        jnp.where(at.first, first_out, second_out), jnp.where(at.first, first_far, second_far)
    )
    input_grad = both_sequences(
        jnp.where(at.first, first_grad, second_grad),
        jnp.where(at.first, last.grad_far.reshape(first_grad.shape), grad_far),
    )
    g_gate, g_up, g_down = [
        jnp.where(at.first, whole_of(zero), whole_of(one)).astype(F32) for zero, one in zip(wide_zero, wide_one)
    ]
    low_part, high_part = whole_of(low_part).astype(F32), whole_of(high_part).astype(F32)
    g_query, g_key_up = low_part[:model], low_part[model:]
    g_value_up = high_part[:LH]
    columns = high_part.shape[1]
    g_out = [high_part[start : start + columns] for start in range(LH, LH + model, columns)]
    g_out = jnp.concatenate(g_out, axis=1)
    width = model // at.count
    depth = latent.shape[1] - GAIN_ROWS
    g_latent = latent[:, :depth].reshape(width, KVH * LH).astype(F32)
    gains = latent[0, depth : depth + 2, :width].astype(F32)
    return (
        layer_out,
        input_grad,
        g_query[None],
        g_latent[None],
        g_key_up[None],
        g_value_up[None],
        g_out[None],
        g_gate.T[None],
        g_up.T[None],
        g_down[None],
        gains[0:1],
        gains[1:2],
    )


def solution(mesh):
    columns = P(SEC, None, TEN)
    rows = P(SEC, TEN, None)
    return jax.shard_map(
        local,
        mesh=mesh,
        in_specs=(
            P(DP, None),
            P(DP, None),
            columns,
            P(SEC, None, None),
            columns,
            columns,
            rows,
            columns,
            columns,
            rows,
            P(SEC, None),
            P(SEC, None),
        ),
        out_specs=(
            P(SEC, DP, None),
            P(SEC, DP, None),
            columns,
            rows,
            columns,
            columns,
            rows,
            columns,
            columns,
            rows,
            P(SEC, TEN),
            P(SEC, TEN),
        ),
        check_vma=False,
    )
```

```python
import functools
import math
import types

import jax
import jax.numpy as jnp
from jax import lax
from jax.experimental import pallas as pl
from jax.experimental.pallas import tpu as pltpu
from jax.sharding import PartitionSpec as P

QH = 16
HD = 64
KVH = 2
LH = 256
LEN = 1024
EPS = 1e-05
F32 = jnp.float32
BF16 = jnp.bfloat16
SEC, DP, TEN = "section", "dp", "tensor"
LOG2_SCALE = HD**-0.5 * math.log2(math.e)
KEY_ROWS = 256


def mm(left, right, left_dim=1, right_dim=0):
    dims = (((left_dim,), (right_dim,)), ((), ()))
    return lax.dot_general(left, right, dims, preferred_element_type=F32)


def head_masks(width):
    if width == HD:
        return [None]
    lane = lax.broadcasted_iota(jnp.int32, (1, width), 1)
    return [lane // HD == j for j in range(width // HD)]


def keep_head(block, mask):
    return block if mask is None else jnp.where(mask, block, jnp.zeros_like(block))


def attend_rows(start, q_ref, k_ref, v_ref, o_ref, norm_ref):
    columns = q_ref.shape[1]
    width = min(2 * HD, columns)
    masks = head_masks(width)
    rows = KEY_ROWS
    place_k = lax.broadcasted_iota(jnp.int32, (rows, rows), 0)
    place_q = lax.broadcasted_iota(jnp.int32, (rows, rows), 1)
    for pair in range(columns // width):
        lanes = slice(pair * width, (pair + 1) * width)
        query = q_ref[start : start + rows, lanes]
        total = None
        for j, mask in enumerate(masks):
            query_j = keep_head(query, mask)
            scores = mm(k_ref[start : start + rows, lanes], query_j, 1, 1) * LOG2_SCALE
            scores = jnp.where(place_k <= place_q, scores, -jnp.inf)
            largest = jnp.max(scores, axis=0, keepdims=True)
            if start:
                before = mm(k_ref[0:start, lanes], query_j, 1, 1) * LOG2_SCALE
                largest = jnp.maximum(largest, jnp.max(before, axis=0, keepdims=True))
            weight = jnp.exp2(scores - largest)
            norm = jnp.sum(weight, axis=0, keepdims=True)
            value = keep_head(v_ref[start : start + rows, lanes], mask)
            out = mm(value, weight.astype(BF16), 0, 0)
            if start:
                weight = jnp.exp2(before - largest)
                norm = norm + jnp.sum(weight, axis=0, keepdims=True)
                value = keep_head(v_ref[0:start, lanes], mask)
                out = out + mm(value, weight.astype(BF16), 0, 0)
            out = out / norm
            total = out if total is None else total + out
            norm_ref[pair, j : j + 1, start : start + rows] = largest + jnp.log2(norm)
        o_ref[start : start + rows, lanes] = total.T.astype(BF16)


def attend_rows_back(start, q_ref, k_ref, v_ref, o_ref, g_ref, norm_ref, dq_ref, key_total, value_total):
    columns = q_ref.shape[1]
    width = min(2 * HD, columns)
    masks = head_masks(width)
    rows = KEY_ROWS
    end = start + rows
    place_k = lax.broadcasted_iota(jnp.int32, (rows, rows), 0)
    place_q = lax.broadcasted_iota(jnp.int32, (rows, rows), 1)
    for pair in range(columns // width):
        lanes = slice(pair * width, (pair + 1) * width)
        query, grad = q_ref[start:end, lanes], g_ref[start:end, lanes]
        key, value = k_ref[0:end, lanes], v_ref[0:end, lanes]
        product = (grad.astype(F32) * o_ref[start:end, lanes].astype(F32)).T
        grad_query = grad_key = grad_value = None
        for j, mask in enumerate(masks):
            query_j = keep_head(query, mask)
            grad_j = keep_head(grad, mask)
            delta = jnp.sum(product[j * HD : (j + 1) * HD, :], axis=0, keepdims=True)
            scores = mm(key, query_j, 1, 1) * LOG2_SCALE
            probs = jnp.exp2(scores - norm_ref[pair, j : j + 1, start:end])
            last = jnp.where(place_k <= place_q, probs[start:], 0.0)
            probs = jnp.concatenate([probs[:start], last], axis=0) if start else last
            grad_probs = mm(value, grad_j, 1, 1)
            grad_scores = (probs * (grad_probs - delta)).astype(BF16)
            value_term = mm(probs.astype(BF16), grad_j)
            key_term = mm(grad_scores, query_j)
            query_term = mm(keep_head(key, mask), grad_scores, 0, 0)
            grad_key = key_term if grad_key is None else grad_key + key_term
            grad_value = value_term if grad_value is None else grad_value + value_term
            grad_query = query_term if grad_query is None else grad_query + query_term
        dq_ref[start:end, lanes] = (grad_query.T * HD**-0.5).astype(BF16)
        if end == LEN:
            key_total[:, lanes] = grad_key
            value_total[:, lanes] = grad_value
        else:
            key_total[0:end, lanes] += grad_key
            value_total[0:end, lanes] += grad_value


def rms_scale(features):
    return features * lax.rsqrt(jnp.mean(features * features, axis=-1, keepdims=True) + EPS)


class Place:
    def __init__(self):
        self.count = lax.axis_size(TEN)
        self.team = self.count // 2
        self.z = lax.axis_index(TEN)
        self.core = lax.axis_index(SEC)
        self.dp = lax.axis_index(DP)
        self.sequence = self.z // self.team
        self.first = self.core == 0

    def opposite(self, block, cores=(0, 1)):
        n, t = self.count, self.team
        route = [(core * n + z, core * n + (z + t) % n) for core in cores for z in range(n)]
        return lax.ppermute(block, (SEC, TEN), route)

    def across(self, block, core):
        n, t = self.count, self.team
        route = [(core * n + z, (1 - core) * n + (z + t) % n) for z in range(n)]
        return lax.ppermute(block, (SEC, TEN), route)


def pack_columns(matrix, width):
    return [matrix[:, i : i + width] for i in range(0, matrix.shape[1], width)]


def pack_attention(query, key_up, value_up, out):
    width = query.shape[1]
    return jnp.concatenate([query, key_up, value_up] + pack_columns(out, width), axis=0)


def by_dp(matrix):
    count = lax.axis_size(DP)
    return matrix.reshape(count, matrix.shape[0] // count, matrix.shape[1])


def whole_of(pieces):
    return pieces.reshape(-1, pieces.shape[2])


MESH = pl.DeviceIdType.MESH
PIECES = 4
VMEM_LIMIT = 58 * 2**20
LINK_FLOPS = 4 * 10**9
GAIN_ROWS = 16
FEED = 3
DMA = pltpu.SemaphoreType.DMA


def reciprocal_rms(features):
    return lax.rsqrt(jnp.mean(features * features, axis=-1, keepdims=True) + EPS)


def send_to(source, target, sent, here, device):
    return pltpu.make_async_remote_copy(
        src_ref=source,
        dst_ref=target,
        send_sem=sent,
        recv_sem=here,
        device_id=device,
        device_id_type=MESH,
    )


def greet(partners):
    barrier = pltpu.get_barrier_semaphore()
    for partner in partners:
        pl.semaphore_signal(barrier, inc=1, device_id=partner, device_id_type=MESH)
    pl.semaphore_wait(barrier, len(partners))


class Team:
    def __init__(self):
        count = lax.axis_size(TEN)
        self.size = count // 2
        self.core = lax.axis_index(SEC)
        z = lax.axis_index(TEN)
        self.place = lax.rem(z, self.size)
        self.base = z - self.place
        self.other = {SEC: 1 - self.core}

    def peer(self, step):
        place = lax.rem(self.place + step, self.size)
        return place, {TEN: self.base + place}

    def partners(self):
        return [self.other] + [self.peer(step)[1] for step in range(1, self.size)]


class Plane:
    def __init__(self):
        me = lax.axis_index(DP)
        self.me = me
        self.one = me + 1 - 2 * lax.rem(me, 2)
        self.two = lax.rem(me + 2, 4)
        self.both = lax.rem(self.one + 2, 4)

    def partners(self):
        return [{DP: self.one}, {DP: self.two}]

    def order(self, turn):
        return (self.one, self.two) if turn % 2 == 0 else (self.two, self.one)


def scatter_scratch(load):
    piece = load.shape[1:]
    return [pltpu.VMEM((3,) + piece, BF16), pltpu.VMEM((3,) + piece, BF16), DMA((3,)), DMA((3,)), DMA((2,))]


class Scatter:
    def __init__(self, plane, turn, load, slots, held, sent, here, local):
        near, far = plane.order(turn)
        self.slots, self.held = slots, held
        self.copies = [
            send_to(load.at[near], slots.at[0], sent.at[0], here.at[0], {DP: near}),
            send_to(load.at[plane.both], slots.at[1], sent.at[1], here.at[1], {DP: near}),
            send_to(held.at[2], slots.at[2], sent.at[2], here.at[2], {DP: far}),
        ]
        self.local = [
            pltpu.make_async_copy(load.at[plane.me], held.at[0], local.at[0]),
            pltpu.make_async_copy(load.at[far], held.at[1], local.at[1]),
        ]

    def start(self):
        self.copies[1].start()
        self.copies[0].start()
        for copy in self.local:
            copy.start()

    def middle(self):
        self.local[1].wait()
        self.copies[1].wait_recv()
        self.held[2] = (self.held[1].astype(F32) + self.slots[1].astype(F32)).astype(BF16)
        self.copies[2].start()

    def total(self):
        self.local[0].wait()
        self.copies[0].wait_recv()
        total = self.held[0].astype(F32) + self.slots[0].astype(F32)
        self.copies[2].wait_recv()
        return total + self.slots[2].astype(F32)

    def drain(self):
        for copy in self.copies:
            copy.wait_send()


class Gather:
    def __init__(self, plane, turn, whole, sent, here, active=None, piece=None, local=None):
        self.active = active
        near, far = plane.order(turn)
        me = plane.me
        source = whole.at[me] if piece is None else piece

        def copy(k, source, place, device):
            return send_to(source, whole.at[place], sent.at[k], here.at[place], {DP: device})

        self.first = copy(0, source, me, near)
        self.second = [copy(1, source, me, far), copy(2, whole.at[near], near, far)]
        self.coming = [copy(0, whole.at[place], place, near) for place in (near, far, plane.both)]
        self.local = [] if piece is None else [pltpu.make_async_copy(piece, whole.at[me], local)]

    def when(self, body):
        if self.active is None:
            body()
        else:
            pl.when(self.active)(body)

    def start(self):
        def body():
            for copy in [self.first, self.second[0]] + self.local:
                copy.start()

        self.when(body)

    def middle(self):
        def body():
            self.coming[0].wait_recv()
            self.second[1].start()

        self.when(body)

    def finish(self):
        def body():
            self.coming[1].wait_recv()
            self.coming[2].wait_recv()
            for copy in [self.first] + self.second:
                copy.wait_send()
            for copy in self.local:
                copy.wait()

        self.when(body)


def across_device():
    count = lax.axis_size(TEN)
    opposite = lax.rem(lax.axis_index(TEN) + count // 2, count)
    return {SEC: 1 - lax.axis_index(SEC), TEN: opposite}


class Beside:
    def __init__(self, loads=(), crosses=(), gathered=False, shares=(), spreads=()):
        team = lax.axis_size(TEN) // 2
        self.shared = [[core for _, core in group] for group in (shares, spreads)]
        shares, spreads = ([block for block, _ in group] for group in (shares, spreads))
        self.far = dict(loads=list(loads), crosses=list(crosses), shares=shares, spreads=spreads)
        pieces = [cross.shape for cross in crosses]
        dp = lax.axis_size(DP)
        self.outs = dict(
            sums=[(load.shape[1:], BF16) for load in loads], totals=[(piece, BF16) for piece in pieces]
        )
        self.far_outs = dict(
            wholes=[((dp,) + piece, BF16) for piece in pieces] if gathered else [],
            shares_here=[(block.shape, BF16) for block in shares],
            spreads_here=[(block.shape, BF16) for block in spreads],
        )
        count = max(1, len(pieces))
        self.scratch = dict(
            scatter=[item for load in loads for item in scatter_scratch(load)],
            comes=[pltpu.VMEM(piece, BF16) for piece in pieces],
            cross_sems=[DMA((count,)), DMA((count,)), DMA((count,)), DMA((count,))],
            gather_sems=[DMA((count, 3)), DMA((count, dp))],
            share_sems=[DMA((PIECES,))] * (2 * len(shares)),
            spread_sems=[DMA((team, PIECES)), DMA((PIECES,))] * len(spreads),
        )


class BesideRun:
    def __init__(self, r, plane, sender, shared):
        self.outputs = Outputs(r, shared)
        self.totals, self.comes, self.sums = r.totals, r.comes, r.sums
        self.scatters = [
            Scatter(plane, k, load, *r.scatter[5 * k : 5 * k + 5]) for k, load in enumerate(r.loads)
        ]
        self.sends = lax.axis_index(SEC) == sender
        self.takes = jnp.logical_not(self.sends)
        across = across_device()
        sent, here, own, local = r.cross_sems
        self.copies = [
            send_to(cross, r.comes[k], sent.at[k], here.at[k], across) for k, cross in enumerate(r.crosses)
        ]
        self.own = [pltpu.make_async_copy(cross, r.totals[k], own.at[k]) for k, cross in enumerate(r.crosses)]
        self.gathers = [
            Gather(
                plane, k, whole, r.gather_sems[0].at[k], r.gather_sems[1].at[k], self.takes, r.totals[k], local.at[k]
            )
            for k, whole in enumerate(r.wholes)
        ]
        self.partners = (plane.partners() if self.scatters or self.gathers else []) + (
            [across] if self.copies else []
        )
        self.partners = self.partners + self.outputs.partners

    def start(self):
        self.outputs.start()
        for scatter in self.scatters:
            scatter.start()
        for copy, own in zip(self.copies, self.own):
            pl.when(self.sends)(copy.start)
            own.start()

    def add(self):
        for own in self.own:
            own.wait()

        @pl.when(self.takes)
        def _():
            for copy, come, total in zip(self.copies, self.comes, self.totals):
                copy.wait_recv()
                total[...] = (total[...].astype(F32) + come[...].astype(F32)).astype(BF16)

    def middle(self):
        for scatter in self.scatters:
            scatter.middle()
        if self.gathers:
            self.add()
            for gather in self.gathers:
                gather.start()

    def late(self):
        for gather in self.gathers:
            gather.middle()

    def finish(self):
        for scatter, total in zip(self.scatters, self.sums):
            total[...] = scatter.total().astype(BF16)
            scatter.drain()
        if self.copies and not self.gathers:
            self.add()
        for gather in self.gathers:
            gather.finish()
        for copy in self.copies:
            pl.when(self.sends)(copy.wait_send)
        self.outputs.finish()


def owner(piece):
    return piece * (lax.axis_size(TEN) // 2) // PIECES


class Outputs:
    def __init__(self, r, shared):
        team = Team()
        core = lax.axis_index(SEC)
        opposite = {TEN: across_device()[TEN]}
        self.partners = [opposite] if r.shares else []
        self.out, self.come = [], []
        for piece in range(PIECES):
            mine = team.place == owner(piece)
            for k, block in enumerate(r.shares):
                sent, here = r.share_sems[2 * k : 2 * k + 2]
                target = r.shares_here[k].at[piece]
                copy = send_to(block.at[piece], target, sent.at[piece], here.at[piece], opposite)
                active = jnp.logical_and(core == shared[0][k], mine)
                self.out.append((active, copy))
                self.come.append((active, copy))
            for k, block in enumerate(r.spreads):
                sent, here = r.spread_sems[2 * k : 2 * k + 2]
                for step in range(1, team.size):
                    copy = send_to(
                        block.at[piece], r.spreads_here[k].at[piece], sent.at[step, piece], here.at[piece],
                        team.peer(step)[1],
                    )
                    self.out.append((jnp.logical_and(core == shared[1][k], mine), copy))
                theirs = jnp.logical_and(core == shared[1][k], jnp.logical_not(mine))
                self.come.append((theirs, copy))

    def start(self):
        for active, copy in self.out:
            pl.when(active)(copy.start)

    def finish(self):
        for active, copy in self.out:
            pl.when(active)(copy.wait_send)
        for active, copy in self.come:
            pl.when(active)(copy.wait_recv)


def exchange_scratch(rows, model):
    team = lax.axis_size(TEN) // 2
    half = rows // PIECES // 2
    return [
        pltpu.VMEM((2, half, model), F32),
        pltpu.VMEM((PIECES, half, model), F32),
        pltpu.VMEM((PIECES, half, model), BF16),
        pltpu.VMEM((PIECES, half, model), BF16),
        pltpu.VMEM((team, PIECES, half, model), BF16),
        DMA((PIECES,)),
        DMA((PIECES,)),
        DMA((team, PIECES)),
        DMA((team, PIECES)),
        DMA((PIECES,)),
        DMA((PIECES,)),
    ]


EXCHANGE = 11


class Exchange:
    def __init__(self, team, refs):
        self.team = team
        (self.part, self.keep, self.out, self.got, self.far) = refs[:5]
        (self.core_sent, self.core_here, self.far_sent, self.far_here) = refs[5:9]
        (self.join_sent, self.join_here) = refs[9:]

    def core_copy(self, i):
        return send_to(
            self.out.at[i], self.got.at[i], self.core_sent.at[i], self.core_here.at[i], self.team.other
        )

    def far_copy(self, i, step, place):
        at = self.far.at[place, i]
        return send_to(
            at, at, self.far_sent.at[step, i], self.far_here.at[place, i], self.team.peer(step)[1]
        )

    def join_copy(self, i, whole):
        at = whole.at[i, self.team.core]
        return send_to(at, at, self.join_sent.at[i], self.join_here.at[i], self.team.other)

    def push(self, i, product):
        core = self.team.core
        self.part[...] = product.reshape(self.part.shape)
        self.out[i] = self.part[1 - core].astype(BF16)
        self.core_copy(i).start()
        self.keep[i] = self.part[core]

    def combine(self, i):
        self.core_copy(i).wait_recv()
        self.far[self.team.place, i] = (self.keep[i] + self.got[i].astype(F32)).astype(BF16)
        for step in range(1, self.team.size):
            self.far_copy(i, step, self.team.place).start()

    def send_all(self, product):
        def send(i):
            self.push(i, product(i))

            @pl.when(i > 0)
            def _():
                self.combine(i - 1)

        each_piece(send)
        self.combine(PIECES - 1)

    def total(self, i):
        for step in range(1, self.team.size):
            self.far_copy(i, step, self.team.peer(step)[0]).wait_recv()
        total = self.far[0, i].astype(F32)
        for place in range(1, self.team.size):
            total = total + self.far[place, i].astype(F32)
        return total

    def join(self, i, whole, half):
        whole[i, self.team.core] = half
        self.join_copy(i, whole).start()

    def finish(self, whole, coming=True):
        def drain(i):
            self.core_copy(i).wait_send()
            for step in range(1, self.team.size):
                self.far_copy(i, step, self.team.place).wait_send()
            self.join_copy(i, whole).wait_send()
            if coming:
                self.join_copy(i, whole).wait_recv()

        each_piece(drain)


def each_piece(body):
    lax.fori_loop(0, PIECES, lambda i, _: (body(i), 0)[1], 0)


def piece_rows(i, rows):
    size = rows // PIECES
    return pl.ds(pl.multiple_of(i * size, size), size)


def rms_back(block, gain, upstream):
    inverse = reciprocal_rms(block)
    normed = block * inverse
    scaled = upstream * gain
    grad = inverse * (scaled - normed * jnp.mean(scaled * normed, axis=-1, keepdims=True))
    return grad, jnp.sum(upstream * normed, axis=0, keepdims=True)


def feed_back(shared, r):
    team, plane = Team(), Plane()
    ex = Exchange(team, r.exchange)
    beside = BesideRun(r, plane, 0, shared)
    greet(team.partners() + beside.partners)
    beside.start()
    rows, model = r.mlp_in.shape
    size = rows // PIECES
    shape = (size, model)
    wide = (r.d_gate.shape[1], model)
    width = r.queries.shape[1]
    last = PIECES - 1
    upstream, gate, up, d_gate, d_up = r.upstream, r.gate, r.up, r.d_gate, r.d_up
    w_gate, w_up, w_down = r.feed
    r.ready(upstream, gate, up, *r.feed)

    def product(i):
        at = piece_rows(i, rows)
        grad_hidden = mm(upstream[i].reshape(shape), w_down[...].reshape(wide), 1, 1)
        gate_block = gate[at, :]
        sigmoid = jax.nn.sigmoid(gate_block)
        silu = gate_block * sigmoid
        d_gate_block = grad_hidden * up[at, :] * (sigmoid + silu * (1.0 - sigmoid))
        d_gate[at, :] = d_gate_block.astype(BF16)
        d_up[at, :] = (grad_hidden * silu).astype(BF16)
        term = mm(d_gate[at, :], w_gate[...].reshape(wide))
        return term + mm(d_up[at, :], w_up[...].reshape(wide))

    def send(step, _):
        i = last - step
        ex.push(i, product(i))

        @pl.when(step > 0)
        def _():
            ex.combine(i + 1)

        return 0

    lax.fori_loop(0, PIECES, send, 0)
    ex.combine(0)
    r.ready(r.mlp_in, r.hidden)
    g_gate, g_up, g_down = r.grads
    g_gate[...] = mm(d_gate[...], r.mlp_in[...], 0, 0).astype(BF16).reshape(g_gate.shape)
    g_up[...] = mm(d_up[...], r.mlp_in[...], 0, 0).astype(BF16).reshape(g_up.shape)
    g_down[...] = mm(r.hidden[...], upstream[...].reshape(rows, model), 0, 0).astype(BF16).reshape(g_down.shape)
    r.flush(*r.grads)
    beside.middle()
    r.ready(r.residual, r.packed, r.queries, r.keys, r.values, r.heads_out, r.norms)
    gain_grad, res_grad = r.gain_grad, r.res_grad
    gain_grad[...] = jnp.zeros_like(gain_grad)
    weights = r.packed[...].reshape(2 * model + 2 * LH, width)
    w_out = weights[model + 2 * LH :]

    def receive(i):
        part, gain_part = rms_back(r.residual[i], r.gain[...], ex.total(i))
        block = upstream[i, ex.team.core].astype(F32) + part
        r.d_residual[i] = block
        gain_grad[...] += gain_part
        ex.join(i, res_grad, block.astype(BF16))

    def attend(i):
        ex.join_copy(i, res_grad).wait_recv()
        at = slice(i * size, (i + 1) * size)
        block = res_grad[i].reshape(shape)
        total = None
        for j in range(model // width):
            columns = slice(j * width, (j + 1) * width)
            term = mm(block[:, columns], w_out[columns], 1, 1)
            total = term if total is None else total + term
        r.d_heads[at, :] = total.astype(BF16)
        attend_rows_back(
            i * size, r.queries, r.keys, r.values, r.heads_out, r.d_heads, r.norms,
            r.d_queries, r.key_total, r.value_total,
        )

    receive(last)
    for i in range(last, 0, -1):
        receive(i - 1)
        if i == 2:
            beside.late()
        attend(i)
    r.flush(r.d_residual)
    attend(0)
    ex.finish(res_grad, False)
    r.flush(res_grad, r.d_queries)
    r.d_keys[...] = (r.key_total[...] * HD**-0.5).astype(BF16)
    r.d_values[...] = r.value_total[...].astype(BF16)
    term = mm(r.d_keys[...], weights[model : model + LH], 1, 1)
    term = term + mm(r.d_values[...], weights[model + LH : model + 2 * LH], 1, 1)
    r.d_latents[...] = term.astype(BF16)
    r.flush(r.d_keys, r.d_values, r.d_latents)
    beside.finish()


def attend_in_back(shared, early, r):
    team, plane = Team(), Plane()
    opposite = {TEN: across_device()[TEN]}
    ex = Exchange(team, r.exchange)
    beside = BesideRun(r, plane, 0, shared)
    greet(team.partners() + beside.partners + ([opposite] if early else []))
    beside.start()
    rows, model = r.attn_in.shape
    width = r.d_queries.shape[1]
    r.ready(r.d_queries, r.d_latents, r.packed, r.w_latent)
    w_query = r.packed[...].reshape(2 * model + 2 * LH, width)[:model]

    def product(i):
        at = piece_rows(i, rows)
        return mm(r.d_queries[at, :], w_query, 1, 1) + mm(r.d_latents[at, :], r.w_latent[...], 1, 1)

    ex.send_all(product)
    r.ready(r.attn_in, r.latents, r.heads_out, r.d_keys, r.d_values, r.res_grad)
    half = model + LH
    grads = r.grads
    grads[0:model, :] = mm(r.attn_in[...], r.d_queries[...], 0, 0).astype(BF16)
    count, pieces = lax.axis_size(TEN), r.g_latent.shape[0]
    span = model // count
    depth = span // pieces
    stride = depth + GAIN_ROWS
    g_latent = mm(r.attn_in[...], r.d_latents[...], 0, 0).astype(BF16)
    for piece in range(pieces):
        for chip in range(count):
            start = chip * span + piece * depth
            r.g_latent[piece, chip * stride : chip * stride + depth, :] = g_latent[start : start + depth]
    grads[model:half, :] = mm(r.latents[...], r.d_keys[...], 0, 0).astype(BF16)
    grads[half : half + LH, :] = mm(r.latents[...], r.d_values[...], 0, 0).astype(BF16)
    g_out = mm(r.heads_out[...], r.res_grad[...].reshape(rows, model), 0, 0).astype(BF16)
    for j, block in enumerate(pack_columns(g_out, width)):
        start = half + LH + j * width
        grads[start : start + width, :] = block
    r.g_packed[0][...] = grads[:half].reshape(r.g_packed[0].shape)
    r.g_packed[1][...] = grads[half:].reshape(r.g_packed[1].shape)
    r.flush(*r.g_packed)
    beside.middle()
    r.ready(r.source, r.d_residual)
    r.gain_grad[...] = jnp.zeros_like(r.gain_grad)

    def receive(i):
        part, gain_part = rms_back(r.source[i, team.core].astype(F32), r.gain[...], ex.total(i))
        r.gain_grad[...] += gain_part
        ex.join(i, r.input_grad, (r.d_residual[i] + part).astype(BF16))

    def leave(i):
        ex.join_copy(i, r.input_grad).wait_recv()
        if early:
            copy = send_to(r.input_grad.at[i], r.grad_here.at[i], r.early_sems[0].at[i], r.early_sems[1].at[i], opposite)
            copies.append((jnp.logical_and(team.core == 0, team.place == owner(i)), copy))
            pl.when(copies[-1][0])(copy.start)

    copies = []
    receive(0)
    for i in range(1, PIECES):
        receive(i)
        leave(i - 1)
    leave(PIECES - 1)
    place = lax.broadcasted_iota(jnp.int32, (GAIN_ROWS, LH), 0)
    nothing = jnp.zeros((GAIN_ROWS, LH), F32)
    for chip in range(count):
        columns = slice(chip * span, (chip + 1) * span)
        rows_of = slice(chip * stride + depth, (chip + 1) * stride)
        gains = [grad[:, columns] for grad in (r.gain_grad, r.mlp_gain)]
        if span < LH:
            gains = [jnp.concatenate([part, jnp.zeros((1, LH - span), F32)], axis=1) for part in gains]
        gains = jnp.where(place == 0, gains[0], jnp.where(place == 1, gains[1], nothing))
        r.g_latent[0, rows_of, :] = gains.astype(BF16)
        for piece in range(1, pieces):
            r.g_latent[piece, rows_of, :] = nothing.astype(BF16)
    r.flush(r.g_latent)
    beside.late()
    ex.finish(r.input_grad, False)
    r.flush(r.input_grad)
    beside.finish()
    for active, copy in copies:
        pl.when(active)(copy.wait)


class Part:
    def __init__(self, block):
        self.block = block.reshape((2,) + pieces_of(block[: block.shape[0] // 2]).shape)
        self.shape, self.dtype = self.block.shape[1:], block.dtype


def named_call(kernel, number, ins=(), lazy=(), far=(), outs=(), late=(), far_outs=(), scratch=()):
    groups = [dict(group) for group in (ins, lazy, far, outs, late, far_outs, scratch)]

    def listed(group):
        return [(k, v if isinstance(v, list) else [v], isinstance(v, list)) for k, v in group.items()]

    groups = [listed(group) for group in groups]
    ins, lazy, far, outs, late, far_outs, scratch = groups
    vmem, anywhere = pl.BlockSpec(memory_space=pltpu.VMEM), pl.BlockSpec(memory_space=pl.ANY)

    def flat(*parts):
        return [value for part in parts for _, values, _ in part for value in values]

    stages = [pltpu.VMEM(x.shape, x.dtype) for x in flat(lazy)] + [pltpu.VMEM(*x) for x in flat(late)]
    lazy_count, late_count = len(flat(lazy)), len(flat(late))

    def body(*refs):
        refs = list(refs)

        def take(count):
            taken, refs[:] = refs[:count], refs[count:]
            return taken

        named = {}

        def name(part, taken):
            for key, values, is_list in part:
                mine, taken = taken[: len(values)], taken[len(values) :]
                named[key] = mine if is_list else mine[0]

        name(ins, take(len(flat(ins))))
        lazy_refs = take(lazy_count)
        name(far, take(len(flat(far))))
        name(outs, take(len(flat(outs))))
        late_refs = take(late_count)
        name(far_outs, take(len(flat(far_outs))))
        lazy_held, late_held = take(lazy_count), take(late_count)
        in_sem, out_sem = take(1)[0], take(1)[0]
        name(lazy, lazy_held)
        name(late, late_held)
        name(scratch, take(len(flat(scratch))))
        sequence = lax.axis_index(TEN) // (lax.axis_size(TEN) // 2)
        parts = [isinstance(value, Part) for value in flat(lazy)]
        lazy_refs = [ref.at[sequence] if part else ref for ref, part in zip(lazy_refs, parts)]
        arrive = {
            id(held): pltpu.make_async_copy(ref, held, in_sem.at[k])
            for k, (ref, held) in enumerate(zip(lazy_refs, lazy_held))
        }
        leave = {
            id(held): pltpu.make_async_copy(held, ref, out_sem.at[k])
            for k, (ref, held) in enumerate(zip(late_refs, late_held))
        }
        for copy in arrive.values():
            copy.start()

        def ready(*buffers):
            for buffer in buffers:
                arrive[id(buffer)].wait()

        def flush(*buffers):
            for buffer in buffers:
                leave[id(buffer)].start()

        kernel(types.SimpleNamespace(ready=ready, flush=flush, **named))
        for copy in leave.values():
            copy.wait()

    results = pl.pallas_call(
        body,
        in_specs=[vmem] * len(flat(ins)) + [anywhere] * len(flat(lazy, far)),
        out_specs=[vmem] * len(flat(outs)) + [anywhere] * len(flat(late, far_outs)),
        out_shape=[jax.ShapeDtypeStruct(*x) for x in flat(outs, late, far_outs)],
        scratch_shapes=stages + [DMA((max(1, lazy_count),)), DMA((max(1, late_count),))] + flat(scratch),
        compiler_params=pltpu.CompilerParams(
            collective_id=number, has_side_effects=number is not None, vmem_limit_bytes=VMEM_LIMIT
        ),
        cost_estimate=pl.CostEstimate(flops=LINK_FLOPS, bytes_accessed=2**20, transcendentals=0),
    )(*[value.block if isinstance(value, Part) else value for value in flat(ins, lazy, far)])
    named, results = {}, list(results)
    for key, values, is_list in outs + late + far_outs:
        mine, results = results[: len(values)], results[len(values) :]
        named[key] = mine if is_list else mine[0]
    return types.SimpleNamespace(**named)


def forward_kernel(layer, r):
    team = Team()
    plane = Plane()
    core = lax.axis_index(SEC)
    holder = core == layer
    taker = jnp.logical_not(holder)
    across = across_device()
    ex_a, ex_b = Exchange(team, r.ex_a), Exchange(team, r.ex_b)
    greet(team.partners() + plane.partners() + [across])
    rows, width = r.queries.shape
    model = r.w_latent.shape[0]
    size = rows // PIECES
    feeds = range(3)

    own_copies = [pltpu.make_async_copy(r.own_feed[k], r.feed[k], r.own_sem.at[k]) for k in feeds]
    for copy in own_copies:
        pl.when(holder)(copy.start)
    gathers = [
        Gather(plane, k, r.feed[k], r.gather_sent.at[k], r.gather_here.at[k], taker) for k in feeds
    ]

    def cross(k, source, target):
        return send_to(source, target, r.cross_sent.at[k], r.cross_here.at[k], across)

    come = [cross(1 + k, r.own_feed[k].at[plane.me], r.come[k]) for k in feeds]
    if layer == 0:
        mine = cross(0, r.own_packed.at[plane.me], r.packed.at[plane.me])
        small = [
            send_to(r.pass_latent, r.far_latent, r.small_sent.at[0], r.small_here.at[0], team.other),
            send_to(r.own_gains, r.far_gains, r.small_sent.at[1], r.small_here.at[1], team.other),
        ]
        next_packed = cross(4, r.own_packed.at[plane.me], r.packed_next.at[plane.me])
        packed_gather = Gather(plane, 0, r.packed, r.packed_sent, r.packed_here)
        next_gather = Gather(plane, 1, r.packed_next, r.next_sent, r.next_here)
        own_packed = [
            pltpu.make_async_copy(r.own_packed, target, r.own_sem.at[3]) for target in (r.packed, r.packed_next)
        ]
        pl.when(holder)(mine.start)
        pl.when(holder)(own_packed[0].start)
        pl.when(taker)(own_packed[1].start)
        for copy in small:
            copy.start()
        for copy in small:
            copy.wait()
    else:
        pl.when(holder)(come[0].start)

    def next_come(k):
        @pl.when(holder)
        def _():
            come[k - 1].wait_send()
            come[k].start()

    def take_come(k):
        @pl.when(taker)
        def _():
            come[k].wait_recv()
            r.feed[k][plane.me] = r.come[k][...]

        gathers[k].start()

    gains = jnp.where(holder, r.own_gains[...], r.far_gains[...])
    r.gains[...] = gains
    r.w_latent[...] = jnp.where(holder, r.own_latent[...], r.far_latent[...])
    r.flush(r.w_latent)
    r.ready(r.source)

    def norm(i):
        block = r.source[i].reshape(size, model).astype(F32)
        r.attn_in[piece_rows(i, rows), :] = (block * reciprocal_rms(block) * gains[0:1]).astype(BF16)

    if layer == 0:
        each_piece(norm)

        @pl.when(taker)
        def _():
            mine.wait_recv()
            packed_gather.start()
            packed_gather.middle()
            packed_gather.finish()

        @pl.when(holder)
        def _():
            own_packed[0].wait()
            mine.wait_send()
            come[0].start()

        r.flush(r.packed)
        take_come(0)
    else:
        r.ready(r.packed)
    weights = r.packed[...].reshape(2 * model + 2 * LH, width)

    def project(i):
        at = piece_rows(i, rows)
        block = r.attn_in[at, :]
        r.queries[at, :] = mm(block, weights[:model]).astype(BF16)
        latents = mm(block, r.w_latent[...]).astype(BF16)
        r.latents[at, :] = latents
        r.keys[at, :] = mm(latents, weights[model : model + LH]).astype(BF16)
        r.values[at, :] = mm(latents, weights[model + LH : model + 2 * LH]).astype(BF16)

    w_out = [
        weights[model + 2 * LH + start : model + 2 * LH + start + width] for start in range(0, model, width)
    ]
    for i in range(PIECES):
        if layer == 1:
            norm(i)
        project(i)
        attend_rows(i * size, r.queries, r.keys, r.values, r.heads_out, r.norms)
        heads = r.heads_out[i * size : (i + 1) * size, :]
        ex_a.push(i, jnp.concatenate([mm(heads, block) for block in w_out], axis=1))
        if i == layer:
            next_come(1)
        if i == 0 and layer == 1:
            take_come(0)
        if i:
            ex_a.combine(i - 1)
        if i == 1:
            gathers[0].middle()
        if i == 2:
            next_come(2)
            if layer == 0:
                take_come(1)
    ex_a.combine(PIECES - 1)
    if layer == 1:
        take_come(1)
    r.flush(r.attn_in, r.queries, r.latents, r.keys, r.values, r.heads_out, r.norms)
    if layer == 0:

        @pl.when(taker)
        def _():
            next_packed.start()


    def receive(i):
        block = r.source[i, core].astype(F32) + ex_a.total(i)
        r.residual[i] = block
        ex_a.join(i, r.mlp_in, (block * reciprocal_rms(block) * gains[1:2]).astype(BF16))

    def feed(i):
        ex_a.join_copy(i, r.mlp_in).wait_recv()
        at = piece_rows(i, rows)
        block = r.mlp_in[i].reshape(size, model)
        shape = (r.hidden.shape[1], model)
        gate = mm(block, r.feed[0][...].reshape(shape), 1, 1)
        up = mm(block, r.feed[1][...].reshape(shape), 1, 1)
        hidden = (jax.nn.silu(gate) * up).astype(BF16)
        r.gate[at, :] = gate
        r.up[at, :] = up
        r.hidden[at, :] = hidden
        ex_b.push(i, mm(hidden, r.feed[2][...].reshape(shape)))

    receive(0)
    gathers[1].middle()
    take_come(2)
    receive(1)
    gathers[2].middle()

    @pl.when(holder)
    def _():
        for copy in own_copies:
            copy.wait()

    for gather in gathers:
        gather.finish()
    r.flush(*r.feed)
    feed(0)
    if layer == 0:

        @pl.when(holder)
        def _():
            next_packed.wait_recv()
            next_gather.start()

    def steady(i, _):
        receive(i)
        feed(i - 1)
        ex_b.combine(i - 2)
        return 0

    lax.fori_loop(2, PIECES, steady, 0)
    feed(PIECES - 1)
    ex_b.combine(PIECES - 2)
    ex_b.combine(PIECES - 1)
    ex_a.finish(r.mlp_in, False)
    r.flush(r.residual, r.mlp_in, r.gate, r.up, r.hidden)
    if layer == 0:

        @pl.when(holder)
        def _():
            next_gather.middle()
            next_gather.finish()

        @pl.when(taker)
        def _():
            own_packed[1].wait()
            next_packed.wait_send()

        r.flush(r.packed_next)
    each_piece(lambda i: ex_b.join(i, r.output, (r.residual[i] + ex_b.total(i)).astype(BF16)))
    ex_b.finish(r.output)
    r.flush(r.output)

    pl.when(holder)(come[2].wait_send)


def finish_kernel(groups, r):
    plane = Plane()
    team = Team()
    late = len(r.late)
    scatters = [Scatter(plane, k, r.late[k], *r.scatter[5 * k : 5 * k + 5]) for k in range(late)]
    count = lax.axis_size(TEN)
    z = lax.axis_index(TEN)
    core = lax.axis_index(SEC)
    first, second = core == 0, core == 1
    across = across_device()
    opposite = {TEN: across[TEN]}
    chips = [lax.rem(z + step, count) for step in range(1, count)]
    greet(plane.partners() + [across] + [{TEN: chip} for chip in chips])
    for scatter in scatters:
        scatter.start()
    sources = r.pieces + r.leave
    cross_sent, cross_here = r.cross_sems
    crosses = [
        send_to(source, r.come[k], cross_sent.at[k], cross_here.at[k], across) for k, source in enumerate(sources)
    ]

    pl.when(second)(crosses[0].start)

    def next_cross(k):
        @pl.when(second)
        def _():
            crosses[k - 1].wait_send()
            crosses[k].start()

    outputs = Outputs(r, [[], [0]])
    outputs.start()
    gather_sent, gather_here, gather_own = r.gather_sems
    gathers = [
        Gather(
            plane, k, whole, gather_sent.at[k], gather_here.at[k], first if k < FEED else None,
            r.total[k], gather_own.at[k],
        )
        for k, whole in enumerate(r.wholes)
    ]
    last = FEED + late - 1

    def arrive(k):
        crosses[k].wait_recv()
        return (sources[k][...].astype(F32) + r.come[k][...].astype(F32)).astype(BF16)

    def take_cross(k):
        @pl.when(first)
        def _():
            r.total[k][...] = arrive(k)

        gathers[k].start()

    scatters[0].middle()
    next_cross(1)
    take_cross(0)
    for scatter in scatters[1:]:
        scatter.middle()
    for k, scatter in enumerate(scatters):
        r.leave[k][...] = scatter.total().astype(BF16)
        if k == 0:
            next_cross(2)
            gathers[0].middle()
        pl.when(second)(crosses[FEED + k].start)
    take_cross(1)
    take_cross(2)
    gathers[1].middle()
    gathers[2].middle()

    @pl.when(first)
    def _():
        for k in range(FEED, last):
            r.total[k][...] = arrive(k)
        r.held[...] = arrive(last).reshape(r.held.shape)

    @pl.when(second)
    def _():
        for k in range(FEED, last):
            r.total[k][...] = r.done[k - FEED][...]
        r.held[...] = r.done[late - 1][...].reshape(r.held.shape)

    for k in range(FEED, last):
        gathers[k].start()
    block_sent, block_here = r.block_sems

    def block(step, chip, slot):
        return send_to(r.held.at[chip], r.slots.at[slot], block_sent.at[step], block_here.at[slot], {TEN: chip})

    for step, chip in enumerate(chips):
        block(step, chip, z).start()
    r.slots[z] = r.held[z]
    for step, chip in enumerate(chips):
        block(step, chip, chip).wait_recv()
    shares = [r.slots[shard].astype(F32) for shard in range(count)]
    sums = [sum(s for s, g in zip(shares, groups) if g == group) for group in range(KVH)]
    gain_rows = sums[0]
    for extra in sums[1:]:
        gain_rows = gain_rows + extra
    depth = gain_rows.shape[0] - GAIN_ROWS
    gain_rows = gain_rows * (2.0 / count)
    blocks = [jnp.concatenate([part[:depth], gain_rows[depth:]], axis=0) for part in sums]
    r.total[last][...] = jnp.concatenate(blocks, axis=1).astype(BF16)
    gathers[last].start()
    for k in range(FEED, last + 1):
        gathers[k].middle()

    for gather in gathers:
        gather.finish()
    for scatter in scatters:
        scatter.drain()
    for step, chip in enumerate(chips):
        block(step, chip, z).wait_send()

    @pl.when(second)
    def _():
        for copy in crosses[2:]:
            copy.wait_send()

    outputs.finish()


def finish(number, groups, feed, late, done, grad):
    dp, count = lax.axis_size(DP), lax.axis_size(TEN)
    depth = done[-1].shape[0] // count
    shapes = [part.shape for part in list(feed) + list(done)]
    totals = shapes[:-1] + [(depth, KVH * LH)]
    items = len(shapes)
    blocks = pltpu.VMEM((count, depth, LH), BF16)
    return named_call(
        functools.partial(finish_kernel, groups),
        number,
        ins=dict(pieces=list(feed), done=list(done)),
        far=dict(late=list(late), shares=[], spreads=[grad]),
        far_outs=dict(wholes=[((dp,) + total, BF16) for total in totals], spreads_here=[(grad.shape, BF16)]),
        scratch=dict(
            scatter=[item for load in late for item in scatter_scratch(load)],
            come=[pltpu.VMEM(shape, BF16) for shape in shapes],
            leave=[pltpu.VMEM(part.shape, BF16) for part in done],
            total=[pltpu.VMEM(total, BF16) for total in totals],
            slots=blocks,
            held=blocks,
            cross_sems=[DMA((items,)), DMA((items,))],
            gather_sems=[DMA((items, 3)), DMA((items, dp)), DMA((items,))],
            block_sems=[DMA((count,)), DMA((count,))],
            spread_sems=[DMA((count // 2, PIECES)), DMA((PIECES,))],
        ),
    )


def emit_kernel(r):
    core = lax.axis_index(SEC)
    sequence = lax.axis_index(TEN) // (lax.axis_size(TEN) // 2)
    placed = []
    place = lax.rem(lax.axis_index(TEN), lax.axis_size(TEN) // 2)
    for k, (mine, share, spread, out) in enumerate(
        ((r.outs, r.outs_share, r.outs_spread, r.layer_out), (r.grads, r.grads_share, r.grads_spread, r.input_grad))
    ):
        for piece in range(PIECES):
            passed = place == owner(piece)
            for side, to in enumerate((sequence, 1 - sequence)):
                at = (2 * k + side, piece)
                held = r.held.at[at]
                for layer in range(2):
                    sources = [(mine, True)] if side == 0 else [(share, passed), (spread, jnp.logical_not(passed))]
                    for blocks, active in sources:
                        come = pltpu.make_async_copy(blocks[layer].at[piece], held, r.held_here.at[at])
                        pl.when(jnp.logical_and(core == layer, active))(come.start)
                placed.append((come, pltpu.make_async_copy(held, out.at[to, piece], r.placed.at[at])))
    wide = []
    for k in range(FEED):
        for layer, source in enumerate((r.zero[k], r.one[k])):
            copy = pltpu.make_async_copy(source, r.wide[k], r.wide_here.at[k])
            pl.when(core == layer)(copy.start)
            if layer == 0:
                wide.append(copy)
    for come, leave in placed:
        come.wait()
        leave.start()
    r.ready(r.low, r.high, r.latent)
    model = r.g_query.shape[0]
    columns = r.g_query.shape[1]
    low = r.low[...].reshape(-1, columns).astype(F32)
    high = r.high[...].reshape(-1, columns).astype(F32)
    r.g_query[...] = low[:model]
    r.g_key_up[...] = low[model:]
    r.g_value_up[...] = high[:LH]
    r.g_out[...] = jnp.concatenate(
        [high[start : start + columns] for start in range(LH, LH + model, columns)], axis=1
    )
    depth = r.latent.shape[1] - GAIN_ROWS
    r.g_latent[...] = r.latent[:, :depth, :].astype(F32).reshape(r.g_latent.shape)
    r.gains[...] = r.latent[0, depth:, :LH].astype(F32)
    r.flush(r.g_query, r.g_key_up, r.g_value_up, r.g_out, r.g_latent, r.gains)
    for k in range(FEED):
        wide[k].wait()
        r.g_wide[k][...] = r.wide[k][...].reshape(r.g_wide[k].shape).astype(F32)
        r.flush(r.g_wide[k])
    for come, leave in placed:
        leave.wait()


def emit(outs, outs_share, outs_spread, grads, grads_share, grads_spread, zero, one, parts):
    low, high, latent = parts
    pieces, depth, model = zero[0].shape
    columns = low.shape[2]
    split = pieces * (latent.shape[1] - GAIN_ROWS)
    both = ((2,) + outs[0].shape, BF16)
    out = named_call(
        emit_kernel,
        None,
        lazy=dict(low=low, high=high, latent=latent),
        far=dict(
            outs=outs, outs_share=outs_share, outs_spread=outs_spread,
            grads=grads, grads_share=grads_share, grads_spread=grads_spread,
            zero=zero, one=one,
        ),
        late=dict(
            g_query=((model, columns), F32),
            g_key_up=((LH, columns), F32),
            g_value_up=((LH, columns), F32),
            g_out=((columns, model), F32),
            g_latent=((split, KVH * LH), F32),
            gains=((GAIN_ROWS, LH), F32),
            g_wide=[((pieces * depth, model), F32)] * FEED,
        ),
        far_outs=dict(layer_out=both, input_grad=both),
        scratch=dict(
            placed=DMA((4, PIECES)),
            held_here=DMA((4, PIECES)),
            held=pltpu.VMEM((4,) + outs[0].shape, BF16),
            wide_here=DMA((FEED,)),
            wide=[pltpu.VMEM((pieces, depth, model), BF16)] * FEED,
        ),
    )
    wide = [part for part in out.g_wide]
    rest = (out.g_query, out.g_key_up, out.g_value_up, out.g_out, out.g_latent, out.gains)
    return (out.layer_out, out.input_grad, *wide, *rest)


def pieces_of(block):
    if isinstance(block, Part) or len(block.shape) == 4:
        return block
    return block.reshape(PIECES, 2, block.shape[0] // PIECES // 2, block.shape[1])


def shapes_of(rows, model):
    return (PIECES, 2, rows // PIECES // 2, model), (PIECES, rows // PIECES // 2, model)


def forward_layer(layer, number, source, own_feed, own_packed=None, packed=None, **small):
    rows, model = LEN, own_feed[0].shape[2]
    split, own = shapes_of(rows, model)
    pieces, depth, width = (packed if own_packed is None else own_packed).shape
    wide = (rows, pieces * own_feed[0].shape[1])
    pair = min(2 * HD, width)
    narrow = ((rows, width), BF16)
    outs = dict(gains=((2, model), F32))
    late = dict(
        w_latent=((model, LH), BF16),
        attn_in=((rows, model), BF16),
        queries=narrow,
        latents=((rows, LH), BF16),
        keys=narrow,
        values=narrow,
        heads_out=narrow,
        norms=((width // pair, pair // HD, rows), F32),
        residual=(own, F32),
        mlp_in=(split, BF16),
        gate=(wide, F32),
        up=(wide, F32),
        hidden=(wide, BF16),
        output=(split, BF16),
        feed=[(w.shape, BF16) for w in own_feed],
    )
    scratch = dict(
        ex_a=exchange_scratch(rows, model),
        ex_b=exchange_scratch(rows, model),
        come=[pltpu.VMEM(w.shape[1:], BF16) for w in own_feed],
        own_sem=DMA((4,)),
        gather_sent=DMA((3, 3)),
        gather_here=DMA((3, pieces)),
        cross_sent=DMA((5,)),
        cross_here=DMA((5,)),
    )
    lazy, far = dict(source=pieces_of(source)), dict(own_feed=own_feed)
    if layer == 0:
        far.update(own_packed=own_packed)
        outs.update(far_latent=((model, LH), BF16), far_gains=((2, model), F32))
        late.update(packed=((pieces, depth, width), BF16), packed_next=((pieces, depth, width), BF16))
        scratch.update(
            small_sent=DMA((2,)),
            small_here=DMA((2,)),
            packed_sent=DMA((3,)),
            packed_here=DMA((pieces,)),
            next_sent=DMA((3,)),
            next_here=DMA((pieces,)),
        )
    else:
        lazy.update(packed=packed)
    return named_call(
        functools.partial(forward_kernel, layer),
        number,
        ins=small,
        lazy=lazy,
        far=far,
        outs=outs,
        late=late,
        scratch=scratch,
    )


def feed_layer_back(number, upstream, result, beside):
    rows, model = result.attn_in.shape
    split, half = shapes_of(rows, model)
    columns = result.queries.shape[1]
    wide = pltpu.VMEM(result.hidden.shape, BF16)
    narrow = ((rows, columns), BF16)
    total = pltpu.VMEM((rows, columns), F32)
    return named_call(
        functools.partial(feed_back, beside.shared),
        number,
        ins=dict(gain=result.gains[1:2]),
        lazy=dict(
            upstream=pieces_of(upstream),
            feed=result.feed,
            gate=result.gate,
            up=result.up,
            mlp_in=result.mlp_in.reshape(rows, model),
            hidden=result.hidden,
            residual=result.residual,
            packed=result.packed,
            queries=result.queries,
            keys=result.keys,
            values=result.values,
            heads_out=result.heads_out,
            norms=result.norms,
        ),
        far=beside.far,
        outs=dict(gain_grad=((1, model), F32), **beside.outs),
        late=dict(
            d_residual=(half, F32),
            res_grad=(split, BF16),
            grads=[(w.shape, BF16) for w in result.feed],
            d_queries=narrow,
            d_keys=narrow,
            d_values=narrow,
            d_latents=((rows, LH), BF16),
        ),
        far_outs=beside.far_outs,
        scratch=dict(
            exchange=exchange_scratch(rows, model),
            d_gate=wide,
            d_up=wide,
            d_heads=pltpu.VMEM((rows, columns), BF16),
            key_total=total,
            value_total=total,
            **beside.scratch,
        ),
    )


def attend_layer_back(number, source, result, back, beside, early=False):
    rows, model = result.attn_in.shape
    pieces, depth, width = result.packed.shape
    out = named_call(
        functools.partial(attend_in_back, beside.shared, early),
        number,
        ins=dict(gain=result.gains[0:1], mlp_gain=back.gain_grad),
        lazy=dict(
            d_queries=back.d_queries,
            d_latents=back.d_latents,
            packed=result.packed,
            w_latent=result.w_latent,
            attn_in=result.attn_in,
            latents=result.latents,
            heads_out=result.heads_out,
            d_keys=back.d_keys,
            d_values=back.d_values,
            res_grad=back.res_grad,
            source=pieces_of(source),
            d_residual=back.d_residual,
        ),
        far=beside.far,
        outs=beside.outs,
        late=dict(
            input_grad=(shapes_of(rows, model)[0], BF16),
            g_packed=[((pieces, depth // 2, width), BF16)] * 2,
            g_latent=((pieces, model // pieces + lax.axis_size(TEN) * GAIN_ROWS, LH), BF16),
        ),
        far_outs=dict(grad_here=(shapes_of(rows, model)[0], BF16), **beside.far_outs) if early else beside.far_outs,
        scratch=dict(
            exchange=exchange_scratch(rows, model),
            grads=pltpu.VMEM((pieces * depth, width), BF16),
            gain_grad=pltpu.VMEM((1, model), F32),
            early_sems=[DMA((PIECES,)), DMA((PIECES,))],
            **beside.scratch,
        ),
    )
    out.parts = out.g_packed + [out.g_latent]
    return out


def tie(*arrays):
    return lax.optimization_barrier(arrays)


def local(
    inputs,
    out_grad,
    w_query,
    w_latent,
    w_key_up,
    w_value_up,
    w_out,
    w_gate,
    w_up,
    w_down,
    norm_attn,
    norm_mlp,
):
    at = Place()
    model = inputs.shape[1]
    heads = w_query.shape[2] // HD

    def group_of(shard):
        return shard * heads // (QH // KVH)

    opposite_z = (at.z + at.team) % at.count

    def latent_of(shard):
        return lax.dynamic_slice_in_dim(w_latent[0], group_of(shard) * LH, LH, 1)

    own_feed = [by_dp(w) for w in (w_gate[0].T, w_up[0].T, w_down[0])]
    own_packed = by_dp(pack_attention(w_query[0], w_key_up[0], w_value_up[0], w_out[0]))
    own_gains = jnp.concatenate([norm_attn, norm_mlp], axis=0)
    own_latent = latent_of(at.z)
    source = Part(inputs)
    zero = forward_layer(
        0,
        0,
        source,
        own_feed,
        own_packed=own_packed,
        own_gains=own_gains,
        own_latent=own_latent,
        pass_latent=latent_of(opposite_z),
    )
    first_out = zero.output
    one = forward_layer(
        1,
        1,
        first_out,
        own_feed,
        packed=zero.packed_next,
        own_gains=own_gains,
        far_gains=zero.far_gains,
        own_latent=own_latent,
        far_latent=zero.far_latent,
    )
    one.packed = zero.packed_next
    second_out = one.output

    back = feed_layer_back(2, Part(out_grad), one, Beside(shares=[(first_out, 0)]))
    first_share = back.shares_here[0]
    beside = Beside(back.grads, shares=[(second_out, 1)], spreads=[(first_share, 0)])
    above = attend_layer_back(3, first_out, one, back, beside)
    second_share, second_grad = above.shares_here[0], above.input_grad
    beside = Beside(above.parts, above.sums, True, [(second_grad, 1)], [(second_share, 1)])
    back = feed_layer_back(4, second_grad, zero, beside)
    wide_one, grad_share = back.wholes, back.shares_here[0]
    beside = Beside(back.grads, back.sums, spreads=[(grad_share, 1)])
    below = attend_layer_back(5, source, zero, back, beside, True)
    first_grad = below.input_grad
    groups = tuple(group_of(shard) for shard in range(at.count))
    last = finish(6, groups, below.sums, below.parts, below.totals, below.grad_here)
    *wide_zero, low_part, high_part, latent = last.wholes
    out = emit(
        [first_out, second_out],
        [first_share, second_share],
        [above.spreads_here[0], back.spreads_here[0]],
        [first_grad, second_grad],
        [below.grad_here, grad_share],
        [last.spreads_here[0], below.spreads_here[0]],
        wide_zero,
        wide_one,
        [low_part, high_part, latent],
    )
    layer_out, input_grad, g_gate, g_up, g_down, g_query, g_key_up, g_value_up, g_out, g_latent, gains = out
    gains = gains[:, : model // at.count]
    layer_out, input_grad = (both.reshape(1, 2 * LEN, model) for both in (layer_out, input_grad))
    return (
        layer_out,
        input_grad,
        g_query[None],
        g_latent[None],
        g_key_up[None],
        g_value_up[None],
        g_out[None],
        g_gate.T[None],
        g_up.T[None],
        g_down[None],
        gains[0:1],
        gains[1:2],
    )


def solution(mesh):
    columns = P(SEC, None, TEN)
    rows = P(SEC, TEN, None)
    return jax.shard_map(
        local,
        mesh=mesh,
        in_specs=(
            P(DP, None),
            P(DP, None),
            columns,
            P(SEC, None, None),
            columns,
            columns,
            rows,
            columns,
            columns,
            rows,
            P(SEC, None),
            P(SEC, None),
        ),
        out_specs=(
            P(SEC, DP, None),
            P(SEC, DP, None),
            columns,
            rows,
            columns,
            columns,
            rows,
            columns,
            columns,
            rows,
            P(SEC, TEN),
            P(SEC, TEN),
        ),
        check_vma=False,
    )
```

```python
import functools
import math
import types

import jax
import jax.numpy as jnp
from jax import lax
from jax.experimental import pallas as pl
from jax.experimental.pallas import tpu as pltpu
from jax.sharding import PartitionSpec as P

QH = 16
HD = 64
KVH = 2
LH = 256
LEN = 1024
EPS = 1e-05
F32 = jnp.float32
BF16 = jnp.bfloat16
SEC, DP, TEN = "section", "dp", "tensor"
LOG2_SCALE = HD**-0.5 * math.log2(math.e)
KEY_ROWS = 256


def mm(left, right, left_dim=1, right_dim=0):
    dims = (((left_dim,), (right_dim,)), ((), ()))
    return lax.dot_general(left, right, dims, preferred_element_type=F32)


def head_masks(width):
    if width == HD:
        return [None]
    lane = lax.broadcasted_iota(jnp.int32, (1, width), 1)
    return [lane // HD == j for j in range(width // HD)]


def keep_head(block, mask):
    return block if mask is None else jnp.where(mask, block, jnp.zeros_like(block))


def attend_rows(start, q_ref, k_ref, v_ref, o_ref, norm_ref):
    columns = q_ref.shape[1]
    width = min(2 * HD, columns)
    masks = head_masks(width)
    rows = KEY_ROWS
    place_k = lax.broadcasted_iota(jnp.int32, (rows, rows), 0)
    place_q = lax.broadcasted_iota(jnp.int32, (rows, rows), 1)
    for pair in range(columns // width):
        lanes = slice(pair * width, (pair + 1) * width)
        query = q_ref[start : start + rows, lanes]
        total = None
        for j, mask in enumerate(masks):
            query_j = keep_head(query, mask)
            scores = mm(k_ref[start : start + rows, lanes], query_j, 1, 1) * LOG2_SCALE
            scores = jnp.where(place_k <= place_q, scores, -jnp.inf)
            largest = jnp.max(scores, axis=0, keepdims=True)
            if start:
                before = mm(k_ref[0:start, lanes], query_j, 1, 1) * LOG2_SCALE
                largest = jnp.maximum(largest, jnp.max(before, axis=0, keepdims=True))
            weight = jnp.exp2(scores - largest)
            norm = jnp.sum(weight, axis=0, keepdims=True)
            value = keep_head(v_ref[start : start + rows, lanes], mask)
            out = mm(value, weight.astype(BF16), 0, 0)
            if start:
                weight = jnp.exp2(before - largest)
                norm = norm + jnp.sum(weight, axis=0, keepdims=True)
                value = keep_head(v_ref[0:start, lanes], mask)
                out = out + mm(value, weight.astype(BF16), 0, 0)
            out = out / norm
            total = out if total is None else total + out
            norm_ref[pair, j : j + 1, start : start + rows] = largest + jnp.log2(norm)
        o_ref[start : start + rows, lanes] = total.T.astype(BF16)


def attend_rows_back(start, q_ref, k_ref, v_ref, o_ref, g_ref, norm_ref, dq_ref, key_total, value_total):
    columns = q_ref.shape[1]
    width = min(2 * HD, columns)
    masks = head_masks(width)
    rows = KEY_ROWS
    end = start + rows
    place_k = lax.broadcasted_iota(jnp.int32, (rows, rows), 0)
    place_q = lax.broadcasted_iota(jnp.int32, (rows, rows), 1)
    for pair in range(columns // width):
        lanes = slice(pair * width, (pair + 1) * width)
        query, grad = q_ref[start:end, lanes], g_ref[start:end, lanes]
        key, value = k_ref[0:end, lanes], v_ref[0:end, lanes]
        product = (grad.astype(F32) * o_ref[start:end, lanes].astype(F32)).T
        grad_query = grad_key = grad_value = None
        for j, mask in enumerate(masks):
            query_j = keep_head(query, mask)
            grad_j = keep_head(grad, mask)
            delta = jnp.sum(product[j * HD : (j + 1) * HD, :], axis=0, keepdims=True)
            scores = mm(key, query_j, 1, 1) * LOG2_SCALE
            probs = jnp.exp2(scores - norm_ref[pair, j : j + 1, start:end])
            last = jnp.where(place_k <= place_q, probs[start:], 0.0)
            probs = jnp.concatenate([probs[:start], last], axis=0) if start else last
            grad_probs = mm(value, grad_j, 1, 1)
            grad_scores = (probs * (grad_probs - delta)).astype(BF16)
            value_term = mm(probs.astype(BF16), grad_j)
            key_term = mm(grad_scores, query_j)
            query_term = mm(keep_head(key, mask), grad_scores, 0, 0)
            grad_key = key_term if grad_key is None else grad_key + key_term
            grad_value = value_term if grad_value is None else grad_value + value_term
            grad_query = query_term if grad_query is None else grad_query + query_term
        dq_ref[start:end, lanes] = (grad_query.T * HD**-0.5).astype(BF16)
        if end == LEN:
            key_total[:, lanes] = grad_key
            value_total[:, lanes] = grad_value
        else:
            key_total[0:end, lanes] += grad_key
            value_total[0:end, lanes] += grad_value


def rms_scale(features):
    return features * lax.rsqrt(jnp.mean(features * features, axis=-1, keepdims=True) + EPS)


class Place:
    def __init__(self):
        self.count = lax.axis_size(TEN)
        self.team = self.count // 2
        self.z = lax.axis_index(TEN)
        self.core = lax.axis_index(SEC)
        self.dp = lax.axis_index(DP)
        self.sequence = self.z // self.team
        self.first = self.core == 0

    def opposite(self, block, cores=(0, 1)):
        n, t = self.count, self.team
        route = [(core * n + z, core * n + (z + t) % n) for core in cores for z in range(n)]
        return lax.ppermute(block, (SEC, TEN), route)

    def across(self, block, core):
        n, t = self.count, self.team
        route = [(core * n + z, (1 - core) * n + (z + t) % n) for z in range(n)]
        return lax.ppermute(block, (SEC, TEN), route)


def pack_columns(matrix, width):
    return [matrix[:, i : i + width] for i in range(0, matrix.shape[1], width)]


def pack_attention(query, key_up, value_up, out):
    width = query.shape[1]
    return jnp.concatenate([query, key_up, value_up] + pack_columns(out, width), axis=0)


def by_dp(matrix):
    count = lax.axis_size(DP)
    return matrix.reshape(count, matrix.shape[0] // count, matrix.shape[1])


def whole_of(pieces):
    return pieces.reshape(-1, pieces.shape[2])


MESH = pl.DeviceIdType.MESH
PIECES = 4
VMEM_LIMIT = 58 * 2**20
LINK_FLOPS = 4 * 10**9
GAIN_ROWS = 16
FEED = 3
DMA = pltpu.SemaphoreType.DMA


def reciprocal_rms(features):
    return lax.rsqrt(jnp.mean(features * features, axis=-1, keepdims=True) + EPS)


def send_to(source, target, sent, here, device):
    return pltpu.make_async_remote_copy(
        src_ref=source,
        dst_ref=target,
        send_sem=sent,
        recv_sem=here,
        device_id=device,
        device_id_type=MESH,
    )


def greet(partners):
    barrier = pltpu.get_barrier_semaphore()
    for partner in partners:
        pl.semaphore_signal(barrier, inc=1, device_id=partner, device_id_type=MESH)
    pl.semaphore_wait(barrier, len(partners))


class Team:
    def __init__(self):
        count = lax.axis_size(TEN)
        self.size = count // 2
        self.core = lax.axis_index(SEC)
        z = lax.axis_index(TEN)
        self.place = lax.rem(z, self.size)
        self.base = z - self.place
        self.other = {SEC: 1 - self.core}

    def peer(self, step):
        place = lax.rem(self.place + step, self.size)
        return place, {TEN: self.base + place}

    def partners(self):
        return [self.other] + [self.peer(step)[1] for step in range(1, self.size)]


class Plane:
    def __init__(self):
        me = lax.axis_index(DP)
        self.me = me
        self.one = me + 1 - 2 * lax.rem(me, 2)
        self.two = lax.rem(me + 2, 4)
        self.both = lax.rem(self.one + 2, 4)

    def partners(self):
        return [{DP: self.one}, {DP: self.two}]

    def order(self, turn):
        return (self.one, self.two) if turn % 2 == 0 else (self.two, self.one)


def scatter_scratch(load):
    piece = load.shape[1:]
    return [pltpu.VMEM((3,) + piece, BF16), pltpu.VMEM((3,) + piece, BF16), DMA((3,)), DMA((3,)), DMA((2,))]


class Scatter:
    def __init__(self, plane, turn, load, slots, held, sent, here, local):
        near, far = plane.order(turn)
        self.slots, self.held = slots, held
        self.copies = [
            send_to(load.at[near], slots.at[0], sent.at[0], here.at[0], {DP: near}),
            send_to(load.at[plane.both], slots.at[1], sent.at[1], here.at[1], {DP: near}),
            send_to(held.at[2], slots.at[2], sent.at[2], here.at[2], {DP: far}),
        ]
        self.local = [
            pltpu.make_async_copy(load.at[plane.me], held.at[0], local.at[0]),
            pltpu.make_async_copy(load.at[far], held.at[1], local.at[1]),
        ]

    def start(self):
        self.copies[1].start()
        self.copies[0].start()
        for copy in self.local:
            copy.start()

    def middle(self):
        self.local[1].wait()
        self.copies[1].wait_recv()
        self.held[2] = (self.held[1].astype(F32) + self.slots[1].astype(F32)).astype(BF16)
        self.copies[2].start()

    def total(self):
        self.local[0].wait()
        self.copies[0].wait_recv()
        total = self.held[0].astype(F32) + self.slots[0].astype(F32)
        self.copies[2].wait_recv()
        return total + self.slots[2].astype(F32)

    def drain(self):
        for copy in self.copies:
            copy.wait_send()


class Gather:
    def __init__(self, plane, turn, whole, sent, here, active=None, piece=None, local=None, rows=slice(None)):
        self.active = active
        near, far = plane.order(turn)
        me = plane.me

        def part(place):
            return whole.at[place, rows]

        source = part(me) if piece is None else piece

        def copy(k, source, place, device):
            return send_to(source, part(place), sent.at[k], here.at[place], {DP: device})

        self.first = copy(0, source, me, near)
        self.second = [copy(1, source, me, far), copy(2, part(near), near, far)]
        self.coming = [copy(0, part(place), place, near) for place in (near, far, plane.both)]
        self.local = [] if piece is None else [pltpu.make_async_copy(piece, whole.at[me], local)]

    def when(self, body):
        if self.active is None:
            body()
        else:
            pl.when(self.active)(body)

    def start(self):
        def body():
            for copy in [self.first, self.second[0]] + self.local:
                copy.start()

        self.when(body)

    def middle(self):
        def body():
            self.coming[0].wait_recv()
            self.second[1].start()

        self.when(body)

    def finish(self):
        def body():
            self.coming[1].wait_recv()
            self.coming[2].wait_recv()
            for copy in [self.first] + self.second:
                copy.wait_send()
            for copy in self.local:
                copy.wait()

        self.when(body)


def across_device():
    count = lax.axis_size(TEN)
    opposite = lax.rem(lax.axis_index(TEN) + count // 2, count)
    return {SEC: 1 - lax.axis_index(SEC), TEN: opposite}


class Beside:
    def __init__(self, loads=(), crosses=(), gathered=False, shares=(), spreads=()):
        team = lax.axis_size(TEN) // 2
        self.shared = [[core for _, core in group] for group in (shares, spreads)]
        shares, spreads = ([block for block, _ in group] for group in (shares, spreads))
        self.far = dict(loads=list(loads), crosses=list(crosses), shares=shares, spreads=spreads)
        pieces = [cross.shape for cross in crosses]
        dp = lax.axis_size(DP)
        self.outs = dict(
            sums=[(load.shape[1:], BF16) for load in loads], totals=[(piece, BF16) for piece in pieces]
        )
        self.far_outs = dict(
            wholes=[((dp,) + piece, BF16) for piece in pieces] if gathered else [],
            shares_here=[(block.shape, BF16) for block in shares],
            spreads_here=[(block.shape, BF16) for block in spreads],
        )
        count = max(1, len(pieces))
        self.scratch = dict(
            scatter=[item for load in loads for item in scatter_scratch(load)],
            comes=[pltpu.VMEM(piece, BF16) for piece in pieces],
            cross_sems=[DMA((count,)), DMA((count,)), DMA((count,)), DMA((count,))],
            gather_sems=[DMA((count, 3)), DMA((count, dp))],
            share_sems=[DMA((PIECES,))] * (2 * len(shares)),
            spread_sems=[DMA((team, PIECES)), DMA((PIECES,))] * len(spreads),
        )


class BesideRun:
    def __init__(self, r, plane, sender, shared):
        self.outputs = Outputs(r, shared)
        self.totals, self.comes, self.sums = r.totals, r.comes, r.sums
        self.scatters = [
            Scatter(plane, k, load, *r.scatter[5 * k : 5 * k + 5]) for k, load in enumerate(r.loads)
        ]
        self.sends = lax.axis_index(SEC) == sender
        self.takes = jnp.logical_not(self.sends)
        across = across_device()
        sent, here, own, local = r.cross_sems
        self.copies = [
            send_to(cross, r.comes[k], sent.at[k], here.at[k], across) for k, cross in enumerate(r.crosses)
        ]
        self.own = [pltpu.make_async_copy(cross, r.totals[k], own.at[k]) for k, cross in enumerate(r.crosses)]
        self.gathers = [
            Gather(
                plane, k, whole, r.gather_sems[0].at[k], r.gather_sems[1].at[k], self.takes, r.totals[k], local.at[k]
            )
            for k, whole in enumerate(r.wholes)
        ]
        self.partners = (plane.partners() if self.scatters or self.gathers else []) + (
            [across] if self.copies else []
        )
        self.partners = self.partners + self.outputs.partners

    def start(self):
        self.outputs.start()
        for scatter in self.scatters:
            scatter.start()
        for copy, own in zip(self.copies, self.own):
            pl.when(self.sends)(copy.start)
            own.start()

    def add(self):
        for own in self.own:
            own.wait()

        @pl.when(self.takes)
        def _():
            for copy, come, total in zip(self.copies, self.comes, self.totals):
                copy.wait_recv()
                total[...] = (total[...].astype(F32) + come[...].astype(F32)).astype(BF16)

    def middle(self):
        for scatter in self.scatters:
            scatter.middle()
        if self.gathers:
            self.add()
            for gather in self.gathers:
                gather.start()

    def late(self):
        for gather in self.gathers:
            gather.middle()

    def finish(self):
        for scatter, total in zip(self.scatters, self.sums):
            total[...] = scatter.total().astype(BF16)
            scatter.drain()
        if self.copies and not self.gathers:
            self.add()
        for gather in self.gathers:
            gather.finish()
        for copy in self.copies:
            pl.when(self.sends)(copy.wait_send)
        self.outputs.finish()


def owner(piece):
    return piece * (lax.axis_size(TEN) // 2) // PIECES


class Outputs:
    def __init__(self, r, shared):
        team = Team()
        core = lax.axis_index(SEC)
        opposite = {TEN: across_device()[TEN]}
        self.partners = [opposite] if r.shares else []
        self.out, self.come = [], []
        for piece in range(PIECES):
            mine = team.place == owner(piece)
            for k, block in enumerate(r.shares):
                sent, here = r.share_sems[2 * k : 2 * k + 2]
                target = r.shares_here[k].at[piece]
                copy = send_to(block.at[piece], target, sent.at[piece], here.at[piece], opposite)
                active = jnp.logical_and(core == shared[0][k], mine)
                self.out.append((active, copy))
                self.come.append((active, copy))
            for k, block in enumerate(r.spreads):
                sent, here = r.spread_sems[2 * k : 2 * k + 2]
                for step in range(1, team.size):
                    copy = send_to(
                        block.at[piece], r.spreads_here[k].at[piece], sent.at[step, piece], here.at[piece],
                        team.peer(step)[1],
                    )
                    self.out.append((jnp.logical_and(core == shared[1][k], mine), copy))
                theirs = jnp.logical_and(core == shared[1][k], jnp.logical_not(mine))
                self.come.append((theirs, copy))

    def start(self):
        for active, copy in self.out:
            pl.when(active)(copy.start)

    def finish(self):
        for active, copy in self.out:
            pl.when(active)(copy.wait_send)
        for active, copy in self.come:
            pl.when(active)(copy.wait_recv)


def exchange_scratch(rows, model):
    team = lax.axis_size(TEN) // 2
    half = rows // PIECES // 2
    return [
        pltpu.VMEM((2, half, model), F32),
        pltpu.VMEM((2, half, model), F32),
        pltpu.VMEM((PIECES, half, model), BF16),
        pltpu.VMEM((PIECES, half, model), BF16),
        pltpu.VMEM((team, PIECES, half, model), BF16),
        DMA((PIECES,)),
        DMA((PIECES,)),
        DMA((team, PIECES)),
        DMA((team, PIECES)),
        DMA((PIECES,)),
        DMA((PIECES,)),
    ]


EXCHANGE = 11


class Exchange:
    def __init__(self, team, refs):
        self.team = team
        (self.part, self.keep, self.out, self.got, self.far) = refs[:5]
        (self.core_sent, self.core_here, self.far_sent, self.far_here) = refs[5:9]
        (self.join_sent, self.join_here) = refs[9:]

    def core_copy(self, i):
        return send_to(
            self.out.at[i], self.got.at[i], self.core_sent.at[i], self.core_here.at[i], self.team.other
        )

    def far_copy(self, i, step, place):
        at = self.far.at[place, i]
        return send_to(
            at, at, self.far_sent.at[step, i], self.far_here.at[place, i], self.team.peer(step)[1]
        )

    def join_copy(self, i, whole):
        at = whole.at[i, self.team.core]
        return send_to(at, at, self.join_sent.at[i], self.join_here.at[i], self.team.other)

    def push(self, i, product):
        core = self.team.core
        self.part[...] = product.reshape(self.part.shape)
        self.out[i] = self.part[1 - core].astype(BF16)
        self.core_copy(i).start()
        self.keep[i % 2] = self.part[core]

    def combine(self, i):
        self.core_copy(i).wait_recv()
        self.far[self.team.place, i] = (self.keep[i % 2] + self.got[i].astype(F32)).astype(BF16)
        for step in range(1, self.team.size):
            self.far_copy(i, step, self.team.place).start()

    def send_all(self, product):
        def send(i):
            self.push(i, product(i))

            @pl.when(i > 0)
            def _():
                self.combine(i - 1)

        each_piece(send)
        self.combine(PIECES - 1)

    def total(self, i):
        for step in range(1, self.team.size):
            self.far_copy(i, step, self.team.peer(step)[0]).wait_recv()
        total = self.far[0, i].astype(F32)
        for place in range(1, self.team.size):
            total = total + self.far[place, i].astype(F32)
        return total

    def join(self, i, whole, half):
        whole[i, self.team.core] = half
        self.join_copy(i, whole).start()

    def finish(self, whole, coming=True):
        def drain(i):
            self.core_copy(i).wait_send()
            for step in range(1, self.team.size):
                self.far_copy(i, step, self.team.place).wait_send()
            self.join_copy(i, whole).wait_send()
            if coming:
                self.join_copy(i, whole).wait_recv()

        each_piece(drain)


def each_piece(body):
    lax.fori_loop(0, PIECES, lambda i, _: (body(i), 0)[1], 0)


def piece_rows(i, rows):
    size = rows // PIECES
    return pl.ds(pl.multiple_of(i * size, size), size)


def rms_back(block, gain, upstream):
    inverse = reciprocal_rms(block)
    normed = block * inverse
    scaled = upstream * gain
    grad = inverse * (scaled - normed * jnp.mean(scaled * normed, axis=-1, keepdims=True))
    return grad, jnp.sum(upstream * normed, axis=0, keepdims=True)


def feed_back(shared, r):
    team, plane = Team(), Plane()
    ex = Exchange(team, r.exchange)
    beside = BesideRun(r, plane, 0, shared)
    greet(team.partners() + beside.partners)
    beside.start()
    rows, model = r.mlp_in.shape
    size = rows // PIECES
    shape = (size, model)
    wide = (r.d_gate.shape[1], model)
    width = r.queries.shape[1]
    last = PIECES - 1
    upstream, gate, up, d_gate, d_up = r.upstream, r.gate, r.up, r.d_gate, r.d_up
    w_gate, w_up, w_down = r.feed
    r.ready(upstream, gate, up, *r.feed)

    def product(i):
        at = piece_rows(i, rows)
        grad_hidden = mm(upstream[i].reshape(shape), w_down[...].reshape(wide), 1, 1)
        gate_block = gate[at, :]
        sigmoid = jax.nn.sigmoid(gate_block)
        silu = gate_block * sigmoid
        d_gate_block = grad_hidden * up[at, :] * (sigmoid + silu * (1.0 - sigmoid))
        d_gate[at, :] = d_gate_block.astype(BF16)
        d_up[at, :] = (grad_hidden * silu).astype(BF16)
        term = mm(d_gate[at, :], w_gate[...].reshape(wide))
        return term + mm(d_up[at, :], w_up[...].reshape(wide))

    def send(step, _):
        i = last - step
        ex.push(i, product(i))

        @pl.when(step > 0)
        def _():
            ex.combine(i + 1)

        return 0

    lax.fori_loop(0, PIECES, send, 0)
    ex.combine(0)
    r.ready(r.mlp_in, r.hidden)
    g_gate, g_up, g_down = r.grads
    g_gate[...] = mm(d_gate[...], r.mlp_in[...], 0, 0).astype(BF16).reshape(g_gate.shape)
    g_up[...] = mm(d_up[...], r.mlp_in[...], 0, 0).astype(BF16).reshape(g_up.shape)
    g_down[...] = mm(r.hidden[...], upstream[...].reshape(rows, model), 0, 0).astype(BF16).reshape(g_down.shape)
    r.flush(*r.grads)
    beside.middle()
    r.ready(r.residual, r.packed, r.queries, r.keys, r.values, r.heads_out, r.norms)
    gain_grad, res_grad = r.gain_grad, r.res_grad
    gain_grad[...] = jnp.zeros_like(gain_grad)
    weights = r.packed[...].reshape(2 * model + 2 * LH, width)
    w_out = weights[model + 2 * LH :]

    def receive(i):
        part, gain_part = rms_back(r.residual[i], r.gain[...], ex.total(i))
        block = upstream[i, ex.team.core].astype(F32) + part
        r.d_residual[i] = block
        gain_grad[...] += gain_part
        ex.join(i, res_grad, block.astype(BF16))

    def attend(i):
        ex.join_copy(i, res_grad).wait_recv()
        at = slice(i * size, (i + 1) * size)
        block = res_grad[i].reshape(shape)
        total = None
        for j in range(model // width):
            columns = slice(j * width, (j + 1) * width)
            term = mm(block[:, columns], w_out[columns], 1, 1)
            total = term if total is None else total + term
        r.d_heads[at, :] = total.astype(BF16)
        attend_rows_back(
            i * size, r.queries, r.keys, r.values, r.heads_out, r.d_heads, r.norms,
            r.d_queries, r.key_total, r.value_total,
        )

    receive(last)
    for i in range(last, 0, -1):
        receive(i - 1)
        if i == 2:
            beside.late()
        attend(i)
    r.flush(r.d_residual)
    attend(0)
    ex.finish(res_grad, False)
    r.flush(res_grad, r.d_queries)
    r.d_keys[...] = (r.key_total[...] * HD**-0.5).astype(BF16)
    r.d_values[...] = r.value_total[...].astype(BF16)
    term = mm(r.d_keys[...], weights[model : model + LH], 1, 1)
    term = term + mm(r.d_values[...], weights[model + LH : model + 2 * LH], 1, 1)
    r.d_latents[...] = term.astype(BF16)
    r.flush(r.d_keys, r.d_values, r.d_latents)
    beside.finish()


def attend_in_back(shared, early, r):
    team, plane = Team(), Plane()
    opposite = {TEN: across_device()[TEN]}
    ex = Exchange(team, r.exchange)
    beside = BesideRun(r, plane, 0, shared)
    greet(team.partners() + beside.partners + ([opposite] if early else []))
    beside.start()
    rows, model = r.attn_in.shape
    width = r.d_queries.shape[1]
    r.ready(r.d_queries, r.d_latents, r.packed, r.w_latent)
    w_query = r.packed[...].reshape(2 * model + 2 * LH, width)[:model]

    def product(i):
        at = piece_rows(i, rows)
        return mm(r.d_queries[at, :], w_query, 1, 1) + mm(r.d_latents[at, :], r.w_latent[...], 1, 1)

    ex.send_all(product)
    r.ready(r.attn_in, r.latents, r.heads_out, r.d_keys, r.d_values, r.res_grad)
    half = model + LH
    grads = r.grads
    grads[0:model, :] = mm(r.attn_in[...], r.d_queries[...], 0, 0).astype(BF16)
    count, pieces = lax.axis_size(TEN), r.g_latent.shape[0]
    span = model // count
    depth = span // pieces
    stride = depth + GAIN_ROWS
    g_latent = mm(r.attn_in[...], r.d_latents[...], 0, 0).astype(BF16)
    for piece in range(pieces):
        for chip in range(count):
            start = chip * span + piece * depth
            r.g_latent[piece, chip * stride : chip * stride + depth, :] = g_latent[start : start + depth]
    grads[model:half, :] = mm(r.latents[...], r.d_keys[...], 0, 0).astype(BF16)
    grads[half : half + LH, :] = mm(r.latents[...], r.d_values[...], 0, 0).astype(BF16)
    g_out = mm(r.heads_out[...], r.res_grad[...].reshape(rows, model), 0, 0).astype(BF16)
    for j, block in enumerate(pack_columns(g_out, width)):
        start = half + LH + j * width
        grads[start : start + width, :] = block
    r.g_packed[0][...] = grads[:half].reshape(r.g_packed[0].shape)
    r.g_packed[1][...] = grads[half:].reshape(r.g_packed[1].shape)
    r.flush(*r.g_packed)
    beside.middle()
    r.ready(r.source, r.d_residual)
    r.gain_grad[...] = jnp.zeros_like(r.gain_grad)

    def receive(i):
        part, gain_part = rms_back(r.source[i, team.core].astype(F32), r.gain[...], ex.total(i))
        r.gain_grad[...] += gain_part
        ex.join(i, r.input_grad, (r.d_residual[i] + part).astype(BF16))

    def leave(i):
        ex.join_copy(i, r.input_grad).wait_recv()
        if early:
            copy = send_to(r.input_grad.at[i], r.grad_here.at[i], r.early_sems[0].at[i], r.early_sems[1].at[i], opposite)
            copies.append((jnp.logical_and(team.core == 0, team.place == owner(i)), copy))
            pl.when(copies[-1][0])(copy.start)

    copies = []
    receive(0)
    for i in range(1, PIECES):
        receive(i)
        leave(i - 1)
    leave(PIECES - 1)
    place = lax.broadcasted_iota(jnp.int32, (GAIN_ROWS, LH), 0)
    nothing = jnp.zeros((GAIN_ROWS, LH), F32)
    for chip in range(count):
        columns = slice(chip * span, (chip + 1) * span)
        rows_of = slice(chip * stride + depth, (chip + 1) * stride)
        gains = [grad[:, columns] for grad in (r.gain_grad, r.mlp_gain)]
        if span < LH:
            gains = [jnp.concatenate([part, jnp.zeros((1, LH - span), F32)], axis=1) for part in gains]
        gains = jnp.where(place == 0, gains[0], jnp.where(place == 1, gains[1], nothing))
        r.g_latent[0, rows_of, :] = gains.astype(BF16)
        for piece in range(1, pieces):
            r.g_latent[piece, rows_of, :] = nothing.astype(BF16)
    r.flush(r.g_latent)
    ex.finish(r.input_grad, False)
    r.flush(r.input_grad)
    beside.finish()
    for active, copy in copies:
        pl.when(active)(copy.wait)


class Part:
    def __init__(self, block):
        self.block = block.reshape((2,) + pieces_of(block[: block.shape[0] // 2]).shape)
        self.shape, self.dtype = self.block.shape[1:], block.dtype


def named_call(kernel, number, ins=(), lazy=(), far=(), outs=(), late=(), far_outs=(), scratch=()):
    groups = [dict(group) for group in (ins, lazy, far, outs, late, far_outs, scratch)]

    def listed(group):
        return [(k, v if isinstance(v, list) else [v], isinstance(v, list)) for k, v in group.items()]

    groups = [listed(group) for group in groups]
    ins, lazy, far, outs, late, far_outs, scratch = groups
    vmem, anywhere = pl.BlockSpec(memory_space=pltpu.VMEM), pl.BlockSpec(memory_space=pl.ANY)

    def flat(*parts):
        return [value for part in parts for _, values, _ in part for value in values]

    stages = [pltpu.VMEM(x.shape, x.dtype) for x in flat(lazy)] + [pltpu.VMEM(*x) for x in flat(late)]
    lazy_count, late_count = len(flat(lazy)), len(flat(late))

    def body(*refs):
        refs = list(refs)

        def take(count):
            taken, refs[:] = refs[:count], refs[count:]
            return taken

        named = {}

        def name(part, taken):
            for key, values, is_list in part:
                mine, taken = taken[: len(values)], taken[len(values) :]
                named[key] = mine if is_list else mine[0]

        name(ins, take(len(flat(ins))))
        lazy_refs = take(lazy_count)
        name(far, take(len(flat(far))))
        name(outs, take(len(flat(outs))))
        late_refs = take(late_count)
        name(far_outs, take(len(flat(far_outs))))
        lazy_held, late_held = take(lazy_count), take(late_count)
        in_sem, out_sem = take(1)[0], take(1)[0]
        name(lazy, lazy_held)
        name(late, late_held)
        name(scratch, take(len(flat(scratch))))
        sequence = lax.axis_index(TEN) // (lax.axis_size(TEN) // 2)
        parts = [isinstance(value, Part) for value in flat(lazy)]
        lazy_refs = [ref.at[sequence] if part else ref for ref, part in zip(lazy_refs, parts)]
        arrive = {
            id(held): pltpu.make_async_copy(ref, held, in_sem.at[k])
            for k, (ref, held) in enumerate(zip(lazy_refs, lazy_held))
        }
        leave = {
            id(held): pltpu.make_async_copy(held, ref, out_sem.at[k])
            for k, (ref, held) in enumerate(zip(late_refs, late_held))
        }
        for copy in arrive.values():
            copy.start()

        def ready(*buffers):
            for buffer in buffers:
                arrive[id(buffer)].wait()

        def flush(*buffers):
            for buffer in buffers:
                leave[id(buffer)].start()

        kernel(types.SimpleNamespace(ready=ready, flush=flush, **named))
        for copy in leave.values():
            copy.wait()

    results = pl.pallas_call(
        body,
        in_specs=[vmem] * len(flat(ins)) + [anywhere] * len(flat(lazy, far)),
        out_specs=[vmem] * len(flat(outs)) + [anywhere] * len(flat(late, far_outs)),
        out_shape=[jax.ShapeDtypeStruct(*x) for x in flat(outs, late, far_outs)],
        scratch_shapes=stages + [DMA((max(1, lazy_count),)), DMA((max(1, late_count),))] + flat(scratch),
        compiler_params=pltpu.CompilerParams(
            collective_id=number, has_side_effects=number is not None, vmem_limit_bytes=VMEM_LIMIT
        ),
        cost_estimate=pl.CostEstimate(flops=LINK_FLOPS, bytes_accessed=2**20, transcendentals=0),
    )(*[value.block if isinstance(value, Part) else value for value in flat(ins, lazy, far)])
    named, results = {}, list(results)
    for key, values, is_list in outs + late + far_outs:
        mine, results = results[: len(values)], results[len(values) :]
        named[key] = mine if is_list else mine[0]
    return types.SimpleNamespace(**named)


def forward_kernel(layer, r):
    team = Team()
    plane = Plane()
    core = lax.axis_index(SEC)
    holder = core == layer
    taker = jnp.logical_not(holder)
    across = across_device()
    ex_a, ex_b = Exchange(team, r.ex_a), Exchange(team, r.ex_b)
    greet(team.partners() + plane.partners() + ([across] if layer == 0 else []))
    rows, width = r.queries.shape
    model = r.w_latent.shape[0]
    size = rows // PIECES
    feeds = range(3)

    own_copies = [pltpu.make_async_copy(r.own_feed[k], r.feed[k], r.own_sem.at[k]) for k in feeds]
    for copy in own_copies:
        pl.when(holder)(copy.start)
    gathers = [
        Gather(
            plane, k, r.feed[k], r.gather_sent.at[k], r.gather_here.at[k], taker,
            r.pieces[k] if layer else None, r.piece_sem.at[k],
        )
        for k in feeds
    ]

    def cross(k, source, target):
        return send_to(source, target, r.cross_sent.at[k], r.cross_here.at[k], across)

    if layer == 0:
        come = [cross(1 + k, r.own_feed[k].at[plane.me], r.come[k]) for k in feeds]
        next_feed = [cross(5 + k, r.own_feed[k].at[plane.me], r.feed_next[k]) for k in feeds]
        mine = cross(0, r.own_packed.at[plane.me], r.packed.at[plane.me])
        small = [
            send_to(r.pass_latent, r.far_latent, r.small_sent.at[0], r.small_here.at[0], team.other),
            send_to(r.own_gains, r.far_gains, r.small_sent.at[1], r.small_here.at[1], team.other),
        ]
        next_packed = cross(4, r.own_packed.at[plane.me], r.packed_next.at[plane.me])
        depth = r.packed.shape[1] // 2
        halves = [slice(0, depth), slice(depth, 2 * depth)]
        packed_gathers, next_gathers = (
            [Gather(plane, k, whole, sent.at[k], here.at[k], rows=half) for k, half in enumerate(halves)]
            for whole, sent, here in (
                (r.packed, r.packed_sent, r.packed_here), (r.packed_next, r.next_sent, r.next_here)
            )
        )
        own_packed = [
            pltpu.make_async_copy(r.own_packed, target, r.own_sem.at[3]) for target in (r.packed, r.packed_next)
        ]
        pl.when(holder)(mine.start)
        pl.when(holder)(own_packed[0].start)
        pl.when(taker)(own_packed[1].start)
        for copy in small:
            copy.start()
        for copy in small:
            copy.wait()
    else:
        for gather in gathers:
            gather.start()

    def next_come(k):
        @pl.when(holder)
        def _():
            come[k - 1].wait_send()
            come[k].start()

    def take_come(k):
        @pl.when(taker)
        def _():
            come[k].wait_recv()
            r.feed[k][plane.me] = r.come[k][...]

        gathers[k].start()

    gains = jnp.where(holder, r.own_gains[...], r.far_gains[...])
    r.gains[...] = gains
    r.w_latent[...] = jnp.where(holder, r.own_latent[...], r.far_latent[...])
    r.flush(r.w_latent)
    r.ready(r.source)

    def norm(i):
        block = r.source[i].reshape(size, model).astype(F32)
        r.attn_in[piece_rows(i, rows), :] = (block * reciprocal_rms(block) * gains[0:1]).astype(BF16)

    if layer == 0:
        each_piece(norm)

        @pl.when(taker)
        def _():
            mine.wait_recv()
            for gather in packed_gathers:
                gather.start()
            for gather in packed_gathers:
                gather.middle()
            for gather in packed_gathers:
                gather.finish()

        @pl.when(holder)
        def _():
            own_packed[0].wait()
            mine.wait_send()
            come[0].start()

        r.flush(r.packed)
        take_come(0)
    else:
        r.ready(r.packed)
    weights = r.packed[...].reshape(2 * model + 2 * LH, width)

    def project(i):
        at = piece_rows(i, rows)
        block = r.attn_in[at, :]
        r.queries[at, :] = mm(block, weights[:model]).astype(BF16)
        latents = mm(block, r.w_latent[...]).astype(BF16)
        r.latents[at, :] = latents
        r.keys[at, :] = mm(latents, weights[model : model + LH]).astype(BF16)
        r.values[at, :] = mm(latents, weights[model + LH : model + 2 * LH]).astype(BF16)

    w_out = [
        weights[model + 2 * LH + start : model + 2 * LH + start + width] for start in range(0, model, width)
    ]
    for i in range(PIECES):
        if layer == 1:
            norm(i)
        project(i)
        attend_rows(i * size, r.queries, r.keys, r.values, r.heads_out, r.norms)
        heads = r.heads_out[i * size : (i + 1) * size, :]
        ex_a.push(i, jnp.concatenate([mm(heads, block) for block in w_out], axis=1))
        if i == 0 and layer == 0:
            next_come(1)
        if i:
            ex_a.combine(i - 1)
        if i == 1:
            gathers[0].middle()
        if i == 2 and layer == 0:
            next_come(2)
            take_come(1)
    ex_a.combine(PIECES - 1)
    r.flush(r.attn_in, r.queries, r.latents, r.keys, r.values, r.heads_out, r.norms)
    if layer == 0:

        @pl.when(taker)
        def _():
            next_packed.start()


    def receive(i):
        block = r.source[i, core].astype(F32) + ex_a.total(i)
        r.residual[i] = block
        ex_a.join(i, r.mlp_in, (block * reciprocal_rms(block) * gains[1:2]).astype(BF16))

    def feed(i):
        ex_a.join_copy(i, r.mlp_in).wait_recv()
        at = piece_rows(i, rows)
        block = r.mlp_in[i].reshape(size, model)
        shape = (r.hidden.shape[1], model)
        gate = mm(block, r.feed[0][...].reshape(shape), 1, 1)
        up = mm(block, r.feed[1][...].reshape(shape), 1, 1)
        hidden = (jax.nn.silu(gate) * up).astype(BF16)
        r.gate[at, :] = gate
        r.up[at, :] = up
        r.hidden[at, :] = hidden
        ex_b.push(i, mm(hidden, r.feed[2][...].reshape(shape)))

    receive(0)
    gathers[1].middle()
    if layer == 0:
        take_come(2)
    receive(1)
    gathers[2].middle()

    @pl.when(holder)
    def _():
        for copy in own_copies:
            copy.wait()

    for gather in gathers:
        gather.finish()
    r.flush(*r.feed)
    if layer == 0:

        @pl.when(taker)
        def _():
            for copy in next_feed:
                copy.start()

    feed(0)
    if layer == 0:

        @pl.when(holder)
        def _():
            next_packed.wait_recv()
            for gather in next_gathers:
                gather.start()

    def steady(i, _):
        receive(i)
        feed(i - 1)
        ex_b.combine(i - 2)
        return 0

    lax.fori_loop(2, PIECES, steady, 0)
    feed(PIECES - 1)
    ex_b.combine(PIECES - 2)
    ex_b.combine(PIECES - 1)
    ex_a.finish(r.mlp_in, False)
    r.flush(r.residual, r.mlp_in, r.gate, r.up, r.hidden)
    if layer == 0:

        @pl.when(holder)
        def _():
            for gather in next_gathers:
                gather.middle()
            for gather in next_gathers:
                gather.finish()

        @pl.when(taker)
        def _():
            own_packed[1].wait()
            next_packed.wait_send()

        r.flush(r.packed_next)
    each_piece(lambda i: ex_b.join(i, r.output, (r.residual[i] + ex_b.total(i)).astype(BF16)))
    ex_b.finish(r.output)
    r.flush(r.output)

    if layer == 0:

        @pl.when(holder)
        def _():
            come[2].wait_send()
            for copy in next_feed:
                copy.wait_recv()

        @pl.when(taker)
        def _():
            for copy in next_feed:
                copy.wait_send()


def finish_kernel(groups, r):
    plane = Plane()
    team = Team()
    late = len(r.late)
    scatters = [Scatter(plane, k, r.late[k], *r.scatter[5 * k : 5 * k + 5]) for k in range(late)]
    count = lax.axis_size(TEN)
    z = lax.axis_index(TEN)
    core = lax.axis_index(SEC)
    first, second = core == 0, core == 1
    across = across_device()
    opposite = {TEN: across[TEN]}
    chips = [lax.rem(z + step, count) for step in range(1, count)]
    greet(plane.partners() + [across] + [{TEN: chip} for chip in chips])
    for scatter in scatters:
        scatter.start()
    sources = r.pieces + r.leave
    cross_sent, cross_here = r.cross_sems
    crosses = [
        send_to(source, r.come[k], cross_sent.at[k], cross_here.at[k], across) for k, source in enumerate(sources)
    ]

    pl.when(second)(crosses[0].start)

    def next_cross(k):
        @pl.when(second)
        def _():
            crosses[k - 1].wait_send()
            crosses[k].start()

    outputs = Outputs(r, [[], [0, 1]])
    outputs.start()
    gather_sent, gather_here, gather_own = r.gather_sems
    gathers = [
        Gather(
            plane, k, whole, gather_sent.at[k], gather_here.at[k], first if k < FEED else None,
            r.total[k], gather_own.at[k],
        )
        for k, whole in enumerate(r.wholes)
    ]
    last = FEED + late - 1

    def arrive(k):
        crosses[k].wait_recv()
        return (sources[k][...].astype(F32) + r.come[k][...].astype(F32)).astype(BF16)

    def take_cross(k):
        @pl.when(first)
        def _():
            r.total[k][...] = arrive(k)

        gathers[k].start()

    scatters[0].middle()
    next_cross(1)
    take_cross(0)
    for scatter in scatters[1:]:
        scatter.middle()
    for k, scatter in enumerate(scatters):
        r.leave[k][...] = scatter.total().astype(BF16)
        if k == 0:
            next_cross(2)
            gathers[0].middle()
        pl.when(second)(crosses[FEED + k].start)
    take_cross(1)
    take_cross(2)
    gathers[1].middle()
    gathers[2].middle()

    @pl.when(first)
    def _():
        for k in range(FEED, last):
            r.total[k][...] = arrive(k)
        r.held[...] = arrive(last).reshape(r.held.shape)

    @pl.when(second)
    def _():
        for k in range(FEED, last):
            r.total[k][...] = r.done[k - FEED][...]
        r.held[...] = r.done[late - 1][...].reshape(r.held.shape)

    for k in range(FEED, last):
        gathers[k].start()
    block_sent, block_here = r.block_sems

    def block(step, chip, slot):
        return send_to(r.held.at[chip], r.slots.at[slot], block_sent.at[step], block_here.at[slot], {TEN: chip})

    for step, chip in enumerate(chips):
        block(step, chip, z).start()
    r.slots[z] = r.held[z]
    for step, chip in enumerate(chips):
        block(step, chip, chip).wait_recv()
    shares = [r.slots[shard].astype(F32) for shard in range(count)]
    sums = [sum(s for s, g in zip(shares, groups) if g == group) for group in range(KVH)]
    gain_rows = sums[0]
    for extra in sums[1:]:
        gain_rows = gain_rows + extra
    depth = gain_rows.shape[0] - GAIN_ROWS
    gain_rows = gain_rows * (2.0 / count)
    blocks = [jnp.concatenate([part[:depth], gain_rows[depth:]], axis=0) for part in sums]
    r.total[last][...] = jnp.concatenate(blocks, axis=1).astype(BF16)
    gathers[last].start()
    for k in range(FEED, last + 1):
        gathers[k].middle()

    for gather in gathers:
        gather.finish()
    for scatter in scatters:
        scatter.drain()
    for step, chip in enumerate(chips):
        block(step, chip, z).wait_send()

    @pl.when(second)
    def _():
        for copy in crosses[2:]:
            copy.wait_send()

    outputs.finish()


def finish(number, groups, feed, late, done, grads):
    dp, count = lax.axis_size(DP), lax.axis_size(TEN)
    depth = done[-1].shape[0] // count
    shapes = [part.shape for part in list(feed) + list(done)]
    totals = shapes[:-1] + [(depth, KVH * LH)]
    items = len(shapes)
    blocks = pltpu.VMEM((count, depth, LH), BF16)
    return named_call(
        functools.partial(finish_kernel, groups),
        number,
        ins=dict(pieces=list(feed), done=list(done)),
        far=dict(late=list(late), shares=[], spreads=grads),
        far_outs=dict(wholes=[((dp,) + total, BF16) for total in totals], spreads_here=[(grad.shape, BF16) for grad in grads]),
        scratch=dict(
            scatter=[item for load in late for item in scatter_scratch(load)],
            come=[pltpu.VMEM(shape, BF16) for shape in shapes],
            leave=[pltpu.VMEM(part.shape, BF16) for part in done],
            total=[pltpu.VMEM(total, BF16) for total in totals],
            slots=blocks,
            held=blocks,
            cross_sems=[DMA((items,)), DMA((items,))],
            gather_sems=[DMA((items, 3)), DMA((items, dp)), DMA((items,))],
            block_sems=[DMA((count,)), DMA((count,))],
            spread_sems=[DMA((count // 2, PIECES)), DMA((PIECES,))] * len(grads),
        ),
    )


def emit_kernel(r):
    core = lax.axis_index(SEC)
    sequence = lax.axis_index(TEN) // (lax.axis_size(TEN) // 2)
    placed = []
    place = lax.rem(lax.axis_index(TEN), lax.axis_size(TEN) // 2)
    for k, (mine, share, spread, out) in enumerate(
        ((r.outs, r.outs_share, r.outs_spread, r.layer_out), (r.grads, r.grads_share, r.grads_spread, r.input_grad))
    ):
        for piece in range(PIECES):
            passed = place == owner(piece)
            for side, to in enumerate((sequence, 1 - sequence)):
                at = (2 * k + side, piece)
                held = r.held.at[at]
                for layer in range(2):
                    sources = [(mine, True)] if side == 0 else [(share, passed), (spread, jnp.logical_not(passed))]
                    for blocks, active in sources:
                        come = pltpu.make_async_copy(blocks[layer].at[piece], held, r.held_here.at[at])
                        pl.when(jnp.logical_and(core == layer, active))(come.start)
                placed.append((come, pltpu.make_async_copy(held, out.at[to, piece], r.placed.at[at])))
    wide = []
    for k in range(FEED):
        for layer, source in enumerate((r.zero[k], r.one[k])):
            copy = pltpu.make_async_copy(source, r.wide[k], r.wide_here.at[k])
            pl.when(core == layer)(copy.start)
            if layer == 0:
                wide.append(copy)
    for come, leave in placed:
        come.wait()
        leave.start()
    r.ready(r.low, r.high, r.latent)
    model = r.g_query.shape[0]
    columns = r.g_query.shape[1]
    low = r.low[...].reshape(-1, columns).astype(F32)
    high = r.high[...].reshape(-1, columns).astype(F32)
    r.g_query[...] = low[:model]
    r.g_key_up[...] = low[model:]
    r.g_value_up[...] = high[:LH]
    r.g_out[...] = jnp.concatenate(
        [high[start : start + columns] for start in range(LH, LH + model, columns)], axis=1
    )
    depth = r.latent.shape[1] - GAIN_ROWS
    r.g_latent[...] = r.latent[:, :depth, :].astype(F32).reshape(r.g_latent.shape)
    r.gains[...] = r.latent[0, depth:, :LH].astype(F32)
    r.flush(r.g_query, r.g_key_up, r.g_value_up, r.g_out, r.g_latent, r.gains)
    for k in range(FEED):
        wide[k].wait()
        r.g_wide[k][...] = r.wide[k][...].reshape(r.g_wide[k].shape).astype(F32)
        r.flush(r.g_wide[k])
    for come, leave in placed:
        leave.wait()


def emit(outs, outs_share, outs_spread, grads, grads_share, grads_spread, zero, one, parts):
    low, high, latent = parts
    pieces, depth, model = zero[0].shape
    columns = low.shape[2]
    split = pieces * (latent.shape[1] - GAIN_ROWS)
    both = ((2,) + outs[0].shape, BF16)
    out = named_call(
        emit_kernel,
        None,
        lazy=dict(low=low, high=high, latent=latent),
        far=dict(
            outs=outs, outs_share=outs_share, outs_spread=outs_spread,
            grads=grads, grads_share=grads_share, grads_spread=grads_spread,
            zero=zero, one=one,
        ),
        late=dict(
            g_query=((model, columns), F32),
            g_key_up=((LH, columns), F32),
            g_value_up=((LH, columns), F32),
            g_out=((columns, model), F32),
            g_latent=((split, KVH * LH), F32),
            gains=((GAIN_ROWS, LH), F32),
            g_wide=[((pieces * depth, model), F32)] * FEED,
        ),
        far_outs=dict(layer_out=both, input_grad=both),
        scratch=dict(
            placed=DMA((4, PIECES)),
            held_here=DMA((4, PIECES)),
            held=pltpu.VMEM((4,) + outs[0].shape, BF16),
            wide_here=DMA((FEED,)),
            wide=[pltpu.VMEM((pieces, depth, model), BF16)] * FEED,
        ),
    )
    wide = [part for part in out.g_wide]
    rest = (out.g_query, out.g_key_up, out.g_value_up, out.g_out, out.g_latent, out.gains)
    return (out.layer_out, out.input_grad, *wide, *rest)


def pieces_of(block):
    if isinstance(block, Part) or len(block.shape) == 4:
        return block
    return block.reshape(PIECES, 2, block.shape[0] // PIECES // 2, block.shape[1])


def shapes_of(rows, model):
    return (PIECES, 2, rows // PIECES // 2, model), (PIECES, rows // PIECES // 2, model)


def forward_layer(layer, number, source, own_feed, own_packed=None, packed=None, pieces_in=(), **small):
    rows, model = LEN, own_feed[0].shape[2]
    split, own = shapes_of(rows, model)
    pieces, depth, width = (packed if own_packed is None else own_packed).shape
    wide = (rows, pieces * own_feed[0].shape[1])
    pair = min(2 * HD, width)
    narrow = ((rows, width), BF16)
    outs = dict(gains=((2, model), F32))
    late = dict(
        w_latent=((model, LH), BF16),
        attn_in=((rows, model), BF16),
        queries=narrow,
        latents=((rows, LH), BF16),
        keys=narrow,
        values=narrow,
        heads_out=narrow,
        norms=((width // pair, pair // HD, rows), F32),
        residual=(own, F32),
        mlp_in=(split, BF16),
        gate=(wide, F32),
        up=(wide, F32),
        hidden=(wide, BF16),
        output=(split, BF16),
        feed=[(w.shape, BF16) for w in own_feed],
    )
    scratch = dict(
        ex_a=exchange_scratch(rows, model),
        ex_b=exchange_scratch(rows, model),
        own_sem=DMA((4,)),
        piece_sem=DMA((3,)),
        gather_sent=DMA((3, 3)),
        gather_here=DMA((3, pieces)),
        cross_sent=DMA((8,)),
        cross_here=DMA((8,)),
    )
    far_outs = dict()
    lazy, far = dict(source=pieces_of(source)), dict(own_feed=own_feed)
    if layer == 0:
        far.update(own_packed=own_packed)
        far_outs.update(feed_next=[(w.shape[1:], BF16) for w in own_feed])
        outs.update(far_latent=((model, LH), BF16), far_gains=((2, model), F32))
        late.update(packed=((pieces, depth, width), BF16), packed_next=((pieces, depth, width), BF16))
        scratch.update(
            come=[pltpu.VMEM(w.shape[1:], BF16) for w in own_feed],
            small_sent=DMA((2,)),
            small_here=DMA((2,)),
            packed_sent=DMA((2, 3)),
            packed_here=DMA((2, pieces)),
            next_sent=DMA((2, 3)),
            next_here=DMA((2, pieces)),
        )
    else:
        lazy.update(packed=packed)
        small.update(pieces=list(pieces_in))
    return named_call(
        functools.partial(forward_kernel, layer),
        number,
        ins=small,
        lazy=lazy,
        far=far,
        outs=outs,
        late=late,
        far_outs=far_outs,
        scratch=scratch,
    )


def feed_layer_back(number, upstream, result, beside):
    rows, model = result.attn_in.shape
    split, half = shapes_of(rows, model)
    columns = result.queries.shape[1]
    wide = pltpu.VMEM(result.hidden.shape, BF16)
    narrow = ((rows, columns), BF16)
    total = pltpu.VMEM((rows, columns), F32)
    return named_call(
        functools.partial(feed_back, beside.shared),
        number,
        ins=dict(gain=result.gains[1:2]),
        lazy=dict(
            upstream=pieces_of(upstream),
            feed=result.feed,
            gate=result.gate,
            up=result.up,
            mlp_in=result.mlp_in.reshape(rows, model),
            hidden=result.hidden,
            residual=result.residual,
            packed=result.packed,
            queries=result.queries,
            keys=result.keys,
            values=result.values,
            heads_out=result.heads_out,
            norms=result.norms,
        ),
        far=beside.far,
        outs=dict(gain_grad=((1, model), F32), **beside.outs),
        late=dict(
            d_residual=(half, F32),
            res_grad=(split, BF16),
            grads=[(w.shape, BF16) for w in result.feed],
            d_queries=narrow,
            d_keys=narrow,
            d_values=narrow,
            d_latents=((rows, LH), BF16),
        ),
        far_outs=beside.far_outs,
        scratch=dict(
            exchange=exchange_scratch(rows, model),
            d_gate=wide,
            d_up=wide,
            d_heads=pltpu.VMEM((rows, columns), BF16),
            key_total=total,
            value_total=total,
            **beside.scratch,
        ),
    )


def attend_layer_back(number, source, result, back, beside, early=False):
    rows, model = result.attn_in.shape
    pieces, depth, width = result.packed.shape
    out = named_call(
        functools.partial(attend_in_back, beside.shared, early),
        number,
        ins=dict(gain=result.gains[0:1], mlp_gain=back.gain_grad),
        lazy=dict(
            d_queries=back.d_queries,
            d_latents=back.d_latents,
            packed=result.packed,
            w_latent=result.w_latent,
            attn_in=result.attn_in,
            latents=result.latents,
            heads_out=result.heads_out,
            d_keys=back.d_keys,
            d_values=back.d_values,
            res_grad=back.res_grad,
            source=pieces_of(source),
            d_residual=back.d_residual,
        ),
        far=beside.far,
        outs=beside.outs,
        late=dict(
            input_grad=(shapes_of(rows, model)[0], BF16),
            g_packed=[((pieces, depth // 2, width), BF16)] * 2,
            g_latent=((pieces, model // pieces + lax.axis_size(TEN) * GAIN_ROWS, LH), BF16),
        ),
        far_outs=dict(grad_here=(shapes_of(rows, model)[0], BF16), **beside.far_outs) if early else beside.far_outs,
        scratch=dict(
            exchange=exchange_scratch(rows, model),
            grads=pltpu.VMEM((pieces * depth, width), BF16),
            gain_grad=pltpu.VMEM((1, model), F32),
            early_sems=[DMA((PIECES,)), DMA((PIECES,))],
            **beside.scratch,
        ),
    )
    out.parts = out.g_packed + [out.g_latent]
    return out


def tie(*arrays):
    return lax.optimization_barrier(arrays)


def local(
    inputs,
    out_grad,
    w_query,
    w_latent,
    w_key_up,
    w_value_up,
    w_out,
    w_gate,
    w_up,
    w_down,
    norm_attn,
    norm_mlp,
):
    at = Place()
    model = inputs.shape[1]
    heads = w_query.shape[2] // HD

    def group_of(shard):
        return shard * heads // (QH // KVH)

    opposite_z = (at.z + at.team) % at.count

    def latent_of(shard):
        return lax.dynamic_slice_in_dim(w_latent[0], group_of(shard) * LH, LH, 1)

    own_feed = [by_dp(w) for w in (w_gate[0].T, w_up[0].T, w_down[0])]
    own_packed = by_dp(pack_attention(w_query[0], w_key_up[0], w_value_up[0], w_out[0]))
    own_gains = jnp.concatenate([norm_attn, norm_mlp], axis=0)
    own_latent = latent_of(at.z)
    source = Part(inputs)
    zero = forward_layer(
        0,
        0,
        source,
        own_feed,
        own_packed=own_packed,
        own_gains=own_gains,
        own_latent=own_latent,
        pass_latent=latent_of(opposite_z),
    )
    first_out = zero.output
    one = forward_layer(
        1,
        1,
        first_out,
        own_feed,
        packed=zero.packed_next,
        pieces_in=zero.feed_next,
        own_gains=own_gains,
        far_gains=zero.far_gains,
        own_latent=own_latent,
        far_latent=zero.far_latent,
    )
    one.packed = zero.packed_next
    second_out = one.output

    back = feed_layer_back(2, Part(out_grad), one, Beside(shares=[(first_out, 0)]))
    first_share = back.shares_here[0]
    beside = Beside(back.grads, shares=[(second_out, 1)], spreads=[(first_share, 0)])
    above = attend_layer_back(3, first_out, one, back, beside)
    second_share, second_grad, first_spread = above.shares_here[0], above.input_grad, above.spreads_here[0]
    beside = Beside(above.parts, above.sums, True, spreads=[(second_share, 1)])
    back = feed_layer_back(4, second_grad, zero, beside)
    wide_one, second_spread = back.wholes, back.spreads_here[0]
    beside = Beside(back.grads, back.sums, shares=[(second_grad, 1)])
    below = attend_layer_back(5, source, zero, back, beside, True)
    first_grad, grad_share = below.input_grad, below.shares_here[0]
    groups = tuple(group_of(shard) for shard in range(at.count))
    last = finish(6, groups, below.sums, below.parts, below.totals, [below.grad_here, grad_share])
    *wide_zero, low_part, high_part, latent = last.wholes
    out = emit(
        [first_out, second_out],
        [first_share, second_share],
        [first_spread, second_spread],
        [first_grad, second_grad],
        [below.grad_here, grad_share],
        last.spreads_here,
        wide_zero,
        wide_one,
        [low_part, high_part, latent],
    )
    layer_out, input_grad, g_gate, g_up, g_down, g_query, g_key_up, g_value_up, g_out, g_latent, gains = out
    gains = gains[:, : model // at.count]
    layer_out, input_grad = (both.reshape(1, 2 * LEN, model) for both in (layer_out, input_grad))
    return (
        layer_out,
        input_grad,
        g_query[None],
        g_latent[None],
        g_key_up[None],
        g_value_up[None],
        g_out[None],
        g_gate.T[None],
        g_up.T[None],
        g_down[None],
        gains[0:1],
        gains[1:2],
    )


def solution(mesh):
    columns = P(SEC, None, TEN)
    rows = P(SEC, TEN, None)
    return jax.shard_map(
        local,
        mesh=mesh,
        in_specs=(
            P(DP, None),
            P(DP, None),
            columns,
            P(SEC, None, None),
            columns,
            columns,
            rows,
            columns,
            columns,
            rows,
            P(SEC, None),
            P(SEC, None),
        ),
        out_specs=(
            P(SEC, DP, None),
            P(SEC, DP, None),
            columns,
            rows,
            columns,
            columns,
            rows,
            columns,
            columns,
            rows,
            P(SEC, TEN),
            P(SEC, TEN),
        ),
        check_vma=False,
    )
```

```python
import functools
import math
import types

import jax
import jax.numpy as jnp
from jax import lax
from jax.experimental import pallas as pl
from jax.experimental.pallas import tpu as pltpu
from jax.sharding import PartitionSpec as P

QH = 16
HD = 64
KVH = 2
LH = 256
LEN = 1024
EPS = 1e-05
F32 = jnp.float32
BF16 = jnp.bfloat16
SEC, DP, TEN = "section", "dp", "tensor"
LOG2_SCALE = HD**-0.5 * math.log2(math.e)
KEY_ROWS = 256


def mm(left, right, left_dim=1, right_dim=0):
    dims = (((left_dim,), (right_dim,)), ((), ()))
    return lax.dot_general(left, right, dims, preferred_element_type=F32)


def head_masks(width):
    if width == HD:
        return [None]
    lane = lax.broadcasted_iota(jnp.int32, (1, width), 1)
    return [lane // HD == j for j in range(width // HD)]


def keep_head(block, mask):
    return block if mask is None else jnp.where(mask, block, jnp.zeros_like(block))


def attend_rows(start, q_ref, k_ref, v_ref, o_ref, norm_ref):
    columns = q_ref.shape[1]
    width = min(2 * HD, columns)
    masks = head_masks(width)
    rows = KEY_ROWS
    place_k = lax.broadcasted_iota(jnp.int32, (rows, rows), 0)
    place_q = lax.broadcasted_iota(jnp.int32, (rows, rows), 1)
    for pair in range(columns // width):
        lanes = slice(pair * width, (pair + 1) * width)
        query = q_ref[start : start + rows, lanes]
        total = None
        for j, mask in enumerate(masks):
            query_j = keep_head(query, mask)
            scores = mm(k_ref[start : start + rows, lanes], query_j, 1, 1) * LOG2_SCALE
            scores = jnp.where(place_k <= place_q, scores, -jnp.inf)
            largest = jnp.max(scores, axis=0, keepdims=True)
            if start:
                before = mm(k_ref[0:start, lanes], query_j, 1, 1) * LOG2_SCALE
                largest = jnp.maximum(largest, jnp.max(before, axis=0, keepdims=True))
            weight = jnp.exp2(scores - largest)
            norm = jnp.sum(weight, axis=0, keepdims=True)
            value = keep_head(v_ref[start : start + rows, lanes], mask)
            out = mm(value, weight.astype(BF16), 0, 0)
            if start:
                weight = jnp.exp2(before - largest)
                norm = norm + jnp.sum(weight, axis=0, keepdims=True)
                value = keep_head(v_ref[0:start, lanes], mask)
                out = out + mm(value, weight.astype(BF16), 0, 0)
            out = out / norm
            total = out if total is None else total + out
            norm_ref[pair, j : j + 1, start : start + rows] = largest + jnp.log2(norm)
        o_ref[start : start + rows, lanes] = total.T.astype(BF16)


def attend_rows_back(start, q_ref, k_ref, v_ref, o_ref, g_ref, norm_ref, dq_ref, key_total, value_total):
    columns = q_ref.shape[1]
    width = min(2 * HD, columns)
    masks = head_masks(width)
    rows = KEY_ROWS
    end = start + rows
    place_k = lax.broadcasted_iota(jnp.int32, (rows, rows), 0)
    place_q = lax.broadcasted_iota(jnp.int32, (rows, rows), 1)
    for pair in range(columns // width):
        lanes = slice(pair * width, (pair + 1) * width)
        query, grad = q_ref[start:end, lanes], g_ref[start:end, lanes]
        key, value = k_ref[0:end, lanes], v_ref[0:end, lanes]
        product = (grad.astype(F32) * o_ref[start:end, lanes].astype(F32)).T
        grad_query = grad_key = grad_value = None
        for j, mask in enumerate(masks):
            query_j = keep_head(query, mask)
            grad_j = keep_head(grad, mask)
            delta = jnp.sum(product[j * HD : (j + 1) * HD, :], axis=0, keepdims=True)
            scores = mm(key, query_j, 1, 1) * LOG2_SCALE
            probs = jnp.exp2(scores - norm_ref[pair, j : j + 1, start:end])
            last = jnp.where(place_k <= place_q, probs[start:], 0.0)
            probs = jnp.concatenate([probs[:start], last], axis=0) if start else last
            grad_probs = mm(value, grad_j, 1, 1)
            grad_scores = (probs * (grad_probs - delta)).astype(BF16)
            value_term = mm(probs.astype(BF16), grad_j)
            key_term = mm(grad_scores, query_j)
            query_term = mm(keep_head(key, mask), grad_scores, 0, 0)
            grad_key = key_term if grad_key is None else grad_key + key_term
            grad_value = value_term if grad_value is None else grad_value + value_term
            grad_query = query_term if grad_query is None else grad_query + query_term
        dq_ref[start:end, lanes] = (grad_query.T * HD**-0.5).astype(BF16)
        if end == LEN:
            key_total[:, lanes] = grad_key
            value_total[:, lanes] = grad_value
        else:
            key_total[0:end, lanes] += grad_key
            value_total[0:end, lanes] += grad_value


def rms_scale(features):
    return features * lax.rsqrt(jnp.mean(features * features, axis=-1, keepdims=True) + EPS)


class Place:
    def __init__(self):
        self.count = lax.axis_size(TEN)
        self.team = self.count // 2
        self.z = lax.axis_index(TEN)
        self.core = lax.axis_index(SEC)
        self.dp = lax.axis_index(DP)
        self.sequence = self.z // self.team
        self.first = self.core == 0

    def opposite(self, block, cores=(0, 1)):
        n, t = self.count, self.team
        route = [(core * n + z, core * n + (z + t) % n) for core in cores for z in range(n)]
        return lax.ppermute(block, (SEC, TEN), route)

    def across(self, block, core):
        n, t = self.count, self.team
        route = [(core * n + z, (1 - core) * n + (z + t) % n) for z in range(n)]
        return lax.ppermute(block, (SEC, TEN), route)


def pack_columns(matrix, width):
    return [matrix[:, i : i + width] for i in range(0, matrix.shape[1], width)]


def pack_attention(query, key_up, value_up, out):
    width = query.shape[1]
    return jnp.concatenate([query, key_up, value_up] + pack_columns(out, width), axis=0)


def by_dp(matrix):
    count = lax.axis_size(DP)
    return matrix.reshape(count, matrix.shape[0] // count, matrix.shape[1])


def whole_of(pieces):
    return pieces.reshape(-1, pieces.shape[2])


MESH = pl.DeviceIdType.MESH
PIECES = 4
VMEM_LIMIT = 58 * 2**20
LINK_FLOPS = 4 * 10**9
GAIN_ROWS = 16
FEED = 3
DMA = pltpu.SemaphoreType.DMA


def reciprocal_rms(features):
    return lax.rsqrt(jnp.mean(features * features, axis=-1, keepdims=True) + EPS)


def send_to(source, target, sent, here, device):
    return pltpu.make_async_remote_copy(
        src_ref=source,
        dst_ref=target,
        send_sem=sent,
        recv_sem=here,
        device_id=device,
        device_id_type=MESH,
    )


def greet(partners):
    barrier = pltpu.get_barrier_semaphore()
    for partner in partners:
        pl.semaphore_signal(barrier, inc=1, device_id=partner, device_id_type=MESH)
    pl.semaphore_wait(barrier, len(partners))


class Team:
    def __init__(self):
        count = lax.axis_size(TEN)
        self.size = count // 2
        self.core = lax.axis_index(SEC)
        z = lax.axis_index(TEN)
        self.place = lax.rem(z, self.size)
        self.base = z - self.place
        self.other = {SEC: 1 - self.core}

    def peer(self, step):
        place = lax.rem(self.place + step, self.size)
        return place, {TEN: self.base + place}

    def partners(self):
        return [self.other] + [self.peer(step)[1] for step in range(1, self.size)]


class Plane:
    def __init__(self):
        me = lax.axis_index(DP)
        self.me = me
        self.one = me + 1 - 2 * lax.rem(me, 2)
        self.two = lax.rem(me + 2, 4)
        self.both = lax.rem(self.one + 2, 4)

    def partners(self):
        return [{DP: self.one}, {DP: self.two}]

    def order(self, turn):
        return (self.one, self.two) if turn % 2 == 0 else (self.two, self.one)


def scatter_scratch(load):
    piece = load.shape[1:]
    return [pltpu.VMEM((3,) + piece, BF16), pltpu.VMEM((3,) + piece, BF16), DMA((3,)), DMA((3,)), DMA((2,))]


class Scatter:
    def __init__(self, plane, turn, load, slots, held, sent, here, local):
        near, far = plane.order(turn)
        self.slots, self.held = slots, held
        self.copies = [
            send_to(load.at[near], slots.at[0], sent.at[0], here.at[0], {DP: near}),
            send_to(load.at[plane.both], slots.at[1], sent.at[1], here.at[1], {DP: near}),
            send_to(held.at[2], slots.at[2], sent.at[2], here.at[2], {DP: far}),
        ]
        self.local = [
            pltpu.make_async_copy(load.at[plane.me], held.at[0], local.at[0]),
            pltpu.make_async_copy(load.at[far], held.at[1], local.at[1]),
        ]

    def start(self):
        self.copies[1].start()
        self.copies[0].start()
        for copy in self.local:
            copy.start()

    def middle(self):
        self.local[1].wait()
        self.copies[1].wait_recv()
        self.held[2] = (self.held[1].astype(F32) + self.slots[1].astype(F32)).astype(BF16)
        self.copies[2].start()

    def total(self):
        self.local[0].wait()
        self.copies[0].wait_recv()
        total = self.held[0].astype(F32) + self.slots[0].astype(F32)
        self.copies[2].wait_recv()
        return total + self.slots[2].astype(F32)

    def drain(self):
        for copy in self.copies:
            copy.wait_send()


class Gather:
    def __init__(self, plane, turn, whole, sent, here, active=None, piece=None, local=None, rows=slice(None)):
        self.active = active
        near, far = plane.order(turn)
        me = plane.me

        def part(place):
            return whole.at[place, rows]

        source = part(me) if piece is None else piece

        def copy(k, source, place, device):
            return send_to(source, part(place), sent.at[k], here.at[place], {DP: device})

        self.first = copy(0, source, me, near)
        self.second = [copy(1, source, me, far), copy(2, part(near), near, far)]
        self.coming = [copy(0, part(place), place, near) for place in (near, far, plane.both)]
        self.local = [] if piece is None else [pltpu.make_async_copy(piece, whole.at[me], local)]

    def when(self, body):
        if self.active is None:
            body()
        else:
            pl.when(self.active)(body)

    def start(self):
        def body():
            for copy in [self.first, self.second[0]] + self.local:
                copy.start()

        self.when(body)

    def middle(self):
        def body():
            self.coming[0].wait_recv()
            self.second[1].start()

        self.when(body)

    def finish(self):
        def body():
            self.coming[1].wait_recv()
            self.coming[2].wait_recv()
            for copy in [self.first] + self.second:
                copy.wait_send()
            for copy in self.local:
                copy.wait()

        self.when(body)


def across_device():
    count = lax.axis_size(TEN)
    opposite = lax.rem(lax.axis_index(TEN) + count // 2, count)
    return {SEC: 1 - lax.axis_index(SEC), TEN: opposite}


class Beside:
    def __init__(self, loads=(), crosses=(), gathered=False, shares=(), spreads=()):
        team = lax.axis_size(TEN) // 2
        self.shared = [[core for _, core in group] for group in (shares, spreads)]
        shares, spreads = ([block for block, _ in group] for group in (shares, spreads))
        self.far = dict(loads=list(loads), crosses=list(crosses), shares=shares, spreads=spreads)
        pieces = [cross.shape for cross in crosses]
        dp = lax.axis_size(DP)
        self.outs = dict(
            sums=[(load.shape[1:], BF16) for load in loads], totals=[(piece, BF16) for piece in pieces]
        )
        self.far_outs = dict(
            wholes=[((dp,) + piece, BF16) for piece in pieces] if gathered else [],
            shares_here=[(block.shape, BF16) for block in shares],
            spreads_here=[(block.shape, BF16) for block in spreads],
        )
        count = max(1, len(pieces))
        self.scratch = dict(
            scatter=[item for load in loads for item in scatter_scratch(load)],
            comes=[pltpu.VMEM(piece, BF16) for piece in pieces],
            cross_sems=[DMA((count,)), DMA((count,)), DMA((count,)), DMA((count,))],
            gather_sems=[DMA((count, 3)), DMA((count, dp))],
            share_sems=[DMA((PIECES,))] * (2 * len(shares)),
            spread_sems=[DMA((team, PIECES)), DMA((PIECES,))] * len(spreads),
        )


class BesideRun:
    def __init__(self, r, plane, sender, shared):
        self.outputs = Outputs(r, shared)
        self.totals, self.comes, self.sums = r.totals, r.comes, r.sums
        self.scatters = [
            Scatter(plane, k, load, *r.scatter[5 * k : 5 * k + 5]) for k, load in enumerate(r.loads)
        ]
        self.sends = lax.axis_index(SEC) == sender
        self.takes = jnp.logical_not(self.sends)
        across = across_device()
        sent, here, own, local = r.cross_sems
        self.copies = [
            send_to(cross, r.comes[k], sent.at[k], here.at[k], across) for k, cross in enumerate(r.crosses)
        ]
        self.own = [pltpu.make_async_copy(cross, r.totals[k], own.at[k]) for k, cross in enumerate(r.crosses)]
        self.gathers = [
            Gather(
                plane, k, whole, r.gather_sems[0].at[k], r.gather_sems[1].at[k], self.takes, r.totals[k], local.at[k]
            )
            for k, whole in enumerate(r.wholes)
        ]
        self.partners = (plane.partners() if self.scatters or self.gathers else []) + (
            [across] if self.copies else []
        )
        self.partners = self.partners + self.outputs.partners

    def start(self):
        self.outputs.start()
        for scatter in self.scatters:
            scatter.start()
        for copy, own in zip(self.copies, self.own):
            pl.when(self.sends)(copy.start)
            own.start()

    def add(self):
        for own in self.own:
            own.wait()

        @pl.when(self.takes)
        def _():
            for copy, come, total in zip(self.copies, self.comes, self.totals):
                copy.wait_recv()
                total[...] = (total[...].astype(F32) + come[...].astype(F32)).astype(BF16)

    def middle(self):
        for scatter in self.scatters:
            scatter.middle()
        if self.gathers:
            self.add()
            for gather in self.gathers:
                gather.start()

    def late(self):
        for gather in self.gathers:
            gather.middle()

    def finish(self):
        for scatter, total in zip(self.scatters, self.sums):
            total[...] = scatter.total().astype(BF16)
            scatter.drain()
        if self.copies and not self.gathers:
            self.add()
        for gather in self.gathers:
            gather.finish()
        for copy in self.copies:
            pl.when(self.sends)(copy.wait_send)
        self.outputs.finish()


def owner(piece):
    return piece * (lax.axis_size(TEN) // 2) // PIECES


class Outputs:
    def __init__(self, r, shared):
        team = Team()
        core = lax.axis_index(SEC)
        opposite = {TEN: across_device()[TEN]}
        self.partners = [opposite] if r.shares else []
        self.out, self.come = [], []
        for piece in range(PIECES):
            mine = team.place == owner(piece)
            for k, block in enumerate(r.shares):
                sent, here = r.share_sems[2 * k : 2 * k + 2]
                target = r.shares_here[k].at[piece]
                copy = send_to(block.at[piece], target, sent.at[piece], here.at[piece], opposite)
                active = jnp.logical_and(core == shared[0][k], mine)
                self.out.append((active, copy))
                self.come.append((active, copy))
            for k, block in enumerate(r.spreads):
                sent, here = r.spread_sems[2 * k : 2 * k + 2]
                for step in range(1, team.size):
                    copy = send_to(
                        block.at[piece], r.spreads_here[k].at[piece], sent.at[step, piece], here.at[piece],
                        team.peer(step)[1],
                    )
                    self.out.append((jnp.logical_and(core == shared[1][k], mine), copy))
                theirs = jnp.logical_and(core == shared[1][k], jnp.logical_not(mine))
                self.come.append((theirs, copy))

    def start(self):
        for active, copy in self.out:
            pl.when(active)(copy.start)

    def finish(self):
        for active, copy in self.out:
            pl.when(active)(copy.wait_send)
        for active, copy in self.come:
            pl.when(active)(copy.wait_recv)


def exchange_scratch(rows, model):
    team = lax.axis_size(TEN) // 2
    half = rows // PIECES // 2
    return [
        pltpu.VMEM((2, half, model), F32),
        pltpu.VMEM((2, half, model), F32),
        pltpu.VMEM((PIECES, half, model), BF16),
        pltpu.VMEM((PIECES, half, model), BF16),
        pltpu.VMEM((team, PIECES, half, model), BF16),
        DMA((PIECES,)),
        DMA((PIECES,)),
        DMA((team, PIECES)),
        DMA((team, PIECES)),
        DMA((PIECES,)),
        DMA((PIECES,)),
    ]


EXCHANGE = 11


class Exchange:
    def __init__(self, team, refs):
        self.team = team
        (self.part, self.keep, self.out, self.got, self.far) = refs[:5]
        (self.core_sent, self.core_here, self.far_sent, self.far_here) = refs[5:9]
        (self.join_sent, self.join_here) = refs[9:]

    def core_copy(self, i):
        return send_to(
            self.out.at[i], self.got.at[i], self.core_sent.at[i], self.core_here.at[i], self.team.other
        )

    def far_copy(self, i, step, place):
        at = self.far.at[place, i]
        return send_to(
            at, at, self.far_sent.at[step, i], self.far_here.at[place, i], self.team.peer(step)[1]
        )

    def join_copy(self, i, whole):
        at = whole.at[i, self.team.core]
        return send_to(at, at, self.join_sent.at[i], self.join_here.at[i], self.team.other)

    def push(self, i, product):
        core = self.team.core
        self.part[...] = product.reshape(self.part.shape)
        self.out[i] = self.part[1 - core].astype(BF16)
        self.core_copy(i).start()
        self.keep[i % 2] = self.part[core]

    def combine(self, i):
        self.core_copy(i).wait_recv()
        self.far[self.team.place, i] = (self.keep[i % 2] + self.got[i].astype(F32)).astype(BF16)
        for step in range(1, self.team.size):
            self.far_copy(i, step, self.team.place).start()

    def send_all(self, product):
        def send(i):
            self.push(i, product(i))

            @pl.when(i > 0)
            def _():
                self.combine(i - 1)

        each_piece(send)
        self.combine(PIECES - 1)

    def total(self, i):
        for step in range(1, self.team.size):
            self.far_copy(i, step, self.team.peer(step)[0]).wait_recv()
        total = self.far[0, i].astype(F32)
        for place in range(1, self.team.size):
            total = total + self.far[place, i].astype(F32)
        return total

    def join(self, i, whole, half):
        whole[i, self.team.core] = half
        self.join_copy(i, whole).start()

    def finish(self, whole, coming=True):
        def drain(i):
            self.core_copy(i).wait_send()
            for step in range(1, self.team.size):
                self.far_copy(i, step, self.team.place).wait_send()
            self.join_copy(i, whole).wait_send()
            if coming:
                self.join_copy(i, whole).wait_recv()

        each_piece(drain)


def each_piece(body):
    lax.fori_loop(0, PIECES, lambda i, _: (body(i), 0)[1], 0)


def piece_rows(i, rows):
    size = rows // PIECES
    return pl.ds(pl.multiple_of(i * size, size), size)


def rms_back(block, gain, upstream):
    inverse = reciprocal_rms(block)
    normed = block * inverse
    scaled = upstream * gain
    grad = inverse * (scaled - normed * jnp.mean(scaled * normed, axis=-1, keepdims=True))
    return grad, jnp.sum(upstream * normed, axis=0, keepdims=True)


def feed_back(shared, r):
    team, plane = Team(), Plane()
    ex = Exchange(team, r.exchange)
    beside = BesideRun(r, plane, 0, shared)
    greet(team.partners() + beside.partners)
    beside.start()
    rows, model = r.mlp_in.shape
    size = rows // PIECES
    shape = (size, model)
    wide = (r.d_gate.shape[1], model)
    width = r.queries.shape[1]
    last = PIECES - 1
    upstream, gate, up, d_gate, d_up = r.upstream, r.gate, r.up, r.d_gate, r.d_up
    w_gate, w_up, w_down = r.feed
    r.ready(upstream, gate, up, *r.feed)

    def product(i):
        at = piece_rows(i, rows)
        grad_hidden = mm(upstream[i].reshape(shape), w_down[...].reshape(wide), 1, 1)
        gate_block = gate[at, :]
        sigmoid = jax.nn.sigmoid(gate_block)
        silu = gate_block * sigmoid
        d_gate_block = grad_hidden * up[at, :] * (sigmoid + silu * (1.0 - sigmoid))
        d_gate[at, :] = d_gate_block.astype(BF16)
        d_up[at, :] = (grad_hidden * silu).astype(BF16)
        term = mm(d_gate[at, :], w_gate[...].reshape(wide))
        return term + mm(d_up[at, :], w_up[...].reshape(wide))

    def send(step, _):
        i = last - step
        ex.push(i, product(i))

        @pl.when(step > 0)
        def _():
            ex.combine(i + 1)

        return 0

    lax.fori_loop(0, PIECES, send, 0)
    ex.combine(0)
    r.ready(r.mlp_in, r.hidden)
    g_gate, g_up, g_down = r.grads
    g_gate[...] = mm(d_gate[...], r.mlp_in[...], 0, 0).astype(BF16).reshape(g_gate.shape)
    g_up[...] = mm(d_up[...], r.mlp_in[...], 0, 0).astype(BF16).reshape(g_up.shape)
    g_down[...] = mm(r.hidden[...], upstream[...].reshape(rows, model), 0, 0).astype(BF16).reshape(g_down.shape)
    r.flush(*r.grads)
    beside.middle()
    r.ready(r.residual, r.packed, r.queries, r.keys, r.values, r.heads_out, r.norms)
    gain_grad, res_grad = r.gain_grad, r.res_grad
    gain_grad[...] = jnp.zeros_like(gain_grad)
    weights = r.packed[...].reshape(2 * model + 2 * LH, width)
    w_out = weights[model + 2 * LH :]

    def receive(i):
        part, gain_part = rms_back(r.residual[i], r.gain[1:2, :], ex.total(i))
        block = upstream[i, ex.team.core].astype(F32) + part
        r.d_residual[i] = block
        gain_grad[...] += gain_part
        ex.join(i, res_grad, block.astype(BF16))

    def attend(i):
        ex.join_copy(i, res_grad).wait_recv()
        at = slice(i * size, (i + 1) * size)
        block = res_grad[i].reshape(shape)
        total = None
        for j in range(model // width):
            columns = slice(j * width, (j + 1) * width)
            term = mm(block[:, columns], w_out[columns], 1, 1)
            total = term if total is None else total + term
        r.d_heads[at, :] = total.astype(BF16)
        attend_rows_back(
            i * size, r.queries, r.keys, r.values, r.heads_out, r.d_heads, r.norms,
            r.d_queries, r.key_total, r.value_total,
        )

    receive(last)
    for i in range(last, 0, -1):
        receive(i - 1)
        if i == 2:
            beside.late()
        attend(i)
    r.flush(r.d_residual)
    attend(0)
    ex.finish(res_grad, False)
    r.flush(res_grad, r.d_queries)
    r.d_keys[...] = (r.key_total[...] * HD**-0.5).astype(BF16)
    r.d_values[...] = r.value_total[...].astype(BF16)
    term = mm(r.d_keys[...], weights[model : model + LH], 1, 1)
    term = term + mm(r.d_values[...], weights[model + LH : model + 2 * LH], 1, 1)
    r.d_latents[...] = term.astype(BF16)
    r.flush(r.d_keys, r.d_values, r.d_latents)
    beside.finish()


def attend_in_back(shared, early, r):
    team, plane = Team(), Plane()
    opposite = {TEN: across_device()[TEN]}
    ex = Exchange(team, r.exchange)
    beside = BesideRun(r, plane, 0, shared)
    greet(team.partners() + beside.partners + ([opposite] if early else []))
    beside.start()
    rows, model = r.attn_in.shape
    width = r.d_queries.shape[1]
    r.ready(r.d_queries, r.d_latents, r.packed, r.w_latent)
    w_query = r.packed[...].reshape(2 * model + 2 * LH, width)[:model]

    def product(i):
        at = piece_rows(i, rows)
        return mm(r.d_queries[at, :], w_query, 1, 1) + mm(r.d_latents[at, :], r.w_latent[...], 1, 1)

    ex.send_all(product)
    r.ready(r.attn_in, r.latents, r.heads_out, r.d_keys, r.d_values, r.res_grad)
    half = model + LH
    grads = r.grads
    grads[0:model, :] = mm(r.attn_in[...], r.d_queries[...], 0, 0).astype(BF16)
    count, pieces = lax.axis_size(TEN), r.g_latent.shape[0]
    span = model // count
    depth = span // pieces
    stride = depth + GAIN_ROWS
    g_latent = mm(r.attn_in[...], r.d_latents[...], 0, 0).astype(BF16)
    for piece in range(pieces):
        for chip in range(count):
            start = chip * span + piece * depth
            r.g_latent[piece, chip * stride : chip * stride + depth, :] = g_latent[start : start + depth]
    grads[model:half, :] = mm(r.latents[...], r.d_keys[...], 0, 0).astype(BF16)
    grads[half : half + LH, :] = mm(r.latents[...], r.d_values[...], 0, 0).astype(BF16)
    g_out = mm(r.heads_out[...], r.res_grad[...].reshape(rows, model), 0, 0).astype(BF16)
    for j, block in enumerate(pack_columns(g_out, width)):
        start = half + LH + j * width
        grads[start : start + width, :] = block
    r.g_packed[0][...] = grads[:half].reshape(r.g_packed[0].shape)
    r.g_packed[1][...] = grads[half:].reshape(r.g_packed[1].shape)
    r.flush(*r.g_packed)
    beside.middle()
    r.ready(r.source, r.d_residual)
    r.gain_grad[...] = jnp.zeros_like(r.gain_grad)

    def receive(i):
        part, gain_part = rms_back(r.source[i, team.core].astype(F32), r.gain[0:1, :], ex.total(i))
        r.gain_grad[...] += gain_part
        ex.join(i, r.input_grad, (r.d_residual[i] + part).astype(BF16))

    def leave(i):
        ex.join_copy(i, r.input_grad).wait_recv()
        if early:
            copy = send_to(r.input_grad.at[i], r.grad_here.at[i], r.early_sems[0].at[i], r.early_sems[1].at[i], opposite)
            copies.append((jnp.logical_and(team.core == 0, team.place == owner(i)), copy))
            pl.when(copies[-1][0])(copy.start)

    copies = []
    receive(0)
    for i in range(1, PIECES):
        receive(i)
        leave(i - 1)
    leave(PIECES - 1)
    place = lax.broadcasted_iota(jnp.int32, (GAIN_ROWS, LH), 0)
    nothing = jnp.zeros((GAIN_ROWS, LH), F32)
    for chip in range(count):
        columns = slice(chip * span, (chip + 1) * span)
        rows_of = slice(chip * stride + depth, (chip + 1) * stride)
        gains = [grad[:, columns] for grad in (r.gain_grad, r.mlp_gain)]
        if span < LH:
            gains = [jnp.concatenate([part, jnp.zeros((1, LH - span), F32)], axis=1) for part in gains]
        gains = jnp.where(place == 0, gains[0], jnp.where(place == 1, gains[1], nothing))
        r.g_latent[0, rows_of, :] = gains.astype(BF16)
        for piece in range(1, pieces):
            r.g_latent[piece, rows_of, :] = nothing.astype(BF16)
    r.flush(r.g_latent)
    ex.finish(r.input_grad, False)
    r.flush(r.input_grad)
    beside.finish()
    for active, copy in copies:
        pl.when(active)(copy.wait)


class Part:
    def __init__(self, block):
        self.block = block.reshape((2,) + pieces_of(block[: block.shape[0] // 2]).shape)
        self.shape, self.dtype = self.block.shape[1:], block.dtype


def named_call(kernel, number, ins=(), lazy=(), far=(), outs=(), late=(), far_outs=(), scratch=()):
    groups = [dict(group) for group in (ins, lazy, far, outs, late, far_outs, scratch)]

    def listed(group):
        return [(k, v if isinstance(v, list) else [v], isinstance(v, list)) for k, v in group.items()]

    groups = [listed(group) for group in groups]
    ins, lazy, far, outs, late, far_outs, scratch = groups
    vmem, anywhere = pl.BlockSpec(memory_space=pltpu.VMEM), pl.BlockSpec(memory_space=pl.ANY)

    def flat(*parts):
        return [value for part in parts for _, values, _ in part for value in values]

    stages = [pltpu.VMEM(x.shape, x.dtype) for x in flat(lazy)] + [pltpu.VMEM(*x) for x in flat(late)]
    lazy_count, late_count = len(flat(lazy)), len(flat(late))

    def body(*refs):
        refs = list(refs)

        def take(count):
            taken, refs[:] = refs[:count], refs[count:]
            return taken

        named = {}

        def name(part, taken):
            for key, values, is_list in part:
                mine, taken = taken[: len(values)], taken[len(values) :]
                named[key] = mine if is_list else mine[0]

        name(ins, take(len(flat(ins))))
        lazy_refs = take(lazy_count)
        name(far, take(len(flat(far))))
        name(outs, take(len(flat(outs))))
        late_refs = take(late_count)
        name(far_outs, take(len(flat(far_outs))))
        lazy_held, late_held = take(lazy_count), take(late_count)
        in_sem, out_sem = take(1)[0], take(1)[0]
        name(lazy, lazy_held)
        name(late, late_held)
        name(scratch, take(len(flat(scratch))))
        sequence = lax.axis_index(TEN) // (lax.axis_size(TEN) // 2)
        parts = [isinstance(value, Part) for value in flat(lazy)]
        lazy_refs = [ref.at[sequence] if part else ref for ref, part in zip(lazy_refs, parts)]
        arrive = {
            id(held): pltpu.make_async_copy(ref, held, in_sem.at[k])
            for k, (ref, held) in enumerate(zip(lazy_refs, lazy_held))
        }
        leave = {
            id(held): pltpu.make_async_copy(held, ref, out_sem.at[k])
            for k, (ref, held) in enumerate(zip(late_refs, late_held))
        }
        for copy in arrive.values():
            copy.start()

        def ready(*buffers):
            for buffer in buffers:
                arrive[id(buffer)].wait()

        def flush(*buffers):
            for buffer in buffers:
                leave[id(buffer)].start()

        kernel(types.SimpleNamespace(ready=ready, flush=flush, **named))
        for copy in leave.values():
            copy.wait()

    results = pl.pallas_call(
        body,
        in_specs=[vmem] * len(flat(ins)) + [anywhere] * len(flat(lazy, far)),
        out_specs=[vmem] * len(flat(outs)) + [anywhere] * len(flat(late, far_outs)),
        out_shape=[jax.ShapeDtypeStruct(*x) for x in flat(outs, late, far_outs)],
        scratch_shapes=stages + [DMA((max(1, lazy_count),)), DMA((max(1, late_count),))] + flat(scratch),
        compiler_params=pltpu.CompilerParams(
            collective_id=number, has_side_effects=number is not None, vmem_limit_bytes=VMEM_LIMIT
        ),
        cost_estimate=pl.CostEstimate(flops=LINK_FLOPS, bytes_accessed=2**20, transcendentals=0),
    )(*[value.block if isinstance(value, Part) else value for value in flat(ins, lazy, far)])
    named, results = {}, list(results)
    for key, values, is_list in outs + late + far_outs:
        mine, results = results[: len(values)], results[len(values) :]
        named[key] = mine if is_list else mine[0]
    return types.SimpleNamespace(**named)


def forward_kernel(layer, r):
    team = Team()
    plane = Plane()
    core = lax.axis_index(SEC)
    holder = core == layer
    taker = jnp.logical_not(holder)
    across = across_device()
    ex_a, ex_b = Exchange(team, r.ex_a), Exchange(team, r.ex_b)
    greet(team.partners() + plane.partners() + ([across] if layer == 0 else []))
    rows, width = r.queries.shape
    model = r.w_latent.shape[0]
    size = rows // PIECES
    feeds = range(3)

    own_copies = [pltpu.make_async_copy(r.own_feed[k], r.feed[k], r.own_sem.at[k]) for k in feeds]
    for copy in own_copies:
        pl.when(holder)(copy.start)
    gathers = [
        Gather(
            plane, k, r.feed[k], r.gather_sent.at[k], r.gather_here.at[k], taker,
            r.pieces[k] if layer else None, r.piece_sem.at[k],
        )
        for k in feeds
    ]

    def cross(k, source, target):
        return send_to(source, target, r.cross_sent.at[k], r.cross_here.at[k], across)

    if layer == 0:
        come = [cross(1 + k, r.own_feed[k].at[plane.me], r.come[k]) for k in feeds]
        next_feed = [cross(5 + k, r.own_feed[k].at[plane.me], r.feed_next[k]) for k in feeds]
        mine = cross(0, r.own_packed.at[plane.me], r.packed.at[plane.me])
        small = [
            send_to(r.pass_latent, r.far_latent, r.small_sent.at[0], r.small_here.at[0], team.other),
            send_to(r.own_gains, r.far_gains, r.small_sent.at[1], r.small_here.at[1], team.other),
        ]
        next_packed = cross(4, r.own_packed.at[plane.me], r.packed_next.at[plane.me])
        depth = r.packed.shape[1] // 2
        halves = [slice(0, depth), slice(depth, 2 * depth)]
        packed_gathers, next_gathers = (
            [Gather(plane, k, whole, sent.at[k], here.at[k], rows=half) for k, half in enumerate(halves)]
            for whole, sent, here in (
                (r.packed, r.packed_sent, r.packed_here), (r.packed_next, r.next_sent, r.next_here)
            )
        )
        own_packed = [
            pltpu.make_async_copy(r.own_packed, target, r.own_sem.at[3]) for target in (r.packed, r.packed_next)
        ]
        pl.when(holder)(mine.start)
        pl.when(holder)(own_packed[0].start)
        pl.when(taker)(own_packed[1].start)
        for copy in small:
            copy.start()
        for copy in small:
            copy.wait()
    else:
        for gather in gathers:
            gather.start()

    def next_come(k):
        @pl.when(holder)
        def _():
            come[k - 1].wait_send()
            come[k].start()

    def take_come(k):
        @pl.when(taker)
        def _():
            come[k].wait_recv()
            r.feed[k][plane.me] = r.come[k][...]

        gathers[k].start()

    gains = jnp.where(holder, r.own_gains[...], r.far_gains[...])
    r.gains[...] = gains
    r.w_latent[...] = jnp.where(holder, r.own_latent[...], r.far_latent[...])
    r.flush(r.w_latent)
    r.ready(r.source)

    def norm(i):
        block = r.source[i].reshape(size, model).astype(F32)
        r.attn_in[piece_rows(i, rows), :] = (block * reciprocal_rms(block) * gains[0:1]).astype(BF16)

    if layer == 0:
        each_piece(norm)

        @pl.when(taker)
        def _():
            mine.wait_recv()
            for gather in packed_gathers:
                gather.start()
            for gather in packed_gathers:
                gather.middle()
            for gather in packed_gathers:
                gather.finish()

        @pl.when(holder)
        def _():
            own_packed[0].wait()
            mine.wait_send()
            come[0].start()

        r.flush(r.packed)
        take_come(0)
    else:
        r.ready(r.packed)
    weights = r.packed[...].reshape(2 * model + 2 * LH, width)

    def project(i):
        at = piece_rows(i, rows)
        block = r.attn_in[at, :]
        r.queries[at, :] = mm(block, weights[:model]).astype(BF16)
        latents = mm(block, r.w_latent[...]).astype(BF16)
        r.latents[at, :] = latents
        r.keys[at, :] = mm(latents, weights[model : model + LH]).astype(BF16)
        r.values[at, :] = mm(latents, weights[model + LH : model + 2 * LH]).astype(BF16)

    w_out = [
        weights[model + 2 * LH + start : model + 2 * LH + start + width] for start in range(0, model, width)
    ]
    for i in range(PIECES):
        if layer == 1:
            norm(i)
        project(i)
        attend_rows(i * size, r.queries, r.keys, r.values, r.heads_out, r.norms)
        heads = r.heads_out[i * size : (i + 1) * size, :]
        ex_a.push(i, jnp.concatenate([mm(heads, block) for block in w_out], axis=1))
        if i == 0 and layer == 0:
            next_come(1)
        if i:
            ex_a.combine(i - 1)
        if i == 1:
            gathers[0].middle()
        if i == 2 and layer == 0:
            next_come(2)
            take_come(1)
    ex_a.combine(PIECES - 1)
    r.flush(r.attn_in, r.queries, r.latents, r.keys, r.values, r.heads_out, r.norms)
    if layer == 0:

        @pl.when(taker)
        def _():
            next_packed.start()


    def receive(i):
        block = r.source[i, core].astype(F32) + ex_a.total(i)
        r.residual[i] = block
        ex_a.join(i, r.mlp_in, (block * reciprocal_rms(block) * gains[1:2]).astype(BF16))

    def feed(i):
        ex_a.join_copy(i, r.mlp_in).wait_recv()
        at = piece_rows(i, rows)
        block = r.mlp_in[i].reshape(size, model)
        shape = (r.hidden.shape[1], model)
        gate = mm(block, r.feed[0][...].reshape(shape), 1, 1)
        up = mm(block, r.feed[1][...].reshape(shape), 1, 1)
        hidden = (jax.nn.silu(gate) * up).astype(BF16)
        r.gate[at, :] = gate
        r.up[at, :] = up
        r.hidden[at, :] = hidden
        ex_b.push(i, mm(hidden, r.feed[2][...].reshape(shape)))

    receive(0)
    gathers[1].middle()
    if layer == 0:
        take_come(2)

        @pl.when(taker)
        def _():
            for copy in next_feed:
                copy.start()

    receive(1)
    gathers[2].middle()

    @pl.when(holder)
    def _():
        for copy in own_copies:
            copy.wait()

    for gather in gathers:
        gather.finish()
    r.flush(*r.feed)
    feed(0)
    if layer == 0:

        @pl.when(holder)
        def _():
            next_packed.wait_recv()
            for gather in next_gathers:
                gather.start()

    def steady(i, _):
        receive(i)
        feed(i - 1)
        ex_b.combine(i - 2)
        return 0

    lax.fori_loop(2, PIECES, steady, 0)
    feed(PIECES - 1)
    ex_b.combine(PIECES - 2)
    ex_b.combine(PIECES - 1)
    ex_a.finish(r.mlp_in, False)
    r.flush(r.residual, r.mlp_in, r.gate, r.up, r.hidden)
    if layer == 0:

        @pl.when(holder)
        def _():
            for gather in next_gathers:
                gather.middle()
            for gather in next_gathers:
                gather.finish()

        @pl.when(taker)
        def _():
            own_packed[1].wait()
            next_packed.wait_send()

        r.flush(r.packed_next)
    each_piece(lambda i: ex_b.join(i, r.output, (r.residual[i] + ex_b.total(i)).astype(BF16)))
    ex_b.finish(r.output)
    r.flush(r.output)

    if layer == 0:

        @pl.when(holder)
        def _():
            come[2].wait_send()
            for copy in next_feed:
                copy.wait_recv()

        @pl.when(taker)
        def _():
            for copy in next_feed:
                copy.wait_send()


def finish_kernel(groups, r):
    plane = Plane()
    team = Team()
    late = len(r.late)
    scatters = [Scatter(plane, k, r.late[k], *r.scatter[5 * k : 5 * k + 5]) for k in range(late)]
    count = lax.axis_size(TEN)
    z = lax.axis_index(TEN)
    core = lax.axis_index(SEC)
    first, second = core == 0, core == 1
    across = across_device()
    opposite = {TEN: across[TEN]}
    chips = [lax.rem(z + step, count) for step in range(1, count)]
    greet(plane.partners() + [across] + [{TEN: chip} for chip in chips])
    for scatter in scatters:
        scatter.start()
    sources = r.pieces + r.leave
    cross_sent, cross_here = r.cross_sems
    crosses = [
        send_to(source, r.come[k], cross_sent.at[k], cross_here.at[k], across) for k, source in enumerate(sources)
    ]

    @pl.when(second)
    def _():
        for copy in crosses[:FEED]:
            copy.start()

    outputs = Outputs(r, [[], [0, 1]])
    outputs.start()
    gather_sent, gather_here, gather_own = r.gather_sems
    gathers = [
        Gather(
            plane, k, whole, gather_sent.at[k], gather_here.at[k], first if k < FEED else None,
            r.total[k], gather_own.at[k],
        )
        for k, whole in enumerate(r.wholes)
    ]
    last = FEED + late - 1

    def arrive(k):
        crosses[k].wait_recv()
        return (sources[k][...].astype(F32) + r.come[k][...].astype(F32)).astype(BF16)

    def take_cross(k):
        @pl.when(first)
        def _():
            r.total[k][...] = arrive(k)

        gathers[k].start()

    scatters[0].middle()
    take_cross(0)
    for scatter in scatters[1:]:
        scatter.middle()
    for k, scatter in enumerate(scatters):
        r.leave[k][...] = scatter.total().astype(BF16)
        if k == 0:
            gathers[0].middle()
        pl.when(second)(crosses[FEED + k].start)
    take_cross(1)
    take_cross(2)
    gathers[1].middle()
    gathers[2].middle()

    @pl.when(first)
    def _():
        for k in range(FEED, last):
            r.total[k][...] = arrive(k)
        r.held[...] = arrive(last).reshape(r.held.shape)

    @pl.when(second)
    def _():
        for k in range(FEED, last):
            r.total[k][...] = r.done[k - FEED][...]
        r.held[...] = r.done[late - 1][...].reshape(r.held.shape)

    for k in range(FEED, last):
        gathers[k].start()
    block_sent, block_here = r.block_sems

    def block(step, chip, slot):
        return send_to(r.held.at[chip], r.slots.at[slot], block_sent.at[step], block_here.at[slot], {TEN: chip})

    for step, chip in enumerate(chips):
        block(step, chip, z).start()
    r.slots[z] = r.held[z]
    for step, chip in enumerate(chips):
        block(step, chip, chip).wait_recv()
    shares = [r.slots[shard].astype(F32) for shard in range(count)]
    sums = [sum(s for s, g in zip(shares, groups) if g == group) for group in range(KVH)]
    gain_rows = sums[0]
    for extra in sums[1:]:
        gain_rows = gain_rows + extra
    depth = gain_rows.shape[0] - GAIN_ROWS
    gain_rows = gain_rows * (2.0 / count)
    blocks = [jnp.concatenate([part[:depth], gain_rows[depth:]], axis=0) for part in sums]
    r.total[last][...] = jnp.concatenate(blocks, axis=1).astype(BF16)
    gathers[last].start()
    for k in range(FEED, last + 1):
        gathers[k].middle()

    for gather in gathers:
        gather.finish()
    for scatter in scatters:
        scatter.drain()
    for step, chip in enumerate(chips):
        block(step, chip, z).wait_send()

    @pl.when(second)
    def _():
        for copy in crosses:
            copy.wait_send()

    outputs.finish()


def finish(number, groups, feed, late, done, grads):
    dp, count = lax.axis_size(DP), lax.axis_size(TEN)
    depth = done[-1].shape[0] // count
    shapes = [part.shape for part in list(feed) + list(done)]
    totals = shapes[:-1] + [(depth, KVH * LH)]
    items = len(shapes)
    blocks = pltpu.VMEM((count, depth, LH), BF16)
    return named_call(
        functools.partial(finish_kernel, groups),
        number,
        ins=dict(pieces=list(feed), done=list(done)),
        far=dict(late=list(late), shares=[], spreads=grads),
        far_outs=dict(wholes=[((dp,) + total, BF16) for total in totals], spreads_here=[(grad.shape, BF16) for grad in grads]),
        scratch=dict(
            scatter=[item for load in late for item in scatter_scratch(load)],
            come=[pltpu.VMEM(shape, BF16) for shape in shapes],
            leave=[pltpu.VMEM(part.shape, BF16) for part in done],
            total=[pltpu.VMEM(total, BF16) for total in totals],
            slots=blocks,
            held=blocks,
            cross_sems=[DMA((items,)), DMA((items,))],
            gather_sems=[DMA((items, 3)), DMA((items, dp)), DMA((items,))],
            block_sems=[DMA((count,)), DMA((count,))],
            spread_sems=[DMA((count // 2, PIECES)), DMA((PIECES,))] * len(grads),
        ),
    )


def emit_kernel(r):
    core = lax.axis_index(SEC)
    sequence = lax.axis_index(TEN) // (lax.axis_size(TEN) // 2)
    wide = []
    for k in range(FEED):
        for layer, source in enumerate((r.zero[k], r.one[k])):
            copy = pltpu.make_async_copy(source, r.wide[k], r.wide_here.at[k])
            pl.when(core == layer)(copy.start)
            if layer == 0:
                wide.append(copy)
    placed = []
    place = lax.rem(lax.axis_index(TEN), lax.axis_size(TEN) // 2)
    for k, (mine, share, spread, out) in enumerate(
        ((r.outs, r.outs_share, r.outs_spread, r.layer_out), (r.grads, r.grads_share, r.grads_spread, r.input_grad))
    ):
        for piece in range(PIECES):
            passed = place == owner(piece)
            for side, to in enumerate((sequence, 1 - sequence)):
                at = (2 * k + side, piece)
                held = r.held.at[at]
                for layer in range(2):
                    sources = [(mine, True)] if side == 0 else [(share, passed), (spread, jnp.logical_not(passed))]
                    for blocks, active in sources:
                        come = pltpu.make_async_copy(blocks[layer].at[piece], held, r.held_here.at[at])
                        pl.when(jnp.logical_and(core == layer, active))(come.start)
                placed.append((come, pltpu.make_async_copy(held, out.at[to, piece], r.placed.at[at])))
    for k in range(FEED):
        wide[k].wait()
        r.g_wide[k][...] = r.wide[k][...].reshape(r.g_wide[k].shape).astype(F32)
        r.flush(r.g_wide[k])
    for come, leave in placed:
        come.wait()
        leave.start()
    r.ready(r.low, r.high, r.latent)
    model = r.g_query.shape[0]
    columns = r.g_query.shape[1]
    low = r.low[...].reshape(-1, columns).astype(F32)
    high = r.high[...].reshape(-1, columns).astype(F32)
    r.g_query[...] = low[:model]
    r.g_key_up[...] = low[model:]
    r.g_value_up[...] = high[:LH]
    r.g_out[...] = jnp.concatenate(
        [high[start : start + columns] for start in range(LH, LH + model, columns)], axis=1
    )
    depth = r.latent.shape[1] - GAIN_ROWS
    r.g_latent[...] = r.latent[:, :depth, :].astype(F32).reshape(r.g_latent.shape)
    r.gains[...] = r.latent[0, depth:, :LH].astype(F32)
    r.flush(r.g_query, r.g_key_up, r.g_value_up, r.g_out, r.g_latent, r.gains)
    for come, leave in placed:
        leave.wait()


def emit(outs, outs_share, outs_spread, grads, grads_share, grads_spread, zero, one, parts):
    low, high, latent = parts
    pieces, depth, model = zero[0].shape
    columns = low.shape[2]
    split = pieces * (latent.shape[1] - GAIN_ROWS)
    both = ((2,) + outs[0].shape, BF16)
    out = named_call(
        emit_kernel,
        None,
        lazy=dict(low=low, high=high, latent=latent),
        far=dict(
            outs=outs, outs_share=outs_share, outs_spread=outs_spread,
            grads=grads, grads_share=grads_share, grads_spread=grads_spread,
            zero=zero, one=one,
        ),
        late=dict(
            g_query=((model, columns), F32),
            g_key_up=((LH, columns), F32),
            g_value_up=((LH, columns), F32),
            g_out=((columns, model), F32),
            g_latent=((split, KVH * LH), F32),
            gains=((GAIN_ROWS, LH), F32),
            g_wide=[((pieces * depth, model), F32)] * FEED,
        ),
        far_outs=dict(layer_out=both, input_grad=both),
        scratch=dict(
            placed=DMA((4, PIECES)),
            held_here=DMA((4, PIECES)),
            held=pltpu.VMEM((4,) + outs[0].shape, BF16),
            wide_here=DMA((FEED,)),
            wide=[pltpu.VMEM((pieces, depth, model), BF16)] * FEED,
        ),
    )
    wide = [part for part in out.g_wide]
    rest = (out.g_query, out.g_key_up, out.g_value_up, out.g_out, out.g_latent, out.gains)
    return (out.layer_out, out.input_grad, *wide, *rest)


def pieces_of(block):
    if isinstance(block, Part) or len(block.shape) == 4:
        return block
    return block.reshape(PIECES, 2, block.shape[0] // PIECES // 2, block.shape[1])


def shapes_of(rows, model):
    return (PIECES, 2, rows // PIECES // 2, model), (PIECES, rows // PIECES // 2, model)


def forward_layer(layer, number, source, own_feed, own_packed=None, packed=None, pieces_in=(), **small):
    rows, model = LEN, own_feed[0].shape[2]
    split, own = shapes_of(rows, model)
    pieces, depth, width = (packed if own_packed is None else own_packed).shape
    wide = (rows, pieces * own_feed[0].shape[1])
    pair = min(2 * HD, width)
    narrow = ((rows, width), BF16)
    outs = dict(gains=((2, model), F32))
    late = dict(
        w_latent=((model, LH), BF16),
        attn_in=((rows, model), BF16),
        queries=narrow,
        latents=((rows, LH), BF16),
        keys=narrow,
        values=narrow,
        heads_out=narrow,
        norms=((width // pair, pair // HD, rows), F32),
        residual=(own, F32),
        mlp_in=(split, BF16),
        gate=(wide, F32),
        up=(wide, F32),
        hidden=(wide, BF16),
        output=(split, BF16),
        feed=[(w.shape, BF16) for w in own_feed],
    )
    scratch = dict(
        ex_a=exchange_scratch(rows, model),
        ex_b=exchange_scratch(rows, model),
        own_sem=DMA((4,)),
        piece_sem=DMA((3,)),
        gather_sent=DMA((3, 3)),
        gather_here=DMA((3, pieces)),
        cross_sent=DMA((8,)),
        cross_here=DMA((8,)),
    )
    far_outs = dict()
    lazy, far = dict(source=pieces_of(source)), dict(own_feed=own_feed)
    if layer == 0:
        far.update(own_packed=own_packed)
        far_outs.update(feed_next=[(w.shape[1:], BF16) for w in own_feed])
        outs.update(far_latent=((model, LH), BF16), far_gains=((2, model), F32))
        late.update(packed=((pieces, depth, width), BF16), packed_next=((pieces, depth, width), BF16))
        scratch.update(
            come=[pltpu.VMEM(w.shape[1:], BF16) for w in own_feed],
            small_sent=DMA((2,)),
            small_here=DMA((2,)),
            packed_sent=DMA((2, 3)),
            packed_here=DMA((2, pieces)),
            next_sent=DMA((2, 3)),
            next_here=DMA((2, pieces)),
        )
    else:
        lazy.update(packed=packed)
        small.update(pieces=list(pieces_in))
    return named_call(
        functools.partial(forward_kernel, layer),
        number,
        ins=small,
        lazy=lazy,
        far=far,
        outs=outs,
        late=late,
        far_outs=far_outs,
        scratch=scratch,
    )


def feed_layer_back(number, upstream, result, beside):
    rows, model = result.attn_in.shape
    split, half = shapes_of(rows, model)
    columns = result.queries.shape[1]
    wide = pltpu.VMEM(result.hidden.shape, BF16)
    narrow = ((rows, columns), BF16)
    total = pltpu.VMEM((rows, columns), F32)
    return named_call(
        functools.partial(feed_back, beside.shared),
        number,
        ins=dict(gain=result.gains),
        lazy=dict(
            upstream=pieces_of(upstream),
            feed=result.feed,
            gate=result.gate,
            up=result.up,
            mlp_in=result.mlp_in.reshape(rows, model),
            hidden=result.hidden,
            residual=result.residual,
            packed=result.packed,
            queries=result.queries,
            keys=result.keys,
            values=result.values,
            heads_out=result.heads_out,
            norms=result.norms,
        ),
        far=beside.far,
        outs=dict(gain_grad=((1, model), F32), **beside.outs),
        late=dict(
            d_residual=(half, F32),
            res_grad=(split, BF16),
            grads=[(w.shape, BF16) for w in result.feed],
            d_queries=narrow,
            d_keys=narrow,
            d_values=narrow,
            d_latents=((rows, LH), BF16),
        ),
        far_outs=beside.far_outs,
        scratch=dict(
            exchange=exchange_scratch(rows, model),
            d_gate=wide,
            d_up=wide,
            d_heads=pltpu.VMEM((rows, columns), BF16),
            key_total=total,
            value_total=total,
            **beside.scratch,
        ),
    )


def attend_layer_back(number, source, result, back, beside, early=False):
    rows, model = result.attn_in.shape
    pieces, depth, width = result.packed.shape
    out = named_call(
        functools.partial(attend_in_back, beside.shared, early),
        number,
        ins=dict(gain=result.gains, mlp_gain=back.gain_grad),
        lazy=dict(
            d_queries=back.d_queries,
            d_latents=back.d_latents,
            packed=result.packed,
            w_latent=result.w_latent,
            attn_in=result.attn_in,
            latents=result.latents,
            heads_out=result.heads_out,
            d_keys=back.d_keys,
            d_values=back.d_values,
            res_grad=back.res_grad,
            source=pieces_of(source),
            d_residual=back.d_residual,
        ),
        far=beside.far,
        outs=beside.outs,
        late=dict(
            input_grad=(shapes_of(rows, model)[0], BF16),
            g_packed=[((pieces, depth // 2, width), BF16)] * 2,
            g_latent=((pieces, model // pieces + lax.axis_size(TEN) * GAIN_ROWS, LH), BF16),
        ),
        far_outs=dict(grad_here=(shapes_of(rows, model)[0], BF16), **beside.far_outs) if early else beside.far_outs,
        scratch=dict(
            exchange=exchange_scratch(rows, model),
            grads=pltpu.VMEM((pieces * depth, width), BF16),
            gain_grad=pltpu.VMEM((1, model), F32),
            early_sems=[DMA((PIECES,)), DMA((PIECES,))],
            **beside.scratch,
        ),
    )
    out.parts = out.g_packed + [out.g_latent]
    return out


def tie(*arrays):
    return lax.optimization_barrier(arrays)


def local(
    inputs,
    out_grad,
    w_query,
    w_latent,
    w_key_up,
    w_value_up,
    w_out,
    w_gate,
    w_up,
    w_down,
    norm_attn,
    norm_mlp,
):
    at = Place()
    model = inputs.shape[1]
    heads = w_query.shape[2] // HD

    def group_of(shard):
        return shard * heads // (QH // KVH)

    opposite_z = (at.z + at.team) % at.count

    def latent_of(shard):
        return lax.dynamic_slice_in_dim(w_latent[0], group_of(shard) * LH, LH, 1)

    own_feed = [by_dp(w) for w in (w_gate[0].T, w_up[0].T, w_down[0])]
    own_packed = by_dp(pack_attention(w_query[0], w_key_up[0], w_value_up[0], w_out[0]))
    own_gains = jnp.concatenate([norm_attn, norm_mlp], axis=0)
    own_latent = latent_of(at.z)
    source = Part(inputs)
    zero = forward_layer(
        0,
        0,
        source,
        own_feed,
        own_packed=own_packed,
        own_gains=own_gains,
        own_latent=own_latent,
        pass_latent=latent_of(opposite_z),
    )
    first_out = zero.output
    one = forward_layer(
        1,
        1,
        first_out,
        own_feed,
        packed=zero.packed_next,
        pieces_in=zero.feed_next,
        own_gains=own_gains,
        far_gains=zero.far_gains,
        own_latent=own_latent,
        far_latent=zero.far_latent,
    )
    one.packed = zero.packed_next
    second_out = one.output

    back = feed_layer_back(2, Part(out_grad), one, Beside(shares=[(first_out, 0)]))
    first_share = back.shares_here[0]
    beside = Beside(back.grads, shares=[(second_out, 1)], spreads=[(first_share, 0)])
    above = attend_layer_back(3, first_out, one, back, beside)
    second_share, second_grad, first_spread = above.shares_here[0], above.input_grad, above.spreads_here[0]
    beside = Beside(above.parts, above.sums, True, spreads=[(second_share, 1)])
    back = feed_layer_back(4, second_grad, zero, beside)
    wide_one, second_spread = back.wholes, back.spreads_here[0]
    beside = Beside(back.grads, back.sums, shares=[(second_grad, 1)])
    below = attend_layer_back(5, source, zero, back, beside, True)
    first_grad, grad_share = below.input_grad, below.shares_here[0]
    groups = tuple(group_of(shard) for shard in range(at.count))
    last = finish(6, groups, below.sums, below.parts, below.totals, [below.grad_here, grad_share])
    *wide_zero, low_part, high_part, latent = last.wholes
    out = emit(
        [first_out, second_out],
        [first_share, second_share],
        [first_spread, second_spread],
        [first_grad, second_grad],
        [below.grad_here, grad_share],
        last.spreads_here,
        wide_zero,
        wide_one,
        [low_part, high_part, latent],
    )
    layer_out, input_grad, g_gate, g_up, g_down, g_query, g_key_up, g_value_up, g_out, g_latent, gains = out
    gains = gains[:, : model // at.count]
    layer_out, input_grad = (both.reshape(1, 2 * LEN, model) for both in (layer_out, input_grad))
    return (
        layer_out,
        input_grad,
        g_query[None],
        g_latent[None],
        g_key_up[None],
        g_value_up[None],
        g_out[None],
        g_gate.T[None],
        g_up.T[None],
        g_down[None],
        gains[0:1],
        gains[1:2],
    )


def solution(mesh):
    columns = P(SEC, None, TEN)
    rows = P(SEC, TEN, None)
    return jax.shard_map(
        local,
        mesh=mesh,
        in_specs=(
            P(DP, None),
            P(DP, None),
            columns,
            P(SEC, None, None),
            columns,
            columns,
            rows,
            columns,
            columns,
            rows,
            P(SEC, None),
            P(SEC, None),
        ),
        out_specs=(
            P(SEC, DP, None),
            P(SEC, DP, None),
            columns,
            rows,
            columns,
            columns,
            rows,
            columns,
            columns,
            rows,
            P(SEC, TEN),
            P(SEC, TEN),
        ),
        check_vma=False,
    )
```
